32 devices in a mesh: seq: 8 (over y, x, core), wshard: 4 (over z).
Axes of the slice: x: 2, y: 2, z: 4, core: 2. Of those that a mesh axis runs over, the one named last changes fastest.
Arguments:
- hidden: bfloat16 [2, 4, 2048, 1536], P(None, 'wshard', 'seq'), may hold values from -6 to 6
- lengths: int32 [2, 4], P(None, 'wshard'), may hold values from 512 to 2048, as said below
- out_grad: bfloat16 [2, 4, 2048, 1536], P(None, 'wshard', 'seq'), may hold values from -6 to 6
- norm_gain: bfloat16 [1536], P('wshard'), may hold values from 0.099609375 to 1.8984375
- in_weight: bfloat16 [1536, 6448], P('wshard'), may hold values from -0.15625 to 0.15625
- conv_weight: bfloat16 [3328, 4], P('wshard'), may hold values from -0.5 to 0.5
- conv_bias: bfloat16 [3328], P('wshard'), may hold values from -0.5 to 0.5
- dt_bias: bfloat16 [48], P('wshard'), may hold values from -8 to -3
- a_log: bfloat16 [48], P('wshard'), may hold values from -1 to 1
- skip_gain: bfloat16 [48], P('wshard'), may hold values from 0.5 to 1.5
- gated_gain: bfloat16 [3072], P('wshard'), may hold values from 0.099609375 to 1.8984375
- out_weight: bfloat16 [3072, 1536], P('wshard'), may hold values from -0.109375 to 0.109375
Outputs:
- output: bfloat16 [2, 4, 2048, 1536], P(None, 'wshard', 'seq')
- input_grad: bfloat16 [2, 4, 2048, 1536], P(None, 'wshard', 'seq')
- norm_gain_grad: float32 [1536], P('wshard')
- in_weight_grad: float32 [1536, 6448], P('wshard')
- conv_weight_grad: float32 [3328, 4], P('wshard')
- conv_bias_grad: float32 [3328], P('wshard')
- dt_bias_grad: float32 [48], P('wshard')
- a_log_grad: float32 [48], P('wshard')
- skip_gain_grad: float32 [48], P('wshard')
- gated_gain_grad: float32 [3072], P('wshard')
- out_weight_grad: float32 [3072, 1536], P('wshard')
The draws below stay inside these ranges and needn't reach their ends.
Inputs may be any that keep to these rules, and one draw needn't show every extreme that they name: `lengths`: for every sequence index, one micro-batch drawn from the seed has length 2048.
All inputs are finite; a program needn't handle non-finite values.
Results may differ from the reference program's by a relative error of at most 0.011.
Values may be sent and summed in bfloat16 or wider, within the bound.
A program may use at most 256 MiB of HBM per device.

```python
import jax
import jax.numpy as jnp
from jax import lax

D = 1536
HEADS = 48
CONV = 4
STRETCH = 256
MICRO = 2
D_INNER = 3072
CONV_CH = 3328
IN_W = 6448
SEQLEN = 2048
SEQS = 4
MIN_LEN = 512


def draw_lengths(key, part):
    key = jax.random.fold_in(key, 7)
    first_key, second_key = jax.random.split(key)
    drawn = jax.random.randint(first_key, (MICRO, SEQS), MIN_LEN, SEQLEN + 1)
    chosen = jax.random.randint(second_key, (SEQS,), 0, MICRO)
    picked = jnp.arange(MICRO)[:, None] == chosen[None, :]
    return jnp.where(picked, SEQLEN, drawn).astype(jnp.int32)


def level_of(own_key, extent, cuts, low, high):
    def one(position, blocks):
        steps = jax.random.uniform(jax.random.fold_in(jax.random.fold_in(own_key, 6), position), (blocks,), jnp.float32, low / len(cuts), high / len(cuts))
        return jnp.repeat(jnp.exp(steps), extent[position] // blocks).reshape((-1,) + (1,) * (len(extent) - position - 1))

    level = one(*cuts[0])
    for cut in cuts[1:]:
        level = level * one(*cut)
    return level


def gaussian(own_key, shape, width, limit, cuts=(), kind=jnp.bfloat16):
    entries = width * jax.random.normal(own_key, shape, jnp.float32)
    if cuts:
        entries = entries * level_of(own_key, shape, cuts, -0.22, 0.18)
    return jnp.clip(entries, -limit, limit).astype(kind)


def setup_inputs(seed: int = 0) -> dict:
    streams_of = jax.random.split(jax.random.key(seed), 13)
    return {
        "hidden": gaussian(streams_of[0], (MICRO, SEQS, SEQLEN, D), 1.0, 6.0, ((1, 4), (2, 8))),
        "lengths": draw_lengths(jax.random.fold_in(streams_of[12], 71), 0),
        "out_grad": gaussian(streams_of[2], (MICRO, SEQS, SEQLEN, D), 1.0, 6.0, ((1, 4), (2, 8))),
        "norm_gain": jnp.clip(1.0 + 0.18 * jax.random.normal(streams_of[3], (D,), jnp.float32), 0.099609375, 1.8984375).astype(jnp.bfloat16),
        "in_weight": gaussian(streams_of[4], (D, IN_W), D ** -0.5, 0.15625, ((0, 4),)),
        "conv_weight": jnp.clip(jax.random.uniform(streams_of[5], (CONV_CH, CONV), jnp.float32, -0.5, 0.5) * level_of(streams_of[5], (CONV_CH, CONV), ((0, 4),), -0.4, 0.0), -0.5, 0.5).astype(jnp.bfloat16),
        "conv_bias": jnp.clip(jax.random.uniform(streams_of[6], (CONV_CH,), jnp.float32, -0.5, 0.5) * level_of(streams_of[6], (CONV_CH,), ((0, 4),), -0.4, 0.0), -0.5, 0.5).astype(jnp.bfloat16),
        "dt_bias": jnp.clip(-8.0 + 5.0 * jax.random.uniform(streams_of[7], (HEADS,), jnp.float32) ** level_of(streams_of[7], (HEADS,), ((0, 4),), -0.2, 0.2), -8.0, -3.0).astype(jnp.bfloat16),
        "a_log": jnp.clip(jax.random.uniform(streams_of[8], (HEADS,), jnp.float32, -1.0, 1.0) * level_of(streams_of[8], (HEADS,), ((0, 4),), -0.4, 0.0), -1.0, 1.0).astype(jnp.bfloat16),
        "skip_gain": jnp.clip(0.5 + 1.0 * jax.random.uniform(streams_of[9], (HEADS,), jnp.float32) ** level_of(streams_of[9], (HEADS,), ((0, 4),), -0.2, 0.2), 0.5, 1.5).astype(jnp.bfloat16),
        "gated_gain": jnp.clip(1.0 + 0.18 * jax.random.normal(streams_of[10], (D_INNER,), jnp.float32), 0.099609375, 1.8984375).astype(jnp.bfloat16),
        "out_weight": gaussian(streams_of[11], (D_INNER, D), D_INNER ** -0.5, 0.109375, ((0, 4),)),
    }


@jax.custom_vjp
def low(v):
    return lax.optimization_barrier(v.astype(jnp.bfloat16)).astype(jnp.float32)

@jax.custom_vjp
def low_back(v):
    return v

def low_keep(v):
    return (low(v), None)

def low_pass(kept, grad):
    return (grad,)

def back_keep(v):
    return (v, None)

def back_low(kept, grad):
    return (low(grad),)
low.defvjp(low_keep, low_pass)
low_back.defvjp(back_keep, back_low)
epsilon = 1e-05
highest = lax.Precision.HIGHEST

def rms_front(hidden_rows, gain):
    power = lax.optimization_barrier(jnp.mean(hidden_rows * hidden_rows, axis=-1, keepdims=True))
    return hidden_rows * lax.rsqrt(power + epsilon) * gain

def conv_act(padded, conv_w, conv_b):
    taps = conv_w.shape[1]
    rows_out = padded.shape[0] - taps + 1
    total = conv_b[None, :] + padded[0:rows_out] * conv_w[:, 0]
    for offset in range(1, taps):
        total = total + padded[offset:offset + rows_out] * conv_w[:, offset]
    return jax.nn.silu(total)

def gate_norm(values, gate_in, gain):
    gated = values * jax.nn.silu(gate_in)
    power = lax.optimization_barrier(jnp.mean(gated * gated, axis=-1, keepdims=True))
    return gated * lax.rsqrt(power + epsilon) * gain

def ssd_scan(x_heads, dt_raw, b_rows, c_rows, dt_shift, a_logs, skip, block_len):
    seq_length, head_count, head_size = x_heads.shape
    blocks = seq_length // block_len
    state_dim = b_rows.shape[1]
    steps_dt = jax.nn.softplus(dt_raw + dt_shift[None, :])
    log_decay = steps_dt * (-jnp.exp(a_logs))[None, :]
    causal = jnp.arange(block_len)[:, None] >= jnp.arange(block_len)[None, :]

    def advance(carry_state, pieces):
        x_blk, dt_blk, decay_blk, b_blk, c_blk = pieces
        cumulative = jnp.cumsum(decay_blk, axis=0)
        across = cumulative.T
        spans = across[:, :, None] - across[:, None, :]
        within = jnp.where(causal[None], jnp.exp(jnp.where(causal[None], spans, 0.0)), 0.0)
        scores = jnp.dot(c_blk, b_blk.T, precision=highest)
        weighted = x_blk * dt_blk[:, :, None]
        local_part = jnp.einsum('hij,jhp->ihp', within * scores[None], weighted, precision=highest)
        carried = jnp.exp(cumulative)[:, :, None] * jnp.einsum('in,hpn->ihp', c_blk, carry_state, precision=highest)
        to_end = jnp.exp(cumulative[-1][None, :] - cumulative)
        new_state = jnp.exp(cumulative[-1])[:, None, None] * carry_state + jnp.einsum('jhp,jn->hpn', weighted * to_end[:, :, None], b_blk, precision=highest)
        return (new_state, local_part + carried)
    pieces = (x_heads.reshape(blocks, block_len, head_count, head_size), steps_dt.reshape(blocks, block_len, head_count), log_decay.reshape(blocks, block_len, head_count), b_rows.reshape(blocks, block_len, state_dim), c_rows.reshape(blocks, block_len, state_dim))
    initial = jnp.zeros((head_count, head_size, state_dim), jnp.float32)
    last_state, results = lax.scan(jax.checkpoint(advance), initial, pieces)
    return results.reshape(seq_length, head_count, head_size) + skip[None, :, None] * x_heads

def layer(hidden_rows, valid, norm_g, in_w, conv_w, conv_b, dt_shift, a_logs, skip, gated_g, out_w):
    inner_dim = out_w.shape[0]
    head_count = dt_shift.shape[0]
    channels = conv_w.shape[0]
    state_dim = (channels - inner_dim) // 2
    seq_rows = hidden_rows.shape[0]
    normed = low(rms_front(hidden_rows, norm_g))
    projected = low_back(jnp.dot(normed, in_w, precision=highest))
    gate_in = projected[:, :inner_dim]
    conv_in = low(projected[:, inner_dim:inner_dim + channels])
    dt_raw = low_back(low(projected[:, inner_dim + channels:]))
    padded = jnp.concatenate([jnp.zeros((conv_w.shape[1] - 1, channels), jnp.float32), conv_in], axis=0)
    mixed = conv_act(padded, conv_w, conv_b)
    x_rows = low_back(low(mixed[:, :inner_dim]))
    b_rows = low(mixed[:, inner_dim:inner_dim + state_dim])
    c_rows = low(mixed[:, inner_dim + state_dim:])
    scanned = ssd_scan(x_rows.reshape(seq_rows, head_count, -1), dt_raw, b_rows, c_rows, dt_shift, a_logs, skip, STRETCH)
    scanned = low_back(low(scanned.reshape(seq_rows, inner_dim)))
    normed_out = low(gate_norm(scanned, gate_in, gated_g))
    branch = jnp.dot(normed_out, out_w, precision=highest)
    return hidden_rows + valid[:, None] * branch

def reference(hidden, lengths, out_grad, norm_gain, in_weight, conv_weight, conv_bias, dt_bias, a_log, skip_gain, gated_gain, out_weight):
    params = jax.tree.map(lambda weight_arr: weight_arr.astype(jnp.float32), (norm_gain, in_weight, conv_weight, conv_bias, dt_bias, a_log, skip_gain, gated_gain, out_weight))
    flat_hidden = hidden.reshape(MICRO * SEQS, SEQLEN, D)
    flat_grad = out_grad.reshape(MICRO * SEQS, SEQLEN, D)
    flat_lengths = lengths.reshape(MICRO * SEQS).astype(jnp.int32)
    positions = jnp.arange(SEQLEN, dtype=jnp.int32)

    def per_sequence(totals, inputs_now):
        seq_rows, cotangent, seq_length = inputs_now
        valid = (positions < seq_length).astype(jnp.float32)

        def forward(rows_in, *weights):
            return layer(rows_in, valid, *weights)
        result, backward = jax.vjp(forward, seq_rows.astype(jnp.float32), *params)
        grads = backward(cotangent.astype(jnp.float32))
        new_totals = jax.tree.map(jnp.add, totals, tuple(grads[1:]))
        return (new_totals, (result.astype(jnp.bfloat16), grads[0].astype(jnp.bfloat16)))
    initial = jax.tree.map(jnp.zeros_like, params)
    totals, (outputs, input_grads) = lax.scan(per_sequence, initial, (flat_hidden, flat_grad, flat_lengths))
    return (outputs.reshape(hidden.shape), input_grads.reshape(hidden.shape), totals[0], totals[1], totals[2], totals[3], totals[4], totals[5], totals[6], totals[7], totals[8])
```

```python
from functools import partial

import jax
import jax.numpy as jnp
from jax import lax
from jax.experimental import pallas as pl
from jax.experimental.pallas import tpu as pltpu
from jax.sharding import PartitionSpec as P

epsilon = 1e-05
highest = lax.Precision.HIGHEST
f32 = jnp.float32
bf16 = jnp.bfloat16
GROUP = 8
VMEM = 48 * 1024 * 1024

NN = (((1,), (0,)), ((), ()))
NT = (((1,), (1,)), ((), ()))
TN = (((0,), (0,)), ((), ()))


def mm(a, b, dims=NN):
    return lax.dot_general(a, b, dims, preferred_element_type=f32)


def params():
    return pltpu.CompilerParams(
        dimension_semantics=("arbitrary", "arbitrary"), vmem_limit_bytes=VMEM
    )


def widen(cols, head_size):
    t, heads = cols.shape
    lane = lax.broadcasted_iota(jnp.int32, (t, 2 * head_size), 1)
    parts = []
    for k in range(0, heads, 2):
        parts.append(jnp.where(lane < head_size, cols[:, k : k + 1], cols[:, k + 1 : k + 2]))
    return jnp.concatenate(parts, axis=1)


def state_kernel(hs, x_ref, w_ref, bt_ref, o_ref):
    weighted = (x_ref[0].astype(f32) * widen(w_ref[0, 0], hs)).astype(bf16)
    o_ref[0] = mm(bt_ref[0], weighted)


def block_states(x, weights, bt, hs):
    micro, t, cols = x.shape
    n = bt.shape[1]
    gc = GROUP * hs
    return pl.pallas_call(
        partial(state_kernel, hs),
        grid=(micro, cols // gc),
        in_specs=[
            pl.BlockSpec((1, t, gc), lambda m, g: (m, 0, g)),
            pl.BlockSpec((1, 1, t, GROUP), lambda m, g: (m, g, 0, 0)),
            pl.BlockSpec((1, n, t), lambda m, g: (m, 0, 0)),
        ],
        out_specs=pl.BlockSpec((1, n, gc), lambda m, g: (m, 0, g)),
        out_shape=jax.ShapeDtypeStruct((micro, n, cols), f32),
        compiler_params=params(),
        name="block_states",
    )(x, weights, bt)


def local_kernel(hs, x_ref, dt_ref, cum_ref, row_ref, b_ref, c_ref, o_ref, scores):
    t = x_ref.shape[1]
    half = t // 2

    @pl.when(pl.program_id(1) == 0)
    def _():
        s = mm(c_ref[0], b_ref[0], NT)
        i = lax.broadcasted_iota(jnp.int32, (t, t), 0)
        j = lax.broadcasted_iota(jnp.int32, (t, t), 1)
        scores[...] = jnp.where(i >= j, s, 0.0)

    cum, dt, rows = cum_ref[0, 0], dt_ref[0, 0], row_ref[0, 0]
    lane = lax.broadcasted_iota(jnp.int32, (half, 2 * hs), 1)
    weighted = (x_ref[0].astype(f32) * widen(dt, hs)).astype(bf16)
    for k in range(0, GROUP, 2):
        at = slice(k * hs, (k + 2) * hs)
        pair = weighted[:, at]
        top, low = [], []
        for h in (k, k + 1):
            col, row = cum[:, h : h + 1], rows[h : h + 1, :]
            m1 = jnp.exp(jnp.minimum(col[:half] - row[:, :half], 0.0)) * scores[:half, :half]
            m2 = jnp.exp(jnp.minimum(col[half:] - row, 0.0)) * scores[half:, :]
            top.append(mm(m1.astype(bf16), pair[:half]))
            low.append(mm(m2.astype(bf16), pair))
        o_ref[0, :half, at] = jnp.where(lane < hs, top[0], top[1])
        o_ref[0, half:, at] = jnp.where(lane < hs, low[0], low[1])


def local_scan(x, dt, cum, rows, b, c, hs):
    micro, t, cols = x.shape
    n = b.shape[2]
    gc = GROUP * hs
    return pl.pallas_call(
        partial(local_kernel, hs),
        grid=(micro, cols // gc),
        in_specs=[
            pl.BlockSpec((1, t, gc), lambda m, g: (m, 0, g)),
            pl.BlockSpec((1, 1, t, GROUP), lambda m, g: (m, g, 0, 0)),
            pl.BlockSpec((1, 1, t, GROUP), lambda m, g: (m, g, 0, 0)),
            pl.BlockSpec((1, 1, GROUP, t), lambda m, g: (m, g, 0, 0)),
            pl.BlockSpec((1, t, n), lambda m, g: (m, 0, 0)),
            pl.BlockSpec((1, t, n), lambda m, g: (m, 0, 0)),
        ],
        out_specs=pl.BlockSpec((1, t, gc), lambda m, g: (m, 0, g)),
        out_shape=jax.ShapeDtypeStruct((micro, t, cols), f32),
        scratch_shapes=[pltpu.VMEM((t, t), f32)],
        compiler_params=params(),
        name="local_scan",
    )(x, dt, cum, rows, b, c)


def carry_kernel(hs, x_ref, y_ref, cum_ref, c_ref, s_ref, skip_ref, scan_ref, low_ref):
    carried = mm(c_ref[0], s_ref[0].astype(bf16)) * widen(jnp.exp(cum_ref[0, 0]), hs)
    scan = y_ref[0] + carried
    scan_ref[0] = scan
    low_ref[0] = (scan + skip_ref[...] * x_ref[0].astype(f32)).astype(bf16)


def add_carry(x, y, cum, c, s_in, skip_wide, hs):
    micro, t, cols = x.shape
    n = c.shape[2]
    gc = GROUP * hs
    wide = pl.BlockSpec((1, t, gc), lambda m, g: (m, 0, g))
    return pl.pallas_call(
        partial(carry_kernel, hs),
        grid=(micro, cols // gc),
        in_specs=[
            wide,
            wide,
            pl.BlockSpec((1, 1, t, GROUP), lambda m, g: (m, g, 0, 0)),
            pl.BlockSpec((1, t, n), lambda m, g: (m, 0, 0)),
            pl.BlockSpec((1, n, gc), lambda m, g: (m, 0, g)),
            pl.BlockSpec((1, gc), lambda m, g: (0, g)),
        ],
        out_specs=[wide, wide],
        out_shape=[
            jax.ShapeDtypeStruct((micro, t, cols), f32),
            jax.ShapeDtypeStruct((micro, t, cols), bf16),
        ],
        compiler_params=params(),
        name="add_carry",
    )(x, y, cum, c, s_in, skip_wide)


def local_back_kernel(
    hs, x_ref, dy_ref, dt_ref, cum_ref, row_ref, b_ref, c_ref, dx_ref, db_ref, dc_ref, scores, total
):
    t = x_ref.shape[1]
    half = t // 2

    @pl.when(pl.program_id(1) == 0)
    def _():
        s = mm(b_ref[0], c_ref[0], NT)
        j = lax.broadcasted_iota(jnp.int32, (t, t), 0)
        i = lax.broadcasted_iota(jnp.int32, (t, t), 1)
        scores[...] = jnp.where(i >= j, s, 0.0)
        total[...] = jnp.zeros_like(total)

    cum, dt, rows = cum_ref[0, 0], dt_ref[0, 0], row_ref[0, 0]
    lane = lax.broadcasted_iota(jnp.int32, (t, 2 * hs), 1)
    lane_half = lax.broadcasted_iota(jnp.int32, (half, 2 * hs), 1)
    weighted = (x_ref[0].astype(f32) * widen(dt, hs)).astype(bf16)
    for k in range(0, GROUP, 2):
        at = slice(k * hs, (k + 2) * hs)
        pair = weighted[:, at]
        dy = dy_ref[0, :, at]
        top, low = [], []
        for h in (k, k + 1):
            col, row = cum[:, h : h + 1], rows[h : h + 1, :]
            mine = jnp.where(lane < hs, pair, 0) if h == k else jnp.where(lane < hs, 0, pair)
            l1 = jnp.exp(jnp.minimum(row - col[:half], 0.0))
            l2 = jnp.exp(jnp.minimum(row[:, half:] - col[half:], 0.0))
            total[:half, :] += l1 * mm(mine[:half], dy, NT)
            total[half:, half:] += l2 * mm(mine[half:], dy[half:], NT)
            top.append(mm((l1 * scores[:half, :]).astype(bf16), dy))
            low.append(mm((l2 * scores[half:, half:]).astype(bf16), dy[half:]))
        dx_ref[0, :half, at] = jnp.where(lane_half < hs, top[0], top[1])
        dx_ref[0, half:, at] = jnp.where(lane_half < hs, low[0], low[1])

    @pl.when(pl.program_id(1) == pl.num_programs(1) - 1)
    def _():
        j = lax.broadcasted_iota(jnp.int32, (t, t), 0)
        i = lax.broadcasted_iota(jnp.int32, (t, t), 1)
        d = jnp.where(i >= j, total[...], 0.0)
        db_ref[0] = mm(d.astype(bf16), c_ref[0])
        dc_ref[0] = mm(d.T.astype(bf16), b_ref[0])


def local_back(x, dy, dt, cum, rows, b, c, hs):
    micro, t, cols = x.shape
    n = b.shape[2]
    gc = GROUP * hs
    wide = pl.BlockSpec((1, t, gc), lambda m, g: (m, 0, g))
    small = pl.BlockSpec((1, 1, t, GROUP), lambda m, g: (m, g, 0, 0))
    state = pl.BlockSpec((1, t, n), lambda m, g: (m, 0, 0))
    return pl.pallas_call(
        partial(local_back_kernel, hs),
        grid=(micro, cols // gc),
        in_specs=[
            wide,
            wide,
            small,
            small,
            pl.BlockSpec((1, 1, GROUP, t), lambda m, g: (m, g, 0, 0)),
            state,
            state,
        ],
        out_specs=[wide, state, state],
        out_shape=[
            jax.ShapeDtypeStruct((micro, t, cols), f32),
            jax.ShapeDtypeStruct((micro, t, n), f32),
            jax.ShapeDtypeStruct((micro, t, n), f32),
        ],
        scratch_shapes=[pltpu.VMEM((t, t), f32), pltpu.VMEM((t, t), f32)],
        compiler_params=params(),
        name="local_back",
    )(x, dy, dt, cum, rows, b, c)


def head_sums(values, ones):
    high = values.astype(bf16)
    rest = (values - high.astype(f32)).astype(bf16)
    return mm(high, ones) + mm(rest, ones)


def carry_back_kernel(
    hs,
    x_ref,
    dy_ref,
    dxl_ref,
    y_ref,
    dt_ref,
    cum_ref,
    b_ref,
    si_ref,
    ds_ref,
    dbl_ref,
    dcl_ref,
    skip_ref,
    dx_ref,
    ddt_ref,
    dcum_ref,
    db_ref,
    dc_ref,
    last_ref,
    dskip_ref,
):
    t = x_ref.shape[1]
    gc = x_ref.shape[2]

    @pl.when(pl.program_id(1) == 0)
    def _():
        db_ref[0] = dbl_ref[0]
        dc_ref[0] = dcl_ref[0]

    cum, dt = cum_ref[0, 0], dt_ref[0, 0]
    x, dy = x_ref[0].astype(f32), dy_ref[0].astype(f32)
    dt_wide = widen(dt, hs)
    weighted = (x * dt_wide).astype(bf16).astype(f32)
    decay = widen(jnp.exp(cum), hs)
    to_end = widen(jnp.exp(cum[t - 1 :, :] - cum), hs)
    s_in, ds = si_ref[0], ds_ref[0]
    s_low, ds_low = s_in.astype(bf16), ds.astype(bf16)
    through = to_end * mm(b_ref[0], ds_low)
    d_weighted = dxl_ref[0] + through
    dx_ref[0] = (dt_wide * d_weighted + skip_ref[...] * dy).astype(bf16)
    db_ref[0] += mm((weighted * to_end).astype(bf16), ds_low, NT)
    dc_ref[0] += mm((dy * decay).astype(bf16), s_low, NT)
    r = lax.broadcasted_iota(jnp.int32, (gc, 128), 0)
    c = lax.broadcasted_iota(jnp.int32, (gc, 128), 1)
    ones = jnp.where(r // hs == c, 1.0, 0.0).astype(bf16)
    ddt_ref[0, 0] = head_sums(x * d_weighted, ones)[:, :GROUP]
    dcum_ref[0, 0] = head_sums(dy * y_ref[0] - weighted * d_weighted, ones)[:, :GROUP]
    last_decay = decay[t - 1 :, :]
    last_ref[0] = jnp.sum(weighted * through, axis=0, keepdims=True) + last_decay * jnp.sum(
        s_low.astype(f32) * ds, axis=0, keepdims=True
    )
    dskip_ref[0] = jnp.sum(x * dy, axis=0, keepdims=True)


def carry_back(x, dy, dxl, y, dt, cum, b, s_in, ds, dbl, dcl, skip_wide, hs):
    micro, t, cols = x.shape
    n = b.shape[2]
    gc = GROUP * hs
    groups = cols // gc
    wide = pl.BlockSpec((1, t, gc), lambda m, g: (m, 0, g))
    small = pl.BlockSpec((1, 1, t, GROUP), lambda m, g: (m, g, 0, 0))
    state = pl.BlockSpec((1, t, n), lambda m, g: (m, 0, 0))
    st = pl.BlockSpec((1, n, gc), lambda m, g: (m, 0, g))
    line = pl.BlockSpec((1, 1, gc), lambda m, g: (m, 0, g))
    return pl.pallas_call(
        partial(carry_back_kernel, hs),
        grid=(micro, groups),
        in_specs=[
            wide,
            wide,
            wide,
            wide,
            small,
            small,
            state,
            st,
            st,
            state,
            state,
            pl.BlockSpec((1, gc), lambda m, g: (0, g)),
        ],
        out_specs=[wide, small, small, state, state, line, line],
        out_shape=[
            jax.ShapeDtypeStruct((micro, t, cols), bf16),
            jax.ShapeDtypeStruct((micro, groups, t, GROUP), f32),
            jax.ShapeDtypeStruct((micro, groups, t, GROUP), f32),
            jax.ShapeDtypeStruct((micro, t, n), f32),
            jax.ShapeDtypeStruct((micro, t, n), f32),
            jax.ShapeDtypeStruct((micro, 1, cols), f32),
            jax.ShapeDtypeStruct((micro, 1, cols), f32),
        ],
        compiler_params=params(),
        name="carry_back",
    )(x, dy, dxl, y, dt, cum, b, s_in, ds, dbl, dcl, skip_wide)


def from_behind(x, axis, by):
    count = lax.axis_size(axis)
    pairs = [(i, i + by) for i in range(count) if 0 <= i + by < count]
    return lax.ppermute(x, axis, pairs)


def swap(x, by):
    count = lax.axis_size("seq")
    return lax.ppermute(x, "seq", [(i, i ^ by) for i in range(count)])


def running_states(terms, decays, hs, forward):
    count = lax.axis_size("seq")
    rank = lax.axis_index("seq")
    index = jnp.arange(count)

    def product(mask):
        d = jnp.prod(jnp.where(mask[:, None, None], decays, 1.0), axis=0)
        return jnp.repeat(d, hs, axis=1)[:, None, :]

    total, before = terms, jnp.zeros_like(terms)
    size = 1
    while size < count:
        other = swap(total.astype(bf16), size).astype(f32)
        mine = index // size == rank // size
        theirs = index // size == (rank // size) ^ 1
        later = (rank // size) % 2 == (1 if forward else 0)
        passed = mine & ((index < rank) if forward else (index > rank))
        before = before + jnp.where(later, product(passed), 0.0) * other
        if 2 * size < count:
            total = total * jnp.where(later, 1.0, product(theirs)) + other * jnp.where(
                later, product(mine), 1.0
            )
        size *= 2
    return before


def rms_front(hidden_rows, gain):
    power = jnp.mean(hidden_rows * hidden_rows, axis=-1, keepdims=True)
    return hidden_rows * lax.rsqrt(power + epsilon) * gain


def conv_act(padded, conv_w, conv_b):
    taps = conv_w.shape[0]
    rows_out = padded.shape[1] - taps + 1
    total = conv_b + padded[:, 0:rows_out] * conv_w[0]
    for offset in range(1, taps):
        total = total + padded[:, offset : offset + rows_out] * conv_w[offset]
    return jax.nn.silu(total)


def gate_norm(values, gate_in, gain):
    gated = values * jax.nn.silu(gate_in)
    power = jnp.mean(gated * gated, axis=-1, keepdims=True)
    return gated * lax.rsqrt(power + epsilon) * gain


def local(
    hidden,
    lengths,
    out_grad,
    norm_gain,
    in_weight,
    conv_weight,
    conv_bias,
    dt_bias,
    a_log,
    skip_gain,
    gated_gain,
    out_weight,
):
    count = lax.axis_size("seq")
    shards = lax.axis_size("wshard")
    rank = lax.axis_index("seq")
    shard = lax.axis_index("wshard")
    micro, _, tokens, width = hidden.shape
    taps = conv_weight.shape[1]
    small = [norm_gain, conv_weight.T.reshape(-1), conv_bias, dt_bias, a_log, skip_gain, gated_gain]
    sizes = [v.shape[0] for v in small]
    packed = lax.all_gather(jnp.concatenate(small), "wshard", axis=0).astype(f32)
    parts, at = [], 0
    for size in sizes:
        parts.append(packed[:, at : at + size])
        at += size
    norm_g = parts[0].reshape(-1)
    conv_w = parts[1].reshape(shards, taps, -1).transpose(1, 0, 2).reshape(taps, -1)
    conv_b = parts[2].reshape(-1)
    dt_shift = parts[3].reshape(-1)
    rate = -jnp.exp(parts[4].reshape(-1))
    skip = parts[5].reshape(-1)
    gated_g = parts[6].reshape(-1)

    in_t = lax.all_gather(in_weight.T, "wshard", axis=0)
    out_w = lax.all_gather(out_weight, "wshard", axis=0, tiled=True)
    in_t = in_t.transpose(1, 0, 2).reshape(in_t.shape[1], -1)

    inner = out_w.shape[0]
    channels = conv_b.shape[0]
    heads = dt_shift.shape[0]
    hs = inner // heads
    n = (channels - inner) // 2
    groups = heads // GROUP
    rows = micro * tokens

    def grouped(v):
        return v.reshape(micro, tokens, groups, GROUP).transpose(0, 2, 1, 3)

    rows_in = hidden.reshape(rows, width).astype(f32)
    cot = out_grad.reshape(rows, width).astype(f32)
    positions = rank * tokens + jnp.arange(tokens, dtype=jnp.int32)
    valid = (positions[None, :] < lengths[:, 0][:, None]).astype(f32).reshape(rows, 1)
    normed, front_back = jax.vjp(rms_front, rows_in, norm_g)
    normed_low = normed.astype(bf16)
    gate_in = mm(normed_low, in_t[:inner], NT)
    conv_low = mm(normed_low, in_t[inner : inner + channels], NT).astype(bf16)
    dt_low = mm(normed_low, in_t[inner + channels :], NT).astype(bf16)
    conv_low = conv_low.reshape(micro, tokens, channels)
    prior = from_behind(conv_low[:, tokens - (taps - 1) :], "seq", 1)
    padded = jnp.concatenate([prior, conv_low], axis=1).astype(f32)
    mixed, conv_back = jax.vjp(conv_act, padded, conv_w, conv_b)
    x_low = mixed[..., :inner].astype(bf16)
    b_low = mixed[..., inner : inner + n].astype(bf16)
    c_low = mixed[..., inner + n :].astype(bf16)

    dt_raw = dt_low.astype(f32).reshape(micro, tokens, heads) + dt_shift
    dt = jax.nn.softplus(dt_raw)
    tri = (jnp.arange(tokens)[:, None] >= jnp.arange(tokens)[None, :]).astype(f32)
    cum = jnp.einsum("ij,mjh->mih", tri, dt * rate, precision=highest)
    dt_g, cum_g = grouped(dt), grouped(cum)
    row_g = cum_g.transpose(0, 1, 3, 2)
    last = cum[:, tokens - 1, :]
    decays = lax.all_gather(jnp.exp(last), "seq", axis=0)
    end_w = grouped(dt * jnp.exp(last[:, None, :] - cum))
    decay_w = grouped(jnp.exp(cum))
    skip_wide = jnp.repeat(skip, hs)[None, :]

    own_state = block_states(x_low, end_w, b_low.transpose(0, 2, 1), hs)
    y_local = local_scan(x_low, dt_g, cum_g, row_g, b_low, c_low, hs)
    s_in = running_states(own_state, decays, hs, True)
    y_scan, scanned_low = add_carry(x_low, y_local, cum_g, c_low, s_in, skip_wide, hs)

    scanned = scanned_low.reshape(rows, inner).astype(f32)
    normed_out, gate_back = jax.vjp(gate_norm, scanned, gate_in, gated_g)
    normed_out_low = normed_out.astype(bf16)
    branch = mm(normed_out_low, out_w)
    output = (rows_in + valid * branch).astype(bf16).reshape(hidden.shape)

    g = (cot * valid).astype(bf16)
    out_terms = mm(normed_out_low, g, TN)
    d_scanned, d_gate_in, d_gated = gate_back(mm(g, out_w, NT))
    dy = d_scanned.astype(bf16).reshape(micro, tokens, inner)
    own_grad = block_states(dy, decay_w, c_low.transpose(0, 2, 1), hs)
    dx_local, db_local, dc_local = local_back(x_low, dy, dt_g, cum_g, row_g, b_low, c_low, hs)
    ds = running_states(own_grad, decays, hs, False)
    dx_low, ddt_g, dcum_g, db, dc, last_term, dskip = carry_back(
        x_low, dy, dx_local, y_scan, dt_g, cum_g, b_low, s_in, ds, db_local, dc_local, skip_wide, hs
    )

    def ungrouped(v):
        return v.transpose(0, 2, 1, 3).reshape(micro, tokens, heads)

    at_end = jnp.sum(last_term.reshape(micro, heads, hs), axis=-1)[:, None, :]
    d_log = jnp.einsum("ij,mih->mjh", tri, ungrouped(dcum_g), precision=highest) + at_end
    d_dt = (ungrouped(ddt_g) + d_log * rate) * jax.nn.sigmoid(dt_raw)
    d_dt_bias = jnp.sum(d_dt, axis=(0, 1))
    d_a_log = jnp.sum(d_log * dt, axis=(0, 1)) * rate
    d_skip = jnp.sum(dskip.reshape(-1, heads, hs), axis=(0, 2))
    mixed_grad = jnp.concatenate([dx_low.astype(f32), db, dc], axis=2)
    d_padded, d_conv_w, d_conv_b = conv_back(mixed_grad)
    from_next = from_behind(d_padded[:, : taps - 1].astype(bf16), "seq", -1).astype(f32)
    d_conv = d_padded[:, taps - 1 :].at[:, tokens - (taps - 1) :].add(from_next)
    d_proj = jnp.concatenate(
        [
            d_gate_in.astype(bf16),
            d_conv.astype(bf16).reshape(rows, channels),
            d_dt.astype(bf16).reshape(rows, heads),
        ],
        axis=1,
    )
    in_terms = mm(d_proj, normed_low, TN)
    d_normed = mm(d_proj, in_t)
    d_hidden, d_norm_g = front_back(d_normed)
    input_grad = (d_hidden + cot).astype(bf16).reshape(hidden.shape)

    def summed(terms, axis):
        t = lax.psum_scatter(terms.astype(bf16), "seq", scatter_dimension=0, tiled=True)
        t = lax.psum_scatter(t, "wshard", scatter_dimension=axis, tiled=True)
        return lax.all_gather(t, "seq", axis=0, tiled=True).astype(f32)

    in_grad = summed(in_terms, 1).T
    blocks = out_terms.reshape(shards, count, -1, width).transpose(1, 0, 2, 3)
    blocks = blocks.reshape(inner, width)
    out_w_grad = summed_rows(blocks, shards, count)
    smalls = [
        d_norm_g.reshape(shards, -1),
        d_conv_w.reshape(taps, shards, -1).transpose(1, 0, 2).reshape(shards, -1),
        d_conv_b.reshape(shards, -1),
        d_dt_bias.reshape(shards, -1),
        d_a_log.reshape(shards, -1),
        d_skip.reshape(shards, -1),
        d_gated.reshape(shards, -1),
    ]
    sums = lax.psum(jnp.concatenate(smalls, axis=1), ("seq", "wshard"))
    sums = lax.dynamic_index_in_dim(sums, shard, 0, keepdims=False)
    found, at = [], 0
    for size in sizes:
        found.append(sums[at : at + size])
        at += size
    return (
        output,
        input_grad,
        found[0],
        in_grad,
        found[1].reshape(taps, -1).T,
        found[2],
        found[3],
        found[4],
        found[5],
        found[6],
        out_w_grad,
    )


def summed_rows(blocks, shards, count):
    t = lax.psum_scatter(blocks.astype(bf16), "seq", scatter_dimension=0, tiled=True)
    t = lax.psum_scatter(t, "wshard", scatter_dimension=0, tiled=True)
    return lax.all_gather(t, "seq", axis=0, tiled=True).astype(f32)


def solution(mesh):
    return jax.shard_map(
        local,
        mesh=mesh,
        in_specs=(
            P(None, "wshard", "seq", None),
            P(None, "wshard"),
            P(None, "wshard", "seq", None),
            P("wshard"),
            P("wshard", None),
            P("wshard", None),
            P("wshard"),
            P("wshard"),
            P("wshard"),
            P("wshard"),
            P("wshard"),
            P("wshard", None),
        ),
        out_specs=(
            P(None, "wshard", "seq", None),
            P(None, "wshard", "seq", None),
            P("wshard"),
            P("wshard", None),
            P("wshard", None),
            P("wshard"),
            P("wshard"),
            P("wshard"),
            P("wshard"),
            P("wshard"),
            P("wshard", None),
        ),
        check_vma=False,
    )
```

```python
from functools import partial

import jax
import jax.numpy as jnp
from jax import lax
from jax.experimental import pallas as pl
from jax.experimental.pallas import tpu as pltpu
from jax.sharding import PartitionSpec as P

epsilon = 1e-05
highest = lax.Precision.HIGHEST
f32 = jnp.float32
bf16 = jnp.bfloat16
GROUP = 8
VMEM = 48 * 1024 * 1024

NN = (((1,), (0,)), ((), ()))
NT = (((1,), (1,)), ((), ()))
TN = (((0,), (0,)), ((), ()))


def mm(a, b, dims=NN):
    return lax.dot_general(a, b, dims, preferred_element_type=f32)


def params():
    return pltpu.CompilerParams(
        dimension_semantics=("arbitrary", "arbitrary"), vmem_limit_bytes=VMEM
    )


def widen(cols, head_size):
    t, heads = cols.shape
    lane = lax.broadcasted_iota(jnp.int32, (t, 2 * head_size), 1)
    parts = []
    for k in range(0, heads, 2):
        parts.append(jnp.where(lane < head_size, cols[:, k : k + 1], cols[:, k + 1 : k + 2]))
    return jnp.concatenate(parts, axis=1)


def state_kernel(hs, x_ref, w_ref, bt_ref, o_ref):
    weighted = (x_ref[0].astype(f32) * widen(w_ref[0, 0], hs)).astype(bf16)
    o_ref[0] = mm(bt_ref[0], weighted)


def block_states(x, weights, bt, hs):
    micro, t, cols = x.shape
    n = bt.shape[1]
    gc = GROUP * hs
    return pl.pallas_call(
        partial(state_kernel, hs),
        grid=(micro, cols // gc),
        in_specs=[
            pl.BlockSpec((1, t, gc), lambda m, g: (m, 0, g)),
            pl.BlockSpec((1, 1, t, GROUP), lambda m, g: (m, g, 0, 0)),
            pl.BlockSpec((1, n, t), lambda m, g: (m, 0, 0)),
        ],
        out_specs=pl.BlockSpec((1, n, gc), lambda m, g: (m, 0, g)),
        out_shape=jax.ShapeDtypeStruct((micro, n, cols), f32),
        compiler_params=params(),
        name="block_states",
    )(x, weights, bt)


def local_kernel(hs, x_ref, dt_ref, cum_ref, row_ref, b_ref, c_ref, o_ref, scores):
    t = x_ref.shape[1]
    half = t // 2

    @pl.when(pl.program_id(1) == 0)
    def _():
        s = mm(c_ref[0], b_ref[0], NT)
        i = lax.broadcasted_iota(jnp.int32, (t, t), 0)
        j = lax.broadcasted_iota(jnp.int32, (t, t), 1)
        scores[...] = jnp.where(i >= j, s, 0.0)

    cum, dt, rows = cum_ref[0, 0], dt_ref[0, 0], row_ref[0, 0]
    lane = lax.broadcasted_iota(jnp.int32, (half, 2 * hs), 1)
    weighted = (x_ref[0].astype(f32) * widen(dt, hs)).astype(bf16)
    for k in range(0, GROUP, 2):
        at = slice(k * hs, (k + 2) * hs)
        pair = weighted[:, at]
        top, low = [], []
        for h in (k, k + 1):
            col, row = cum[:, h : h + 1], rows[h : h + 1, :]
            m1 = jnp.exp(jnp.minimum(col[:half] - row[:, :half], 0.0)) * scores[:half, :half]
            m2 = jnp.exp(jnp.minimum(col[half:] - row, 0.0)) * scores[half:, :]
            top.append(mm(m1.astype(bf16), pair[:half]))
            low.append(mm(m2.astype(bf16), pair))
        o_ref[0, :half, at] = jnp.where(lane < hs, top[0], top[1])
        o_ref[0, half:, at] = jnp.where(lane < hs, low[0], low[1])


def local_scan(x, dt, cum, rows, b, c, hs):
    micro, t, cols = x.shape
    n = b.shape[2]
    gc = GROUP * hs
    return pl.pallas_call(
        partial(local_kernel, hs),
        grid=(micro, cols // gc),
        in_specs=[
            pl.BlockSpec((1, t, gc), lambda m, g: (m, 0, g)),
            pl.BlockSpec((1, 1, t, GROUP), lambda m, g: (m, g, 0, 0)),
            pl.BlockSpec((1, 1, t, GROUP), lambda m, g: (m, g, 0, 0)),
            pl.BlockSpec((1, 1, GROUP, t), lambda m, g: (m, g, 0, 0)),
            pl.BlockSpec((1, t, n), lambda m, g: (m, 0, 0)),
            pl.BlockSpec((1, t, n), lambda m, g: (m, 0, 0)),
        ],
        out_specs=pl.BlockSpec((1, t, gc), lambda m, g: (m, 0, g)),
        out_shape=jax.ShapeDtypeStruct((micro, t, cols), f32),
        scratch_shapes=[pltpu.VMEM((t, t), f32)],
        compiler_params=params(),
        name="local_scan",
    )(x, dt, cum, rows, b, c)


def carry_kernel(hs, x_ref, y_ref, cum_ref, c_ref, s_ref, skip_ref, scan_ref, low_ref):
    carried = mm(c_ref[0], s_ref[0].astype(bf16)) * widen(jnp.exp(cum_ref[0, 0]), hs)
    scan = y_ref[0] + carried
    scan_ref[0] = scan
    low_ref[0] = (scan + skip_ref[...] * x_ref[0].astype(f32)).astype(bf16)


def add_carry(x, y, cum, c, s_in, skip_wide, hs):
    micro, t, cols = x.shape
    n = c.shape[2]
    gc = GROUP * hs
    wide = pl.BlockSpec((1, t, gc), lambda m, g: (m, 0, g))
    return pl.pallas_call(
        partial(carry_kernel, hs),
        grid=(micro, cols // gc),
        in_specs=[
            wide,
            wide,
            pl.BlockSpec((1, 1, t, GROUP), lambda m, g: (m, g, 0, 0)),
            pl.BlockSpec((1, t, n), lambda m, g: (m, 0, 0)),
            pl.BlockSpec((1, n, gc), lambda m, g: (m, 0, g)),
            pl.BlockSpec((1, gc), lambda m, g: (0, g)),
        ],
        out_specs=[wide, wide],
        out_shape=[
            jax.ShapeDtypeStruct((micro, t, cols), f32),
            jax.ShapeDtypeStruct((micro, t, cols), bf16),
        ],
        compiler_params=params(),
        name="add_carry",
    )(x, y, cum, c, s_in, skip_wide)


def local_back_kernel(
    hs, x_ref, dy_ref, dt_ref, cum_ref, row_ref, b_ref, c_ref, dx_ref, db_ref, dc_ref, scores, total
):
    t = x_ref.shape[1]
    half = t // 2

    @pl.when(pl.program_id(1) == 0)
    def _():
        s = mm(b_ref[0], c_ref[0], NT)
        j = lax.broadcasted_iota(jnp.int32, (t, t), 0)
        i = lax.broadcasted_iota(jnp.int32, (t, t), 1)
        scores[...] = jnp.where(i >= j, s, 0.0)
        total[...] = jnp.zeros_like(total)

    cum, dt, rows = cum_ref[0, 0], dt_ref[0, 0], row_ref[0, 0]
    lane = lax.broadcasted_iota(jnp.int32, (t, 2 * hs), 1)
    lane_half = lax.broadcasted_iota(jnp.int32, (half, 2 * hs), 1)
    weighted = (x_ref[0].astype(f32) * widen(dt, hs)).astype(bf16)
    for k in range(0, GROUP, 2):
        at = slice(k * hs, (k + 2) * hs)
        pair = weighted[:, at]
        dy = dy_ref[0, :, at]
        top, low = [], []
        for h in (k, k + 1):
            col, row = cum[:, h : h + 1], rows[h : h + 1, :]
            mine = jnp.where(lane < hs, pair, 0) if h == k else jnp.where(lane < hs, 0, pair)
            l1 = jnp.exp(jnp.minimum(row - col[:half], 0.0))
            l2 = jnp.exp(jnp.minimum(row[:, half:] - col[half:], 0.0))
            total[:half, :] += l1 * mm(mine[:half], dy, NT)
            total[half:, half:] += l2 * mm(mine[half:], dy[half:], NT)
            top.append(mm((l1 * scores[:half, :]).astype(bf16), dy))
            low.append(mm((l2 * scores[half:, half:]).astype(bf16), dy[half:]))
        dx_ref[0, :half, at] = jnp.where(lane_half < hs, top[0], top[1])
        dx_ref[0, half:, at] = jnp.where(lane_half < hs, low[0], low[1])

    @pl.when(pl.program_id(1) == pl.num_programs(1) - 1)
    def _():
        j = lax.broadcasted_iota(jnp.int32, (t, t), 0)
        i = lax.broadcasted_iota(jnp.int32, (t, t), 1)
        d = jnp.where(i >= j, total[...], 0.0)
        db_ref[0] = mm(d.astype(bf16), c_ref[0])
        dc_ref[0] = mm(d.T.astype(bf16), b_ref[0])


def local_back(x, dy, dt, cum, rows, b, c, hs):
    micro, t, cols = x.shape
    n = b.shape[2]
    gc = GROUP * hs
    wide = pl.BlockSpec((1, t, gc), lambda m, g: (m, 0, g))
    small = pl.BlockSpec((1, 1, t, GROUP), lambda m, g: (m, g, 0, 0))
    state = pl.BlockSpec((1, t, n), lambda m, g: (m, 0, 0))
    return pl.pallas_call(
        partial(local_back_kernel, hs),
        grid=(micro, cols // gc),
        in_specs=[
            wide,
            wide,
            small,
            small,
            pl.BlockSpec((1, 1, GROUP, t), lambda m, g: (m, g, 0, 0)),
            state,
            state,
        ],
        out_specs=[wide, state, state],
        out_shape=[
            jax.ShapeDtypeStruct((micro, t, cols), f32),
            jax.ShapeDtypeStruct((micro, t, n), f32),
            jax.ShapeDtypeStruct((micro, t, n), f32),
        ],
        scratch_shapes=[pltpu.VMEM((t, t), f32), pltpu.VMEM((t, t), f32)],
        compiler_params=params(),
        name="local_back",
    )(x, dy, dt, cum, rows, b, c)


def head_sums(values, ones):
    high = values.astype(bf16)
    rest = (values - high.astype(f32)).astype(bf16)
    return mm(high, ones) + mm(rest, ones)


def carry_back_kernel(
    hs,
    x_ref,
    dy_ref,
    dxl_ref,
    y_ref,
    dt_ref,
    cum_ref,
    b_ref,
    si_ref,
    ds_ref,
    dbl_ref,
    dcl_ref,
    skip_ref,
    dx_ref,
    ddt_ref,
    dcum_ref,
    db_ref,
    dc_ref,
    last_ref,
    dskip_ref,
):
    t = x_ref.shape[1]
    gc = x_ref.shape[2]

    @pl.when(pl.program_id(1) == 0)
    def _():
        db_ref[0] = dbl_ref[0]
        dc_ref[0] = dcl_ref[0]

    cum, dt = cum_ref[0, 0], dt_ref[0, 0]
    x, dy = x_ref[0].astype(f32), dy_ref[0].astype(f32)
    dt_wide = widen(dt, hs)
    weighted = (x * dt_wide).astype(bf16).astype(f32)
    decay = widen(jnp.exp(cum), hs)
    to_end = widen(jnp.exp(cum[t - 1 :, :] - cum), hs)
    s_in, ds = si_ref[0], ds_ref[0]
    s_low, ds_low = s_in.astype(bf16), ds.astype(bf16)
    through = to_end * mm(b_ref[0], ds_low)
    d_weighted = dxl_ref[0] + through
    dx_ref[0] = (dt_wide * d_weighted + skip_ref[...] * dy).astype(bf16)
    db_ref[0] += mm((weighted * to_end).astype(bf16), ds_low, NT)
    dc_ref[0] += mm((dy * decay).astype(bf16), s_low, NT)
    r = lax.broadcasted_iota(jnp.int32, (gc, 128), 0)
    c = lax.broadcasted_iota(jnp.int32, (gc, 128), 1)
    ones = jnp.where(r // hs == c, 1.0, 0.0).astype(bf16)
    ddt_ref[0, 0] = head_sums(x * d_weighted, ones)[:, :GROUP]
    dcum_ref[0, 0] = head_sums(dy * y_ref[0] - weighted * d_weighted, ones)[:, :GROUP]
    last_decay = decay[t - 1 :, :]
    last_ref[0] = jnp.sum(weighted * through, axis=0, keepdims=True) + last_decay * jnp.sum(
        s_low.astype(f32) * ds, axis=0, keepdims=True
    )
    dskip_ref[0] = jnp.sum(x * dy, axis=0, keepdims=True)


def carry_back(x, dy, dxl, y, dt, cum, b, s_in, ds, dbl, dcl, skip_wide, hs):
    micro, t, cols = x.shape
    n = b.shape[2]
    gc = GROUP * hs
    groups = cols // gc
    wide = pl.BlockSpec((1, t, gc), lambda m, g: (m, 0, g))
    small = pl.BlockSpec((1, 1, t, GROUP), lambda m, g: (m, g, 0, 0))
    state = pl.BlockSpec((1, t, n), lambda m, g: (m, 0, 0))
    st = pl.BlockSpec((1, n, gc), lambda m, g: (m, 0, g))
    line = pl.BlockSpec((1, 1, gc), lambda m, g: (m, 0, g))
    return pl.pallas_call(
        partial(carry_back_kernel, hs),
        grid=(micro, groups),
        in_specs=[
            wide,
            wide,
            wide,
            wide,
            small,
            small,
            state,
            st,
            st,
            state,
            state,
            pl.BlockSpec((1, gc), lambda m, g: (0, g)),
        ],
        out_specs=[wide, small, small, state, state, line, line],
        out_shape=[
            jax.ShapeDtypeStruct((micro, t, cols), bf16),
            jax.ShapeDtypeStruct((micro, groups, t, GROUP), f32),
            jax.ShapeDtypeStruct((micro, groups, t, GROUP), f32),
            jax.ShapeDtypeStruct((micro, t, n), f32),
            jax.ShapeDtypeStruct((micro, t, n), f32),
            jax.ShapeDtypeStruct((micro, 1, cols), f32),
            jax.ShapeDtypeStruct((micro, 1, cols), f32),
        ],
        compiler_params=params(),
        name="carry_back",
    )(x, dy, dxl, y, dt, cum, b, s_in, ds, dbl, dcl, skip_wide)


def from_behind(x, axis, by):
    count = lax.axis_size(axis)
    pairs = [(i, i + by) for i in range(count) if 0 <= i + by < count]
    return lax.ppermute(x, axis, pairs)


def swap(x, by):
    count = lax.axis_size("seq")
    return lax.ppermute(x, "seq", [(i, i ^ by) for i in range(count)])


def running_states(terms, decays, hs, forward):
    count = lax.axis_size("seq")
    rank = lax.axis_index("seq")
    index = jnp.arange(count)

    def product(mask):
        d = jnp.prod(jnp.where(mask[:, None, None], decays, 1.0), axis=0)
        return jnp.repeat(d, hs, axis=1)[:, None, :]

    total, before = terms, jnp.zeros_like(terms)
    size = 1
    while size < count:
        other = swap(total.astype(bf16), size).astype(f32)
        mine = index // size == rank // size
        theirs = index // size == (rank // size) ^ 1
        later = (rank // size) % 2 == (1 if forward else 0)
        passed = mine & ((index < rank) if forward else (index > rank))
        before = before + jnp.where(later, product(passed), 0.0) * other
        if 2 * size < count:
            total = total * jnp.where(later, 1.0, product(theirs)) + other * jnp.where(
                later, product(mine), 1.0
            )
        size *= 2
    return before


MESH = pl.DeviceIdType.MESH


def around():
    s, z = lax.axis_index("seq"), lax.axis_index("wshard")
    c, x, y = s % 2, (s // 2) % 2, s // 4
    near = {
        "c": (s + 1 - 2 * c, z),
        "x": (s + 2 - 4 * x, z),
        "y": (s + 4 - 8 * y, z),
        "z1": (s, z + 1 - 2 * (z % 2)),
        "z2": (s, z + 2 - 4 * (z // 2)),
        "z3": (s, 3 - z),
    }
    return s, z, c, x, y, near


def greet(near):
    barrier = pltpu.get_barrier_semaphore()
    for where in near.values():
        pl.semaphore_signal(barrier, inc=1, device_id=where, device_id_type=MESH)
    pl.semaphore_wait(barrier, len(near))


CHUNK_DMAS = 10


def gather_kernel(chunks, w_ref, o_ref, send, recv, own_sem):
    s, z, c, x, y, near = around()
    own = pltpu.make_async_copy(w_ref.at[pl.ds(0, o_ref.shape[1])], o_ref.at[0], own_sem)
    own.start()
    greet(near)
    sx, sy, sd = s + 2 - 4 * x, s + 4 - 8 * y, s + 6 - 4 * x - 8 * y
    plans = []
    for q, (base, piece, off, size, first) in enumerate(chunks):

        def rows(who, base=base, piece=piece, off=off, size=size):
            return pl.ds(pl.multiple_of(base + who * piece + off, 16), size)

        def move(src, dst, kind, to, q=q):
            return pltpu.make_async_remote_copy(
                src_ref=src,
                dst_ref=dst,
                send_sem=send.at[q, kind],
                recv_sem=recv.at[q, kind],
                device_id=near[to],
                device_id_type=MESH,
            )

        def block(who, rows=rows):
            return o_ref.at[pl.ds(1, 3), rows(who)]

        def along(who, kind, to, move=move, block=block):
            return move(block(who), block(who), kind, to)

        plan = {}
        for k in (1, 2, 3):
            plan["z%d" % k] = move(w_ref.at[rows(s)], o_ref.at[k, rows(s)], k - 1, "z%d" % k)
        plan["x"] = along(s, 3, "x")
        plan["y"] = along(s, 4, "y")
        plan["d"] = along(sx, 5, "y") if first == "x" else along(sy, 5, "x")
        plan["c0"] = along(s, 6, "c")
        plan["cx"] = along(sx, 7, "c")
        plan["cy"] = along(sy, 8, "c")
        plan["cd"] = along(sd, 9, "c")
        plan["first"] = first
        plans.append(plan)

    for plan in plans:
        for k in (1, 2, 3):
            plan["z%d" % k].start()

    def begin(plan):
        for k in (1, 2, 3):
            plan["z%d" % k].wait_recv()
        for name in ("x", "y", "c0"):
            plan[name].start()

    def middle(plan):
        one, two = ("x", "y") if plan["first"] == "x" else ("y", "x")
        plan[one].wait_recv()
        plan["d"].start()
        plan["c" + one].start()
        plan[two].wait_recv()
        plan["c" + two].start()

    def finish(plan):
        plan["d"].wait_recv()
        plan["cd"].start()

    n = len(plans)
    for i in range(n + 2):
        if i < n:
            begin(plans[i])
        if 0 <= i - 1 < n:
            middle(plans[i - 1])
        if 0 <= i - 2 < n:
            finish(plans[i - 2])
    for plan in plans:
        for name in ("c0", "cx", "cy", "cd"):
            plan[name].wait_recv()
        for name in ("z1", "z2", "z3", "x", "y", "d", "c0", "cx", "cy", "cd"):
            plan[name].wait_send()
    own.wait()


def gather_input_weight(w_t, inner, channels):
    total = inner + channels
    chunks = []
    for base, piece in ((inner, channels // 8), (0, inner // 8)):
        half = piece // 2
        chunks.append((base, piece, 0, half, "x"))
        chunks.append((base, piece, half, half, "y"))
    width = w_t.shape[1]
    return pl.pallas_call(
        partial(gather_kernel, chunks),
        in_specs=[pl.BlockSpec(memory_space=pl.ANY)],
        out_specs=pl.BlockSpec(memory_space=pl.ANY),
        out_shape=jax.ShapeDtypeStruct((4, total, width), bf16),
        scratch_shapes=[
            pltpu.SemaphoreType.DMA((len(chunks), CHUNK_DMAS)),
            pltpu.SemaphoreType.DMA((len(chunks), CHUNK_DMAS)),
            pltpu.SemaphoreType.DMA,
        ],
        compiler_params=pltpu.CompilerParams(collective_id=1, has_side_effects=True),
        cost_estimate=pl.CostEstimate(flops=0, bytes_accessed=200_000_000, transcendentals=0),
        name="gather_input_weight",
    )(w_t)


def reduce_kernel(
    chunks,
    pieces,
    groups,
    dp_ref,
    nm_ref,
    o_ref,
    dp,
    nm,
    g,
    sa1,
    sb1,
    sa2,
    sb2,
    s3,
    ka2,
    kb2,
    f3,
    ra1,
    rb1,
    ra2,
    rb2,
    rz,
    in_sem,
    s_in,
    r_in,
    s_step,
    r_step,
    s_all,
    r_all,
):
    s, z, c, x, y, near = around()
    wide = dp.shape[2]
    shard = rz.shape[-1]

    def remote(src, dst, ss, rs, to):
        return pltpu.make_async_remote_copy(
            src_ref=src, dst_ref=dst, send_sem=ss, recv_sem=rs, device_id=near[to], device_id_type=MESH
        )

    local_copies, core_copies = [], []
    for i, (a, b) in enumerate(pieces):
        here = dp_ref.at[:, pl.ds(pl.multiple_of(c * wide + a, 128), b - a)]
        there = dp_ref.at[:, pl.ds(pl.multiple_of((1 - c) * wide + a, 128), b - a)]
        local_copies.append(
            pltpu.make_async_copy(here, dp.at[0, :, pl.ds(a, b - a)], in_sem.at[i])
        )
        core_copies.append(
            remote(there, dp.at[1, :, pl.ds(a, b - a)], s_in.at[i], r_in.at[i], "c")
        )
    n_in = len(pieces)
    nm_local = pltpu.make_async_copy(nm_ref, nm.at[0], in_sem.at[n_in])
    nm_core = remote(nm_ref, nm.at[1], s_in.at[n_in], r_in.at[n_in], "c")
    nm_local.start()
    for copy in local_copies:
        copy.start()
    greet(near)
    nm_core.start()
    for copy in core_copies:
        copy.start()

    def step_copy(kind, u):
        slot = u % 2
        ss, rs = s_step.at[kind, slot], r_step.at[kind, u]
        if kind == 0:
            return remote(sa1.at[slot], ra1.at[u], ss, rs, "x")
        if kind == 1:
            return remote(sb1.at[slot], rb1.at[u], ss, rs, "y")
        if kind == 2:
            return remote(sa2.at[slot], ra2.at[u], ss, rs, "y")
        if kind == 3:
            return remote(sb2.at[slot], rb2.at[u], ss, rs, "x")
        k = kind - 3
        other = (z + 1 - 2 * (z % 2), z + 2 - 4 * (z // 2), 3 - z)[k - 1]
        cols = pl.ds(pl.multiple_of(other * shard, 128), shard)
        return remote(s3.at[slot, :, :, cols], rz.at[u, k - 1], ss, rs, "z%d" % k)

    def part(px, py, ts, T=None):
        if T is None:
            return o_ref.at[c, ts, :, px, py]
        return o_ref.at[c, ts, T, px, py]

    def all_copy(q, kind):
        a, b = groups[q]
        ts = pl.ds(a, b - a)
        ss, rs = s_all.at[q, kind], r_all.at[q, kind]
        if kind == 0:
            return remote(part(x, y, ts), part(x, y, ts), ss, rs, "x")
        if kind == 1:
            return remote(part(x, y, ts), part(x, y, ts), ss, rs, "y")
        if kind == 2:
            return remote(part(x, y, ts), part(x, y, ts), ss, rs, "c")
        if kind == 3:
            return remote(part(1 - x, y, ts, 0), part(1 - x, y, ts, 0), ss, rs, "y")
        if kind == 4:
            return remote(part(x, 1 - y, ts, 1), part(x, 1 - y, ts, 1), ss, rs, "x")
        if kind == 5:
            return remote(part(1 - x, y, ts), part(1 - x, y, ts), ss, rs, "c")
        if kind == 6:
            return remote(part(x, 1 - y, ts), part(x, 1 - y, ts), ss, rs, "c")
        return remote(part(1 - x, 1 - y, ts), part(1 - x, 1 - y, ts), ss, rs, "c")

    def sl(at, size=16):
        return pl.ds(pl.multiple_of(at, 16), size)

    def free(kind, u):
        @pl.when(u >= 2)
        def _():
            step_copy(kind, u - 2).wait_send()

    def step(t, carry):
        @pl.when(t < chunks)
        def _():
            for i, (a, _) in enumerate(pieces):

                @pl.when(t == a // 128)
                def _(i=i):
                    if i == 0:
                        nm_local.wait()
                        nm_core.wait_recv()
                    local_copies[i].wait()
                    core_copies[i].wait_recv()

            slot = t % 2
            cols = pl.ds(pl.multiple_of(t * 128, 128), 128)
            g[slot] = mm(dp[0, :, cols], nm[0], TN) + mm(dp[1, :, cols], nm[1], TN)
            free(0, t)
            free(1, t)
            sa1[slot] = g[slot, sl((1 - x) * 32, 32)].astype(bf16)
            step_copy(0, t).start()
            sb1[slot, 0:16] = g[slot, sl(64 + (1 - y) * 16)].astype(bf16)
            sb1[slot, 16:32] = g[slot, sl(96 + (1 - y) * 16)].astype(bf16)
            step_copy(1, t).start()

        @pl.when((t >= 1) & (t - 1 < chunks))
        def _():
            u = t - 1
            slot = u % 2
            step_copy(0, u).wait_recv()
            free(2, u)
            sa2[slot] = (
                g[slot, sl(x * 32 + (1 - y) * 16)] + ra1[u, sl((1 - y) * 16)].astype(f32)
            ).astype(bf16)
            step_copy(2, u).start()
            ka2[slot] = g[slot, sl(x * 32 + y * 16)] + ra1[u, sl(y * 16)].astype(f32)
            step_copy(1, u).wait_recv()
            free(3, u)
            sb2[slot] = (
                g[slot, sl(64 + (1 - x) * 32 + y * 16)] + rb1[u, sl((1 - x) * 16)].astype(f32)
            ).astype(bf16)
            step_copy(3, u).start()
            kb2[slot] = g[slot, sl(64 + x * 32 + y * 16)] + rb1[u, sl(x * 16)].astype(f32)

        @pl.when((t >= 2) & (t - 2 < chunks))
        def _():
            u = t - 2
            slot = u % 2
            step_copy(2, u).wait_recv()
            step_copy(3, u).wait_recv()
            for k in (4, 5, 6):
                free(k, u)
            va = ka2[slot] + ra2[u].astype(f32)
            vb = kb2[slot] + rb2[u].astype(f32)
            f3[slot, 0] = va
            f3[slot, 1] = vb
            s3[slot, 0] = va.astype(bf16)
            s3[slot, 1] = vb.astype(bf16)
            for k in (4, 5, 6):
                step_copy(k, u).start()

        @pl.when((t >= 3) & (t - 3 < chunks))
        def _():
            u = t - 3
            slot = u % 2
            for k in (4, 5, 6):
                step_copy(k, u).wait_recv()
            mine = pl.ds(pl.multiple_of(z * shard, 128), shard)
            for T in (0, 1):
                total = f3[slot, T, :, mine]
                for k in range(3):
                    total = total + rz[u, k, T].astype(f32)
                o_ref[c, u, T, x, y] = total.astype(bf16)

        for q, (a, b) in enumerate(groups):

            @pl.when(t == b - 1 + 3)
            def _(q=q):
                for kind in (0, 1, 2):
                    all_copy(q, kind).start()

            @pl.when(t == b - 1 + 4)
            def _(q=q):
                all_copy(q, 0).wait_recv()
                all_copy(q, 3).start()
                all_copy(q, 5).start()
                all_copy(q, 1).wait_recv()
                all_copy(q, 4).start()
                all_copy(q, 6).start()

            @pl.when(t == b - 1 + 5)
            def _(q=q):
                all_copy(q, 3).wait_recv()
                all_copy(q, 4).wait_recv()
                all_copy(q, 7).start()

        return carry

    lax.fori_loop(0, chunks + 5, step, 0)
    for q in range(len(groups)):
        for kind in (2, 5, 6, 7):
            all_copy(q, kind).wait_recv()
        for kind in range(8):
            all_copy(q, kind).wait_send()
    for u in (chunks - 2, chunks - 1):
        for kind in range(7):
            step_copy(kind, u).wait_send()
    nm_core.wait_send()
    for copy in core_copies:
        copy.wait_send()


def reduce_products(dp, nm, collective_id):
    rows, total = dp.shape
    width = nm.shape[1]
    shard = width // 4
    wide = total // 2
    chunks = wide // 128
    cuts = sorted({0, min(256, wide), min(1280, wide), wide})
    pieces = list(zip(cuts[:-1], cuts[1:]))
    marks = sorted({0, chunks * 2 // 5, chunks * 7 // 10, chunks * 9 // 10, chunks})
    groups = list(zip(marks[:-1], marks[1:]))
    n = len(pieces)
    dma = pltpu.SemaphoreType.DMA
    out = pl.pallas_call(
        partial(reduce_kernel, chunks, pieces, groups),
        in_specs=[pl.BlockSpec(memory_space=pl.ANY)] * 2,
        out_specs=pl.BlockSpec(memory_space=pltpu.VMEM),
        out_shape=jax.ShapeDtypeStruct((2, chunks, 2, 2, 2, 16, shard), bf16),
        scratch_shapes=[
            pltpu.VMEM((2, rows, wide), bf16),
            pltpu.VMEM((2, rows, width), bf16),
            pltpu.VMEM((2, 128, width), f32),
            pltpu.VMEM((2, 32, width), bf16),
            pltpu.VMEM((2, 32, width), bf16),
            pltpu.VMEM((2, 16, width), bf16),
            pltpu.VMEM((2, 16, width), bf16),
            pltpu.VMEM((2, 2, 16, width), bf16),
            pltpu.VMEM((2, 16, width), f32),
            pltpu.VMEM((2, 16, width), f32),
            pltpu.VMEM((2, 2, 16, width), f32),
            pltpu.VMEM((chunks, 32, width), bf16),
            pltpu.VMEM((chunks, 32, width), bf16),
            pltpu.VMEM((chunks, 16, width), bf16),
            pltpu.VMEM((chunks, 16, width), bf16),
            pltpu.VMEM((chunks, 3, 2, 16, shard), bf16),
            dma((n + 1,)),
            dma((n + 1,)),
            dma((n + 1,)),
            dma((7, 2)),
            dma((7, chunks)),
            dma((len(groups), 8)),
            dma((len(groups), 8)),
        ],
        compiler_params=pltpu.CompilerParams(
            collective_id=collective_id, has_side_effects=True, vmem_limit_bytes=VMEM
        ),
        cost_estimate=pl.CostEstimate(
            flops=4 * rows * wide * width, bytes_accessed=200_000_000, transcendentals=0
        ),
        name="reduce_products",
    )(dp, nm)
    return out.reshape(total, shard)


def project_kernel(n_ref, w_ref, o_ref):
    total = mm(n_ref[0], w_ref[0], NT)
    for k in range(1, n_ref.shape[0]):
        total += mm(n_ref[k], w_ref[k], NT)
    o_ref[...] = total.astype(o_ref.dtype)


def project(parts, weight, first, count, tile, dtype):
    shards, rows, depth = parts.shape
    return pl.pallas_call(
        project_kernel,
        grid=(count // tile,),
        in_specs=[
            pl.BlockSpec((shards, rows, depth), lambda i: (0, 0, 0)),
            pl.BlockSpec((shards, tile, depth), lambda i: (0, first // tile + i, 0)),
        ],
        out_specs=pl.BlockSpec((rows, tile), lambda i: (0, i)),
        out_shape=jax.ShapeDtypeStruct((rows, count), dtype),
        compiler_params=pltpu.CompilerParams(vmem_limit_bytes=VMEM),
        name="project",
    )(parts, weight)


def unproject_kernel(d_ref, w_ref, o_ref):
    @pl.when(pl.program_id(0) == 0)
    def _():
        o_ref[...] = jnp.zeros_like(o_ref)

    for k in range(o_ref.shape[0]):
        o_ref[k] += mm(d_ref[...], w_ref[k])


def unproject(d, weight, tile):
    shards, count, depth = weight.shape
    rows = d.shape[0]
    return pl.pallas_call(
        unproject_kernel,
        grid=(count // tile,),
        in_specs=[
            pl.BlockSpec((rows, tile), lambda i: (0, i)),
            pl.BlockSpec((shards, tile, depth), lambda i: (0, i, 0)),
        ],
        out_specs=pl.BlockSpec((shards, rows, depth), lambda i: (0, 0, 0)),
        out_shape=jax.ShapeDtypeStruct((shards, rows, depth), f32),
        compiler_params=pltpu.CompilerParams(vmem_limit_bytes=VMEM),
        name="unproject",
    )(d, weight)


def rms_front(hidden_rows, gain):
    power = jnp.mean(hidden_rows * hidden_rows, axis=-1, keepdims=True)
    return hidden_rows * lax.rsqrt(power + epsilon) * gain


def conv_act(padded, conv_w, conv_b):
    taps = conv_w.shape[0]
    rows_out = padded.shape[1] - taps + 1
    total = conv_b + padded[:, 0:rows_out] * conv_w[0]
    for offset in range(1, taps):
        total = total + padded[:, offset : offset + rows_out] * conv_w[offset]
    return jax.nn.silu(total)


def gate_norm(values, gate_in, gain):
    gated = values * jax.nn.silu(gate_in)
    power = jnp.mean(gated * gated, axis=-1, keepdims=True)
    return gated * lax.rsqrt(power + epsilon) * gain


def local(
    hidden,
    lengths,
    out_grad,
    norm_gain,
    in_weight,
    conv_weight,
    conv_bias,
    dt_bias,
    a_log,
    skip_gain,
    gated_gain,
    out_weight,
):
    count = lax.axis_size("seq")
    shards = lax.axis_size("wshard")
    rank = lax.axis_index("seq")
    shard = lax.axis_index("wshard")
    micro, _, tokens, width = hidden.shape
    taps = conv_weight.shape[1]
    inner = out_weight.shape[0] * shards
    channels = conv_bias.shape[0] * shards
    heads = dt_bias.shape[0] * shards
    hs = inner // heads
    n = (channels - inner) // 2
    groups = heads // GROUP
    rows = micro * tokens
    fast = count == 8 and shards == 4
    in_local = in_weight.T
    small = [norm_gain, conv_weight.T.reshape(-1), conv_bias, dt_bias, a_log, skip_gain, gated_gain]
    sizes = [v.shape[0] for v in small]
    small.append(in_local[inner + channels :].reshape(-1))
    packed_low = lax.all_gather(jnp.concatenate(small), "wshard", axis=0)
    packed = packed_low.astype(f32)
    parts, at = [], 0
    for size in sizes:
        parts.append(packed[:, at : at + size])
        at += size
    norm_g = parts[0].reshape(-1)
    conv_w = parts[1].reshape(shards, taps, -1).transpose(1, 0, 2).reshape(taps, -1)
    conv_b = parts[2].reshape(-1)
    dt_shift = parts[3].reshape(-1)
    rate = -jnp.exp(parts[4].reshape(-1))
    skip = parts[5].reshape(-1)
    gated_g = parts[6].reshape(-1)

    dt_w = packed_low[:, at:].reshape(shards, heads, -1).transpose(1, 0, 2).reshape(heads, -1)
    order = jnp.arange(shards) ^ shard if fast else jnp.arange(shards)
    if fast:
        in_w = gather_input_weight(in_local, inner, channels)
        out_part = lax.optimization_barrier((out_weight, in_w[0, 0, 0]))[0]
    else:
        in_w = lax.all_gather(in_local[: inner + channels], "wshard", axis=0)
        out_part = out_weight
    out_w = lax.all_gather(out_part, "wshard", axis=0, tiled=True)

    def grouped(v):
        return v.reshape(micro, tokens, groups, GROUP).transpose(0, 2, 1, 3)

    rows_in = hidden.reshape(rows, width).astype(f32)
    cot = out_grad.reshape(rows, width).astype(f32)
    positions = rank * tokens + jnp.arange(tokens, dtype=jnp.int32)
    valid = (positions[None, :] < lengths[:, 0][:, None]).astype(f32).reshape(rows, 1)
    normed, front_back = jax.vjp(rms_front, rows_in, norm_g)
    normed_low = normed.astype(bf16)
    normed_parts = normed_low.reshape(rows, shards, -1).transpose(1, 0, 2)[order]
    tile = 256
    conv_low = project(normed_parts, in_w, inner, channels, tile, bf16)
    gate_in = project(normed_parts, in_w, 0, inner, tile, f32)
    dt_low = mm(normed_low, dt_w, NT).astype(bf16)
    conv_low = conv_low.reshape(micro, tokens, channels)
    prior = from_behind(conv_low[:, tokens - (taps - 1) :], "seq", 1)
    padded = jnp.concatenate([prior, conv_low], axis=1).astype(f32)
    mixed, conv_back = jax.vjp(conv_act, padded, conv_w, conv_b)
    x_low = mixed[..., :inner].astype(bf16)
    b_low = mixed[..., inner : inner + n].astype(bf16)
    c_low = mixed[..., inner + n :].astype(bf16)

    dt_raw = dt_low.astype(f32).reshape(micro, tokens, heads) + dt_shift
    dt = jax.nn.softplus(dt_raw)
    tri = (jnp.arange(tokens)[:, None] >= jnp.arange(tokens)[None, :]).astype(f32)
    cum = jnp.einsum("ij,mjh->mih", tri, dt * rate, precision=highest)
    dt_g, cum_g = grouped(dt), grouped(cum)
    row_g = cum_g.transpose(0, 1, 3, 2)
    last = cum[:, tokens - 1, :]
    decays = lax.all_gather(jnp.exp(last), "seq", axis=0)
    end_w = grouped(dt * jnp.exp(last[:, None, :] - cum))
    decay_w = grouped(jnp.exp(cum))
    skip_wide = jnp.repeat(skip, hs)[None, :]

    own_state = block_states(x_low, end_w, b_low.transpose(0, 2, 1), hs)
    y_local = local_scan(x_low, dt_g, cum_g, row_g, b_low, c_low, hs)
    s_in = running_states(own_state, decays, hs, True)
    y_scan, scanned_low = add_carry(x_low, y_local, cum_g, c_low, s_in, skip_wide, hs)

    scanned = scanned_low.reshape(rows, inner).astype(f32)
    normed_out, gate_back = jax.vjp(gate_norm, scanned, gate_in, gated_g)
    normed_out_low = normed_out.astype(bf16)
    branch = mm(normed_out_low, out_w)
    output = (rows_in + valid * branch).astype(bf16).reshape(hidden.shape)

    g = (cot * valid).astype(bf16)
    out_terms = mm(normed_out_low, g, TN)
    d_scanned, d_gate_in, d_gated = gate_back(mm(g, out_w, NT))
    dy = d_scanned.astype(bf16).reshape(micro, tokens, inner)
    own_grad = block_states(dy, decay_w, c_low.transpose(0, 2, 1), hs)
    dx_local, db_local, dc_local = local_back(x_low, dy, dt_g, cum_g, row_g, b_low, c_low, hs)
    ds = running_states(own_grad, decays, hs, False)
    dx_low, ddt_g, dcum_g, db, dc, last_term, dskip = carry_back(
        x_low, dy, dx_local, y_scan, dt_g, cum_g, b_low, s_in, ds, db_local, dc_local, skip_wide, hs
    )

    def ungrouped(v):
        return v.transpose(0, 2, 1, 3).reshape(micro, tokens, heads)

    at_end = jnp.sum(last_term.reshape(micro, heads, hs), axis=-1)[:, None, :]
    d_log = jnp.einsum("ij,mih->mjh", tri, ungrouped(dcum_g), precision=highest) + at_end
    d_dt = (ungrouped(ddt_g) + d_log * rate) * jax.nn.sigmoid(dt_raw)
    d_dt_bias = jnp.sum(d_dt, axis=(0, 1))
    d_a_log = jnp.sum(d_log * dt, axis=(0, 1)) * rate
    d_skip = jnp.sum(dskip.reshape(-1, heads, hs), axis=(0, 2))
    mixed_grad = jnp.concatenate([dx_low.astype(f32), db, dc], axis=2)
    d_padded, d_conv_w, d_conv_b = conv_back(mixed_grad)
    from_next = from_behind(d_padded[:, : taps - 1].astype(bf16), "seq", -1).astype(f32)
    d_conv = d_padded[:, taps - 1 :].at[:, tokens - (taps - 1) :].add(from_next)
    d_dt_low = d_dt.astype(bf16).reshape(rows, heads)
    total_cols = inner + channels + heads
    pad = -total_cols % 256 if fast else 0
    d_proj = jnp.concatenate(
        [
            d_gate_in.astype(bf16),
            d_conv.astype(bf16).reshape(rows, channels),
            d_dt_low,
            jnp.zeros((rows, pad), bf16),
        ],
        axis=1,
    )
    d_parts = unproject(d_proj, in_w, tile)
    d_normed = d_parts[order].transpose(1, 0, 2).reshape(rows, width) + mm(d_dt_low, dt_w)
    d_hidden, d_norm_g = front_back(d_normed)
    input_grad = (d_hidden + cot).astype(bf16).reshape(hidden.shape)

    def summed(terms, axis):
        t = lax.psum_scatter(terms.astype(bf16), "seq", scatter_dimension=0, tiled=True)
        t = lax.psum_scatter(t, "wshard", scatter_dimension=axis, tiled=True)
        return lax.all_gather(t, "seq", axis=0, tiled=True).astype(f32)

    if fast:
        in_grad = reduce_products(d_proj, normed_low, 2)[:total_cols].astype(f32).T
    else:
        in_grad = summed(mm(d_proj, normed_low, TN), 1).T
    blocks = out_terms.reshape(shards, count, -1, width).transpose(1, 0, 2, 3)
    blocks = blocks.reshape(inner, width)
    out_w_grad = summed_rows(blocks, shards, count)
    smalls = [
        d_norm_g.reshape(shards, -1),
        d_conv_w.reshape(taps, shards, -1).transpose(1, 0, 2).reshape(shards, -1),
        d_conv_b.reshape(shards, -1),
        d_dt_bias.reshape(shards, -1),
        d_a_log.reshape(shards, -1),
        d_skip.reshape(shards, -1),
        d_gated.reshape(shards, -1),
    ]
    sums = lax.psum(jnp.concatenate(smalls, axis=1), ("seq", "wshard"))
    sums = lax.dynamic_index_in_dim(sums, shard, 0, keepdims=False)
    found, at = [], 0
    for size in sizes:
        found.append(sums[at : at + size])
        at += size
    return (
        output,
        input_grad,
        found[0],
        in_grad,
        found[1].reshape(taps, -1).T,
        found[2],
        found[3],
        found[4],
        found[5],
        found[6],
        out_w_grad,
    )


def summed_rows(blocks, shards, count):
    t = lax.psum_scatter(blocks.astype(bf16), "seq", scatter_dimension=0, tiled=True)
    t = lax.psum_scatter(t, "wshard", scatter_dimension=0, tiled=True)
    return lax.all_gather(t, "seq", axis=0, tiled=True).astype(f32)


def solution(mesh):
    return jax.shard_map(
        local,
        mesh=mesh,
        in_specs=(
            P(None, "wshard", "seq", None),
            P(None, "wshard"),
            P(None, "wshard", "seq", None),
            P("wshard"),
            P("wshard", None),
            P("wshard", None),
            P("wshard"),
            P("wshard"),
            P("wshard"),
            P("wshard"),
            P("wshard"),
            P("wshard", None),
        ),
        out_specs=(
            P(None, "wshard", "seq", None),
            P(None, "wshard", "seq", None),
            P("wshard"),
            P("wshard", None),
            P("wshard", None),
            P("wshard"),
            P("wshard"),
            P("wshard"),
            P("wshard"),
            P("wshard"),
            P("wshard", None),
        ),
        check_vma=False,
    )
```

```python
from functools import partial

import jax
import jax.numpy as jnp
from jax import lax
from jax.experimental import pallas as pl
from jax.experimental.pallas import tpu as pltpu
from jax.sharding import PartitionSpec as P

epsilon = 1e-05
highest = lax.Precision.HIGHEST
f32 = jnp.float32
bf16 = jnp.bfloat16
GROUP = 8
VMEM = 48 * 1024 * 1024
VMEM_MOST = 60 * 1024 * 1024

NN = (((1,), (0,)), ((), ()))
NT = (((1,), (1,)), ((), ()))
TN = (((0,), (0,)), ((), ()))


def mm(a, b, dims=NN):
    return lax.dot_general(a, b, dims, preferred_element_type=f32)


def params():
    return pltpu.CompilerParams(
        dimension_semantics=("arbitrary", "arbitrary"), vmem_limit_bytes=VMEM
    )


def widen(cols, head_size):
    t, heads = cols.shape
    lane = lax.broadcasted_iota(jnp.int32, (t, 2 * head_size), 1)
    parts = []
    for k in range(0, heads, 2):
        parts.append(jnp.where(lane < head_size, cols[:, k : k + 1], cols[:, k + 1 : k + 2]))
    return jnp.concatenate(parts, axis=1)


def state_kernel(hs, x_ref, w_ref, bt_ref, o_ref):
    weighted = (x_ref[0].astype(f32) * widen(w_ref[0, 0], hs)).astype(bf16)
    o_ref[0] = mm(bt_ref[0], weighted)


def block_states(x, weights, bt, hs):
    micro, t, cols = x.shape
    n = bt.shape[1]
    gc = GROUP * hs
    return pl.pallas_call(
        partial(state_kernel, hs),
        grid=(micro, cols // gc),
        in_specs=[
            pl.BlockSpec((1, t, gc), lambda m, g: (m, 0, g)),
            pl.BlockSpec((1, 1, t, GROUP), lambda m, g: (m, g, 0, 0)),
            pl.BlockSpec((1, n, t), lambda m, g: (m, 0, 0)),
        ],
        out_specs=pl.BlockSpec((1, n, gc), lambda m, g: (m, 0, g)),
        out_shape=jax.ShapeDtypeStruct((micro, n, cols), f32),
        compiler_params=params(),
        name="block_states",
    )(x, weights, bt)


def local_kernel(hs, x_ref, dt_ref, cum_ref, row_ref, b_ref, c_ref, o_ref, scores):
    t = x_ref.shape[1]
    half = t // 2

    @pl.when(pl.program_id(1) == 0)
    def _():
        s = mm(c_ref[0], b_ref[0], NT)
        i = lax.broadcasted_iota(jnp.int32, (t, t), 0)
        j = lax.broadcasted_iota(jnp.int32, (t, t), 1)
        scores[...] = jnp.where(i >= j, s, 0.0)

    cum, dt, rows = cum_ref[0, 0], dt_ref[0, 0], row_ref[0, 0]
    lane = lax.broadcasted_iota(jnp.int32, (half, 2 * hs), 1)
    weighted = (x_ref[0].astype(f32) * widen(dt, hs)).astype(bf16)
    for k in range(0, GROUP, 2):
        at = slice(k * hs, (k + 2) * hs)
        pair = weighted[:, at]
        top, low = [], []
        for h in (k, k + 1):
            col, row = cum[:, h : h + 1], rows[h : h + 1, :]
            m1 = jnp.exp(jnp.minimum(col[:half] - row[:, :half], 0.0)) * scores[:half, :half]
            m2 = jnp.exp(jnp.minimum(col[half:] - row, 0.0)) * scores[half:, :]
            top.append(mm(m1.astype(bf16), pair[:half]))
            low.append(mm(m2.astype(bf16), pair))
        o_ref[0, :half, at] = jnp.where(lane < hs, top[0], top[1])
        o_ref[0, half:, at] = jnp.where(lane < hs, low[0], low[1])


def local_scan(x, dt, cum, rows, b, c, hs):
    micro, t, cols = x.shape
    n = b.shape[2]
    gc = GROUP * hs
    return pl.pallas_call(
        partial(local_kernel, hs),
        grid=(micro, cols // gc),
        in_specs=[
            pl.BlockSpec((1, t, gc), lambda m, g: (m, 0, g)),
            pl.BlockSpec((1, 1, t, GROUP), lambda m, g: (m, g, 0, 0)),
            pl.BlockSpec((1, 1, t, GROUP), lambda m, g: (m, g, 0, 0)),
            pl.BlockSpec((1, 1, GROUP, t), lambda m, g: (m, g, 0, 0)),
            pl.BlockSpec((1, t, n), lambda m, g: (m, 0, 0)),
            pl.BlockSpec((1, t, n), lambda m, g: (m, 0, 0)),
        ],
        out_specs=pl.BlockSpec((1, t, gc), lambda m, g: (m, 0, g)),
        out_shape=jax.ShapeDtypeStruct((micro, t, cols), f32),
        scratch_shapes=[pltpu.VMEM((t, t), f32)],
        compiler_params=params(),
        name="local_scan",
    )(x, dt, cum, rows, b, c)


def carry_kernel(hs, x_ref, y_ref, cum_ref, c_ref, s_ref, skip_ref, scan_ref, low_ref):
    carried = mm(c_ref[0], s_ref[0].astype(bf16)) * widen(jnp.exp(cum_ref[0, 0]), hs)
    scan = y_ref[0] + carried
    scan_ref[0] = scan
    low_ref[0] = (scan + skip_ref[...] * x_ref[0].astype(f32)).astype(bf16)


def add_carry(x, y, cum, c, s_in, skip_wide, hs):
    micro, t, cols = x.shape
    n = c.shape[2]
    gc = GROUP * hs
    wide = pl.BlockSpec((1, t, gc), lambda m, g: (m, 0, g))
    return pl.pallas_call(
        partial(carry_kernel, hs),
        grid=(micro, cols // gc),
        in_specs=[
            wide,
            wide,
            pl.BlockSpec((1, 1, t, GROUP), lambda m, g: (m, g, 0, 0)),
            pl.BlockSpec((1, t, n), lambda m, g: (m, 0, 0)),
            pl.BlockSpec((1, n, gc), lambda m, g: (m, 0, g)),
            pl.BlockSpec((1, gc), lambda m, g: (0, g)),
        ],
        out_specs=[wide, wide],
        out_shape=[
            jax.ShapeDtypeStruct((micro, t, cols), f32),
            jax.ShapeDtypeStruct((micro, t, cols), bf16),
        ],
        compiler_params=params(),
        name="add_carry",
    )(x, y, cum, c, s_in, skip_wide)


def local_back_kernel(
    hs, x_ref, dy_ref, dt_ref, cum_ref, row_ref, b_ref, c_ref, dx_ref, db_ref, dc_ref, scores, total
):
    t = x_ref.shape[1]
    half = t // 2

    @pl.when(pl.program_id(1) == 0)
    def _():
        s = mm(b_ref[0], c_ref[0], NT)
        j = lax.broadcasted_iota(jnp.int32, (t, t), 0)
        i = lax.broadcasted_iota(jnp.int32, (t, t), 1)
        scores[...] = jnp.where(i >= j, s, 0.0)
        total[...] = jnp.zeros_like(total)

    cum, dt, rows = cum_ref[0, 0], dt_ref[0, 0], row_ref[0, 0]
    lane = lax.broadcasted_iota(jnp.int32, (t, 2 * hs), 1)
    lane_half = lax.broadcasted_iota(jnp.int32, (half, 2 * hs), 1)
    weighted = (x_ref[0].astype(f32) * widen(dt, hs)).astype(bf16)
    for k in range(0, GROUP, 2):
        at = slice(k * hs, (k + 2) * hs)
        pair = weighted[:, at]
        dy = dy_ref[0, :, at]
        top, low = [], []
        for h in (k, k + 1):
            col, row = cum[:, h : h + 1], rows[h : h + 1, :]
            mine = jnp.where(lane < hs, pair, 0) if h == k else jnp.where(lane < hs, 0, pair)
            l1 = jnp.exp(jnp.minimum(row - col[:half], 0.0))
            l2 = jnp.exp(jnp.minimum(row[:, half:] - col[half:], 0.0))
            total[:half, :] += l1 * mm(mine[:half], dy, NT)
            total[half:, half:] += l2 * mm(mine[half:], dy[half:], NT)
            top.append(mm((l1 * scores[:half, :]).astype(bf16), dy))
            low.append(mm((l2 * scores[half:, half:]).astype(bf16), dy[half:]))
        dx_ref[0, :half, at] = jnp.where(lane_half < hs, top[0], top[1])
        dx_ref[0, half:, at] = jnp.where(lane_half < hs, low[0], low[1])

    @pl.when(pl.program_id(1) == pl.num_programs(1) - 1)
    def _():
        j = lax.broadcasted_iota(jnp.int32, (t, t), 0)
        i = lax.broadcasted_iota(jnp.int32, (t, t), 1)
        d = jnp.where(i >= j, total[...], 0.0)
        db_ref[0] = mm(d.astype(bf16), c_ref[0])
        dc_ref[0] = mm(d.T.astype(bf16), b_ref[0])


def local_back(x, dy, dt, cum, rows, b, c, hs):
    micro, t, cols = x.shape
    n = b.shape[2]
    gc = GROUP * hs
    wide = pl.BlockSpec((1, t, gc), lambda m, g: (m, 0, g))
    small = pl.BlockSpec((1, 1, t, GROUP), lambda m, g: (m, g, 0, 0))
    state = pl.BlockSpec((1, t, n), lambda m, g: (m, 0, 0))
    return pl.pallas_call(
        partial(local_back_kernel, hs),
        grid=(micro, cols // gc),
        in_specs=[
            wide,
            wide,
            small,
            small,
            pl.BlockSpec((1, 1, GROUP, t), lambda m, g: (m, g, 0, 0)),
            state,
            state,
        ],
        out_specs=[wide, state, state],
        out_shape=[
            jax.ShapeDtypeStruct((micro, t, cols), f32),
            jax.ShapeDtypeStruct((micro, t, n), f32),
            jax.ShapeDtypeStruct((micro, t, n), f32),
        ],
        scratch_shapes=[pltpu.VMEM((t, t), f32), pltpu.VMEM((t, t), f32)],
        compiler_params=params(),
        name="local_back",
    )(x, dy, dt, cum, rows, b, c)


def head_sums(values, ones):
    high = values.astype(bf16)
    rest = (values - high.astype(f32)).astype(bf16)
    return mm(high, ones) + mm(rest, ones)


def carry_back_kernel(
    hs,
    x_ref,
    dy_ref,
    dxl_ref,
    y_ref,
    dt_ref,
    cum_ref,
    b_ref,
    si_ref,
    ds_ref,
    dbl_ref,
    dcl_ref,
    skip_ref,
    dx_ref,
    ddt_ref,
    dcum_ref,
    db_ref,
    dc_ref,
    last_ref,
    dskip_ref,
):
    t = x_ref.shape[1]
    gc = x_ref.shape[2]

    @pl.when(pl.program_id(1) == 0)
    def _():
        db_ref[0] = dbl_ref[0]
        dc_ref[0] = dcl_ref[0]

    cum, dt = cum_ref[0, 0], dt_ref[0, 0]
    x, dy = x_ref[0].astype(f32), dy_ref[0].astype(f32)
    dt_wide = widen(dt, hs)
    weighted = (x * dt_wide).astype(bf16).astype(f32)
    decay = widen(jnp.exp(cum), hs)
    to_end = widen(jnp.exp(cum[t - 1 :, :] - cum), hs)
    s_in, ds = si_ref[0].astype(f32), ds_ref[0]
    s_low, ds_low = s_in.astype(bf16), ds.astype(bf16)
    through = to_end * mm(b_ref[0], ds_low)
    d_weighted = dxl_ref[0] + through
    dx_ref[0] = (dt_wide * d_weighted + skip_ref[...] * dy).astype(bf16)
    db_ref[0] += mm((weighted * to_end).astype(bf16), ds_low, NT)
    dc_ref[0] += mm((dy * decay).astype(bf16), s_low, NT)
    r = lax.broadcasted_iota(jnp.int32, (gc, 128), 0)
    c = lax.broadcasted_iota(jnp.int32, (gc, 128), 1)
    ones = jnp.where(r // hs == c, 1.0, 0.0).astype(bf16)
    ddt_ref[0, 0] = head_sums(x * d_weighted, ones)[:, :GROUP]
    dcum_ref[0, 0] = head_sums(dy * y_ref[0] - weighted * d_weighted, ones)[:, :GROUP]
    last_decay = decay[t - 1 :, :]
    last_ref[0] = jnp.sum(weighted * through, axis=0, keepdims=True) + last_decay * jnp.sum(
        s_low.astype(f32) * ds, axis=0, keepdims=True
    )
    dskip_ref[0] = jnp.sum(x * dy, axis=0, keepdims=True)


def carry_back(x, dy, dxl, y, dt, cum, b, s_in, ds, dbl, dcl, skip_wide, hs):
    micro, t, cols = x.shape
    n = b.shape[2]
    gc = GROUP * hs
    groups = cols // gc
    wide = pl.BlockSpec((1, t, gc), lambda m, g: (m, 0, g))
    small = pl.BlockSpec((1, 1, t, GROUP), lambda m, g: (m, g, 0, 0))
    state = pl.BlockSpec((1, t, n), lambda m, g: (m, 0, 0))
    st = pl.BlockSpec((1, n, gc), lambda m, g: (m, 0, g))
    line = pl.BlockSpec((1, 1, gc), lambda m, g: (m, 0, g))
    return pl.pallas_call(
        partial(carry_back_kernel, hs),
        grid=(micro, groups),
        in_specs=[
            wide,
            wide,
            wide,
            wide,
            small,
            small,
            state,
            st,
            st,
            state,
            state,
            pl.BlockSpec((1, gc), lambda m, g: (0, g)),
        ],
        out_specs=[wide, small, small, state, state, line, line],
        out_shape=[
            jax.ShapeDtypeStruct((micro, t, cols), bf16),
            jax.ShapeDtypeStruct((micro, groups, t, GROUP), f32),
            jax.ShapeDtypeStruct((micro, groups, t, GROUP), f32),
            jax.ShapeDtypeStruct((micro, t, n), f32),
            jax.ShapeDtypeStruct((micro, t, n), f32),
            jax.ShapeDtypeStruct((micro, 1, cols), f32),
            jax.ShapeDtypeStruct((micro, 1, cols), f32),
        ],
        compiler_params=params(),
        name="carry_back",
    )(x, dy, dxl, y, dt, cum, b, s_in, ds, dbl, dcl, skip_wide)


def from_behind(x, axis, by):
    count = lax.axis_size(axis)
    pairs = [(i, i + by) for i in range(count) if 0 <= i + by < count]
    return lax.ppermute(x, axis, pairs)


def swap(x, by):
    count = lax.axis_size("seq")
    return lax.ppermute(x, "seq", [(i, i ^ by) for i in range(count)])


def running_states(terms, decays, hs, forward):
    count = lax.axis_size("seq")
    rank = lax.axis_index("seq")
    index = jnp.arange(count)

    def product(mask):
        d = jnp.prod(jnp.where(mask[:, None, None], decays, 1.0), axis=0)
        return jnp.repeat(d, hs, axis=1)[:, None, :]

    total, before = terms, jnp.zeros_like(terms)
    size = 1
    while size < count:
        other = swap(total.astype(bf16), size).astype(f32)
        mine = index // size == rank // size
        theirs = index // size == (rank // size) ^ 1
        later = (rank // size) % 2 == (1 if forward else 0)
        passed = mine & ((index < rank) if forward else (index > rank))
        before = before + jnp.where(later, product(passed), 0.0) * other
        if 2 * size < count:
            total = total * jnp.where(later, 1.0, product(theirs)) + other * jnp.where(
                later, product(mine), 1.0
            )
        size *= 2
    return before


MESH = pl.DeviceIdType.MESH


def around():
    s, z = lax.axis_index("seq"), lax.axis_index("wshard")
    c, x, y = s % 2, (s // 2) % 2, s // 4
    near = {
        "c": (s + 1 - 2 * c, z),
        "x": (s + 2 - 4 * x, z),
        "y": (s + 4 - 8 * y, z),
        "z1": (s, z + 1 - 2 * (z % 2)),
        "z2": (s, z + 2 - 4 * (z // 2)),
        "z3": (s, 3 - z),
    }
    return s, z, c, x, y, near


def greet(near):
    barrier = pltpu.get_barrier_semaphore()
    for where in near.values():
        pl.semaphore_signal(barrier, inc=1, device_id=where, device_id_type=MESH)
    pl.semaphore_wait(barrier, len(near))


CHUNK_DMAS = 10
AHEAD = 2


def gather_kernel(chunks, w_ref, o_ref, send, recv):
    s, z, c, x, y, near = around()
    greet(near)
    sx, sy, sd = s + 2 - 4 * x, s + 4 - 8 * y, s + 6 - 4 * x - 8 * y
    plans = []
    for q, (base, piece, off, size, first) in enumerate(chunks):

        def rows(who, base=base, piece=piece, off=off, size=size):
            return pl.ds(pl.multiple_of(base + who * piece + off, 16), size)

        def move(src, dst, kind, to, q=q):
            return pltpu.make_async_remote_copy(
                src_ref=src,
                dst_ref=dst,
                send_sem=send.at[q, kind],
                recv_sem=recv.at[q, kind],
                device_id=near[to],
                device_id_type=MESH,
            )

        def block(who, rows=rows):
            return o_ref.at[:, rows(who)]

        def along(who, kind, to, move=move, block=block):
            return move(block(who), block(who), kind, to)

        plan = {}
        for k in (1, 2, 3):
            plan["z%d" % k] = move(w_ref.at[rows(s)], o_ref.at[k - 1, rows(s)], k - 1, "z%d" % k)
        plan["x"] = along(s, 3, "x")
        plan["y"] = along(s, 4, "y")
        plan["d"] = along(sx, 5, "y") if first == "x" else along(sy, 5, "x")
        plan["c0"] = along(s, 6, "c")
        plan["cx"] = along(sx, 7, "c")
        plan["cy"] = along(sy, 8, "c")
        plan["cd"] = along(sd, 9, "c")
        plan["first"] = first
        plans.append(plan)

    def fetch(plan):
        for k in (1, 2, 3):
            plan["z%d" % k].start()

    def begin(plan):
        for k in (1, 2, 3):
            plan["z%d" % k].wait_recv()
        for name in ("x", "y", "c0"):
            plan[name].start()

    def middle(plan):
        one, two = ("x", "y") if plan["first"] == "x" else ("y", "x")
        plan[one].wait_recv()
        plan["d"].start()
        plan["c" + one].start()
        plan[two].wait_recv()
        plan["c" + two].start()

    def finish(plan):
        plan["d"].wait_recv()
        plan["cd"].start()

    n = len(plans)
    for i in range(min(AHEAD, n)):
        fetch(plans[i])
    for i in range(n + 2):
        if i < n:
            begin(plans[i])
            if i + AHEAD < n:
                fetch(plans[i + AHEAD])
        if 0 <= i - 1 < n:
            middle(plans[i - 1])
        if 0 <= i - 2 < n:
            finish(plans[i - 2])
    for plan in plans:
        for name in ("c0", "cx", "cy", "cd"):
            plan[name].wait_recv()
        for name in ("z1", "z2", "z3", "x", "y", "d", "c0", "cx", "cy", "cd"):
            plan[name].wait_send()


def split_rows(piece, parts=6):
    tiles = piece // 16
    return [16 * (tiles * (i + 1) // parts - tiles * i // parts) for i in range(parts)]


def gather_input_weight(w_t, inner, channels):
    total = inner + channels
    chunks = []
    for base, piece in ((inner, channels // 8), (0, inner // 8)):
        off = 0
        for i, size in enumerate(split_rows(piece)):
            chunks.append((base, piece, off, size, "xy"[i % 2]))
            off += size
    width = w_t.shape[1]
    return pl.pallas_call(
        partial(gather_kernel, chunks),
        in_specs=[pl.BlockSpec(memory_space=pl.ANY)],
        out_specs=pl.BlockSpec(memory_space=pl.ANY),
        out_shape=jax.ShapeDtypeStruct((3, total, width), bf16),
        scratch_shapes=[
            pltpu.SemaphoreType.DMA((len(chunks), CHUNK_DMAS)),
            pltpu.SemaphoreType.DMA((len(chunks), CHUNK_DMAS)),
        ],
        compiler_params=pltpu.CompilerParams(collective_id=1, has_side_effects=True),
        cost_estimate=pl.CostEstimate(flops=0, bytes_accessed=200_000_000, transcendentals=0),
        name="gather_input_weight",
    )(w_t)


def reduce_kernel(
    chunks,
    pieces,
    groups,
    dp_ref,
    nm_ref,
    o_ref,
    dp,
    nm,
    g,
    sa1,
    sb1,
    sa2,
    sb2,
    s3,
    ka2,
    kb2,
    f3,
    ra1,
    rb1,
    ra2,
    rb2,
    rz,
    in_sem,
    s_in,
    r_in,
    s_step,
    r_step,
    s_all,
    r_all,
):
    s, z, c, x, y, near = around()
    wide = dp.shape[2]
    shard = rz.shape[-1]

    def remote(src, dst, ss, rs, to):
        return pltpu.make_async_remote_copy(
            src_ref=src, dst_ref=dst, send_sem=ss, recv_sem=rs, device_id=near[to], device_id_type=MESH
        )

    local_copies, core_copies = [], []
    for i, (a, b) in enumerate(pieces):
        here = dp_ref.at[:, pl.ds(pl.multiple_of(c * wide + a, 128), b - a)]
        there = dp_ref.at[:, pl.ds(pl.multiple_of((1 - c) * wide + a, 128), b - a)]
        local_copies.append(
            pltpu.make_async_copy(here, dp.at[0, :, pl.ds(a, b - a)], in_sem.at[i])
        )
        core_copies.append(
            remote(there, dp.at[1, :, pl.ds(a, b - a)], s_in.at[i], r_in.at[i], "c")
        )
    n_in = len(pieces)
    nm_local = pltpu.make_async_copy(nm_ref, nm.at[0], in_sem.at[n_in])
    nm_core = remote(nm_ref, nm.at[1], s_in.at[n_in], r_in.at[n_in], "c")
    nm_local.start()
    for copy in local_copies:
        copy.start()
    greet(near)
    nm_core.start()
    for copy in core_copies:
        copy.start()

    def step_copy(kind, u):
        slot = u % 2
        ss, rs = s_step.at[kind, slot], r_step.at[kind, u]
        if kind == 0:
            return remote(sa1.at[slot], ra1.at[u], ss, rs, "x")
        if kind == 1:
            return remote(sb1.at[slot], rb1.at[u], ss, rs, "y")
        if kind == 2:
            return remote(sa2.at[slot], ra2.at[u], ss, rs, "y")
        if kind == 3:
            return remote(sb2.at[slot], rb2.at[u], ss, rs, "x")
        k = kind - 3
        other = (z + 1 - 2 * (z % 2), z + 2 - 4 * (z // 2), 3 - z)[k - 1]
        cols = pl.ds(pl.multiple_of(other * shard, 128), shard)
        return remote(s3.at[slot, :, :, cols], rz.at[u, k - 1], ss, rs, "z%d" % k)

    def part(px, py, ts, T=None):
        if T is None:
            return o_ref.at[c, ts, :, px, py]
        return o_ref.at[c, ts, T, px, py]

    def all_copy(q, kind):
        a, b = groups[q]
        ts = pl.ds(a, b - a)
        ss, rs = s_all.at[q, kind], r_all.at[q, kind]
        if kind == 0:
            return remote(part(x, y, ts), part(x, y, ts), ss, rs, "x")
        if kind == 1:
            return remote(part(x, y, ts), part(x, y, ts), ss, rs, "y")
        if kind == 2:
            return remote(part(x, y, ts), part(x, y, ts), ss, rs, "c")
        if kind == 3:
            return remote(part(1 - x, y, ts, 0), part(1 - x, y, ts, 0), ss, rs, "y")
        if kind == 4:
            return remote(part(x, 1 - y, ts, 1), part(x, 1 - y, ts, 1), ss, rs, "x")
        if kind == 5:
            return remote(part(1 - x, y, ts), part(1 - x, y, ts), ss, rs, "c")
        if kind == 6:
            return remote(part(x, 1 - y, ts), part(x, 1 - y, ts), ss, rs, "c")
        return remote(part(1 - x, 1 - y, ts), part(1 - x, 1 - y, ts), ss, rs, "c")

    def sl(at, size=16):
        return pl.ds(pl.multiple_of(at, 16), size)

    def free(kind, u):
        @pl.when(u >= 2)
        def _():
            step_copy(kind, u - 2).wait_send()

    def step(t, carry):
        @pl.when(t < chunks)
        def _():
            for i, (a, _) in enumerate(pieces):

                @pl.when(t == a // 128)
                def _(i=i):
                    if i == 0:
                        nm_local.wait()
                        nm_core.wait_recv()
                    local_copies[i].wait()
                    core_copies[i].wait_recv()

            slot = t % 2
            cols = pl.ds(pl.multiple_of(t * 128, 128), 128)
            g[slot] = mm(dp[0, :, cols], nm[0], TN) + mm(dp[1, :, cols], nm[1], TN)
            free(0, t)
            free(1, t)
            sa1[slot] = g[slot, sl((1 - x) * 32, 32)].astype(bf16)
            step_copy(0, t).start()
            sb1[slot, 0:16] = g[slot, sl(64 + (1 - y) * 16)].astype(bf16)
            sb1[slot, 16:32] = g[slot, sl(96 + (1 - y) * 16)].astype(bf16)
            step_copy(1, t).start()

        @pl.when((t >= 1) & (t - 1 < chunks))
        def _():
            u = t - 1
            slot = u % 2
            step_copy(0, u).wait_recv()
            free(2, u)
            sa2[slot] = (
                g[slot, sl(x * 32 + (1 - y) * 16)] + ra1[u, sl((1 - y) * 16)].astype(f32)
            ).astype(bf16)
            step_copy(2, u).start()
            ka2[slot] = g[slot, sl(x * 32 + y * 16)] + ra1[u, sl(y * 16)].astype(f32)
            step_copy(1, u).wait_recv()
            free(3, u)
            sb2[slot] = (
                g[slot, sl(64 + (1 - x) * 32 + y * 16)] + rb1[u, sl((1 - x) * 16)].astype(f32)
            ).astype(bf16)
            step_copy(3, u).start()
            kb2[slot] = g[slot, sl(64 + x * 32 + y * 16)] + rb1[u, sl(x * 16)].astype(f32)

        @pl.when((t >= 2) & (t - 2 < chunks))
        def _():
            u = t - 2
            slot = u % 2
            step_copy(2, u).wait_recv()
            step_copy(3, u).wait_recv()
            for k in (4, 5, 6):
                free(k, u)
            va = ka2[slot] + ra2[u].astype(f32)
            vb = kb2[slot] + rb2[u].astype(f32)
            f3[slot, 0] = va
            f3[slot, 1] = vb
            s3[slot, 0] = va.astype(bf16)
            s3[slot, 1] = vb.astype(bf16)
            for k in (4, 5, 6):
                step_copy(k, u).start()

        @pl.when((t >= 3) & (t - 3 < chunks))
        def _():
            u = t - 3
            slot = u % 2
            for k in (4, 5, 6):
                step_copy(k, u).wait_recv()
            mine = pl.ds(pl.multiple_of(z * shard, 128), shard)
            for T in (0, 1):
                total = f3[slot, T, :, mine]
                for k in range(3):
                    total = total + rz[u, k, T].astype(f32)
                o_ref[c, u, T, x, y] = total.astype(bf16)

        for q, (a, b) in enumerate(groups):

            @pl.when(t == b - 1 + 3)
            def _(q=q):
                for kind in (0, 1, 2):
                    all_copy(q, kind).start()

            @pl.when(t == b - 1 + 4)
            def _(q=q):
                all_copy(q, 0).wait_recv()
                all_copy(q, 3).start()
                all_copy(q, 5).start()
                all_copy(q, 1).wait_recv()
                all_copy(q, 4).start()
                all_copy(q, 6).start()

            @pl.when(t == b - 1 + 5)
            def _(q=q):
                all_copy(q, 3).wait_recv()
                all_copy(q, 4).wait_recv()
                all_copy(q, 7).start()

        return carry

    lax.fori_loop(0, chunks + 5, step, 0)
    for q in range(len(groups)):
        for kind in (2, 5, 6, 7):
            all_copy(q, kind).wait_recv()
        for kind in range(8):
            all_copy(q, kind).wait_send()
    for u in (chunks - 2, chunks - 1):
        for kind in range(7):
            step_copy(kind, u).wait_send()
    nm_core.wait_send()
    for copy in core_copies:
        copy.wait_send()


def reduce_products(dp, nm, collective_id):
    rows, total = dp.shape
    width = nm.shape[1]
    shard = width // 4
    wide = total // 2
    chunks = wide // 128
    cuts = sorted({0, min(256, wide), min(1280, wide), wide})
    pieces = list(zip(cuts[:-1], cuts[1:]))
    marks = sorted({0, chunks * 2 // 5, chunks * 7 // 10, chunks * 9 // 10, chunks})
    groups = list(zip(marks[:-1], marks[1:]))
    n = len(pieces)
    dma = pltpu.SemaphoreType.DMA
    out = pl.pallas_call(
        partial(reduce_kernel, chunks, pieces, groups),
        in_specs=[pl.BlockSpec(memory_space=pl.ANY)] * 2,
        out_specs=pl.BlockSpec(memory_space=pltpu.VMEM),
        out_shape=jax.ShapeDtypeStruct((2, chunks, 2, 2, 2, 16, shard), bf16),
        scratch_shapes=[
            pltpu.VMEM((2, rows, wide), bf16),
            pltpu.VMEM((2, rows, width), bf16),
            pltpu.VMEM((2, 128, width), f32),
            pltpu.VMEM((2, 32, width), bf16),
            pltpu.VMEM((2, 32, width), bf16),
            pltpu.VMEM((2, 16, width), bf16),
            pltpu.VMEM((2, 16, width), bf16),
            pltpu.VMEM((2, 2, 16, width), bf16),
            pltpu.VMEM((2, 16, width), f32),
            pltpu.VMEM((2, 16, width), f32),
            pltpu.VMEM((2, 2, 16, width), f32),
            pltpu.VMEM((chunks, 32, width), bf16),
            pltpu.VMEM((chunks, 32, width), bf16),
            pltpu.VMEM((chunks, 16, width), bf16),
            pltpu.VMEM((chunks, 16, width), bf16),
            pltpu.VMEM((chunks, 3, 2, 16, shard), bf16),
            dma((n + 1,)),
            dma((n + 1,)),
            dma((n + 1,)),
            dma((7, 2)),
            dma((7, chunks)),
            dma((len(groups), 8)),
            dma((len(groups), 8)),
        ],
        compiler_params=pltpu.CompilerParams(
            collective_id=collective_id, has_side_effects=True, vmem_limit_bytes=VMEM
        ),
        cost_estimate=pl.CostEstimate(
            flops=4 * rows * wide * width, bytes_accessed=200_000_000, transcendentals=0
        ),
        name="reduce_products",
    )(dp, nm)
    return out.reshape(total, shard)


LANES = 128
HALO = 16


def silu_parts(v):
    s = 1.0 / (1.0 + jnp.exp(-v))
    return v * s, s


def softplus(v):
    return jnp.maximum(v, 0.0) + jnp.log1p(jnp.exp(-jnp.abs(v)))


def lower_ones(t):
    i = lax.broadcasted_iota(jnp.int32, (t, t), 0)
    j = lax.broadcasted_iota(jnp.int32, (t, t), 1)
    return jnp.where(i >= j, 1.0, 0.0)


def exact(a, b, dims=NN):
    return lax.dot_general(a, b, dims, precision=highest, preferred_element_type=f32)


def head_columns(values, g):
    return pltpu.roll(values, (LANES - GROUP * g) % LANES, 1)[:, :GROUP]


class Exchange:
    def __init__(self, forward, own, own_low, got, t_low, t_got, u_low, u_got, p_low, p_got, before, send, recv):
        self.s, self.z, self.c, self.x, self.y, self.near = around()
        later = (lambda v: v) if forward else (lambda v: 1 - v)
        self.second = (later(self.c) == 1, later(self.x) == 1, later(self.y) == 1)
        self.own, self.own_low, self.got = own, own_low, got
        self.t_low, self.t_got, self.u_low, self.u_got = t_low, t_got, u_low, u_got
        self.p_low, self.p_got, self.before = p_low, p_got, before
        self.send, self.recv = send, recv
        self.n = own.shape[1]
        self.half = own.shape[2] // 2
        self.mine = pl.ds(pl.multiple_of(self.c * self.half, LANES), self.half)
        self.other = pl.ds(pl.multiple_of((1 - self.c) * self.half, LANES), self.half)

    def copy(self, kind, m):
        src, dst, to = (
            (self.own_low, self.got, "c"),
            (self.t_low, self.t_got, "x"),
            (self.u_low, self.u_got, "y"),
            (self.p_low, self.p_got, "c"),
        )[kind]
        return pltpu.make_async_remote_copy(
            src_ref=src.at[m],
            dst_ref=dst.at[m],
            send_sem=self.send.at[kind, m],
            recv_sem=self.recv.at[kind, m],
            device_id=self.near[to],
            device_id_type=MESH,
        )

    def put_decay(self, ref, m, lanes, decay):
        high = decay.astype(bf16).astype(f32)
        row = lax.broadcasted_iota(jnp.int32, (16, decay.shape[1]), 0)
        both = jnp.where(row == 0, high, jnp.where(row == 1, decay - high, 0.0))
        ref[m, pl.ds(self.n, 16), lanes] = both.astype(bf16)

    def decay_of(self, ref, m, lanes):
        rows = ref[m, pl.ds(self.n, 16), lanes].astype(f32)
        return rows[0:1] + rows[1:2]

    def put_own(self, m, lanes, state, decay):
        self.own[m, :, lanes] = state
        self.own_low[m, pl.ds(0, self.n), lanes] = state.astype(bf16)
        self.put_decay(self.own_low, m, lanes, decay)

    def core(self, m):
        self.copy(0, m).start()

    def along_x(self, m):
        self.copy(0, m).wait_recv()
        second = self.second[0]
        mine = self.own[m, :, self.mine]
        theirs = self.got[m, pl.ds(0, self.n), self.mine].astype(f32)
        d_mine = self.decay_of(self.own_low, m, self.mine)
        d_theirs = self.decay_of(self.got, m, self.mine)
        total = theirs * jnp.where(second, d_mine, 1.0) + mine * jnp.where(second, 1.0, d_theirs)
        self.t_low[m, pl.ds(0, self.n), :] = total.astype(bf16)
        self.put_decay(self.t_low, m, pl.ds(0, self.half), d_mine * d_theirs)
        self.copy(1, m).start()

    def along_y(self, m):
        self.copy(1, m).wait_recv()
        second = self.second[1]
        every = pl.ds(0, self.half)
        mine = self.t_low[m, pl.ds(0, self.n), :].astype(f32)
        theirs = self.t_got[m, pl.ds(0, self.n), :].astype(f32)
        d_mine = self.decay_of(self.t_low, m, every)
        d_theirs = self.decay_of(self.t_got, m, every)
        total = theirs * jnp.where(second, d_mine, 1.0) + mine * jnp.where(second, 1.0, d_theirs)
        self.u_low[m] = total.astype(bf16)
        self.copy(2, m).start()

    def back_to_core(self, m):
        self.copy(2, m).wait_recv()
        every = pl.ds(0, self.half)
        x_second = jnp.where(self.second[1], 1.0, 0.0)
        y_second = jnp.where(self.second[2], 1.0, 0.0)
        theirs = self.t_got[m, pl.ds(0, self.n), :].astype(f32)
        d_theirs = self.decay_of(self.t_got, m, every)
        over = y_second * jnp.where(self.second[1], d_theirs, 1.0)
        before = x_second * theirs + over * self.u_got[m].astype(f32)
        self.before[m] = before
        self.p_low[m] = before.astype(bf16)
        self.copy(3, m).start()

    def begin_state(self, m, out):
        self.copy(3, m).wait_recv()
        second = jnp.where(self.second[0], 1.0, 0.0)
        for lanes, before in (
            (self.mine, self.before[m]),
            (self.other, self.p_got[m].astype(f32)),
        ):
            d_theirs = self.decay_of(self.got, m, lanes)
            theirs = self.got[m, pl.ds(0, self.n), lanes].astype(f32)
            over = jnp.where(self.second[0], d_theirs, 1.0)
            out[m, :, lanes] = (before * over + second * theirs).astype(bf16)

    def sent(self):
        for m in range(self.own.shape[0]):
            for kind in range(4):
                self.copy(kind, m).wait_send()


def exchange_scratch(micro, n, inner):
    half = inner // 2
    dma = pltpu.SemaphoreType.DMA
    return [
        pltpu.VMEM((micro, n, inner), f32),
        pltpu.VMEM((micro, n + 16, inner), bf16),
        pltpu.VMEM((micro, n + 16, inner), bf16),
        pltpu.VMEM((micro, n + 16, half), bf16),
        pltpu.VMEM((micro, n + 16, half), bf16),
        pltpu.VMEM((micro, n, half), bf16),
        pltpu.VMEM((micro, n, half), bf16),
        pltpu.VMEM((micro, n, half), bf16),
        pltpu.VMEM((micro, n, half), bf16),
        pltpu.VMEM((micro, n, half), f32),
        dma((4, micro)),
        dma((4, micro)),
    ]


EXCHANGE = 12


def steps_of(raw, shift, rate):
    t = raw.shape[0]
    dt = softplus(raw + shift)
    cum = exact(lower_ones(t), dt * rate)
    return dt, cum


def conv_rows(buf, cw, cb):
    taps = cw.shape[0]
    t = buf.shape[0] - HALO
    total = cb + buf[HALO - taps + 1 : HALO - taps + 1 + t, :] * cw[0:1]
    for k in range(1, taps):
        at = HALO - taps + 1 + k
        total = total + buf[at : at + t, :] * cw[k : k + 1]
    return total


def scan_forward_kernel(
    hs,
    conv_ref,
    raw_ref,
    cw_ref,
    cb_ref,
    shift_ref,
    rate_ref,
    skip_ref,
    x_ref,
    bc_ref,
    y_ref,
    low_ref,
    halo,
    begin_ref,
    *scratch,
):
    buf, wide_buf, scores, dts, cums, rows_t, h_send, h_recv = scratch[EXCHANGE:]
    ex = Exchange(True, *scratch[:EXCHANGE])
    s, z = ex.s, ex.z
    micro, t, channels = conv_ref.shape
    inner = x_ref.shape[2]
    n = begin_ref.shape[1]
    gc = GROUP * hs
    groups = inner // gc
    half_t = t // 2
    near = dict(ex.near)
    near = {k: near[k] for k in ("c", "x", "y")}
    near["next"] = ((s + 1) % 8, z)
    near["last"] = ((s + 7) % 8, z)
    greet(near)

    tail = [
        pltpu.make_async_remote_copy(
            src_ref=conv_ref.at[m, pl.ds(t - HALO, HALO)],
            dst_ref=halo.at[m],
            send_sem=h_send.at[m],
            recv_sem=h_recv.at[m],
            device_id=near["next"],
            device_id_type=MESH,
        )
        for m in range(micro)
    ]
    for copy in tail:
        copy.start()
    for m in range(micro):
        dt, cum = steps_of(raw_ref[m], shift_ref[...], rate_ref[...])
        dts[m] = dt
        cums[m] = cum
        rows_t[m] = cum.T
    for copy in tail:
        copy.wait_recv()
    has_prior = jnp.where(s > 0, 1.0, 0.0)

    def activate(m, lanes, into):
        into[0:HALO] = halo[m, :, lanes].astype(f32) * has_prior
        into[pl.ds(HALO, t)] = conv_ref[m, :, lanes].astype(f32)
        return silu_parts(conv_rows(into, cw_ref[:, lanes], cb_ref[:, lanes]))[0]

    def own_states(m, a, b):
        def body(g, carry):
            lanes = pl.ds(pl.multiple_of(g * gc, gc), gc)
            x = activate(m, lanes, buf).astype(bf16)
            x_ref[m, :, lanes] = x
            cum = head_columns(cums[m], g)
            to_end = head_columns(dts[m], g) * jnp.exp(cum[t - 1 :] - cum)
            weighted = (x.astype(f32) * widen(to_end, hs)).astype(bf16)
            state = mm(bc_ref[m, :, 0:n], weighted, TN)
            ex.put_own(m, lanes, state, widen(jnp.exp(cum[t - 1 :]), hs))
            return carry

        lax.fori_loop(a, b, body, 0)

    def local_scans(m, a, b):
        lane = lax.broadcasted_iota(jnp.int32, (half_t, 2 * hs), 1)

        def body(g, carry):
            lanes = pl.ds(pl.multiple_of(g * gc, gc), gc)
            cum = head_columns(cums[m], g)
            rows = rows_t[m, pl.ds(pl.multiple_of(g * GROUP, GROUP), GROUP), :]
            dt_wide = widen(head_columns(dts[m], g), hs)
            weighted = (x_ref[m, :, lanes].astype(f32) * dt_wide).astype(bf16)
            for k in range(0, GROUP, 2):
                pair = weighted[:, k * hs : (k + 2) * hs]
                at = pl.ds(pl.multiple_of(g * gc + k * hs, 2 * hs), 2 * hs)
                top, low = [], []
                for h in (k, k + 1):
                    col, row = cum[:, h : h + 1], rows[h : h + 1, :]
                    m1 = jnp.exp(jnp.minimum(col[:half_t] - row[:, :half_t], 0.0))
                    m2 = jnp.exp(jnp.minimum(col[half_t:] - row, 0.0))
                    m1 = (m1 * scores[m, :half_t, :half_t]).astype(bf16)
                    m2 = (m2 * scores[m, half_t:, :]).astype(bf16)
                    top.append(mm(m1, pair[:half_t]))
                    low.append(mm(m2, pair))
                y_ref[m, :half_t, at] = jnp.where(lane < hs, top[0], top[1])
                y_ref[m, half_t:, at] = jnp.where(lane < hs, low[0], low[1])
            return carry

        lax.fori_loop(a, b, body, 0)

    def carried(m):
        def body(g, carry):
            lanes = pl.ds(pl.multiple_of(g * gc, gc), gc)
            decay = widen(jnp.exp(head_columns(cums[m], g)), hs)
            scan = y_ref[m, :, lanes] + decay * mm(bc_ref[m, :, n:], begin_ref[m, :, lanes])
            y_ref[m, :, lanes] = scan
            x = x_ref[m, :, lanes].astype(f32)
            low_ref[m, :, lanes] = (scan + skip_ref[:, lanes] * x).astype(bf16)
            return carry

        lax.fori_loop(0, groups, body, 0)

    for m in range(micro):
        lanes = pl.ds(inner, channels - inner)
        bc = activate(m, lanes, wide_buf).astype(bf16)
        bc_ref[m] = bc
        scores[m] = mm(bc[:, n:], bc[:, :n], NT) * lower_ones(t)
    middle = groups // 2
    own_states(0, 0, groups)
    ex.core(0)
    own_states(1, 0, middle)
    ex.along_x(0)
    own_states(1, middle, groups)
    ex.core(1)
    local_scans(0, 0, middle)
    ex.along_x(1)
    ex.along_y(0)
    local_scans(0, middle, groups)
    local_scans(1, 0, middle)
    ex.along_y(1)
    ex.back_to_core(0)
    local_scans(1, middle, groups)
    ex.begin_state(0, begin_ref)
    carried(0)
    ex.back_to_core(1)
    ex.begin_state(1, begin_ref)
    carried(1)
    ex.sent()
    for copy in tail:
        copy.wait_send()


def scan_forward(conv_low, raw, conv_w, conv_b, shift, rate, skip_wide, inner, hs, collective_id):
    micro, t, channels = conv_low.shape
    n = (channels - inner) // 2
    gc = GROUP * hs
    dma = pltpu.SemaphoreType.DMA
    vmem = pl.BlockSpec(memory_space=pltpu.VMEM)
    return pl.pallas_call(
        partial(scan_forward_kernel, hs),
        in_specs=[vmem] * 7,
        out_specs=[vmem] * 6,
        out_shape=[
            jax.ShapeDtypeStruct((micro, t, inner), bf16),
            jax.ShapeDtypeStruct((micro, t, 2 * n), bf16),
            jax.ShapeDtypeStruct((micro, t, inner), f32),
            jax.ShapeDtypeStruct((micro, t, inner), bf16),
            jax.ShapeDtypeStruct((micro, HALO, channels), bf16),
            jax.ShapeDtypeStruct((micro, n, inner), bf16),
        ],
        scratch_shapes=exchange_scratch(micro, n, inner)
        + [
            pltpu.VMEM((HALO + t, gc), f32),
            pltpu.VMEM((HALO + t, 2 * n), f32),
            pltpu.VMEM((micro, t, t), f32),
            pltpu.VMEM((micro, t, LANES), f32),
            pltpu.VMEM((micro, t, LANES), f32),
            pltpu.VMEM((micro, LANES, t), f32),
            dma((micro,)),
            dma((micro,)),
        ],
        compiler_params=pltpu.CompilerParams(
            collective_id=collective_id, has_side_effects=True, vmem_limit_bytes=VMEM_MOST
        ),
        cost_estimate=pl.CostEstimate(
            flops=4 * micro * t * inner * (t + 3 * n), bytes_accessed=100_000_000, transcendentals=0
        ),
        name="scan_forward",
    )(conv_low, raw, conv_w, conv_b, shift, rate, skip_wide)


def project_kernel(n_ref, w_ref, v_ref, o_ref):
    total = mm(n_ref[0], w_ref[...], NT)
    for k in range(1, n_ref.shape[0]):
        total += mm(n_ref[k], v_ref[k - 1], NT)
    o_ref[...] = total.astype(o_ref.dtype)


def project(parts, own, others, first, count, tile, dtype):
    shards, rows, depth = parts.shape
    return pl.pallas_call(
        project_kernel,
        grid=(count // tile,),
        in_specs=[
            pl.BlockSpec((shards, rows, depth), lambda i: (0, 0, 0)),
            pl.BlockSpec((tile, depth), lambda i: (first // tile + i, 0)),
            pl.BlockSpec((shards - 1, tile, depth), lambda i: (0, first // tile + i, 0)),
        ],
        out_specs=pl.BlockSpec((rows, tile), lambda i: (0, i)),
        out_shape=jax.ShapeDtypeStruct((rows, count), dtype),
        compiler_params=pltpu.CompilerParams(vmem_limit_bytes=VMEM),
        name="project",
    )(parts, own, others)


def unproject_kernel(d_ref, w_ref, v_ref, o_ref):
    @pl.when(pl.program_id(0) == 0)
    def _():
        o_ref[...] = jnp.zeros_like(o_ref)

    o_ref[0] += mm(d_ref[...], w_ref[...])
    for k in range(1, o_ref.shape[0]):
        o_ref[k] += mm(d_ref[...], v_ref[k - 1])


def unproject(d, own, others, tile):
    shards, count, depth = others.shape
    shards += 1
    rows = d.shape[0]
    return pl.pallas_call(
        unproject_kernel,
        grid=(count // tile,),
        in_specs=[
            pl.BlockSpec((rows, tile), lambda i: (0, i)),
            pl.BlockSpec((tile, depth), lambda i: (i, 0)),
            pl.BlockSpec((shards - 1, tile, depth), lambda i: (0, i, 0)),
        ],
        out_specs=pl.BlockSpec((shards, rows, depth), lambda i: (0, 0, 0)),
        out_shape=jax.ShapeDtypeStruct((shards, rows, depth), f32),
        compiler_params=pltpu.CompilerParams(vmem_limit_bytes=VMEM),
        name="unproject",
    )(d, own, others)


def rms_front(hidden_rows, gain):
    power = jnp.mean(hidden_rows * hidden_rows, axis=-1, keepdims=True)
    return hidden_rows * lax.rsqrt(power + epsilon) * gain


def conv_act(padded, conv_w, conv_b):
    taps = conv_w.shape[0]
    rows_out = padded.shape[1] - taps + 1
    total = conv_b + padded[:, 0:rows_out] * conv_w[0]
    for offset in range(1, taps):
        total = total + padded[:, offset : offset + rows_out] * conv_w[offset]
    return jax.nn.silu(total)


def gate_norm(values, gate_in, gain):
    gated = values * jax.nn.silu(gate_in)
    power = jnp.mean(gated * gated, axis=-1, keepdims=True)
    return gated * lax.rsqrt(power + epsilon) * gain


def local(
    hidden,
    lengths,
    out_grad,
    norm_gain,
    in_weight,
    conv_weight,
    conv_bias,
    dt_bias,
    a_log,
    skip_gain,
    gated_gain,
    out_weight,
):
    count = lax.axis_size("seq")
    shards = lax.axis_size("wshard")
    rank = lax.axis_index("seq")
    shard = lax.axis_index("wshard")
    micro, _, tokens, width = hidden.shape
    taps = conv_weight.shape[1]
    inner = out_weight.shape[0] * shards
    channels = conv_bias.shape[0] * shards
    heads = dt_bias.shape[0] * shards
    hs = inner // heads
    n = (channels - inner) // 2
    groups = heads // GROUP
    rows = micro * tokens
    fast = count == 8 and shards == 4 and micro == 2
    in_local = in_weight.T
    small = [norm_gain, conv_weight.T.reshape(-1), conv_bias, dt_bias, a_log, skip_gain, gated_gain]
    sizes = [v.shape[0] for v in small]
    small.append(in_local[inner + channels :].reshape(-1))
    packed_low = lax.all_gather(jnp.concatenate(small), "wshard", axis=0)
    packed = packed_low.astype(f32)
    parts, at = [], 0
    for size in sizes:
        parts.append(packed[:, at : at + size])
        at += size
    norm_g = parts[0].reshape(-1)
    conv_w = parts[1].reshape(shards, taps, -1).transpose(1, 0, 2).reshape(taps, -1)
    conv_b = parts[2].reshape(-1)
    dt_shift = parts[3].reshape(-1)
    rate = -jnp.exp(parts[4].reshape(-1))
    skip = parts[5].reshape(-1)
    gated_g = parts[6].reshape(-1)

    dt_w = packed_low[:, at:].reshape(shards, heads, -1).transpose(1, 0, 2).reshape(heads, -1)
    order = jnp.arange(shards) ^ shard
    if fast:
        in_w = gather_input_weight(in_local, inner, channels)
        out_part = lax.optimization_barrier((out_weight, in_w[0, 0, 0]))[0]
    else:
        every = lax.all_gather(in_local[: inner + channels], "wshard", axis=0)
        in_w = every[order[1:]]
        out_part = out_weight
    out_w = lax.all_gather(out_part, "wshard", axis=0, tiled=True)

    def grouped(v):
        return v.reshape(micro, tokens, groups, GROUP).transpose(0, 2, 1, 3)

    rows_in = hidden.reshape(rows, width).astype(f32)
    cot = out_grad.reshape(rows, width).astype(f32)
    positions = rank * tokens + jnp.arange(tokens, dtype=jnp.int32)
    valid = (positions[None, :] < lengths[:, 0][:, None]).astype(f32).reshape(rows, 1)
    normed, front_back = jax.vjp(rms_front, rows_in, norm_g)
    normed_low = normed.astype(bf16)
    normed_parts = normed_low.reshape(rows, shards, -1).transpose(1, 0, 2)[order]
    tile = 256
    conv_low = project(normed_parts, in_local, in_w, inner, channels, tile, bf16)
    gate_in = project(normed_parts, in_local, in_w, 0, inner, tile, f32)
    dt_low = mm(normed_low, dt_w, NT).astype(bf16)
    conv_low = conv_low.reshape(micro, tokens, channels)
    dt_raw = dt_low.astype(f32).reshape(micro, tokens, heads) + dt_shift
    skip_wide = jnp.repeat(skip, hs)[None, :]

    def to_lanes(v):
        return jnp.pad(v, ((0, 0),) * (v.ndim - 1) + ((0, LANES - heads),))

    if fast:
        raw = to_lanes(dt_low.astype(f32).reshape(micro, tokens, heads))
        x_low, bc_low, y_scan, scanned_low, halo, s_in = scan_forward(
            conv_low,
            raw,
            conv_w,
            conv_b[None, :],
            to_lanes(dt_shift[None, :]),
            to_lanes(rate[None, :]),
            skip_wide,
            inner,
            hs,
            3,
        )
        b_low, c_low = bc_low[..., :n], bc_low[..., n:]
        halo = jnp.where(rank > 0, halo, 0)
        padded = jnp.concatenate([halo[:, HALO - (taps - 1) :], conv_low], axis=1).astype(f32)
    else:
        prior = from_behind(conv_low[:, tokens - (taps - 1) :], "seq", 1)
        padded = jnp.concatenate([prior, conv_low], axis=1).astype(f32)
    mixed, conv_back = jax.vjp(conv_act, padded, conv_w, conv_b)
    dt = jax.nn.softplus(dt_raw)
    tri = (jnp.arange(tokens)[:, None] >= jnp.arange(tokens)[None, :]).astype(f32)
    cum = jnp.einsum("ij,mjh->mih", tri, dt * rate, precision=highest)
    dt_g, cum_g = grouped(dt), grouped(cum)
    row_g = cum_g.transpose(0, 1, 3, 2)
    last = cum[:, tokens - 1, :]
    decays = lax.all_gather(jnp.exp(last), "seq", axis=0)
    decay_w = grouped(jnp.exp(cum))
    if not fast:
        x_low = mixed[..., :inner].astype(bf16)
        b_low = mixed[..., inner : inner + n].astype(bf16)
        c_low = mixed[..., inner + n :].astype(bf16)
        end_w = grouped(dt * jnp.exp(last[:, None, :] - cum))
        own_state = block_states(x_low, end_w, b_low.transpose(0, 2, 1), hs)
        y_local = local_scan(x_low, dt_g, cum_g, row_g, b_low, c_low, hs)
        s_in = running_states(own_state, decays, hs, True)
        y_scan, scanned_low = add_carry(x_low, y_local, cum_g, c_low, s_in, skip_wide, hs)

    scanned = scanned_low.reshape(rows, inner).astype(f32)
    normed_out, gate_back = jax.vjp(gate_norm, scanned, gate_in, gated_g)
    normed_out_low = normed_out.astype(bf16)
    branch = mm(normed_out_low, out_w)
    output = (rows_in + valid * branch).astype(bf16).reshape(hidden.shape)

    g = (cot * valid).astype(bf16)
    out_terms = mm(normed_out_low, g, TN)
    d_scanned, d_gate_in, d_gated = gate_back(mm(g, out_w, NT))
    dy = d_scanned.astype(bf16).reshape(micro, tokens, inner)
    own_grad = block_states(dy, decay_w, c_low.transpose(0, 2, 1), hs)
    dx_local, db_local, dc_local = local_back(x_low, dy, dt_g, cum_g, row_g, b_low, c_low, hs)
    ds = running_states(own_grad, decays, hs, False)
    dx_low, ddt_g, dcum_g, db, dc, last_term, dskip = carry_back(
        x_low, dy, dx_local, y_scan, dt_g, cum_g, b_low, s_in, ds, db_local, dc_local, skip_wide, hs
    )

    def ungrouped(v):
        return v.transpose(0, 2, 1, 3).reshape(micro, tokens, heads)

    at_end = jnp.sum(last_term.reshape(micro, heads, hs), axis=-1)[:, None, :]
    d_log = jnp.einsum("ij,mih->mjh", tri, ungrouped(dcum_g), precision=highest) + at_end
    d_dt = (ungrouped(ddt_g) + d_log * rate) * jax.nn.sigmoid(dt_raw)
    d_dt_bias = jnp.sum(d_dt, axis=(0, 1))
    d_a_log = jnp.sum(d_log * dt, axis=(0, 1)) * rate
    d_skip = jnp.sum(dskip.reshape(-1, heads, hs), axis=(0, 2))
    mixed_grad = jnp.concatenate([dx_low.astype(f32), db, dc], axis=2)
    d_padded, d_conv_w, d_conv_b = conv_back(mixed_grad)
    from_next = from_behind(d_padded[:, : taps - 1].astype(bf16), "seq", -1).astype(f32)
    d_conv = d_padded[:, taps - 1 :].at[:, tokens - (taps - 1) :].add(from_next)
    d_dt_low = d_dt.astype(bf16).reshape(rows, heads)
    total_cols = inner + channels + heads
    pad = -total_cols % 256 if fast else 0
    d_proj = jnp.concatenate(
        [
            d_gate_in.astype(bf16),
            d_conv.astype(bf16).reshape(rows, channels),
            d_dt_low,
            jnp.zeros((rows, pad), bf16),
        ],
        axis=1,
    )
    d_parts = unproject(d_proj, in_local, in_w, tile)
    d_normed = d_parts[order].transpose(1, 0, 2).reshape(rows, width) + mm(d_dt_low, dt_w)
    d_hidden, d_norm_g = front_back(d_normed)
    input_grad = (d_hidden + cot).astype(bf16).reshape(hidden.shape)

    def summed(terms, axis):
        t = lax.psum_scatter(terms.astype(bf16), "seq", scatter_dimension=0, tiled=True)
        t = lax.psum_scatter(t, "wshard", scatter_dimension=axis, tiled=True)
        return lax.all_gather(t, "seq", axis=0, tiled=True).astype(f32)

    if fast:
        in_grad = reduce_products(d_proj, normed_low, 2)[:total_cols].astype(f32).T
    else:
        in_grad = summed(mm(d_proj, normed_low, TN), 1).T
    blocks = out_terms.reshape(shards, count, -1, width).transpose(1, 0, 2, 3)
    blocks = blocks.reshape(inner, width)
    out_w_grad = summed_rows(blocks, shards, count)
    smalls = [
        d_norm_g.reshape(shards, -1),
        d_conv_w.reshape(taps, shards, -1).transpose(1, 0, 2).reshape(shards, -1),
        d_conv_b.reshape(shards, -1),
        d_dt_bias.reshape(shards, -1),
        d_a_log.reshape(shards, -1),
        d_skip.reshape(shards, -1),
        d_gated.reshape(shards, -1),
    ]
    sums = lax.psum(jnp.concatenate(smalls, axis=1), ("seq", "wshard"))
    sums = lax.dynamic_index_in_dim(sums, shard, 0, keepdims=False)
    found, at = [], 0
    for size in sizes:
        found.append(sums[at : at + size])
        at += size
    return (
        output,
        input_grad,
        found[0],
        in_grad,
        found[1].reshape(taps, -1).T,
        found[2],
        found[3],
        found[4],
        found[5],
        found[6],
        out_w_grad,
    )


def summed_rows(blocks, shards, count):
    t = lax.psum_scatter(blocks.astype(bf16), "seq", scatter_dimension=0, tiled=True)
    t = lax.psum_scatter(t, "wshard", scatter_dimension=0, tiled=True)
    return lax.all_gather(t, "seq", axis=0, tiled=True).astype(f32)


def solution(mesh):
    return jax.shard_map(
        local,
        mesh=mesh,
        in_specs=(
            P(None, "wshard", "seq", None),
            P(None, "wshard"),
            P(None, "wshard", "seq", None),
            P("wshard"),
            P("wshard", None),
            P("wshard", None),
            P("wshard"),
            P("wshard"),
            P("wshard"),
            P("wshard"),
            P("wshard"),
            P("wshard", None),
        ),
        out_specs=(
            P(None, "wshard", "seq", None),
            P(None, "wshard", "seq", None),
            P("wshard"),
            P("wshard", None),
            P("wshard", None),
            P("wshard"),
            P("wshard"),
            P("wshard"),
            P("wshard"),
            P("wshard"),
            P("wshard", None),
        ),
        check_vma=False,
    )
```

```python
from functools import partial

import jax
import jax.numpy as jnp
from jax import lax
from jax.experimental import pallas as pl
from jax.experimental.pallas import tpu as pltpu
from jax.sharding import PartitionSpec as P

epsilon = 1e-05
highest = lax.Precision.HIGHEST
f32 = jnp.float32
bf16 = jnp.bfloat16
GROUP = 8
VMEM = 48 * 1024 * 1024
VMEM_MOST = 60 * 1024 * 1024

NN = (((1,), (0,)), ((), ()))
NT = (((1,), (1,)), ((), ()))
TN = (((0,), (0,)), ((), ()))


def mm(a, b, dims=NN):
    return lax.dot_general(a, b, dims, preferred_element_type=f32)


def params():
    return pltpu.CompilerParams(
        dimension_semantics=("arbitrary", "arbitrary"), vmem_limit_bytes=VMEM
    )


def widen(cols, head_size):
    t, heads = cols.shape
    lane = lax.broadcasted_iota(jnp.int32, (t, 2 * head_size), 1)
    parts = []
    for k in range(0, heads, 2):
        parts.append(jnp.where(lane < head_size, cols[:, k : k + 1], cols[:, k + 1 : k + 2]))
    return jnp.concatenate(parts, axis=1)


def state_kernel(hs, x_ref, w_ref, bt_ref, o_ref):
    weighted = (x_ref[0].astype(f32) * widen(w_ref[0, 0], hs)).astype(bf16)
    o_ref[0] = mm(bt_ref[0], weighted)


def block_states(x, weights, bt, hs):
    micro, t, cols = x.shape
    n = bt.shape[1]
    gc = GROUP * hs
    return pl.pallas_call(
        partial(state_kernel, hs),
        grid=(micro, cols // gc),
        in_specs=[
            pl.BlockSpec((1, t, gc), lambda m, g: (m, 0, g)),
            pl.BlockSpec((1, 1, t, GROUP), lambda m, g: (m, g, 0, 0)),
            pl.BlockSpec((1, n, t), lambda m, g: (m, 0, 0)),
        ],
        out_specs=pl.BlockSpec((1, n, gc), lambda m, g: (m, 0, g)),
        out_shape=jax.ShapeDtypeStruct((micro, n, cols), f32),
        compiler_params=params(),
        name="block_states",
    )(x, weights, bt)


def local_kernel(hs, x_ref, dt_ref, cum_ref, row_ref, b_ref, c_ref, o_ref, scores):
    t = x_ref.shape[1]
    half = t // 2

    @pl.when(pl.program_id(1) == 0)
    def _():
        s = mm(c_ref[0], b_ref[0], NT)
        i = lax.broadcasted_iota(jnp.int32, (t, t), 0)
        j = lax.broadcasted_iota(jnp.int32, (t, t), 1)
        scores[...] = jnp.where(i >= j, s, 0.0)

    cum, dt, rows = cum_ref[0, 0], dt_ref[0, 0], row_ref[0, 0]
    lane = lax.broadcasted_iota(jnp.int32, (half, 2 * hs), 1)
    weighted = (x_ref[0].astype(f32) * widen(dt, hs)).astype(bf16)
    for k in range(0, GROUP, 2):
        at = slice(k * hs, (k + 2) * hs)
        pair = weighted[:, at]
        top, low = [], []
        for h in (k, k + 1):
            col, row = cum[:, h : h + 1], rows[h : h + 1, :]
            m1 = jnp.exp(jnp.minimum(col[:half] - row[:, :half], 0.0)) * scores[:half, :half]
            m2 = jnp.exp(jnp.minimum(col[half:] - row, 0.0)) * scores[half:, :]
            top.append(mm(m1.astype(bf16), pair[:half]))
            low.append(mm(m2.astype(bf16), pair))
        o_ref[0, :half, at] = jnp.where(lane < hs, top[0], top[1])
        o_ref[0, half:, at] = jnp.where(lane < hs, low[0], low[1])


def local_scan(x, dt, cum, rows, b, c, hs):
    micro, t, cols = x.shape
    n = b.shape[2]
    gc = GROUP * hs
    return pl.pallas_call(
        partial(local_kernel, hs),
        grid=(micro, cols // gc),
        in_specs=[
            pl.BlockSpec((1, t, gc), lambda m, g: (m, 0, g)),
            pl.BlockSpec((1, 1, t, GROUP), lambda m, g: (m, g, 0, 0)),
            pl.BlockSpec((1, 1, t, GROUP), lambda m, g: (m, g, 0, 0)),
            pl.BlockSpec((1, 1, GROUP, t), lambda m, g: (m, g, 0, 0)),
            pl.BlockSpec((1, t, n), lambda m, g: (m, 0, 0)),
            pl.BlockSpec((1, t, n), lambda m, g: (m, 0, 0)),
        ],
        out_specs=pl.BlockSpec((1, t, gc), lambda m, g: (m, 0, g)),
        out_shape=jax.ShapeDtypeStruct((micro, t, cols), f32),
        scratch_shapes=[pltpu.VMEM((t, t), f32)],
        compiler_params=params(),
        name="local_scan",
    )(x, dt, cum, rows, b, c)


def carry_kernel(hs, x_ref, y_ref, cum_ref, c_ref, s_ref, skip_ref, scan_ref, low_ref):
    carried = mm(c_ref[0], s_ref[0].astype(bf16)) * widen(jnp.exp(cum_ref[0, 0]), hs)
    scan = y_ref[0] + carried
    scan_ref[0] = scan
    low_ref[0] = (scan + skip_ref[...] * x_ref[0].astype(f32)).astype(bf16)


def add_carry(x, y, cum, c, s_in, skip_wide, hs):
    micro, t, cols = x.shape
    n = c.shape[2]
    gc = GROUP * hs
    wide = pl.BlockSpec((1, t, gc), lambda m, g: (m, 0, g))
    return pl.pallas_call(
        partial(carry_kernel, hs),
        grid=(micro, cols // gc),
        in_specs=[
            wide,
            wide,
            pl.BlockSpec((1, 1, t, GROUP), lambda m, g: (m, g, 0, 0)),
            pl.BlockSpec((1, t, n), lambda m, g: (m, 0, 0)),
            pl.BlockSpec((1, n, gc), lambda m, g: (m, 0, g)),
            pl.BlockSpec((1, gc), lambda m, g: (0, g)),
        ],
        out_specs=[wide, wide],
        out_shape=[
            jax.ShapeDtypeStruct((micro, t, cols), f32),
            jax.ShapeDtypeStruct((micro, t, cols), bf16),
        ],
        compiler_params=params(),
        name="add_carry",
    )(x, y, cum, c, s_in, skip_wide)


def local_back_kernel(
    hs, x_ref, dy_ref, dt_ref, cum_ref, row_ref, b_ref, c_ref, dx_ref, db_ref, dc_ref, scores, total
):
    t = x_ref.shape[1]
    half = t // 2

    @pl.when(pl.program_id(1) == 0)
    def _():
        s = mm(b_ref[0], c_ref[0], NT)
        j = lax.broadcasted_iota(jnp.int32, (t, t), 0)
        i = lax.broadcasted_iota(jnp.int32, (t, t), 1)
        scores[...] = jnp.where(i >= j, s, 0.0)
        total[...] = jnp.zeros_like(total)

    cum, dt, rows = cum_ref[0, 0], dt_ref[0, 0], row_ref[0, 0]
    lane = lax.broadcasted_iota(jnp.int32, (t, 2 * hs), 1)
    lane_half = lax.broadcasted_iota(jnp.int32, (half, 2 * hs), 1)
    weighted = (x_ref[0].astype(f32) * widen(dt, hs)).astype(bf16)
    for k in range(0, GROUP, 2):
        at = slice(k * hs, (k + 2) * hs)
        pair = weighted[:, at]
        dy = dy_ref[0, :, at]
        top, low = [], []
        for h in (k, k + 1):
            col, row = cum[:, h : h + 1], rows[h : h + 1, :]
            mine = jnp.where(lane < hs, pair, 0) if h == k else jnp.where(lane < hs, 0, pair)
            l1 = jnp.exp(jnp.minimum(row - col[:half], 0.0))
            l2 = jnp.exp(jnp.minimum(row[:, half:] - col[half:], 0.0))
            total[:half, :] += l1 * mm(mine[:half], dy, NT)
            total[half:, half:] += l2 * mm(mine[half:], dy[half:], NT)
            top.append(mm((l1 * scores[:half, :]).astype(bf16), dy))
            low.append(mm((l2 * scores[half:, half:]).astype(bf16), dy[half:]))
        dx_ref[0, :half, at] = jnp.where(lane_half < hs, top[0], top[1])
        dx_ref[0, half:, at] = jnp.where(lane_half < hs, low[0], low[1])

    @pl.when(pl.program_id(1) == pl.num_programs(1) - 1)
    def _():
        j = lax.broadcasted_iota(jnp.int32, (t, t), 0)
        i = lax.broadcasted_iota(jnp.int32, (t, t), 1)
        d = jnp.where(i >= j, total[...], 0.0)
        db_ref[0] = mm(d.astype(bf16), c_ref[0])
        dc_ref[0] = mm(d.T.astype(bf16), b_ref[0])


def local_back(x, dy, dt, cum, rows, b, c, hs):
    micro, t, cols = x.shape
    n = b.shape[2]
    gc = GROUP * hs
    wide = pl.BlockSpec((1, t, gc), lambda m, g: (m, 0, g))
    small = pl.BlockSpec((1, 1, t, GROUP), lambda m, g: (m, g, 0, 0))
    state = pl.BlockSpec((1, t, n), lambda m, g: (m, 0, 0))
    return pl.pallas_call(
        partial(local_back_kernel, hs),
        grid=(micro, cols // gc),
        in_specs=[
            wide,
            wide,
            small,
            small,
            pl.BlockSpec((1, 1, GROUP, t), lambda m, g: (m, g, 0, 0)),
            state,
            state,
        ],
        out_specs=[wide, state, state],
        out_shape=[
            jax.ShapeDtypeStruct((micro, t, cols), f32),
            jax.ShapeDtypeStruct((micro, t, n), f32),
            jax.ShapeDtypeStruct((micro, t, n), f32),
        ],
        scratch_shapes=[pltpu.VMEM((t, t), f32), pltpu.VMEM((t, t), f32)],
        compiler_params=params(),
        name="local_back",
    )(x, dy, dt, cum, rows, b, c)


def head_sums(values, ones):
    high = values.astype(bf16)
    rest = (values - high.astype(f32)).astype(bf16)
    return mm(high, ones) + mm(rest, ones)


def carry_back_kernel(
    hs,
    x_ref,
    dy_ref,
    dxl_ref,
    y_ref,
    dt_ref,
    cum_ref,
    b_ref,
    si_ref,
    ds_ref,
    dbl_ref,
    dcl_ref,
    skip_ref,
    dx_ref,
    ddt_ref,
    dcum_ref,
    db_ref,
    dc_ref,
    last_ref,
    dskip_ref,
):
    t = x_ref.shape[1]
    gc = x_ref.shape[2]

    @pl.when(pl.program_id(1) == 0)
    def _():
        db_ref[0] = dbl_ref[0]
        dc_ref[0] = dcl_ref[0]

    cum, dt = cum_ref[0, 0], dt_ref[0, 0]
    x, dy = x_ref[0].astype(f32), dy_ref[0].astype(f32)
    dt_wide = widen(dt, hs)
    weighted = (x * dt_wide).astype(bf16).astype(f32)
    decay = widen(jnp.exp(cum), hs)
    to_end = widen(jnp.exp(cum[t - 1 :, :] - cum), hs)
    s_in, ds = si_ref[0].astype(f32), ds_ref[0]
    s_low, ds_low = s_in.astype(bf16), ds.astype(bf16)
    through = to_end * mm(b_ref[0], ds_low)
    d_weighted = dxl_ref[0] + through
    dx_ref[0] = (dt_wide * d_weighted + skip_ref[...] * dy).astype(bf16)
    db_ref[0] += mm((weighted * to_end).astype(bf16), ds_low, NT)
    dc_ref[0] += mm((dy * decay).astype(bf16), s_low, NT)
    r = lax.broadcasted_iota(jnp.int32, (gc, 128), 0)
    c = lax.broadcasted_iota(jnp.int32, (gc, 128), 1)
    ones = jnp.where(r // hs == c, 1.0, 0.0).astype(bf16)
    ddt_ref[0, 0] = head_sums(x * d_weighted, ones)[:, :GROUP]
    dcum_ref[0, 0] = head_sums(dy * y_ref[0] - weighted * d_weighted, ones)[:, :GROUP]
    last_decay = decay[t - 1 :, :]
    last_ref[0] = jnp.sum(weighted * through, axis=0, keepdims=True) + last_decay * jnp.sum(
        s_low.astype(f32) * ds, axis=0, keepdims=True
    )
    dskip_ref[0] = jnp.sum(x * dy, axis=0, keepdims=True)


def carry_back(x, dy, dxl, y, dt, cum, b, s_in, ds, dbl, dcl, skip_wide, hs):
    micro, t, cols = x.shape
    n = b.shape[2]
    gc = GROUP * hs
    groups = cols // gc
    wide = pl.BlockSpec((1, t, gc), lambda m, g: (m, 0, g))
    small = pl.BlockSpec((1, 1, t, GROUP), lambda m, g: (m, g, 0, 0))
    state = pl.BlockSpec((1, t, n), lambda m, g: (m, 0, 0))
    st = pl.BlockSpec((1, n, gc), lambda m, g: (m, 0, g))
    line = pl.BlockSpec((1, 1, gc), lambda m, g: (m, 0, g))
    return pl.pallas_call(
        partial(carry_back_kernel, hs),
        grid=(micro, groups),
        in_specs=[
            wide,
            wide,
            wide,
            wide,
            small,
            small,
            state,
            st,
            st,
            state,
            state,
            pl.BlockSpec((1, gc), lambda m, g: (0, g)),
        ],
        out_specs=[wide, small, small, state, state, line, line],
        out_shape=[
            jax.ShapeDtypeStruct((micro, t, cols), bf16),
            jax.ShapeDtypeStruct((micro, groups, t, GROUP), f32),
            jax.ShapeDtypeStruct((micro, groups, t, GROUP), f32),
            jax.ShapeDtypeStruct((micro, t, n), f32),
            jax.ShapeDtypeStruct((micro, t, n), f32),
            jax.ShapeDtypeStruct((micro, 1, cols), f32),
            jax.ShapeDtypeStruct((micro, 1, cols), f32),
        ],
        compiler_params=params(),
        name="carry_back",
    )(x, dy, dxl, y, dt, cum, b, s_in, ds, dbl, dcl, skip_wide)


def from_behind(x, axis, by):
    count = lax.axis_size(axis)
    pairs = [(i, i + by) for i in range(count) if 0 <= i + by < count]
    return lax.ppermute(x, axis, pairs)


def swap(x, by):
    count = lax.axis_size("seq")
    return lax.ppermute(x, "seq", [(i, i ^ by) for i in range(count)])


def running_states(terms, decays, hs, forward):
    count = lax.axis_size("seq")
    rank = lax.axis_index("seq")
    index = jnp.arange(count)

    def product(mask):
        d = jnp.prod(jnp.where(mask[:, None, None], decays, 1.0), axis=0)
        return jnp.repeat(d, hs, axis=1)[:, None, :]

    total, before = terms, jnp.zeros_like(terms)
    size = 1
    while size < count:
        other = swap(total.astype(bf16), size).astype(f32)
        mine = index // size == rank // size
        theirs = index // size == (rank // size) ^ 1
        later = (rank // size) % 2 == (1 if forward else 0)
        passed = mine & ((index < rank) if forward else (index > rank))
        before = before + jnp.where(later, product(passed), 0.0) * other
        if 2 * size < count:
            total = total * jnp.where(later, 1.0, product(theirs)) + other * jnp.where(
                later, product(mine), 1.0
            )
        size *= 2
    return before


MESH = pl.DeviceIdType.MESH


def around():
    s, z = lax.axis_index("seq"), lax.axis_index("wshard")
    c, x, y = s % 2, (s // 2) % 2, s // 4
    near = {
        "c": (s + 1 - 2 * c, z),
        "x": (s + 2 - 4 * x, z),
        "y": (s + 4 - 8 * y, z),
        "z1": (s, z + 1 - 2 * (z % 2)),
        "z2": (s, z + 2 - 4 * (z // 2)),
        "z3": (s, 3 - z),
    }
    return s, z, c, x, y, near


def greet(near):
    barrier = pltpu.get_barrier_semaphore()
    for where in near.values():
        pl.semaphore_signal(barrier, inc=1, device_id=where, device_id_type=MESH)
    pl.semaphore_wait(barrier, len(near))


CHUNK_DMAS = 10
AHEAD = 2


def gather_kernel(chunks, w_ref, o_ref, send, recv):
    s, z, c, x, y, near = around()
    greet(near)
    sx, sy, sd = s + 2 - 4 * x, s + 4 - 8 * y, s + 6 - 4 * x - 8 * y
    plans = []
    for q, (base, piece, off, size, first) in enumerate(chunks):

        def rows(who, base=base, piece=piece, off=off, size=size):
            return pl.ds(pl.multiple_of(base + who * piece + off, 16), size)

        def move(src, dst, kind, to, q=q):
            return pltpu.make_async_remote_copy(
                src_ref=src,
                dst_ref=dst,
                send_sem=send.at[q, kind],
                recv_sem=recv.at[q, kind],
                device_id=near[to],
                device_id_type=MESH,
            )

        def block(who, rows=rows):
            return o_ref.at[:, rows(who)]

        def along(who, kind, to, move=move, block=block):
            return move(block(who), block(who), kind, to)

        plan = {}
        for k in (1, 2, 3):
            plan["z%d" % k] = move(w_ref.at[rows(s)], o_ref.at[k - 1, rows(s)], k - 1, "z%d" % k)
        plan["x"] = along(s, 3, "x")
        plan["y"] = along(s, 4, "y")
        plan["d"] = along(sx, 5, "y") if first == "x" else along(sy, 5, "x")
        plan["c0"] = along(s, 6, "c")
        plan["cx"] = along(sx, 7, "c")
        plan["cy"] = along(sy, 8, "c")
        plan["cd"] = along(sd, 9, "c")
        plan["first"] = first
        plans.append(plan)

    def fetch(plan):
        for k in (1, 2, 3):
            plan["z%d" % k].start()

    def begin(plan):
        for k in (1, 2, 3):
            plan["z%d" % k].wait_recv()
        for name in ("x", "y", "c0"):
            plan[name].start()

    def middle(plan):
        one, two = ("x", "y") if plan["first"] == "x" else ("y", "x")
        plan[one].wait_recv()
        plan["d"].start()
        plan["c" + one].start()
        plan[two].wait_recv()
        plan["c" + two].start()

    def finish(plan):
        plan["d"].wait_recv()
        plan["cd"].start()

    n = len(plans)
    for i in range(min(AHEAD, n)):
        fetch(plans[i])
    for i in range(n + 2):
        if i < n:
            begin(plans[i])
            if i + AHEAD < n:
                fetch(plans[i + AHEAD])
        if 0 <= i - 1 < n:
            middle(plans[i - 1])
        if 0 <= i - 2 < n:
            finish(plans[i - 2])
    for plan in plans:
        for name in ("c0", "cx", "cy", "cd"):
            plan[name].wait_recv()
        for name in ("z1", "z2", "z3", "x", "y", "d", "c0", "cx", "cy", "cd"):
            plan[name].wait_send()


def split_rows(piece, parts=6):
    tiles = piece // 16
    return [16 * (tiles * (i + 1) // parts - tiles * i // parts) for i in range(parts)]


def gather_input_weight(w_t, inner, channels):
    total = inner + channels
    chunks = []
    for base, piece in ((inner, channels // 8), (0, inner // 8)):
        off = 0
        for i, size in enumerate(split_rows(piece)):
            chunks.append((base, piece, off, size, "xy"[i % 2]))
            off += size
    width = w_t.shape[1]
    return pl.pallas_call(
        partial(gather_kernel, chunks),
        in_specs=[pl.BlockSpec(memory_space=pl.ANY)],
        out_specs=pl.BlockSpec(memory_space=pl.ANY),
        out_shape=jax.ShapeDtypeStruct((3, total, width), bf16),
        scratch_shapes=[
            pltpu.SemaphoreType.DMA((len(chunks), CHUNK_DMAS)),
            pltpu.SemaphoreType.DMA((len(chunks), CHUNK_DMAS)),
        ],
        compiler_params=pltpu.CompilerParams(collective_id=1, has_side_effects=True),
        cost_estimate=pl.CostEstimate(flops=0, bytes_accessed=200_000_000, transcendentals=0),
        name="gather_input_weight",
    )(w_t)


class Products:
    IN = 4
    SCRATCH = 22

    @staticmethod
    def sizes(a_list, b):
        rows = b.shape[0]
        wide = sum(a.shape[1] for a in a_list) // 2
        return rows, wide, b.shape[1], wide // 128

    @staticmethod
    def marks(chunks):
        return sorted({0, chunks * 2 // 5, chunks * 7 // 10, chunks * 9 // 10, chunks})

    @staticmethod
    def out_shape(a_list, b):
        _, _, width, chunks = Products.sizes(a_list, b)
        return jax.ShapeDtypeStruct((2, chunks, 2, 2, 2, 16, width // 4), bf16)

    @staticmethod
    def scratch(a_list, b):
        rows, wide, width, chunks = Products.sizes(a_list, b)
        dma = pltpu.SemaphoreType.DMA
        n = Products.IN
        marks = Products.marks(chunks)
        return [
            pltpu.VMEM((2, rows, wide), bf16),
            pltpu.VMEM((2, rows, width), bf16),
            pltpu.VMEM((2, 128, width), f32),
            pltpu.VMEM((2, 32, width), bf16),
            pltpu.VMEM((2, 32, width), bf16),
            pltpu.VMEM((2, 16, width), bf16),
            pltpu.VMEM((2, 16, width), bf16),
            pltpu.VMEM((2, 2, 16, width), bf16),
            pltpu.VMEM((2, 16, width), f32),
            pltpu.VMEM((2, 16, width), f32),
            pltpu.VMEM((2, 2, 16, width), f32),
            pltpu.VMEM((chunks, 32, width), bf16),
            pltpu.VMEM((chunks, 32, width), bf16),
            pltpu.VMEM((chunks, 16, width), bf16),
            pltpu.VMEM((chunks, 16, width), bf16),
            pltpu.VMEM((chunks, 3, 2, 16, width // 4), bf16),
            dma((n,)),
            dma((n,)),
            dma((n,)),
            dma((7, 2)),
            dma((7, chunks)),
            dma((2, len(marks) - 1, 8)),
        ]

    def __init__(self, place, a_refs, b_ref, out, scratch):
        self.s, self.z, self.c, self.x, self.y, self.near = place
        (
            self.a,
            self.b,
            self.g,
            self.sa1,
            self.sb1,
            self.sa2,
            self.sb2,
            self.s3,
            self.ka2,
            self.kb2,
            self.f3,
            self.ra1,
            self.rb1,
            self.ra2,
            self.rb2,
            self.rz,
            self.in_sem,
            self.s_in,
            self.r_in,
            self.s_step,
            self.r_step,
            self.sems_all,
        ) = scratch
        self.out = out
        self.shard = self.rz.shape[-1]
        self.chunks = self.ra1.shape[0]
        marks = Products.marks(self.chunks)
        self.groups = list(zip(marks[:-1], marks[1:]))
        c = self.c
        self.operands = []
        self.operands.append(
            (
                0,
                pltpu.make_async_copy(b_ref, self.b.at[0], self.in_sem.at[0]),
                self.remote(b_ref, self.b.at[1], self.s_in.at[0], self.r_in.at[0], "c"),
            )
        )
        at = 0
        for i, ref in enumerate(a_refs):
            half = ref.shape[1] // 2
            here = ref.at[:, pl.ds(pl.multiple_of(c * half, 128), half)]
            there = ref.at[:, pl.ds(pl.multiple_of((1 - c) * half, 128), half)]
            to = pl.ds(at, half)
            self.operands.append(
                (
                    at // 128,
                    pltpu.make_async_copy(here, self.a.at[0, :, to], self.in_sem.at[i + 1]),
                    self.remote(there, self.a.at[1, :, to], self.s_in.at[i + 1], self.r_in.at[i + 1], "c"),
                )
            )
            at += half

    def remote(self, src, dst, ss, rs, to):
        return pltpu.make_async_remote_copy(
            src_ref=src,
            dst_ref=dst,
            send_sem=ss,
            recv_sem=rs,
            device_id=self.near[to],
            device_id_type=MESH,
        )

    def load(self):
        for _, here, _ in self.operands:
            here.start()

    def share(self):
        for _, _, there in self.operands:
            there.start()

    def step_copy(self, kind, u):
        slot = u % 2
        ss, rs = self.s_step.at[kind, slot], self.r_step.at[kind, u]
        if kind < 4:
            src, dst, to = (
                (self.sa1, self.ra1, "x"),
                (self.sb1, self.rb1, "y"),
                (self.sa2, self.ra2, "y"),
                (self.sb2, self.rb2, "x"),
            )[kind]
            return self.remote(src.at[slot], dst.at[u], ss, rs, to)
        k = kind - 3
        z = self.z
        other = (z + 1 - 2 * (z % 2), z + 2 - 4 * (z // 2), 3 - z)[k - 1]
        cols = pl.ds(pl.multiple_of(other * self.shard, 128), self.shard)
        return self.remote(self.s3.at[slot, :, :, cols], self.rz.at[u, k - 1], ss, rs, "z%d" % k)

    def all_copy(self, q, kind):
        a, b = self.groups[q]
        ts = pl.ds(a, b - a)
        x, y, c = self.x, self.y, self.c
        px = 1 - x if kind in (3, 5, 7) else x
        py = 1 - y if kind in (4, 6, 7) else y
        if kind in (3, 4):
            block = self.out.at[c, ts, kind - 3, px, py]
        else:
            block = self.out.at[c, ts, :, px, py]
        to = ("x", "y", "c", "y", "x", "c", "c", "c")[kind]
        return self.remote(block, block, self.sems_all.at[0, q, kind], self.sems_all.at[1, q, kind], to)

    def step(self, t):
        x, y, z, c = self.x, self.y, self.z, self.c
        g, ra1, rb1 = self.g, self.ra1, self.rb1
        chunks = self.chunks
        copy = self.step_copy

        def sl(at, size=16):
            return pl.ds(pl.multiple_of(at, 16), size)

        def free(kind, u):
            @pl.when(u >= 2)
            def _():
                copy(kind, u - 2).wait_send()

        @pl.when(t < chunks)
        def _():
            for first, here, there in self.operands:

                @pl.when(t == first)
                def _(here=here, there=there):
                    here.wait()
                    there.wait_recv()

            slot = t % 2
            cols = pl.ds(pl.multiple_of(t * 128, 128), 128)
            g[slot] = mm(self.a[0, :, cols], self.b[0], TN) + mm(self.a[1, :, cols], self.b[1], TN)
            free(0, t)
            free(1, t)
            self.sa1[slot] = g[slot, sl((1 - x) * 32, 32)].astype(bf16)
            copy(0, t).start()
            self.sb1[slot, 0:16] = g[slot, sl(64 + (1 - y) * 16)].astype(bf16)
            self.sb1[slot, 16:32] = g[slot, sl(96 + (1 - y) * 16)].astype(bf16)
            copy(1, t).start()

        @pl.when((t >= 1) & (t - 1 < chunks))
        def _():
            u = t - 1
            slot = u % 2
            copy(0, u).wait_recv()
            free(2, u)
            self.sa2[slot] = (
                g[slot, sl(x * 32 + (1 - y) * 16)] + ra1[u, sl((1 - y) * 16)].astype(f32)
            ).astype(bf16)
            copy(2, u).start()
            self.ka2[slot] = g[slot, sl(x * 32 + y * 16)] + ra1[u, sl(y * 16)].astype(f32)
            copy(1, u).wait_recv()
            free(3, u)
            self.sb2[slot] = (
                g[slot, sl(64 + (1 - x) * 32 + y * 16)] + rb1[u, sl((1 - x) * 16)].astype(f32)
            ).astype(bf16)
            copy(3, u).start()
            self.kb2[slot] = g[slot, sl(64 + x * 32 + y * 16)] + rb1[u, sl(x * 16)].astype(f32)

        @pl.when((t >= 2) & (t - 2 < chunks))
        def _():
            u = t - 2
            slot = u % 2
            copy(2, u).wait_recv()
            copy(3, u).wait_recv()
            for k in (4, 5, 6):
                free(k, u)
            va = self.ka2[slot] + self.ra2[u].astype(f32)
            vb = self.kb2[slot] + self.rb2[u].astype(f32)
            self.f3[slot, 0] = va
            self.f3[slot, 1] = vb
            self.s3[slot, 0] = va.astype(bf16)
            self.s3[slot, 1] = vb.astype(bf16)
            for k in (4, 5, 6):
                copy(k, u).start()

        @pl.when((t >= 3) & (t - 3 < chunks))
        def _():
            u = t - 3
            slot = u % 2
            for k in (4, 5, 6):
                copy(k, u).wait_recv()
            mine = pl.ds(pl.multiple_of(z * self.shard, 128), self.shard)
            for part in (0, 1):
                total = self.f3[slot, part, :, mine]
                for k in range(3):
                    total = total + self.rz[u, k, part].astype(f32)
                self.out[c, u, part, x, y] = total.astype(bf16)

        for q, (_, b) in enumerate(self.groups):

            @pl.when(t == b - 1 + 3)
            def _(q=q):
                for kind in (0, 1, 2):
                    self.all_copy(q, kind).start()

            @pl.when(t == b - 1 + 4)
            def _(q=q):
                self.all_copy(q, 0).wait_recv()
                self.all_copy(q, 3).start()
                self.all_copy(q, 5).start()
                self.all_copy(q, 1).wait_recv()
                self.all_copy(q, 4).start()
                self.all_copy(q, 6).start()

            @pl.when(t == b - 1 + 5)
            def _(q=q):
                self.all_copy(q, 3).wait_recv()
                self.all_copy(q, 4).wait_recv()
                self.all_copy(q, 7).start()

    def steps(self):
        return self.chunks + 5

    def close(self):
        for q in range(len(self.groups)):
            for kind in (2, 5, 6, 7):
                self.all_copy(q, kind).wait_recv()
            for kind in range(8):
                self.all_copy(q, kind).wait_send()
        for u in (self.chunks - 2, self.chunks - 1):
            for kind in range(7):
                self.step_copy(kind, u).wait_send()
        for _, _, there in self.operands:
            there.wait_send()


class Smalls:
    SCRATCH = 5

    @staticmethod
    def scratch(v):
        dma = pltpu.SemaphoreType.DMA
        return [
            pltpu.VMEM((3,) + v.shape, f32),
            pltpu.VMEM((3,) + v.shape, f32),
            pltpu.VMEM((3,) + v.shape[1:], f32),
            dma((6,)),
            dma((6,)),
        ]

    def __init__(self, place, v_ref, out, scratch):
        self.s, self.z, self.c, self.x, self.y, self.near = place
        self.v, self.out = v_ref, out
        self.total, self.got, self.got_z, self.send, self.recv = scratch

    def copy(self, kind):
        if kind < 3:
            src = self.v if kind == 0 else self.total.at[kind - 1]
            dst, to = self.got.at[kind], "cxy"[kind]
        else:
            z = self.z
            k = kind - 2
            other = (z + 1 - 2 * (z % 2), z + 2 - 4 * (z // 2), 3 - z)[k - 1]
            src, dst, to = self.total.at[2, other], self.got_z.at[k - 1], "z%d" % k
        return pltpu.make_async_remote_copy(
            src_ref=src,
            dst_ref=dst,
            send_sem=self.send.at[kind],
            recv_sem=self.recv.at[kind],
            device_id=self.near[to],
            device_id_type=MESH,
        )

    def start(self):
        self.copy(0).start()

    def advance(self, kind):
        self.copy(kind).wait_recv()
        mine = self.v[...] if kind == 0 else self.total[kind - 1]
        self.total[kind] = mine + self.got[kind]
        for k in (kind + 1,) if kind < 2 else (3, 4, 5):
            self.copy(k).start()

    def close(self):
        total = self.total[2, self.z]
        for k in (3, 4, 5):
            self.copy(k).wait_recv()
            total = total + self.got_z[k - 3]
        self.out[...] = total
        for k in range(6):
            self.copy(k).wait_send()


def sums_kernel(
    gate_ref,
    conv_ref,
    nm_ref,
    og_ref,
    no_ref,
    v_ref,
    in_out,
    out_out,
    v_out,
    *scratch,
):
    place = around()
    cut = Products.SCRATCH
    inp = Products(place, [gate_ref, conv_ref], nm_ref, in_out, scratch[:cut])
    outp = Products(place, [og_ref], no_ref, out_out, scratch[cut : 2 * cut])
    small = Smalls(place, v_ref, v_out, scratch[2 * cut :])
    outp.load()
    inp.load()
    greet(place[-1])
    outp.share()
    small.start()
    inp.share()

    def first(t, carry):
        outp.step(t)
        return carry

    lax.fori_loop(0, outp.chunks, first, 0)

    def second(t, carry):
        inp.step(t)

        @pl.when(t < outp.steps() - outp.chunks)
        def _():
            outp.step(t + outp.chunks)

        for kind in range(3):

            @pl.when(t == 2 * kind + 1)
            def _(kind=kind):
                small.advance(kind)

        return carry

    lax.fori_loop(0, inp.steps(), second, 0)
    small.close()
    outp.close()
    inp.close()


def weight_sums(d_gate, d_rest, nm, og, no, v, collective_id):
    vmem = pl.BlockSpec(memory_space=pltpu.VMEM)
    hbm = pl.BlockSpec(memory_space=pl.ANY)
    a_in, a_out, total = pl.pallas_call(
        sums_kernel,
        in_specs=[hbm] * 5 + [vmem],
        out_specs=[vmem] * 3,
        out_shape=[
            Products.out_shape([d_gate, d_rest], nm),
            Products.out_shape([og], no),
            jax.ShapeDtypeStruct(v.shape[1:], f32),
        ],
        scratch_shapes=Products.scratch([d_gate, d_rest], nm)
        + Products.scratch([og], no)
        + Smalls.scratch(v),
        compiler_params=pltpu.CompilerParams(
            collective_id=collective_id, has_side_effects=True, vmem_limit_bytes=VMEM_MOST
        ),
        cost_estimate=pl.CostEstimate(
            flops=6 * nm.shape[0] * nm.shape[1] * 9000, bytes_accessed=400_000_000, transcendentals=0
        ),
        name="weight_sums",
    )(d_gate, d_rest, nm, og, no, v)
    return a_in, a_out.reshape(og.shape[1], -1), total


LANES = 128
HALO = 16


def silu_parts(v):
    s = 1.0 / (1.0 + jnp.exp(-v))
    return v * s, s


def softplus(v):
    return jnp.maximum(v, 0.0) + jnp.log1p(jnp.exp(-jnp.abs(v)))


def lower_ones(t):
    i = lax.broadcasted_iota(jnp.int32, (t, t), 0)
    j = lax.broadcasted_iota(jnp.int32, (t, t), 1)
    return jnp.where(i >= j, 1.0, 0.0)


def exact(a, b, dims=NN):
    return lax.dot_general(a, b, dims, precision=highest, preferred_element_type=f32)


def head_columns(values, g):
    return pltpu.roll(values, (LANES - GROUP * g) % LANES, 1)[:, :GROUP]


class Exchange:
    def __init__(self, forward, own, own_low, got, t_low, t_got, u_low, u_got, p_low, p_got, before, send, recv):
        self.s, self.z, self.c, self.x, self.y, self.near = around()
        later = (lambda v: v) if forward else (lambda v: 1 - v)
        self.second = (later(self.c) == 1, later(self.x) == 1, later(self.y) == 1)
        self.own, self.own_low, self.got = own, own_low, got
        self.t_low, self.t_got, self.u_low, self.u_got = t_low, t_got, u_low, u_got
        self.p_low, self.p_got, self.before = p_low, p_got, before
        self.send, self.recv = send, recv
        self.n = own.shape[1]
        self.half = own.shape[2] // 2
        self.mine = pl.ds(pl.multiple_of(self.c * self.half, LANES), self.half)
        self.other = pl.ds(pl.multiple_of((1 - self.c) * self.half, LANES), self.half)

    def copy(self, kind, m):
        src, dst, to = (
            (self.own_low, self.got, "c"),
            (self.t_low, self.t_got, "x"),
            (self.u_low, self.u_got, "y"),
            (self.p_low, self.p_got, "c"),
        )[kind]
        return pltpu.make_async_remote_copy(
            src_ref=src.at[m],
            dst_ref=dst.at[m],
            send_sem=self.send.at[kind, m],
            recv_sem=self.recv.at[kind, m],
            device_id=self.near[to],
            device_id_type=MESH,
        )

    def put_decay(self, ref, m, lanes, decay):
        high = decay.astype(bf16).astype(f32)
        row = lax.broadcasted_iota(jnp.int32, (16, decay.shape[1]), 0)
        both = jnp.where(row == 0, high, jnp.where(row == 1, decay - high, 0.0))
        ref[m, pl.ds(self.n, 16), lanes] = both.astype(bf16)

    def decay_of(self, ref, m, lanes):
        rows = ref[m, pl.ds(self.n, 16), lanes].astype(f32)
        return rows[0:1] + rows[1:2]

    def put_own(self, m, lanes, state, decay):
        self.own[m, :, lanes] = state
        self.own_low[m, pl.ds(0, self.n), lanes] = state.astype(bf16)
        self.put_decay(self.own_low, m, lanes, decay)

    def core(self, m):
        self.copy(0, m).start()

    def along_x(self, m):
        self.copy(0, m).wait_recv()
        second = self.second[0]
        mine = self.own[m, :, self.mine]
        theirs = self.got[m, pl.ds(0, self.n), self.mine].astype(f32)
        d_mine = self.decay_of(self.own_low, m, self.mine)
        d_theirs = self.decay_of(self.got, m, self.mine)
        total = theirs * jnp.where(second, d_mine, 1.0) + mine * jnp.where(second, 1.0, d_theirs)
        self.t_low[m, pl.ds(0, self.n), :] = total.astype(bf16)
        self.put_decay(self.t_low, m, pl.ds(0, self.half), d_mine * d_theirs)
        self.copy(1, m).start()

    def along_y(self, m):
        self.copy(1, m).wait_recv()
        second = self.second[1]
        every = pl.ds(0, self.half)
        mine = self.t_low[m, pl.ds(0, self.n), :].astype(f32)
        theirs = self.t_got[m, pl.ds(0, self.n), :].astype(f32)
        d_mine = self.decay_of(self.t_low, m, every)
        d_theirs = self.decay_of(self.t_got, m, every)
        total = theirs * jnp.where(second, d_mine, 1.0) + mine * jnp.where(second, 1.0, d_theirs)
        self.u_low[m] = total.astype(bf16)
        self.copy(2, m).start()

    def back_to_core(self, m):
        self.copy(2, m).wait_recv()
        every = pl.ds(0, self.half)
        x_second = jnp.where(self.second[1], 1.0, 0.0)
        y_second = jnp.where(self.second[2], 1.0, 0.0)
        theirs = self.t_got[m, pl.ds(0, self.n), :].astype(f32)
        d_theirs = self.decay_of(self.t_got, m, every)
        over = y_second * jnp.where(self.second[1], d_theirs, 1.0)
        before = x_second * theirs + over * self.u_got[m].astype(f32)
        self.before[m] = before
        self.p_low[m] = before.astype(bf16)
        self.copy(3, m).start()

    def begin_state(self, m, out):
        self.copy(3, m).wait_recv()
        second = jnp.where(self.second[0], 1.0, 0.0)
        for lanes, before in (
            (self.mine, self.before[m]),
            (self.other, self.p_got[m].astype(f32)),
        ):
            d_theirs = self.decay_of(self.got, m, lanes)
            theirs = self.got[m, pl.ds(0, self.n), lanes].astype(f32)
            over = jnp.where(self.second[0], d_theirs, 1.0)
            out[m, :, lanes] = (before * over + second * theirs).astype(bf16)

    def sent(self):
        for m in range(self.own.shape[0]):
            for kind in range(4):
                self.copy(kind, m).wait_send()


def exchange_scratch(micro, n, inner):
    half = inner // 2
    dma = pltpu.SemaphoreType.DMA
    return [
        pltpu.VMEM((micro, n, inner), f32),
        pltpu.VMEM((micro, n + 16, inner), bf16),
        pltpu.VMEM((micro, n + 16, inner), bf16),
        pltpu.VMEM((micro, n + 16, half), bf16),
        pltpu.VMEM((micro, n + 16, half), bf16),
        pltpu.VMEM((micro, n, half), bf16),
        pltpu.VMEM((micro, n, half), bf16),
        pltpu.VMEM((micro, n, half), bf16),
        pltpu.VMEM((micro, n, half), bf16),
        pltpu.VMEM((micro, n, half), f32),
        dma((4, micro)),
        dma((4, micro)),
    ]


EXCHANGE = 12


def steps_of(raw, shift, rate):
    t = raw.shape[0]
    dt = softplus(raw + shift)
    cum = exact(lower_ones(t), dt * rate)
    return dt, cum


def conv_rows(buf, cw, cb):
    taps = cw.shape[0]
    t = buf.shape[0] - HALO
    total = cb + buf[HALO - taps + 1 : HALO - taps + 1 + t, :] * cw[0:1]
    for k in range(1, taps):
        at = HALO - taps + 1 + k
        total = total + buf[at : at + t, :] * cw[k : k + 1]
    return total


def scan_forward_kernel(
    hs,
    conv_ref,
    raw_ref,
    cw_ref,
    cb_ref,
    shift_ref,
    rate_ref,
    skip_ref,
    x_ref,
    bc_ref,
    y_ref,
    low_ref,
    halo,
    begin_ref,
    *scratch,
):
    buf, wide_buf, scores, dts, cums, rows_t, h_send, h_recv = scratch[EXCHANGE:]
    ex = Exchange(True, *scratch[:EXCHANGE])
    s, z = ex.s, ex.z
    micro, t, channels = conv_ref.shape
    inner = x_ref.shape[2]
    n = begin_ref.shape[1]
    gc = GROUP * hs
    groups = inner // gc
    half_t = t // 2
    near = dict(ex.near)
    near = {k: near[k] for k in ("c", "x", "y")}
    near["next"] = ((s + 1) % 8, z)
    near["last"] = ((s + 7) % 8, z)
    greet(near)

    tail = [
        pltpu.make_async_remote_copy(
            src_ref=conv_ref.at[m, pl.ds(t - HALO, HALO)],
            dst_ref=halo.at[m],
            send_sem=h_send.at[m],
            recv_sem=h_recv.at[m],
            device_id=near["next"],
            device_id_type=MESH,
        )
        for m in range(micro)
    ]
    for copy in tail:
        copy.start()
    for m in range(micro):
        dt, cum = steps_of(raw_ref[m], shift_ref[...], rate_ref[...])
        dts[m] = dt
        cums[m] = cum
        rows_t[m] = cum.T
    for copy in tail:
        copy.wait_recv()
    has_prior = jnp.where(s > 0, 1.0, 0.0)

    def activate(m, lanes, into):
        into[0:HALO] = halo[m, :, lanes].astype(f32) * has_prior
        into[pl.ds(HALO, t)] = conv_ref[m, :, lanes].astype(f32)
        return silu_parts(conv_rows(into, cw_ref[:, lanes], cb_ref[:, lanes]))[0]

    def own_states(m, a, b):
        def body(g, carry):
            lanes = pl.ds(pl.multiple_of(g * gc, gc), gc)
            x = activate(m, lanes, buf).astype(bf16)
            x_ref[m, :, lanes] = x
            cum = head_columns(cums[m], g)
            to_end = head_columns(dts[m], g) * jnp.exp(cum[t - 1 :] - cum)
            weighted = (x.astype(f32) * widen(to_end, hs)).astype(bf16)
            state = mm(bc_ref[m, :, 0:n], weighted, TN)
            ex.put_own(m, lanes, state, widen(jnp.exp(cum[t - 1 :]), hs))
            return carry

        lax.fori_loop(a, b, body, 0)

    def local_scans(m, a, b):
        lane = lax.broadcasted_iota(jnp.int32, (half_t, 2 * hs), 1)

        def body(g, carry):
            lanes = pl.ds(pl.multiple_of(g * gc, gc), gc)
            cum = head_columns(cums[m], g)
            rows = rows_t[m, pl.ds(pl.multiple_of(g * GROUP, GROUP), GROUP), :]
            dt_wide = widen(head_columns(dts[m], g), hs)
            weighted = (x_ref[m, :, lanes].astype(f32) * dt_wide).astype(bf16)
            for k in range(0, GROUP, 2):
                pair = weighted[:, k * hs : (k + 2) * hs]
                at = pl.ds(pl.multiple_of(g * gc + k * hs, 2 * hs), 2 * hs)
                top, low = [], []
                for h in (k, k + 1):
                    col, row = cum[:, h : h + 1], rows[h : h + 1, :]
                    m1 = jnp.exp(jnp.minimum(col[:half_t] - row[:, :half_t], 0.0))
                    m2 = jnp.exp(jnp.minimum(col[half_t:] - row, 0.0))
                    m1 = (m1 * scores[m, :half_t, :half_t]).astype(bf16)
                    m2 = (m2 * scores[m, half_t:, :]).astype(bf16)
                    top.append(mm(m1, pair[:half_t]))
                    low.append(mm(m2, pair))
                y_ref[m, :half_t, at] = jnp.where(lane < hs, top[0], top[1])
                y_ref[m, half_t:, at] = jnp.where(lane < hs, low[0], low[1])
            return carry

        lax.fori_loop(a, b, body, 0)

    def carried(m):
        def body(g, carry):
            lanes = pl.ds(pl.multiple_of(g * gc, gc), gc)
            decay = widen(jnp.exp(head_columns(cums[m], g)), hs)
            scan = y_ref[m, :, lanes] + decay * mm(bc_ref[m, :, n:], begin_ref[m, :, lanes])
            y_ref[m, :, lanes] = scan
            x = x_ref[m, :, lanes].astype(f32)
            low_ref[m, :, lanes] = (scan + skip_ref[:, lanes] * x).astype(bf16)
            return carry

        lax.fori_loop(0, groups, body, 0)

    for m in range(micro):
        lanes = pl.ds(inner, channels - inner)
        bc = activate(m, lanes, wide_buf).astype(bf16)
        bc_ref[m] = bc
        scores[m] = mm(bc[:, n:], bc[:, :n], NT) * lower_ones(t)
    middle = groups // 2
    own_states(0, 0, groups)
    ex.core(0)
    own_states(1, 0, middle)
    ex.along_x(0)
    own_states(1, middle, groups)
    ex.core(1)
    local_scans(0, 0, middle)
    ex.along_x(1)
    ex.along_y(0)
    local_scans(0, middle, groups)
    local_scans(1, 0, middle)
    ex.along_y(1)
    ex.back_to_core(0)
    local_scans(1, middle, groups)
    ex.begin_state(0, begin_ref)
    carried(0)
    ex.back_to_core(1)
    ex.begin_state(1, begin_ref)
    carried(1)
    ex.sent()
    for copy in tail:
        copy.wait_send()


def scan_forward(conv_low, raw, conv_w, conv_b, shift, rate, skip_wide, inner, hs, collective_id):
    micro, t, channels = conv_low.shape
    n = (channels - inner) // 2
    gc = GROUP * hs
    dma = pltpu.SemaphoreType.DMA
    vmem = pl.BlockSpec(memory_space=pltpu.VMEM)
    return pl.pallas_call(
        partial(scan_forward_kernel, hs),
        in_specs=[vmem] * 7,
        out_specs=[vmem] * 6,
        out_shape=[
            jax.ShapeDtypeStruct((micro, t, inner), bf16),
            jax.ShapeDtypeStruct((micro, t, 2 * n), bf16),
            jax.ShapeDtypeStruct((micro, t, inner), f32),
            jax.ShapeDtypeStruct((micro, t, inner), bf16),
            jax.ShapeDtypeStruct((micro, HALO, channels), bf16),
            jax.ShapeDtypeStruct((micro, n, inner), bf16),
        ],
        scratch_shapes=exchange_scratch(micro, n, inner)
        + [
            pltpu.VMEM((HALO + t, gc), f32),
            pltpu.VMEM((HALO + t, 2 * n), f32),
            pltpu.VMEM((micro, t, t), f32),
            pltpu.VMEM((micro, t, LANES), f32),
            pltpu.VMEM((micro, t, LANES), f32),
            pltpu.VMEM((micro, LANES, t), f32),
            dma((micro,)),
            dma((micro,)),
        ],
        compiler_params=pltpu.CompilerParams(
            collective_id=collective_id, has_side_effects=True, vmem_limit_bytes=VMEM_MOST
        ),
        cost_estimate=pl.CostEstimate(
            flops=4 * micro * t * inner * (t + 3 * n), bytes_accessed=100_000_000, transcendentals=0
        ),
        name="scan_forward",
    )(conv_low, raw, conv_w, conv_b, shift, rate, skip_wide)


def scan_backward_kernel(
    hs,
    dy_ref,
    x_ref,
    bc_ref,
    y_ref,
    begin_ref,
    raw_ref,
    conv_ref,
    halo_ref,
    cw_ref,
    cb_ref,
    shift_ref,
    rate_ref,
    skip_ref,
    dconv_ref,
    dcw_ref,
    dcb_ref,
    heads_ref,
    *scratch,
):
    (
        buf,
        wide_buf,
        scores,
        total,
        dts,
        cums,
        rows_t,
        ends,
        dxl,
        dbc,
        ddt_sum,
        dcum_sum,
        head_low,
        next_low,
        h_send,
        h_recv,
    ) = scratch[EXCHANGE:]
    ex = Exchange(False, *scratch[:EXCHANGE])
    s, z = ex.s, ex.z
    micro, t, channels = conv_ref.shape
    inner = x_ref.shape[2]
    n = begin_ref.shape[1]
    gc = GROUP * hs
    groups = inner // gc
    half = t // 2
    taps = cw_ref.shape[0]
    near = {k: ex.near[k] for k in ("c", "x", "y")}
    near["next"] = ((s + 1) % 8, z)
    near["last"] = ((s + 7) % 8, z)
    greet(near)
    first_rows = [
        pltpu.make_async_remote_copy(
            src_ref=head_low.at[m],
            dst_ref=next_low.at[m],
            send_sem=h_send.at[m],
            recv_sem=h_recv.at[m],
            device_id=near["last"],
            device_id_type=MESH,
        )
        for m in range(micro)
    ]
    has_prior = jnp.where(s > 0, 1.0, 0.0)
    has_next = jnp.where(s < 7, 1.0, 0.0)

    def own_states(m, a, b):
        def body(g, carry):
            lanes = pl.ds(pl.multiple_of(g * gc, gc), gc)
            cum = head_columns(cums[m], g)
            weighted = (dy_ref[m, :, lanes].astype(f32) * widen(jnp.exp(cum), hs)).astype(bf16)
            state = mm(bc_ref[m, :, n:], weighted, TN)
            ex.put_own(m, lanes, state, widen(jnp.exp(cum[t - 1 :]), hs))
            return carry

        lax.fori_loop(a, b, body, 0)

    def local_terms(m, a, b):
        lane = lax.broadcasted_iota(jnp.int32, (t, 2 * hs), 1)
        lane_half = lax.broadcasted_iota(jnp.int32, (half, 2 * hs), 1)

        def body(g, carry):
            lanes = pl.ds(pl.multiple_of(g * gc, gc), gc)
            cum = head_columns(cums[m], g)
            rows = rows_t[m, pl.ds(pl.multiple_of(g * GROUP, GROUP), GROUP), :]
            dt_wide = widen(head_columns(dts[m], g), hs)
            weighted = (x_ref[m, :, lanes].astype(f32) * dt_wide).astype(bf16)
            for k in range(0, GROUP, 2):
                pair = weighted[:, k * hs : (k + 2) * hs]
                at = pl.ds(pl.multiple_of(g * gc + k * hs, 2 * hs), 2 * hs)
                dy = dy_ref[m, :, at]
                top, low = [], []
                for h in (k, k + 1):
                    col, row = cum[:, h : h + 1], rows[h : h + 1, :]
                    mine = jnp.where(lane < hs, pair, 0) if h == k else jnp.where(lane < hs, 0, pair)
                    l1 = jnp.exp(jnp.minimum(row - col[:half], 0.0))
                    l2 = jnp.exp(jnp.minimum(row[:, half:] - col[half:], 0.0))
                    total[:half, :] += l1 * mm(mine[:half], dy, NT)
                    total[half:, half:] += l2 * mm(mine[half:], dy[half:], NT)
                    top.append(mm((l1 * scores[m, :half, :]).astype(bf16), dy))
                    low.append(mm((l2 * scores[m, half:, half:]).astype(bf16), dy[half:]))
                dxl[m, :half, at] = jnp.where(lane_half < hs, top[0], top[1])
                dxl[m, half:, at] = jnp.where(lane_half < hs, low[0], low[1])
            return carry

        lax.fori_loop(a, b, body, 0)

    def upper_ones():
        j = lax.broadcasted_iota(jnp.int32, (t, t), 0)
        i = lax.broadcasted_iota(jnp.int32, (t, t), 1)
        return jnp.where(i >= j, 1.0, 0.0)

    def local_close(m):
        d = total[...] * upper_ones()
        dbc[m, :, 0:n] = mm(d.astype(bf16), bc_ref[m, :, n:])
        dbc[m, :, n:] = mm(d.T.astype(bf16), bc_ref[m, :, :n])

    def through_states(m, sums):
        r = lax.broadcasted_iota(jnp.int32, (gc, LANES), 0)
        col = lax.broadcasted_iota(jnp.int32, (gc, LANES), 1)
        ddt_sum[...] = jnp.zeros_like(ddt_sum)
        dcum_sum[...] = jnp.zeros_like(dcum_sum)

        def body(g, carry):
            last, skips = carry
            lanes = pl.ds(pl.multiple_of(g * gc, gc), gc)
            ones = jnp.where(r // hs + g * GROUP == col, 1.0, 0.0).astype(bf16)
            cum = head_columns(cums[m], g)
            dt_wide = widen(head_columns(dts[m], g), hs)
            x, dy = x_ref[m, :, lanes].astype(f32), dy_ref[m, :, lanes].astype(f32)
            weighted = (x * dt_wide).astype(bf16).astype(f32)
            decay = widen(jnp.exp(cum), hs)
            to_end = widen(jnp.exp(cum[t - 1 :] - cum), hs)
            s_in, ds = begin_ref[m, :, lanes], ends[m, :, lanes]
            through = to_end * mm(bc_ref[m, :, 0:n], ds)
            d_weighted = dxl[m, :, lanes] + through
            dconv_ref[m, :, lanes] = (dt_wide * d_weighted + skip_ref[:, lanes] * dy).astype(bf16)
            dbc[m, :, 0:n] += mm((weighted * to_end).astype(bf16), ds, NT)
            dbc[m, :, n:] += mm((dy * decay).astype(bf16), s_in, NT)
            ddt_sum[...] += head_sums(x * d_weighted, ones)
            dcum_sum[...] += head_sums(dy * y_ref[m, :, lanes] - weighted * d_weighted, ones)
            at_end = jnp.sum(weighted * through, axis=0, keepdims=True) + decay[t - 1 :] * jnp.sum(
                s_in.astype(f32) * ds.astype(f32), axis=0, keepdims=True
            )
            last = last + head_sums(jnp.broadcast_to(at_end, (8, gc)), ones)
            by_skip = jnp.sum(x * dy, axis=0, keepdims=True)
            skips = skips + head_sums(jnp.broadcast_to(by_skip, (8, gc)), ones)
            return last, skips

        none = jnp.zeros((8, LANES), f32)
        last, skips = lax.fori_loop(0, groups, body, (none, none))
        d_log = exact(upper_ones(), dcum_sum[...]) + last[0:1]
        v = raw_ref[m] + shift_ref[...]
        d_dt = (ddt_sum[...] + d_log * rate_ref[...]) / (1.0 + jnp.exp(-v))
        rest = dconv_ref.shape[2] - channels - LANES
        dconv_ref[m, :, pl.ds(channels, LANES)] = d_dt.astype(bf16)
        if rest:
            dconv_ref[m, :, pl.ds(channels + LANES, rest)] = jnp.zeros((t, rest), bf16)
        d_bias = jnp.sum(d_dt, axis=0, keepdims=True)
        d_rate = jnp.sum(d_log * dts[m], axis=0, keepdims=True) * rate_ref[...]
        return sums[0] + d_bias, sums[1] + d_rate, sums[2] + skips[0:1]

    def pre_slope(into, lanes, grad, rows):
        v = conv_rows(into[0 : HALO + rows, :], cw_ref[:, lanes], cb_ref[:, lanes])
        sig = 1.0 / (1.0 + jnp.exp(-v))
        return grad * (sig * (1.0 + v * (1.0 - sig)))

    def load(m, lanes, into, rows):
        into[0:HALO] = halo_ref[m, :, lanes].astype(f32) * has_prior
        into[HALO : HALO + rows] = conv_ref[m, 0:rows, lanes].astype(f32)

    def first_slopes(m):
        def one(lanes, into, grad):
            load(m, lanes, into, HALO)
            head_low[m, :, lanes] = pre_slope(into, lanes, grad, HALO).astype(bf16)

        def body(g, carry):
            lanes = pl.ds(pl.multiple_of(g * gc, gc), gc)
            one(lanes, buf, dconv_ref[m, 0:HALO, lanes].astype(f32))
            return carry

        lax.fori_loop(0, groups, body, 0)
        one(pl.ds(inner, channels - inner), wide_buf, dbc[m, 0:HALO, :])
        first_rows[m].start()

    def conv_back(m):
        def one(lanes, into, grad):
            load(m, lanes, into, t)
            slope = pre_slope(into, lanes, grad, t)
            weights = cw_ref[:, lanes]
            lines = []
            for k in range(taps):
                at = HALO - taps + 1 + k
                lines.append(jnp.sum(slope * into[at : at + t, :], axis=0, keepdims=True))
            dcw_ref[:, lanes] += jnp.concatenate(lines, axis=0)
            dcb_ref[:, lanes] += jnp.sum(slope, axis=0, keepdims=True)
            into[0:t] = slope
            into[t : t + HALO] = next_low[m, :, lanes].astype(f32) * has_next
            back = into[taps - 1 : taps - 1 + t, :] * weights[0:1]
            for k in range(1, taps):
                at = taps - 1 - k
                back = back + into[at : at + t, :] * weights[k : k + 1]
            dconv_ref[m, :, lanes] = back.astype(bf16)

        def body(g, carry):
            lanes = pl.ds(pl.multiple_of(g * gc, gc), gc)
            one(lanes, buf, dconv_ref[m, :, lanes].astype(f32))
            return carry

        lax.fori_loop(0, groups, body, 0)
        one(pl.ds(inner, channels - inner), wide_buf, dbc[m])

    for m in range(micro):
        dt, cum = steps_of(raw_ref[m], shift_ref[...], rate_ref[...])
        dts[m] = dt
        cums[m] = cum
        rows_t[m] = cum.T
        scores[m] = mm(bc_ref[m, :, 0:n], bc_ref[m, :, n:], NT) * upper_ones()
    dcw_ref[...] = jnp.zeros_like(dcw_ref)
    dcb_ref[...] = jnp.zeros_like(dcb_ref)
    total[...] = jnp.zeros_like(total)
    middle = groups // 2
    own_states(0, 0, groups)
    ex.core(0)
    own_states(1, 0, middle)
    ex.along_x(0)
    own_states(1, middle, groups)
    ex.core(1)
    local_terms(0, 0, middle)
    ex.along_x(1)
    ex.along_y(0)
    local_terms(0, middle, groups)
    local_close(0)
    total[...] = jnp.zeros_like(total)
    ex.along_y(1)
    ex.back_to_core(0)
    local_terms(1, 0, groups)
    local_close(1)
    ex.begin_state(0, ends)
    ex.back_to_core(1)
    none = jnp.zeros((1, LANES), f32)
    sums = through_states(0, (none, none, none))
    first_slopes(0)
    ex.begin_state(1, ends)
    sums = through_states(1, sums)
    first_slopes(1)
    heads_ref[...] = jnp.concatenate(list(sums) + [jnp.zeros((5, LANES), f32)], axis=0)
    first_rows[0].wait_recv()
    conv_back(0)
    first_rows[1].wait_recv()
    conv_back(1)
    ex.sent()
    for copy in first_rows:
        copy.wait_send()


def scan_backward(
    dy, x, bc, y, begin, raw, conv_low, halo, conv_w, conv_b, shift, rate, skip_wide, hs, collective_id
):
    micro, t, channels = conv_low.shape
    inner = x.shape[2]
    n = begin.shape[1]
    gc = GROUP * hs
    taps = conv_w.shape[0]
    dma = pltpu.SemaphoreType.DMA
    vmem = pl.BlockSpec(memory_space=pltpu.VMEM)
    return pl.pallas_call(
        partial(scan_backward_kernel, hs),
        in_specs=[vmem] * 13,
        out_specs=[vmem] * 4,
        out_shape=[
            jax.ShapeDtypeStruct((micro, t, -(-(channels + LANES) // 256) * 256), bf16),
            jax.ShapeDtypeStruct((taps, channels), f32),
            jax.ShapeDtypeStruct((1, channels), f32),
            jax.ShapeDtypeStruct((8, LANES), f32),
        ],
        scratch_shapes=exchange_scratch(micro, n, inner)
        + [
            pltpu.VMEM((HALO + t, gc), f32),
            pltpu.VMEM((HALO + t, 2 * n), f32),
            pltpu.VMEM((micro, t, t), f32),
            pltpu.VMEM((t, t), f32),
            pltpu.VMEM((micro, t, LANES), f32),
            pltpu.VMEM((micro, t, LANES), f32),
            pltpu.VMEM((micro, LANES, t), f32),
            pltpu.VMEM((micro, n, inner), bf16),
            pltpu.VMEM((micro, t, inner), f32),
            pltpu.VMEM((micro, t, 2 * n), f32),
            pltpu.VMEM((t, LANES), f32),
            pltpu.VMEM((t, LANES), f32),
            pltpu.VMEM((micro, HALO, channels), bf16),
            pltpu.VMEM((micro, HALO, channels), bf16),
            dma((micro,)),
            dma((micro,)),
        ],
        compiler_params=pltpu.CompilerParams(
            collective_id=collective_id, has_side_effects=True, vmem_limit_bytes=VMEM_MOST
        ),
        cost_estimate=pl.CostEstimate(
            flops=8 * micro * t * inner * (t + 3 * n), bytes_accessed=100_000_000, transcendentals=0
        ),
        name="scan_backward",
    )(dy, x, bc, y, begin, raw, conv_low, halo, conv_w, conv_b, shift, rate, skip_wide)


def project_kernel(n_ref, w_ref, v_ref, o_ref):
    total = mm(n_ref[0], w_ref[...], NT)
    for k in range(1, n_ref.shape[0]):
        total += mm(n_ref[k], v_ref[k - 1], NT)
    o_ref[...] = total.astype(o_ref.dtype)


def project(parts, own, others, first, count, tile, dtype):
    shards, rows, depth = parts.shape
    return pl.pallas_call(
        project_kernel,
        grid=(count // tile,),
        in_specs=[
            pl.BlockSpec((shards, rows, depth), lambda i: (0, 0, 0)),
            pl.BlockSpec((tile, depth), lambda i: (first // tile + i, 0)),
            pl.BlockSpec((shards - 1, tile, depth), lambda i: (0, first // tile + i, 0)),
        ],
        out_specs=pl.BlockSpec((rows, tile), lambda i: (0, i)),
        out_shape=jax.ShapeDtypeStruct((rows, count), dtype),
        compiler_params=pltpu.CompilerParams(vmem_limit_bytes=VMEM),
        name="project",
    )(parts, own, others)


def unproject_kernel(steps, d_ref, e_ref, w_ref, v_ref, o_ref):
    def add(ref):
        o_ref[0] += mm(ref[...], w_ref[...])
        for k in range(1, o_ref.shape[0]):
            o_ref[k] += mm(ref[...], v_ref[k - 1])

    @pl.when(pl.program_id(0) == 0)
    def _():
        o_ref[...] = jnp.zeros_like(o_ref)

    @pl.when(pl.program_id(0) < steps)
    def _():
        add(d_ref)

    @pl.when(pl.program_id(0) >= steps)
    def _():
        add(e_ref)


def unproject(d, e, own, others, tile):
    shards, count, depth = others.shape
    shards += 1
    rows = d.shape[0]
    steps = d.shape[1] // tile
    return pl.pallas_call(
        partial(unproject_kernel, steps),
        grid=(count // tile,),
        in_specs=[
            pl.BlockSpec((rows, tile), lambda i: (0, jnp.minimum(i, steps - 1))),
            pl.BlockSpec((rows, tile), lambda i: (0, jnp.maximum(i - steps, 0))),
            pl.BlockSpec((tile, depth), lambda i: (i, 0)),
            pl.BlockSpec((shards - 1, tile, depth), lambda i: (0, i, 0)),
        ],
        out_specs=pl.BlockSpec((shards, rows, depth), lambda i: (0, 0, 0)),
        out_shape=jax.ShapeDtypeStruct((shards, rows, depth), f32),
        compiler_params=pltpu.CompilerParams(vmem_limit_bytes=VMEM),
        name="unproject",
    )(d, e, own, others)


def rms_front(hidden_rows, gain):
    power = jnp.mean(hidden_rows * hidden_rows, axis=-1, keepdims=True)
    return hidden_rows * lax.rsqrt(power + epsilon) * gain


def conv_act(padded, conv_w, conv_b):
    taps = conv_w.shape[0]
    rows_out = padded.shape[1] - taps + 1
    total = conv_b + padded[:, 0:rows_out] * conv_w[0]
    for offset in range(1, taps):
        total = total + padded[:, offset : offset + rows_out] * conv_w[offset]
    return jax.nn.silu(total)


def gate_norm(values, gate_in, gain):
    gated = values * jax.nn.silu(gate_in)
    power = jnp.mean(gated * gated, axis=-1, keepdims=True)
    return gated * lax.rsqrt(power + epsilon) * gain


def local(
    hidden,
    lengths,
    out_grad,
    norm_gain,
    in_weight,
    conv_weight,
    conv_bias,
    dt_bias,
    a_log,
    skip_gain,
    gated_gain,
    out_weight,
):
    count = lax.axis_size("seq")
    shards = lax.axis_size("wshard")
    rank = lax.axis_index("seq")
    shard = lax.axis_index("wshard")
    micro, _, tokens, width = hidden.shape
    taps = conv_weight.shape[1]
    inner = out_weight.shape[0] * shards
    channels = conv_bias.shape[0] * shards
    heads = dt_bias.shape[0] * shards
    hs = inner // heads
    n = (channels - inner) // 2
    groups = heads // GROUP
    rows = micro * tokens
    fast = count == 8 and shards == 4 and micro == 2
    in_local = in_weight.T
    small = [norm_gain, conv_weight.T.reshape(-1), conv_bias, dt_bias, a_log, skip_gain, gated_gain]
    sizes = [v.shape[0] for v in small]
    small.append(in_local[inner + channels :].reshape(-1))
    packed_low = lax.all_gather(jnp.concatenate(small), "wshard", axis=0)
    packed = packed_low.astype(f32)
    parts, at = [], 0
    for size in sizes:
        parts.append(packed[:, at : at + size])
        at += size
    norm_g = parts[0].reshape(-1)
    conv_w = parts[1].reshape(shards, taps, -1).transpose(1, 0, 2).reshape(taps, -1)
    conv_b = parts[2].reshape(-1)
    dt_shift = parts[3].reshape(-1)
    rate = -jnp.exp(parts[4].reshape(-1))
    skip = parts[5].reshape(-1)
    gated_g = parts[6].reshape(-1)

    dt_w = packed_low[:, at:].reshape(shards, heads, -1).transpose(1, 0, 2).reshape(heads, -1)
    order = jnp.arange(shards) ^ shard
    if fast:
        in_w = gather_input_weight(in_local, inner, channels)
        out_part = lax.optimization_barrier((out_weight, in_w[0, 0, 0]))[0]
    else:
        every = lax.all_gather(in_local[: inner + channels], "wshard", axis=0)
        in_w = every[order[1:]]
        out_part = out_weight
    out_w = lax.all_gather(out_part, "wshard", axis=0, tiled=True)

    def grouped(v):
        return v.reshape(micro, tokens, groups, GROUP).transpose(0, 2, 1, 3)

    rows_in = hidden.reshape(rows, width).astype(f32)
    cot = out_grad.reshape(rows, width).astype(f32)
    positions = rank * tokens + jnp.arange(tokens, dtype=jnp.int32)
    valid = (positions[None, :] < lengths[:, 0][:, None]).astype(f32).reshape(rows, 1)
    normed, front_back = jax.vjp(rms_front, rows_in, norm_g)
    normed_low = normed.astype(bf16)
    normed_parts = normed_low.reshape(rows, shards, -1).transpose(1, 0, 2)[order]
    tile = 256
    conv_low = project(normed_parts, in_local, in_w, inner, channels, tile, bf16)
    gate_in = project(normed_parts, in_local, in_w, 0, inner, tile, f32)
    dt_low = mm(normed_low, dt_w, NT).astype(bf16)
    conv_low = conv_low.reshape(micro, tokens, channels)
    dt_raw = dt_low.astype(f32).reshape(micro, tokens, heads) + dt_shift
    skip_wide = jnp.repeat(skip, hs)[None, :]

    def to_lanes(v):
        return jnp.pad(v, ((0, 0),) * (v.ndim - 1) + ((0, LANES - heads),))

    if fast:
        raw = to_lanes(dt_low.astype(f32).reshape(micro, tokens, heads))
        x_low, bc_low, y_scan, scanned_low, halo, s_in = scan_forward(
            conv_low,
            raw,
            conv_w,
            conv_b[None, :],
            to_lanes(dt_shift[None, :]),
            to_lanes(rate[None, :]),
            skip_wide,
            inner,
            hs,
            3,
        )
    else:
        prior = from_behind(conv_low[:, tokens - (taps - 1) :], "seq", 1)
        padded = jnp.concatenate([prior, conv_low], axis=1).astype(f32)
        mixed, conv_back = jax.vjp(conv_act, padded, conv_w, conv_b)
        dt = jax.nn.softplus(dt_raw)
        tri = (jnp.arange(tokens)[:, None] >= jnp.arange(tokens)[None, :]).astype(f32)
        cum = jnp.einsum("ij,mjh->mih", tri, dt * rate, precision=highest)
        dt_g, cum_g = grouped(dt), grouped(cum)
        row_g = cum_g.transpose(0, 1, 3, 2)
        last = cum[:, tokens - 1, :]
        decays = lax.all_gather(jnp.exp(last), "seq", axis=0)
        decay_w = grouped(jnp.exp(cum))
        x_low = mixed[..., :inner].astype(bf16)
        b_low = mixed[..., inner : inner + n].astype(bf16)
        c_low = mixed[..., inner + n :].astype(bf16)
        end_w = grouped(dt * jnp.exp(last[:, None, :] - cum))
        own_state = block_states(x_low, end_w, b_low.transpose(0, 2, 1), hs)
        y_local = local_scan(x_low, dt_g, cum_g, row_g, b_low, c_low, hs)
        s_in = running_states(own_state, decays, hs, True)
        y_scan, scanned_low = add_carry(x_low, y_local, cum_g, c_low, s_in, skip_wide, hs)

    scanned = scanned_low.reshape(rows, inner).astype(f32)
    normed_out, gate_back = jax.vjp(gate_norm, scanned, gate_in, gated_g)
    normed_out_low = normed_out.astype(bf16)
    branch = mm(normed_out_low, out_w)
    output = (rows_in + valid * branch).astype(bf16).reshape(hidden.shape)

    g = (cot * valid).astype(bf16)
    d_scanned, d_gate_in, d_gated = gate_back(mm(g, out_w, NT))
    dy = d_scanned.astype(bf16).reshape(micro, tokens, inner)
    if fast:
        d_rest, d_conv_w, d_conv_b, by_head = scan_backward(
            dy,
            x_low,
            bc_low,
            y_scan,
            s_in,
            raw,
            conv_low,
            halo,
            conv_w,
            conv_b[None, :],
            to_lanes(dt_shift[None, :]),
            to_lanes(rate[None, :]),
            skip_wide,
            hs,
            4,
        )
        d_dt_bias, d_a_log, d_skip = by_head[0, :heads], by_head[1, :heads], by_head[2, :heads]
        d_conv_b = d_conv_b[0]
        d_rest = d_rest.reshape(rows, -1)
        d_dt_low = d_rest[:, channels : channels + heads]
    else:
        own_grad = block_states(dy, decay_w, c_low.transpose(0, 2, 1), hs)
        dx_local, db_local, dc_local = local_back(x_low, dy, dt_g, cum_g, row_g, b_low, c_low, hs)
        ds = running_states(own_grad, decays, hs, False)
        dx_low, ddt_g, dcum_g, db, dc, last_term, dskip = carry_back(
            x_low, dy, dx_local, y_scan, dt_g, cum_g, b_low, s_in, ds, db_local, dc_local, skip_wide, hs
        )

        def ungrouped(v):
            return v.transpose(0, 2, 1, 3).reshape(micro, tokens, heads)

        at_end = jnp.sum(last_term.reshape(micro, heads, hs), axis=-1)[:, None, :]
        d_log = jnp.einsum("ij,mih->mjh", tri, ungrouped(dcum_g), precision=highest) + at_end
        d_dt = (ungrouped(ddt_g) + d_log * rate) * jax.nn.sigmoid(dt_raw)
        d_dt_bias = jnp.sum(d_dt, axis=(0, 1))
        d_a_log = jnp.sum(d_log * dt, axis=(0, 1)) * rate
        d_skip = jnp.sum(dskip.reshape(-1, heads, hs), axis=(0, 2))
        mixed_grad = jnp.concatenate([dx_low.astype(f32), db, dc], axis=2)
        d_padded, d_conv_w, d_conv_b = conv_back(mixed_grad)
        from_next = from_behind(d_padded[:, : taps - 1].astype(bf16), "seq", -1).astype(f32)
        d_conv = d_padded[:, taps - 1 :].at[:, tokens - (taps - 1) :].add(from_next)
        d_dt_low = d_dt.astype(bf16).reshape(rows, heads)
    total_cols = inner + channels + heads
    d_gate_low = d_gate_in.astype(bf16)
    if not fast:
        d_rest = d_conv.astype(bf16).reshape(rows, channels)
    d_parts = unproject(d_gate_low, d_rest, in_local, in_w, tile)
    d_normed = d_parts[order].transpose(1, 0, 2).reshape(rows, width) + mm(d_dt_low, dt_w)
    d_hidden, d_norm_g = front_back(d_normed)
    input_grad = (d_hidden + cot).astype(bf16).reshape(hidden.shape)

    def summed(terms, axis):
        t = lax.psum_scatter(terms.astype(bf16), "seq", scatter_dimension=0, tiled=True)
        t = lax.psum_scatter(t, "wshard", scatter_dimension=axis, tiled=True)
        return lax.all_gather(t, "seq", axis=0, tiled=True).astype(f32)

    smalls = [
        d_norm_g.reshape(shards, -1),
        d_conv_w.reshape(taps, shards, -1).transpose(1, 0, 2).reshape(shards, -1),
        d_conv_b.reshape(shards, -1),
        d_dt_bias.reshape(shards, -1),
        d_a_log.reshape(shards, -1),
        d_skip.reshape(shards, -1),
        d_gated.reshape(shards, -1),
    ]
    smalls = jnp.concatenate(smalls, axis=1)
    if fast:
        smalls = jnp.pad(smalls, ((0, 0), (0, -smalls.shape[1] % 1024))).reshape(shards, -1, LANES)
        by_core, out_sum, sums = weight_sums(d_gate_low, d_rest, normed_low, g, normed_out_low, smalls, 2)
        by_core = by_core.reshape(2, -1, normed_low.shape[1] // shards)
        split = inner // 2
        rest = by_core[:, split:].reshape(-1, by_core.shape[2])[: total_cols - inner]
        in_grad = jnp.concatenate([by_core[:, :split].reshape(inner, -1), rest]).astype(f32).T
        out_w_grad = out_sum.T.astype(f32)
        sums = sums.reshape(-1)
    else:
        d_proj = jnp.concatenate([d_gate_low, d_rest, d_dt_low], axis=1)
        in_grad = summed(mm(d_proj, normed_low, TN), 1).T
        out_terms = mm(normed_out_low, g, TN)
        blocks = out_terms.reshape(shards, count, -1, width).transpose(1, 0, 2, 3)
        out_w_grad = summed(blocks.reshape(inner, width), 0)
        sums = lax.psum(smalls, ("seq", "wshard"))
        sums = lax.dynamic_index_in_dim(sums, shard, 0, keepdims=False)
    found, at = [], 0
    for size in sizes:
        found.append(sums[at : at + size])
        at += size
    return (
        output,
        input_grad,
        found[0],
        in_grad,
        found[1].reshape(taps, -1).T,
        found[2],
        found[3],
        found[4],
        found[5],
        found[6],
        out_w_grad,
    )


def solution(mesh):
    return jax.shard_map(
        local,
        mesh=mesh,
        in_specs=(
            P(None, "wshard", "seq", None),
            P(None, "wshard"),
            P(None, "wshard", "seq", None),
            P("wshard"),
            P("wshard", None),
            P("wshard", None),
            P("wshard"),
            P("wshard"),
            P("wshard"),
            P("wshard"),
            P("wshard"),
            P("wshard", None),
        ),
        out_specs=(
            P(None, "wshard", "seq", None),
            P(None, "wshard", "seq", None),
            P("wshard"),
            P("wshard", None),
            P("wshard", None),
            P("wshard"),
            P("wshard"),
            P("wshard"),
            P("wshard"),
            P("wshard"),
            P("wshard", None),
        ),
        check_vma=False,
    )
```

```python
from functools import partial

import jax
import jax.numpy as jnp
from jax import lax
from jax.experimental import pallas as pl
from jax.experimental.pallas import tpu as pltpu
from jax.sharding import PartitionSpec as P

epsilon = 1e-05
highest = lax.Precision.HIGHEST
f32 = jnp.float32
bf16 = jnp.bfloat16
GROUP = 8
VMEM = 48 * 1024 * 1024
VMEM_MOST = 60 * 1024 * 1024

NN = (((1,), (0,)), ((), ()))
NT = (((1,), (1,)), ((), ()))
TN = (((0,), (0,)), ((), ()))


def mm(a, b, dims=NN):
    return lax.dot_general(a, b, dims, preferred_element_type=f32)


def params():
    return pltpu.CompilerParams(
        dimension_semantics=("arbitrary", "arbitrary"), vmem_limit_bytes=VMEM
    )


def widen(cols, head_size):
    t, heads = cols.shape
    lane = lax.broadcasted_iota(jnp.int32, (t, 2 * head_size), 1)
    parts = []
    for k in range(0, heads, 2):
        parts.append(jnp.where(lane < head_size, cols[:, k : k + 1], cols[:, k + 1 : k + 2]))
    return jnp.concatenate(parts, axis=1)


def state_kernel(hs, x_ref, w_ref, bt_ref, o_ref):
    weighted = (x_ref[0].astype(f32) * widen(w_ref[0, 0], hs)).astype(bf16)
    o_ref[0] = mm(bt_ref[0], weighted)


def block_states(x, weights, bt, hs):
    micro, t, cols = x.shape
    n = bt.shape[1]
    gc = GROUP * hs
    return pl.pallas_call(
        partial(state_kernel, hs),
        grid=(micro, cols // gc),
        in_specs=[
            pl.BlockSpec((1, t, gc), lambda m, g: (m, 0, g)),
            pl.BlockSpec((1, 1, t, GROUP), lambda m, g: (m, g, 0, 0)),
            pl.BlockSpec((1, n, t), lambda m, g: (m, 0, 0)),
        ],
        out_specs=pl.BlockSpec((1, n, gc), lambda m, g: (m, 0, g)),
        out_shape=jax.ShapeDtypeStruct((micro, n, cols), f32),
        compiler_params=params(),
        name="block_states",
    )(x, weights, bt)


def local_kernel(hs, x_ref, dt_ref, cum_ref, row_ref, b_ref, c_ref, o_ref, scores):
    t = x_ref.shape[1]
    half = t // 2

    @pl.when(pl.program_id(1) == 0)
    def _():
        s = mm(c_ref[0], b_ref[0], NT)
        i = lax.broadcasted_iota(jnp.int32, (t, t), 0)
        j = lax.broadcasted_iota(jnp.int32, (t, t), 1)
        scores[...] = jnp.where(i >= j, s, 0.0)

    cum, dt, rows = cum_ref[0, 0], dt_ref[0, 0], row_ref[0, 0]
    lane = lax.broadcasted_iota(jnp.int32, (half, 2 * hs), 1)
    weighted = (x_ref[0].astype(f32) * widen(dt, hs)).astype(bf16)
    for k in range(0, GROUP, 2):
        at = slice(k * hs, (k + 2) * hs)
        pair = weighted[:, at]
        top, low = [], []
        for h in (k, k + 1):
            col, row = cum[:, h : h + 1], rows[h : h + 1, :]
            m1 = jnp.exp(jnp.minimum(col[:half] - row[:, :half], 0.0)) * scores[:half, :half]
            m2 = jnp.exp(jnp.minimum(col[half:] - row, 0.0)) * scores[half:, :]
            top.append(mm(m1.astype(bf16), pair[:half]))
            low.append(mm(m2.astype(bf16), pair))
        o_ref[0, :half, at] = jnp.where(lane < hs, top[0], top[1])
        o_ref[0, half:, at] = jnp.where(lane < hs, low[0], low[1])


def local_scan(x, dt, cum, rows, b, c, hs):
    micro, t, cols = x.shape
    n = b.shape[2]
    gc = GROUP * hs
    return pl.pallas_call(
        partial(local_kernel, hs),
        grid=(micro, cols // gc),
        in_specs=[
            pl.BlockSpec((1, t, gc), lambda m, g: (m, 0, g)),
            pl.BlockSpec((1, 1, t, GROUP), lambda m, g: (m, g, 0, 0)),
            pl.BlockSpec((1, 1, t, GROUP), lambda m, g: (m, g, 0, 0)),
            pl.BlockSpec((1, 1, GROUP, t), lambda m, g: (m, g, 0, 0)),
            pl.BlockSpec((1, t, n), lambda m, g: (m, 0, 0)),
            pl.BlockSpec((1, t, n), lambda m, g: (m, 0, 0)),
        ],
        out_specs=pl.BlockSpec((1, t, gc), lambda m, g: (m, 0, g)),
        out_shape=jax.ShapeDtypeStruct((micro, t, cols), f32),
        scratch_shapes=[pltpu.VMEM((t, t), f32)],
        compiler_params=params(),
        name="local_scan",
    )(x, dt, cum, rows, b, c)


def carry_kernel(hs, x_ref, y_ref, cum_ref, c_ref, s_ref, skip_ref, scan_ref, low_ref):
    carried = mm(c_ref[0], s_ref[0].astype(bf16)) * widen(jnp.exp(cum_ref[0, 0]), hs)
    scan = y_ref[0] + carried
    scan_ref[0] = scan
    low_ref[0] = (scan + skip_ref[...] * x_ref[0].astype(f32)).astype(bf16)


def add_carry(x, y, cum, c, s_in, skip_wide, hs):
    micro, t, cols = x.shape
    n = c.shape[2]
    gc = GROUP * hs
    wide = pl.BlockSpec((1, t, gc), lambda m, g: (m, 0, g))
    return pl.pallas_call(
        partial(carry_kernel, hs),
        grid=(micro, cols // gc),
        in_specs=[
            wide,
            wide,
            pl.BlockSpec((1, 1, t, GROUP), lambda m, g: (m, g, 0, 0)),
            pl.BlockSpec((1, t, n), lambda m, g: (m, 0, 0)),
            pl.BlockSpec((1, n, gc), lambda m, g: (m, 0, g)),
            pl.BlockSpec((1, gc), lambda m, g: (0, g)),
        ],
        out_specs=[wide, wide],
        out_shape=[
            jax.ShapeDtypeStruct((micro, t, cols), f32),
            jax.ShapeDtypeStruct((micro, t, cols), bf16),
        ],
        compiler_params=params(),
        name="add_carry",
    )(x, y, cum, c, s_in, skip_wide)


def local_back_kernel(
    hs, x_ref, dy_ref, dt_ref, cum_ref, row_ref, b_ref, c_ref, dx_ref, db_ref, dc_ref, scores, total
):
    t = x_ref.shape[1]
    half = t // 2

    @pl.when(pl.program_id(1) == 0)
    def _():
        s = mm(b_ref[0], c_ref[0], NT)
        j = lax.broadcasted_iota(jnp.int32, (t, t), 0)
        i = lax.broadcasted_iota(jnp.int32, (t, t), 1)
        scores[...] = jnp.where(i >= j, s, 0.0)
        total[...] = jnp.zeros_like(total)

    cum, dt, rows = cum_ref[0, 0], dt_ref[0, 0], row_ref[0, 0]
    lane = lax.broadcasted_iota(jnp.int32, (t, 2 * hs), 1)
    lane_half = lax.broadcasted_iota(jnp.int32, (half, 2 * hs), 1)
    weighted = (x_ref[0].astype(f32) * widen(dt, hs)).astype(bf16)
    for k in range(0, GROUP, 2):
        at = slice(k * hs, (k + 2) * hs)
        pair = weighted[:, at]
        dy = dy_ref[0, :, at]
        top, low = [], []
        for h in (k, k + 1):
            col, row = cum[:, h : h + 1], rows[h : h + 1, :]
            mine = jnp.where(lane < hs, pair, 0) if h == k else jnp.where(lane < hs, 0, pair)
            l1 = jnp.exp(jnp.minimum(row - col[:half], 0.0))
            l2 = jnp.exp(jnp.minimum(row[:, half:] - col[half:], 0.0))
            total[:half, :] += l1 * mm(mine[:half], dy, NT)
            total[half:, half:] += l2 * mm(mine[half:], dy[half:], NT)
            top.append(mm((l1 * scores[:half, :]).astype(bf16), dy))
            low.append(mm((l2 * scores[half:, half:]).astype(bf16), dy[half:]))
        dx_ref[0, :half, at] = jnp.where(lane_half < hs, top[0], top[1])
        dx_ref[0, half:, at] = jnp.where(lane_half < hs, low[0], low[1])

    @pl.when(pl.program_id(1) == pl.num_programs(1) - 1)
    def _():
        j = lax.broadcasted_iota(jnp.int32, (t, t), 0)
        i = lax.broadcasted_iota(jnp.int32, (t, t), 1)
        d = jnp.where(i >= j, total[...], 0.0)
        db_ref[0] = mm(d.astype(bf16), c_ref[0])
        dc_ref[0] = mm(d.T.astype(bf16), b_ref[0])


def local_back(x, dy, dt, cum, rows, b, c, hs):
    micro, t, cols = x.shape
    n = b.shape[2]
    gc = GROUP * hs
    wide = pl.BlockSpec((1, t, gc), lambda m, g: (m, 0, g))
    small = pl.BlockSpec((1, 1, t, GROUP), lambda m, g: (m, g, 0, 0))
    state = pl.BlockSpec((1, t, n), lambda m, g: (m, 0, 0))
    return pl.pallas_call(
        partial(local_back_kernel, hs),
        grid=(micro, cols // gc),
        in_specs=[
            wide,
            wide,
            small,
            small,
            pl.BlockSpec((1, 1, GROUP, t), lambda m, g: (m, g, 0, 0)),
            state,
            state,
        ],
        out_specs=[wide, state, state],
        out_shape=[
            jax.ShapeDtypeStruct((micro, t, cols), f32),
            jax.ShapeDtypeStruct((micro, t, n), f32),
            jax.ShapeDtypeStruct((micro, t, n), f32),
        ],
        scratch_shapes=[pltpu.VMEM((t, t), f32), pltpu.VMEM((t, t), f32)],
        compiler_params=params(),
        name="local_back",
    )(x, dy, dt, cum, rows, b, c)


def head_sums(values, ones):
    high = values.astype(bf16)
    rest = (values - high.astype(f32)).astype(bf16)
    return mm(high, ones) + mm(rest, ones)


def carry_back_kernel(
    hs,
    x_ref,
    dy_ref,
    dxl_ref,
    y_ref,
    dt_ref,
    cum_ref,
    b_ref,
    si_ref,
    ds_ref,
    dbl_ref,
    dcl_ref,
    skip_ref,
    dx_ref,
    ddt_ref,
    dcum_ref,
    db_ref,
    dc_ref,
    last_ref,
    dskip_ref,
):
    t = x_ref.shape[1]
    gc = x_ref.shape[2]

    @pl.when(pl.program_id(1) == 0)
    def _():
        db_ref[0] = dbl_ref[0]
        dc_ref[0] = dcl_ref[0]

    cum, dt = cum_ref[0, 0], dt_ref[0, 0]
    x, dy = x_ref[0].astype(f32), dy_ref[0].astype(f32)
    dt_wide = widen(dt, hs)
    weighted = (x * dt_wide).astype(bf16).astype(f32)
    decay = widen(jnp.exp(cum), hs)
    to_end = widen(jnp.exp(cum[t - 1 :, :] - cum), hs)
    s_in, ds = si_ref[0].astype(f32), ds_ref[0]
    s_low, ds_low = s_in.astype(bf16), ds.astype(bf16)
    through = to_end * mm(b_ref[0], ds_low)
    d_weighted = dxl_ref[0] + through
    dx_ref[0] = (dt_wide * d_weighted + skip_ref[...] * dy).astype(bf16)
    db_ref[0] += mm((weighted * to_end).astype(bf16), ds_low, NT)
    dc_ref[0] += mm((dy * decay).astype(bf16), s_low, NT)
    r = lax.broadcasted_iota(jnp.int32, (gc, 128), 0)
    c = lax.broadcasted_iota(jnp.int32, (gc, 128), 1)
    ones = jnp.where(r // hs == c, 1.0, 0.0).astype(bf16)
    ddt_ref[0, 0] = head_sums(x * d_weighted, ones)[:, :GROUP]
    dcum_ref[0, 0] = head_sums(dy * y_ref[0] - weighted * d_weighted, ones)[:, :GROUP]
    last_decay = decay[t - 1 :, :]
    last_ref[0] = jnp.sum(weighted * through, axis=0, keepdims=True) + last_decay * jnp.sum(
        s_low.astype(f32) * ds, axis=0, keepdims=True
    )
    dskip_ref[0] = jnp.sum(x * dy, axis=0, keepdims=True)


def carry_back(x, dy, dxl, y, dt, cum, b, s_in, ds, dbl, dcl, skip_wide, hs):
    micro, t, cols = x.shape
    n = b.shape[2]
    gc = GROUP * hs
    groups = cols // gc
    wide = pl.BlockSpec((1, t, gc), lambda m, g: (m, 0, g))
    small = pl.BlockSpec((1, 1, t, GROUP), lambda m, g: (m, g, 0, 0))
    state = pl.BlockSpec((1, t, n), lambda m, g: (m, 0, 0))
    st = pl.BlockSpec((1, n, gc), lambda m, g: (m, 0, g))
    line = pl.BlockSpec((1, 1, gc), lambda m, g: (m, 0, g))
    return pl.pallas_call(
        partial(carry_back_kernel, hs),
        grid=(micro, groups),
        in_specs=[
            wide,
            wide,
            wide,
            wide,
            small,
            small,
            state,
            st,
            st,
            state,
            state,
            pl.BlockSpec((1, gc), lambda m, g: (0, g)),
        ],
        out_specs=[wide, small, small, state, state, line, line],
        out_shape=[
            jax.ShapeDtypeStruct((micro, t, cols), bf16),
            jax.ShapeDtypeStruct((micro, groups, t, GROUP), f32),
            jax.ShapeDtypeStruct((micro, groups, t, GROUP), f32),
            jax.ShapeDtypeStruct((micro, t, n), f32),
            jax.ShapeDtypeStruct((micro, t, n), f32),
            jax.ShapeDtypeStruct((micro, 1, cols), f32),
            jax.ShapeDtypeStruct((micro, 1, cols), f32),
        ],
        compiler_params=params(),
        name="carry_back",
    )(x, dy, dxl, y, dt, cum, b, s_in, ds, dbl, dcl, skip_wide)


def from_behind(x, axis, by):
    count = lax.axis_size(axis)
    pairs = [(i, i + by) for i in range(count) if 0 <= i + by < count]
    return lax.ppermute(x, axis, pairs)


def swap(x, by):
    count = lax.axis_size("seq")
    return lax.ppermute(x, "seq", [(i, i ^ by) for i in range(count)])


def running_states(terms, decays, hs, forward):
    count = lax.axis_size("seq")
    rank = lax.axis_index("seq")
    index = jnp.arange(count)

    def product(mask):
        d = jnp.prod(jnp.where(mask[:, None, None], decays, 1.0), axis=0)
        return jnp.repeat(d, hs, axis=1)[:, None, :]

    total, before = terms, jnp.zeros_like(terms)
    size = 1
    while size < count:
        other = swap(total.astype(bf16), size).astype(f32)
        mine = index // size == rank // size
        theirs = index // size == (rank // size) ^ 1
        later = (rank // size) % 2 == (1 if forward else 0)
        passed = mine & ((index < rank) if forward else (index > rank))
        before = before + jnp.where(later, product(passed), 0.0) * other
        if 2 * size < count:
            total = total * jnp.where(later, 1.0, product(theirs)) + other * jnp.where(
                later, product(mine), 1.0
            )
        size *= 2
    return before


MESH = pl.DeviceIdType.MESH


def around():
    s, z = lax.axis_index("seq"), lax.axis_index("wshard")
    c, x, y = s % 2, (s // 2) % 2, s // 4
    near = {
        "c": (s + 1 - 2 * c, z),
        "x": (s + 2 - 4 * x, z),
        "y": (s + 4 - 8 * y, z),
        "z1": (s, z + 1 - 2 * (z % 2)),
        "z2": (s, z + 2 - 4 * (z // 2)),
        "z3": (s, 3 - z),
    }
    return s, z, c, x, y, near


def greet(near):
    barrier = pltpu.get_barrier_semaphore()
    for where in near.values():
        pl.semaphore_signal(barrier, inc=1, device_id=where, device_id_type=MESH)
    pl.semaphore_wait(barrier, len(near))


CHUNK_DMAS = 10
AHEAD = 2


def split_rows(piece, parts):
    tiles = piece // 16
    return [16 * (tiles * (i + 1) // parts - tiles * i // parts) for i in range(parts)]


class Gather:
    def __init__(self, place, items, send, recv):
        s, z, c, x, y, near = place
        sx, sy, sd = s + 2 - 4 * x, s + 4 - 8 * y, s + 6 - 4 * x - 8 * y
        self.plans = []
        for source, base, target, count, parts in items:
            off = 0
            for i, size in enumerate(split_rows(count // 8, parts)):
                q = len(self.plans)

                def rows(who, first=0, off=off, size=size, piece=count // 8):
                    return pl.ds(pl.multiple_of(first + who * piece + off, 16), size)

                def move(src, dst, kind, to, q=q):
                    return pltpu.make_async_remote_copy(
                        src_ref=src,
                        dst_ref=dst,
                        send_sem=send.at[q, kind],
                        recv_sem=recv.at[q, kind],
                        device_id=near[to],
                        device_id_type=MESH,
                    )

                def along(who, kind, to, move=move, rows=rows, target=target):
                    block = target.at[:, rows(who)]
                    return move(block, block, kind, to)

                plan = {}
                for k in (1, 2, 3):
                    there = target.at[k - 1, rows(s)]
                    plan["z%d" % k] = move(source.at[rows(s, base)], there, k - 1, "z%d" % k)
                plan["x"] = along(s, 3, "x")
                plan["y"] = along(s, 4, "y")
                first = "xy"[i % 2]
                plan["d"] = along(sx, 5, "y") if first == "x" else along(sy, 5, "x")
                plan["c0"] = along(s, 6, "c")
                plan["cx"] = along(sx, 7, "c")
                plan["cy"] = along(sy, 8, "c")
                plan["cd"] = along(sd, 9, "c")
                plan["order"] = first, "yx"[i % 2]
                self.plans.append(plan)
                off += size

    def fetch(self, i):
        for k in (1, 2, 3):
            self.plans[i]["z%d" % k].start()

    def begin(self, i):
        plan = self.plans[i]
        for k in (1, 2, 3):
            plan["z%d" % k].wait_recv()
        for name in ("x", "y", "c0"):
            plan[name].start()

    def middle(self, i):
        plan = self.plans[i]
        one, two = plan["order"]
        plan[one].wait_recv()
        plan["d"].start()
        plan["c" + one].start()
        plan[two].wait_recv()
        plan["c" + two].start()

    def finish(self, i):
        self.plans[i]["d"].wait_recv()
        self.plans[i]["cd"].start()

    def run(self):
        n = len(self.plans)
        for i in range(min(AHEAD, n)):
            self.fetch(i)
        for i in range(n + 2):
            if i < n:
                self.begin(i)
                if i + AHEAD < n:
                    self.fetch(i + AHEAD)
            if 0 <= i - 1 < n:
                self.middle(i - 1)
            if 0 <= i - 2 < n:
                self.finish(i - 2)

    def close(self):
        for plan in self.plans:
            for name in ("c0", "cx", "cy", "cd"):
                plan[name].wait_recv()
            for name in ("z1", "z2", "z3", "x", "y", "d", "c0", "cx", "cy", "cd"):
                plan[name].wait_send()


def gather_kernel(inner, channels, parts, w_ref, conv_ref, gate_ref, send, recv):
    place = around()
    greet(place[-1])
    items = [(w_ref, inner, conv_ref, channels, parts), (w_ref, 0, gate_ref, inner, parts)]
    work = Gather(place, items, send, recv)
    work.run()
    work.close()


def gather_input_weight(w_t, inner, channels, parts=6):
    width = w_t.shape[1]
    hbm = pl.BlockSpec(memory_space=pl.ANY)
    return pl.pallas_call(
        partial(gather_kernel, inner, channels, parts),
        in_specs=[hbm],
        out_specs=[hbm] * 2,
        out_shape=[
            jax.ShapeDtypeStruct((3, channels, width), bf16),
            jax.ShapeDtypeStruct((3, inner, width), bf16),
        ],
        scratch_shapes=[
            pltpu.SemaphoreType.DMA((2 * parts, CHUNK_DMAS)),
            pltpu.SemaphoreType.DMA((2 * parts, CHUNK_DMAS)),
        ],
        compiler_params=pltpu.CompilerParams(collective_id=1, has_side_effects=True),
        cost_estimate=pl.CostEstimate(flops=0, bytes_accessed=200_000_000, transcendentals=0),
        name="gather_input_weight",
    )(w_t)


class Products:
    IN = 4
    SCRATCH = 22

    @staticmethod
    def sizes(a_list, b):
        rows = b.shape[0]
        wide = sum(a.shape[1] for a in a_list) // 2
        return rows, wide, b.shape[1], wide // 128

    @staticmethod
    def marks(chunks):
        return sorted({0, chunks * 2 // 5, chunks * 7 // 10, chunks * 9 // 10, chunks})

    @staticmethod
    def out_shape(a_list, b):
        _, _, width, chunks = Products.sizes(a_list, b)
        return jax.ShapeDtypeStruct((2, chunks, 2, 2, 2, 16, width // 4), bf16)

    @staticmethod
    def scratch(a_list, b):
        rows, wide, width, chunks = Products.sizes(a_list, b)
        dma = pltpu.SemaphoreType.DMA
        n = Products.IN
        marks = Products.marks(chunks)
        return [
            pltpu.VMEM((2, rows, wide), bf16),
            pltpu.VMEM((2, rows, width), bf16),
            pltpu.VMEM((2, 128, width), f32),
            pltpu.VMEM((2, 32, width), bf16),
            pltpu.VMEM((2, 32, width), bf16),
            pltpu.VMEM((2, 16, width), bf16),
            pltpu.VMEM((2, 16, width), bf16),
            pltpu.VMEM((2, 2, 16, width), bf16),
            pltpu.VMEM((2, 16, width), f32),
            pltpu.VMEM((2, 16, width), f32),
            pltpu.VMEM((2, 2, 16, width), f32),
            pltpu.VMEM((chunks, 32, width), bf16),
            pltpu.VMEM((chunks, 32, width), bf16),
            pltpu.VMEM((chunks, 16, width), bf16),
            pltpu.VMEM((chunks, 16, width), bf16),
            pltpu.VMEM((chunks, 3, 2, 16, width // 4), bf16),
            dma((n,)),
            dma((n,)),
            dma((n,)),
            dma((7, 2)),
            dma((7, chunks)),
            dma((2, len(marks) - 1, 8)),
        ]

    def __init__(self, place, a_refs, b_ref, out, scratch):
        self.s, self.z, self.c, self.x, self.y, self.near = place
        (
            self.a,
            self.b,
            self.g,
            self.sa1,
            self.sb1,
            self.sa2,
            self.sb2,
            self.s3,
            self.ka2,
            self.kb2,
            self.f3,
            self.ra1,
            self.rb1,
            self.ra2,
            self.rb2,
            self.rz,
            self.in_sem,
            self.s_in,
            self.r_in,
            self.s_step,
            self.r_step,
            self.sems_all,
        ) = scratch
        self.out = out
        self.shard = self.rz.shape[-1]
        self.chunks = self.ra1.shape[0]
        marks = Products.marks(self.chunks)
        self.groups = list(zip(marks[:-1], marks[1:]))
        c = self.c
        self.operands = []
        self.operands.append(
            (
                0,
                pltpu.make_async_copy(b_ref, self.b.at[0], self.in_sem.at[0]),
                self.remote(b_ref, self.b.at[1], self.s_in.at[0], self.r_in.at[0], "c"),
            )
        )
        at = 0
        for i, ref in enumerate(a_refs):
            half = ref.shape[1] // 2
            here = ref.at[:, pl.ds(pl.multiple_of(c * half, 128), half)]
            there = ref.at[:, pl.ds(pl.multiple_of((1 - c) * half, 128), half)]
            to = pl.ds(at, half)
            self.operands.append(
                (
                    at // 128,
                    pltpu.make_async_copy(here, self.a.at[0, :, to], self.in_sem.at[i + 1]),
                    self.remote(there, self.a.at[1, :, to], self.s_in.at[i + 1], self.r_in.at[i + 1], "c"),
                )
            )
            at += half

    def remote(self, src, dst, ss, rs, to):
        return pltpu.make_async_remote_copy(
            src_ref=src,
            dst_ref=dst,
            send_sem=ss,
            recv_sem=rs,
            device_id=self.near[to],
            device_id_type=MESH,
        )

    def load(self):
        for _, here, _ in self.operands:
            here.start()

    def share(self):
        for _, _, there in self.operands:
            there.start()

    def step_copy(self, kind, u):
        slot = u % 2
        ss, rs = self.s_step.at[kind, slot], self.r_step.at[kind, u]
        if kind < 4:
            src, dst, to = (
                (self.sa1, self.ra1, "x"),
                (self.sb1, self.rb1, "y"),
                (self.sa2, self.ra2, "y"),
                (self.sb2, self.rb2, "x"),
            )[kind]
            return self.remote(src.at[slot], dst.at[u], ss, rs, to)
        k = kind - 3
        z = self.z
        other = (z + 1 - 2 * (z % 2), z + 2 - 4 * (z // 2), 3 - z)[k - 1]
        cols = pl.ds(pl.multiple_of(other * self.shard, 128), self.shard)
        return self.remote(self.s3.at[slot, :, :, cols], self.rz.at[u, k - 1], ss, rs, "z%d" % k)

    def all_copy(self, q, kind):
        a, b = self.groups[q]
        ts = pl.ds(a, b - a)
        x, y, c = self.x, self.y, self.c
        px = 1 - x if kind in (3, 5, 7) else x
        py = 1 - y if kind in (4, 6, 7) else y
        if kind in (3, 4):
            block = self.out.at[c, ts, kind - 3, px, py]
        else:
            block = self.out.at[c, ts, :, px, py]
        to = ("x", "y", "c", "y", "x", "c", "c", "c")[kind]
        return self.remote(block, block, self.sems_all.at[0, q, kind], self.sems_all.at[1, q, kind], to)

    def step(self, t):
        x, y, z, c = self.x, self.y, self.z, self.c
        g, ra1, rb1 = self.g, self.ra1, self.rb1
        chunks = self.chunks
        copy = self.step_copy

        def sl(at, size=16):
            return pl.ds(pl.multiple_of(at, 16), size)

        def free(kind, u):
            @pl.when(u >= 2)
            def _():
                copy(kind, u - 2).wait_send()

        @pl.when(t < chunks)
        def _():
            for first, here, there in self.operands:

                @pl.when(t == first)
                def _(here=here, there=there):
                    here.wait()
                    there.wait_recv()

            slot = t % 2
            cols = pl.ds(pl.multiple_of(t * 128, 128), 128)
            g[slot] = mm(self.a[0, :, cols], self.b[0], TN) + mm(self.a[1, :, cols], self.b[1], TN)
            free(0, t)
            free(1, t)
            self.sa1[slot] = g[slot, sl((1 - x) * 32, 32)].astype(bf16)
            copy(0, t).start()
            self.sb1[slot, 0:16] = g[slot, sl(64 + (1 - y) * 16)].astype(bf16)
            self.sb1[slot, 16:32] = g[slot, sl(96 + (1 - y) * 16)].astype(bf16)
            copy(1, t).start()

        @pl.when((t >= 1) & (t - 1 < chunks))
        def _():
            u = t - 1
            slot = u % 2
            copy(0, u).wait_recv()
            free(2, u)
            self.sa2[slot] = (
                g[slot, sl(x * 32 + (1 - y) * 16)] + ra1[u, sl((1 - y) * 16)].astype(f32)
            ).astype(bf16)
            copy(2, u).start()
            self.ka2[slot] = g[slot, sl(x * 32 + y * 16)] + ra1[u, sl(y * 16)].astype(f32)
            copy(1, u).wait_recv()
            free(3, u)
            self.sb2[slot] = (
                g[slot, sl(64 + (1 - x) * 32 + y * 16)] + rb1[u, sl((1 - x) * 16)].astype(f32)
            ).astype(bf16)
            copy(3, u).start()
            self.kb2[slot] = g[slot, sl(64 + x * 32 + y * 16)] + rb1[u, sl(x * 16)].astype(f32)

        @pl.when((t >= 2) & (t - 2 < chunks))
        def _():
            u = t - 2
            slot = u % 2
            copy(2, u).wait_recv()
            copy(3, u).wait_recv()
            for k in (4, 5, 6):
                free(k, u)
            va = self.ka2[slot] + self.ra2[u].astype(f32)
            vb = self.kb2[slot] + self.rb2[u].astype(f32)
            self.f3[slot, 0] = va
            self.f3[slot, 1] = vb
            self.s3[slot, 0] = va.astype(bf16)
            self.s3[slot, 1] = vb.astype(bf16)
            for k in (4, 5, 6):
                copy(k, u).start()

        @pl.when((t >= 3) & (t - 3 < chunks))
        def _():
            u = t - 3
            slot = u % 2
            for k in (4, 5, 6):
                copy(k, u).wait_recv()
            mine = pl.ds(pl.multiple_of(z * self.shard, 128), self.shard)
            for part in (0, 1):
                total = self.f3[slot, part, :, mine]
                for k in range(3):
                    total = total + self.rz[u, k, part].astype(f32)
                self.out[c, u, part, x, y] = total.astype(bf16)

        for q, (_, b) in enumerate(self.groups):

            @pl.when(t == b - 1 + 3)
            def _(q=q):
                for kind in (0, 1, 2):
                    self.all_copy(q, kind).start()

            @pl.when(t == b - 1 + 4)
            def _(q=q):
                self.all_copy(q, 0).wait_recv()
                self.all_copy(q, 3).start()
                self.all_copy(q, 5).start()
                self.all_copy(q, 1).wait_recv()
                self.all_copy(q, 4).start()
                self.all_copy(q, 6).start()

            @pl.when(t == b - 1 + 5)
            def _(q=q):
                self.all_copy(q, 3).wait_recv()
                self.all_copy(q, 4).wait_recv()
                self.all_copy(q, 7).start()

    def steps(self):
        return self.chunks + 5

    def close(self):
        for q in range(len(self.groups)):
            for kind in (2, 5, 6, 7):
                self.all_copy(q, kind).wait_recv()
            for kind in range(8):
                self.all_copy(q, kind).wait_send()
        for u in (self.chunks - 2, self.chunks - 1):
            for kind in range(7):
                self.step_copy(kind, u).wait_send()
        for _, _, there in self.operands:
            there.wait_send()


class Smalls:
    SCRATCH = 5

    @staticmethod
    def scratch(v):
        dma = pltpu.SemaphoreType.DMA
        return [
            pltpu.VMEM((3,) + v.shape, f32),
            pltpu.VMEM((3,) + v.shape, f32),
            pltpu.VMEM((3,) + v.shape[1:], f32),
            dma((6,)),
            dma((6,)),
        ]

    def __init__(self, place, v_ref, out, scratch):
        self.s, self.z, self.c, self.x, self.y, self.near = place
        self.v, self.out = v_ref, out
        self.total, self.got, self.got_z, self.send, self.recv = scratch

    def copy(self, kind):
        if kind < 3:
            src = self.v if kind == 0 else self.total.at[kind - 1]
            dst, to = self.got.at[kind], "cxy"[kind]
        else:
            z = self.z
            k = kind - 2
            other = (z + 1 - 2 * (z % 2), z + 2 - 4 * (z // 2), 3 - z)[k - 1]
            src, dst, to = self.total.at[2, other], self.got_z.at[k - 1], "z%d" % k
        return pltpu.make_async_remote_copy(
            src_ref=src,
            dst_ref=dst,
            send_sem=self.send.at[kind],
            recv_sem=self.recv.at[kind],
            device_id=self.near[to],
            device_id_type=MESH,
        )

    def start(self):
        self.copy(0).start()

    def advance(self, kind):
        self.copy(kind).wait_recv()
        mine = self.v[...] if kind == 0 else self.total[kind - 1]
        self.total[kind] = mine + self.got[kind]
        for k in (kind + 1,) if kind < 2 else (3, 4, 5):
            self.copy(k).start()

    def close(self):
        total = self.total[2, self.z]
        for k in (3, 4, 5):
            self.copy(k).wait_recv()
            total = total + self.got_z[k - 3]
        self.out[...] = total
        for k in range(6):
            self.copy(k).wait_send()


def sums_kernel(
    gate_ref,
    conv_ref,
    nm_ref,
    og_ref,
    no_ref,
    v_ref,
    in_out,
    out_out,
    v_out,
    *scratch,
):
    place = around()
    cut = Products.SCRATCH
    inp = Products(place, [gate_ref, conv_ref], nm_ref, in_out, scratch[:cut])
    outp = Products(place, [og_ref], no_ref, out_out, scratch[cut : 2 * cut])
    small = Smalls(place, v_ref, v_out, scratch[2 * cut :])
    outp.load()
    inp.load()
    greet(place[-1])
    outp.share()
    small.start()
    inp.share()

    def first(t, carry):
        outp.step(t)
        return carry

    lax.fori_loop(0, outp.chunks, first, 0)

    def second(t, carry):
        inp.step(t)

        @pl.when(t < outp.steps() - outp.chunks)
        def _():
            outp.step(t + outp.chunks)

        for kind in range(3):

            @pl.when(t == 2 * kind + 1)
            def _(kind=kind):
                small.advance(kind)

        return carry

    lax.fori_loop(0, inp.steps(), second, 0)
    small.close()
    outp.close()
    inp.close()


def weight_sums(d_gate, d_rest, nm, og, no, v, collective_id):
    vmem = pl.BlockSpec(memory_space=pltpu.VMEM)
    hbm = pl.BlockSpec(memory_space=pl.ANY)
    a_in, a_out, total = pl.pallas_call(
        sums_kernel,
        in_specs=[hbm] * 5 + [vmem],
        out_specs=[vmem] * 3,
        out_shape=[
            Products.out_shape([d_gate, d_rest], nm),
            Products.out_shape([og], no),
            jax.ShapeDtypeStruct(v.shape[1:], f32),
        ],
        scratch_shapes=Products.scratch([d_gate, d_rest], nm)
        + Products.scratch([og], no)
        + Smalls.scratch(v),
        compiler_params=pltpu.CompilerParams(
            collective_id=collective_id, has_side_effects=True, vmem_limit_bytes=VMEM_MOST
        ),
        cost_estimate=pl.CostEstimate(
            flops=6 * nm.shape[0] * nm.shape[1] * 9000, bytes_accessed=400_000_000, transcendentals=0
        ),
        name="weight_sums",
    )(d_gate, d_rest, nm, og, no, v)
    return a_in, a_out.reshape(og.shape[1], -1), total


LANES = 128
HALO = 16


def silu_parts(v):
    s = 1.0 / (1.0 + jnp.exp(-v))
    return v * s, s


def softplus(v):
    return jnp.maximum(v, 0.0) + jnp.log1p(jnp.exp(-jnp.abs(v)))


def lower_ones(t):
    i = lax.broadcasted_iota(jnp.int32, (t, t), 0)
    j = lax.broadcasted_iota(jnp.int32, (t, t), 1)
    return jnp.where(i >= j, 1.0, 0.0)


def exact(a, b, dims=NN):
    return lax.dot_general(a, b, dims, precision=highest, preferred_element_type=f32)


def head_columns(values, g):
    return pltpu.roll(values, (LANES - GROUP * g) % LANES, 1)[:, :GROUP]


class Exchange:
    def __init__(self, forward, own, own_low, got, t_low, t_got, u_low, u_got, p_low, p_got, before, send, recv):
        self.s, self.z, self.c, self.x, self.y, self.near = around()
        later = (lambda v: v) if forward else (lambda v: 1 - v)
        self.second = (later(self.c) == 1, later(self.x) == 1, later(self.y) == 1)
        self.own, self.own_low, self.got = own, own_low, got
        self.t_low, self.t_got, self.u_low, self.u_got = t_low, t_got, u_low, u_got
        self.p_low, self.p_got, self.before = p_low, p_got, before
        self.send, self.recv = send, recv
        self.n = own.shape[1]
        self.half = own.shape[2] // 2
        self.mine = pl.ds(pl.multiple_of(self.c * self.half, LANES), self.half)
        self.other = pl.ds(pl.multiple_of((1 - self.c) * self.half, LANES), self.half)

    def copy(self, kind, m):
        src, dst, to = (
            (self.own_low, self.got, "c"),
            (self.t_low, self.t_got, "x"),
            (self.u_low, self.u_got, "y"),
            (self.p_low, self.p_got, "c"),
        )[kind]
        return pltpu.make_async_remote_copy(
            src_ref=src.at[m],
            dst_ref=dst.at[m],
            send_sem=self.send.at[kind, m],
            recv_sem=self.recv.at[kind, m],
            device_id=self.near[to],
            device_id_type=MESH,
        )

    def put_decay(self, ref, m, lanes, decay):
        high = decay.astype(bf16).astype(f32)
        row = lax.broadcasted_iota(jnp.int32, (16, decay.shape[1]), 0)
        both = jnp.where(row == 0, high, jnp.where(row == 1, decay - high, 0.0))
        ref[m, pl.ds(self.n, 16), lanes] = both.astype(bf16)

    def decay_of(self, ref, m, lanes):
        rows = ref[m, pl.ds(self.n, 16), lanes].astype(f32)
        return rows[0:1] + rows[1:2]

    def put_own(self, m, lanes, state, decay):
        self.own[m, :, lanes] = state
        self.own_low[m, pl.ds(0, self.n), lanes] = state.astype(bf16)
        self.put_decay(self.own_low, m, lanes, decay)

    def core(self, m):
        self.copy(0, m).start()

    def along_x(self, m):
        self.copy(0, m).wait_recv()
        second = self.second[0]
        mine = self.own[m, :, self.mine]
        theirs = self.got[m, pl.ds(0, self.n), self.mine].astype(f32)
        d_mine = self.decay_of(self.own_low, m, self.mine)
        d_theirs = self.decay_of(self.got, m, self.mine)
        total = theirs * jnp.where(second, d_mine, 1.0) + mine * jnp.where(second, 1.0, d_theirs)
        self.t_low[m, pl.ds(0, self.n), :] = total.astype(bf16)
        self.put_decay(self.t_low, m, pl.ds(0, self.half), d_mine * d_theirs)
        self.copy(1, m).start()

    def along_y(self, m):
        self.copy(1, m).wait_recv()
        second = self.second[1]
        every = pl.ds(0, self.half)
        mine = self.t_low[m, pl.ds(0, self.n), :].astype(f32)
        theirs = self.t_got[m, pl.ds(0, self.n), :].astype(f32)
        d_mine = self.decay_of(self.t_low, m, every)
        d_theirs = self.decay_of(self.t_got, m, every)
        total = theirs * jnp.where(second, d_mine, 1.0) + mine * jnp.where(second, 1.0, d_theirs)
        self.u_low[m] = total.astype(bf16)
        self.copy(2, m).start()

    def back_to_core(self, m):
        self.copy(2, m).wait_recv()
        every = pl.ds(0, self.half)
        x_second = jnp.where(self.second[1], 1.0, 0.0)
        y_second = jnp.where(self.second[2], 1.0, 0.0)
        theirs = self.t_got[m, pl.ds(0, self.n), :].astype(f32)
        d_theirs = self.decay_of(self.t_got, m, every)
        over = y_second * jnp.where(self.second[1], d_theirs, 1.0)
        before = x_second * theirs + over * self.u_got[m].astype(f32)
        self.before[m] = before
        self.p_low[m] = before.astype(bf16)
        self.copy(3, m).start()

    def begin_state(self, m, out):
        self.copy(3, m).wait_recv()
        second = jnp.where(self.second[0], 1.0, 0.0)
        for lanes, before in (
            (self.mine, self.before[m]),
            (self.other, self.p_got[m].astype(f32)),
        ):
            d_theirs = self.decay_of(self.got, m, lanes)
            theirs = self.got[m, pl.ds(0, self.n), lanes].astype(f32)
            over = jnp.where(self.second[0], d_theirs, 1.0)
            out[m, :, lanes] = (before * over + second * theirs).astype(bf16)

    def sent(self):
        for m in range(self.own.shape[0]):
            for kind in range(4):
                self.copy(kind, m).wait_send()


def exchange_scratch(micro, n, inner):
    half = inner // 2
    dma = pltpu.SemaphoreType.DMA
    return [
        pltpu.VMEM((micro, n, inner), f32),
        pltpu.VMEM((micro, n + 16, inner), bf16),
        pltpu.VMEM((micro, n + 16, inner), bf16),
        pltpu.VMEM((micro, n + 16, half), bf16),
        pltpu.VMEM((micro, n + 16, half), bf16),
        pltpu.VMEM((micro, n, half), bf16),
        pltpu.VMEM((micro, n, half), bf16),
        pltpu.VMEM((micro, n, half), bf16),
        pltpu.VMEM((micro, n, half), bf16),
        pltpu.VMEM((micro, n, half), f32),
        dma((4, micro)),
        dma((4, micro)),
    ]


EXCHANGE = 12


def steps_of(raw, shift, rate):
    t = raw.shape[0]
    dt = softplus(raw + shift)
    cum = exact(lower_ones(t), dt * rate)
    return dt, cum


def conv_rows(buf, cw, cb):
    taps = cw.shape[0]
    t = buf.shape[0] - HALO
    total = cb + buf[HALO - taps + 1 : HALO - taps + 1 + t, :] * cw[0:1]
    for k in range(1, taps):
        at = HALO - taps + 1 + k
        total = total + buf[at : at + t, :] * cw[k : k + 1]
    return total


def scan_forward_kernel(
    hs,
    conv_ref,
    raw_ref,
    cw_ref,
    cb_ref,
    shift_ref,
    rate_ref,
    skip_ref,
    ow_ref,
    x_ref,
    bc_ref,
    y_ref,
    low_ref,
    halo,
    begin_ref,
    others_ref,
    *scratch,
):
    buf, wide_buf, scores, dts, cums, rows_t, h_send, h_recv, o_send, o_recv = scratch[EXCHANGE:]
    ex = Exchange(True, *scratch[:EXCHANGE])
    s, z = ex.s, ex.z
    micro, t, channels = conv_ref.shape
    inner = x_ref.shape[2]
    n = begin_ref.shape[1]
    gc = GROUP * hs
    groups = inner // gc
    half_t = t // 2
    place = around()
    near = dict(place[-1])
    near["next"] = ((s + 1) % 8, z)
    near["last"] = ((s + 7) % 8, z)
    greet(near)
    weight = Gather(place, [(ow_ref, 0, others_ref, ow_ref.shape[0], 2)], o_send, o_recv)

    tail = [
        pltpu.make_async_remote_copy(
            src_ref=conv_ref.at[m, pl.ds(t - HALO, HALO)],
            dst_ref=halo.at[m],
            send_sem=h_send.at[m],
            recv_sem=h_recv.at[m],
            device_id=near["next"],
            device_id_type=MESH,
        )
        for m in range(micro)
    ]
    for copy in tail:
        copy.start()
    weight.fetch(0)
    weight.fetch(1)
    for m in range(micro):
        dt, cum = steps_of(raw_ref[m], shift_ref[...], rate_ref[...])
        dts[m] = dt
        cums[m] = cum
        rows_t[m] = cum.T
    for copy in tail:
        copy.wait_recv()
    has_prior = jnp.where(s > 0, 1.0, 0.0)

    def activate(m, lanes, into):
        into[0:HALO] = halo[m, :, lanes].astype(f32) * has_prior
        into[pl.ds(HALO, t)] = conv_ref[m, :, lanes].astype(f32)
        return silu_parts(conv_rows(into, cw_ref[:, lanes], cb_ref[:, lanes]))[0]

    def own_states(m, a, b):
        def body(g, carry):
            lanes = pl.ds(pl.multiple_of(g * gc, gc), gc)
            x = activate(m, lanes, buf).astype(bf16)
            x_ref[m, :, lanes] = x
            cum = head_columns(cums[m], g)
            to_end = head_columns(dts[m], g) * jnp.exp(cum[t - 1 :] - cum)
            weighted = (x.astype(f32) * widen(to_end, hs)).astype(bf16)
            state = mm(bc_ref[m, :, 0:n], weighted, TN)
            ex.put_own(m, lanes, state, widen(jnp.exp(cum[t - 1 :]), hs))
            return carry

        lax.fori_loop(a, b, body, 0)

    def local_scans(m, a, b):
        lane = lax.broadcasted_iota(jnp.int32, (half_t, 2 * hs), 1)

        def body(g, carry):
            lanes = pl.ds(pl.multiple_of(g * gc, gc), gc)
            cum = head_columns(cums[m], g)
            rows = rows_t[m, pl.ds(pl.multiple_of(g * GROUP, GROUP), GROUP), :]
            dt_wide = widen(head_columns(dts[m], g), hs)
            weighted = (x_ref[m, :, lanes].astype(f32) * dt_wide).astype(bf16)
            for k in range(0, GROUP, 2):
                pair = weighted[:, k * hs : (k + 2) * hs]
                at = pl.ds(pl.multiple_of(g * gc + k * hs, 2 * hs), 2 * hs)
                top, low = [], []
                for h in (k, k + 1):
                    col, row = cum[:, h : h + 1], rows[h : h + 1, :]
                    m1 = jnp.exp(jnp.minimum(col[:half_t] - row[:, :half_t], 0.0))
                    m2 = jnp.exp(jnp.minimum(col[half_t:] - row, 0.0))
                    m1 = (m1 * scores[m, :half_t, :half_t]).astype(bf16)
                    m2 = (m2 * scores[m, half_t:, :]).astype(bf16)
                    top.append(mm(m1, pair[:half_t]))
                    low.append(mm(m2, pair))
                y_ref[m, :half_t, at] = jnp.where(lane < hs, top[0], top[1])
                y_ref[m, half_t:, at] = jnp.where(lane < hs, low[0], low[1])
            return carry

        lax.fori_loop(a, b, body, 0)

    def carried(m):
        def body(g, carry):
            lanes = pl.ds(pl.multiple_of(g * gc, gc), gc)
            decay = widen(jnp.exp(head_columns(cums[m], g)), hs)
            scan = y_ref[m, :, lanes] + decay * mm(bc_ref[m, :, n:], begin_ref[m, :, lanes])
            y_ref[m, :, lanes] = scan
            x = x_ref[m, :, lanes].astype(f32)
            low_ref[m, :, lanes] = (scan + skip_ref[:, lanes] * x).astype(bf16)
            return carry

        lax.fori_loop(0, groups, body, 0)

    for m in range(micro):
        lanes = pl.ds(inner, channels - inner)
        bc = activate(m, lanes, wide_buf).astype(bf16)
        bc_ref[m] = bc
        scores[m] = mm(bc[:, n:], bc[:, :n], NT) * lower_ones(t)
    middle = groups // 2
    own_states(0, 0, groups)
    ex.core(0)
    own_states(1, 0, middle)
    ex.along_x(0)
    own_states(1, middle, groups)
    ex.core(1)
    weight.begin(0)
    local_scans(0, 0, middle)
    ex.along_x(1)
    ex.along_y(0)
    weight.begin(1)
    local_scans(0, middle, groups)
    weight.middle(0)
    local_scans(1, 0, middle)
    ex.along_y(1)
    ex.back_to_core(0)
    weight.middle(1)
    local_scans(1, middle, groups)
    ex.begin_state(0, begin_ref)
    carried(0)
    ex.back_to_core(1)
    weight.finish(0)
    weight.finish(1)
    ex.begin_state(1, begin_ref)
    carried(1)
    weight.close()
    ex.sent()
    for copy in tail:
        copy.wait_send()


def scan_forward(
    conv_low, raw, conv_w, conv_b, shift, rate, skip_wide, out_weight, inner, hs, collective_id
):
    micro, t, channels = conv_low.shape
    n = (channels - inner) // 2
    gc = GROUP * hs
    dma = pltpu.SemaphoreType.DMA
    vmem = pl.BlockSpec(memory_space=pltpu.VMEM)
    hbm = pl.BlockSpec(memory_space=pl.ANY)
    return pl.pallas_call(
        partial(scan_forward_kernel, hs),
        in_specs=[vmem] * 7 + [hbm],
        out_specs=[vmem] * 6 + [hbm],
        out_shape=[
            jax.ShapeDtypeStruct((micro, t, inner), bf16),
            jax.ShapeDtypeStruct((micro, t, 2 * n), bf16),
            jax.ShapeDtypeStruct((micro, t, inner), f32),
            jax.ShapeDtypeStruct((micro, t, inner), bf16),
            jax.ShapeDtypeStruct((micro, HALO, channels), bf16),
            jax.ShapeDtypeStruct((micro, n, inner), bf16),
            jax.ShapeDtypeStruct((3,) + out_weight.shape, bf16),
        ],
        scratch_shapes=exchange_scratch(micro, n, inner)
        + [
            pltpu.VMEM((HALO + t, gc), f32),
            pltpu.VMEM((HALO + t, 2 * n), f32),
            pltpu.VMEM((micro, t, t), f32),
            pltpu.VMEM((micro, t, LANES), f32),
            pltpu.VMEM((micro, t, LANES), f32),
            pltpu.VMEM((micro, LANES, t), f32),
            dma((micro,)),
            dma((micro,)),
            dma((2, CHUNK_DMAS)),
            dma((2, CHUNK_DMAS)),
        ],
        compiler_params=pltpu.CompilerParams(
            collective_id=collective_id, has_side_effects=True, vmem_limit_bytes=VMEM_MOST
        ),
        cost_estimate=pl.CostEstimate(
            flops=4 * micro * t * inner * (t + 3 * n), bytes_accessed=100_000_000, transcendentals=0
        ),
        name="scan_forward",
    )(conv_low, raw, conv_w, conv_b, shift, rate, skip_wide, out_weight)


def scan_backward_kernel(
    hs,
    dy_ref,
    x_ref,
    bc_ref,
    y_ref,
    begin_ref,
    raw_ref,
    conv_ref,
    halo_ref,
    cw_ref,
    cb_ref,
    shift_ref,
    rate_ref,
    skip_ref,
    dconv_ref,
    dcw_ref,
    dcb_ref,
    heads_ref,
    *scratch,
):
    (
        buf,
        wide_buf,
        scores,
        total,
        dts,
        cums,
        rows_t,
        ends,
        dxl,
        dbc,
        ddt_sum,
        dcum_sum,
        head_low,
        next_low,
        h_send,
        h_recv,
    ) = scratch[EXCHANGE:]
    ex = Exchange(False, *scratch[:EXCHANGE])
    s, z = ex.s, ex.z
    micro, t, channels = conv_ref.shape
    inner = x_ref.shape[2]
    n = begin_ref.shape[1]
    gc = GROUP * hs
    groups = inner // gc
    half = t // 2
    taps = cw_ref.shape[0]
    near = {k: ex.near[k] for k in ("c", "x", "y")}
    near["next"] = ((s + 1) % 8, z)
    near["last"] = ((s + 7) % 8, z)
    greet(near)
    first_rows = [
        pltpu.make_async_remote_copy(
            src_ref=head_low.at[m],
            dst_ref=next_low.at[m],
            send_sem=h_send.at[m],
            recv_sem=h_recv.at[m],
            device_id=near["last"],
            device_id_type=MESH,
        )
        for m in range(micro)
    ]
    has_prior = jnp.where(s > 0, 1.0, 0.0)
    has_next = jnp.where(s < 7, 1.0, 0.0)

    def own_states(m, a, b):
        def body(g, carry):
            lanes = pl.ds(pl.multiple_of(g * gc, gc), gc)
            cum = head_columns(cums[m], g)
            weighted = (dy_ref[m, :, lanes].astype(f32) * widen(jnp.exp(cum), hs)).astype(bf16)
            state = mm(bc_ref[m, :, n:], weighted, TN)
            ex.put_own(m, lanes, state, widen(jnp.exp(cum[t - 1 :]), hs))
            return carry

        lax.fori_loop(a, b, body, 0)

    def local_terms(m, a, b):
        lane = lax.broadcasted_iota(jnp.int32, (t, 2 * hs), 1)
        lane_half = lax.broadcasted_iota(jnp.int32, (half, 2 * hs), 1)

        def body(g, carry):
            lanes = pl.ds(pl.multiple_of(g * gc, gc), gc)
            cum = head_columns(cums[m], g)
            rows = rows_t[m, pl.ds(pl.multiple_of(g * GROUP, GROUP), GROUP), :]
            dt_wide = widen(head_columns(dts[m], g), hs)
            weighted = (x_ref[m, :, lanes].astype(f32) * dt_wide).astype(bf16)
            for k in range(0, GROUP, 2):
                pair = weighted[:, k * hs : (k + 2) * hs]
                at = pl.ds(pl.multiple_of(g * gc + k * hs, 2 * hs), 2 * hs)
                dy = dy_ref[m, :, at]
                top, low = [], []
                for h in (k, k + 1):
                    col, row = cum[:, h : h + 1], rows[h : h + 1, :]
                    mine = jnp.where(lane < hs, pair, 0) if h == k else jnp.where(lane < hs, 0, pair)
                    l1 = jnp.exp(jnp.minimum(row - col[:half], 0.0))
                    l2 = jnp.exp(jnp.minimum(row[:, half:] - col[half:], 0.0))
                    total[:half, :] += l1 * mm(mine[:half], dy, NT)
                    total[half:, half:] += l2 * mm(mine[half:], dy[half:], NT)
                    top.append(mm((l1 * scores[m, :half, :]).astype(bf16), dy))
                    low.append(mm((l2 * scores[m, half:, half:]).astype(bf16), dy[half:]))
                dxl[m, :half, at] = jnp.where(lane_half < hs, top[0], top[1])
                dxl[m, half:, at] = jnp.where(lane_half < hs, low[0], low[1])
            return carry

        lax.fori_loop(a, b, body, 0)

    def upper_ones():
        j = lax.broadcasted_iota(jnp.int32, (t, t), 0)
        i = lax.broadcasted_iota(jnp.int32, (t, t), 1)
        return jnp.where(i >= j, 1.0, 0.0)

    def local_close(m):
        d = total[...] * upper_ones()
        dbc[m, :, 0:n] = mm(d.astype(bf16), bc_ref[m, :, n:])
        dbc[m, :, n:] = mm(d.T.astype(bf16), bc_ref[m, :, :n])

    def through_states(m, sums):
        r = lax.broadcasted_iota(jnp.int32, (gc, LANES), 0)
        col = lax.broadcasted_iota(jnp.int32, (gc, LANES), 1)
        ddt_sum[...] = jnp.zeros_like(ddt_sum)
        dcum_sum[...] = jnp.zeros_like(dcum_sum)

        def body(g, carry):
            last, skips = carry
            lanes = pl.ds(pl.multiple_of(g * gc, gc), gc)
            ones = jnp.where(r // hs + g * GROUP == col, 1.0, 0.0).astype(bf16)
            cum = head_columns(cums[m], g)
            dt_wide = widen(head_columns(dts[m], g), hs)
            x, dy = x_ref[m, :, lanes].astype(f32), dy_ref[m, :, lanes].astype(f32)
            weighted = (x * dt_wide).astype(bf16).astype(f32)
            decay = widen(jnp.exp(cum), hs)
            to_end = widen(jnp.exp(cum[t - 1 :] - cum), hs)
            s_in, ds = begin_ref[m, :, lanes], ends[m, :, lanes]
            through = to_end * mm(bc_ref[m, :, 0:n], ds)
            d_weighted = dxl[m, :, lanes] + through
            dconv_ref[m, :, lanes] = (dt_wide * d_weighted + skip_ref[:, lanes] * dy).astype(bf16)
            dbc[m, :, 0:n] += mm((weighted * to_end).astype(bf16), ds, NT)
            dbc[m, :, n:] += mm((dy * decay).astype(bf16), s_in, NT)
            ddt_sum[...] += head_sums(x * d_weighted, ones)
            dcum_sum[...] += head_sums(dy * y_ref[m, :, lanes] - weighted * d_weighted, ones)
            at_end = jnp.sum(weighted * through, axis=0, keepdims=True) + decay[t - 1 :] * jnp.sum(
                s_in.astype(f32) * ds.astype(f32), axis=0, keepdims=True
            )
            last = last + head_sums(jnp.broadcast_to(at_end, (8, gc)), ones)
            by_skip = jnp.sum(x * dy, axis=0, keepdims=True)
            skips = skips + head_sums(jnp.broadcast_to(by_skip, (8, gc)), ones)
            return last, skips

        none = jnp.zeros((8, LANES), f32)
        last, skips = lax.fori_loop(0, groups, body, (none, none))
        d_log = exact(upper_ones(), dcum_sum[...]) + last[0:1]
        v = raw_ref[m] + shift_ref[...]
        d_dt = (ddt_sum[...] + d_log * rate_ref[...]) / (1.0 + jnp.exp(-v))
        rest = dconv_ref.shape[2] - channels - LANES
        dconv_ref[m, :, pl.ds(channels, LANES)] = d_dt.astype(bf16)
        if rest:
            dconv_ref[m, :, pl.ds(channels + LANES, rest)] = jnp.zeros((t, rest), bf16)
        d_bias = jnp.sum(d_dt, axis=0, keepdims=True)
        d_rate = jnp.sum(d_log * dts[m], axis=0, keepdims=True) * rate_ref[...]
        return sums[0] + d_bias, sums[1] + d_rate, sums[2] + skips[0:1]

    def pre_slope(into, lanes, grad, rows):
        v = conv_rows(into[0 : HALO + rows, :], cw_ref[:, lanes], cb_ref[:, lanes])
        sig = 1.0 / (1.0 + jnp.exp(-v))
        return grad * (sig * (1.0 + v * (1.0 - sig)))

    def load(m, lanes, into, rows):
        into[0:HALO] = halo_ref[m, :, lanes].astype(f32) * has_prior
        into[HALO : HALO + rows] = conv_ref[m, 0:rows, lanes].astype(f32)

    def first_slopes(m):
        def one(lanes, into, grad):
            load(m, lanes, into, HALO)
            head_low[m, :, lanes] = pre_slope(into, lanes, grad, HALO).astype(bf16)

        def body(g, carry):
            lanes = pl.ds(pl.multiple_of(g * gc, gc), gc)
            one(lanes, buf, dconv_ref[m, 0:HALO, lanes].astype(f32))
            return carry

        lax.fori_loop(0, groups, body, 0)
        one(pl.ds(inner, channels - inner), wide_buf, dbc[m, 0:HALO, :])
        first_rows[m].start()

    def conv_back(m):
        def one(lanes, into, grad):
            load(m, lanes, into, t)
            slope = pre_slope(into, lanes, grad, t)
            weights = cw_ref[:, lanes]
            lines = []
            for k in range(taps):
                at = HALO - taps + 1 + k
                lines.append(jnp.sum(slope * into[at : at + t, :], axis=0, keepdims=True))
            dcw_ref[:, lanes] += jnp.concatenate(lines, axis=0)
            dcb_ref[:, lanes] += jnp.sum(slope, axis=0, keepdims=True)
            into[0:t] = slope
            into[t : t + HALO] = next_low[m, :, lanes].astype(f32) * has_next
            back = into[taps - 1 : taps - 1 + t, :] * weights[0:1]
            for k in range(1, taps):
                at = taps - 1 - k
                back = back + into[at : at + t, :] * weights[k : k + 1]
            dconv_ref[m, :, lanes] = back.astype(bf16)

        def body(g, carry):
            lanes = pl.ds(pl.multiple_of(g * gc, gc), gc)
            one(lanes, buf, dconv_ref[m, :, lanes].astype(f32))
            return carry

        lax.fori_loop(0, groups, body, 0)
        one(pl.ds(inner, channels - inner), wide_buf, dbc[m])

    for m in range(micro):
        dt, cum = steps_of(raw_ref[m], shift_ref[...], rate_ref[...])
        dts[m] = dt
        cums[m] = cum
        rows_t[m] = cum.T
        scores[m] = mm(bc_ref[m, :, 0:n], bc_ref[m, :, n:], NT) * upper_ones()
    dcw_ref[...] = jnp.zeros_like(dcw_ref)
    dcb_ref[...] = jnp.zeros_like(dcb_ref)
    total[...] = jnp.zeros_like(total)
    middle = groups // 2
    own_states(0, 0, groups)
    ex.core(0)
    own_states(1, 0, middle)
    ex.along_x(0)
    own_states(1, middle, groups)
    ex.core(1)
    local_terms(0, 0, middle)
    ex.along_x(1)
    ex.along_y(0)
    local_terms(0, middle, groups)
    local_close(0)
    total[...] = jnp.zeros_like(total)
    ex.along_y(1)
    ex.back_to_core(0)
    local_terms(1, 0, groups)
    local_close(1)
    ex.begin_state(0, ends)
    ex.back_to_core(1)
    none = jnp.zeros((1, LANES), f32)
    sums = through_states(0, (none, none, none))
    first_slopes(0)
    ex.begin_state(1, ends)
    sums = through_states(1, sums)
    first_slopes(1)
    heads_ref[...] = jnp.concatenate(list(sums) + [jnp.zeros((5, LANES), f32)], axis=0)
    first_rows[0].wait_recv()
    conv_back(0)
    first_rows[1].wait_recv()
    conv_back(1)
    ex.sent()
    for copy in first_rows:
        copy.wait_send()


def scan_backward(
    dy, x, bc, y, begin, raw, conv_low, halo, conv_w, conv_b, shift, rate, skip_wide, hs, collective_id
):
    micro, t, channels = conv_low.shape
    inner = x.shape[2]
    n = begin.shape[1]
    gc = GROUP * hs
    taps = conv_w.shape[0]
    dma = pltpu.SemaphoreType.DMA
    vmem = pl.BlockSpec(memory_space=pltpu.VMEM)
    return pl.pallas_call(
        partial(scan_backward_kernel, hs),
        in_specs=[vmem] * 13,
        out_specs=[vmem] * 4,
        out_shape=[
            jax.ShapeDtypeStruct((micro, t, -(-(channels + LANES) // 256) * 256), bf16),
            jax.ShapeDtypeStruct((taps, channels), f32),
            jax.ShapeDtypeStruct((1, channels), f32),
            jax.ShapeDtypeStruct((8, LANES), f32),
        ],
        scratch_shapes=exchange_scratch(micro, n, inner)
        + [
            pltpu.VMEM((HALO + t, gc), f32),
            pltpu.VMEM((HALO + t, 2 * n), f32),
            pltpu.VMEM((micro, t, t), f32),
            pltpu.VMEM((t, t), f32),
            pltpu.VMEM((micro, t, LANES), f32),
            pltpu.VMEM((micro, t, LANES), f32),
            pltpu.VMEM((micro, LANES, t), f32),
            pltpu.VMEM((micro, n, inner), bf16),
            pltpu.VMEM((micro, t, inner), f32),
            pltpu.VMEM((micro, t, 2 * n), f32),
            pltpu.VMEM((t, LANES), f32),
            pltpu.VMEM((t, LANES), f32),
            pltpu.VMEM((micro, HALO, channels), bf16),
            pltpu.VMEM((micro, HALO, channels), bf16),
            dma((micro,)),
            dma((micro,)),
        ],
        compiler_params=pltpu.CompilerParams(
            collective_id=collective_id, has_side_effects=True, vmem_limit_bytes=VMEM_MOST
        ),
        cost_estimate=pl.CostEstimate(
            flops=8 * micro * t * inner * (t + 3 * n), bytes_accessed=100_000_000, transcendentals=0
        ),
        name="scan_backward",
    )(dy, x, bc, y, begin, raw, conv_low, halo, conv_w, conv_b, shift, rate, skip_wide)


def shard_place(k, depth):
    z = lax.axis_index("wshard")
    other = (z, z + 1 - 2 * (z % 2), z + 2 - 4 * (z // 2), 3 - z)[k]
    return pl.ds(pl.multiple_of(other * depth, 128), depth)


def front_kernel(h_ref, g_ref, dtw_ref, w_ref, v_ref, conv_ref, norm_ref, raw_ref, rel):
    depth = w_ref.shape[1]

    @pl.when(pl.program_id(0) == 0)
    def _():
        h = h_ref[...].astype(f32)
        power = jnp.mean(h * h, axis=-1, keepdims=True)
        normed = (h * lax.rsqrt(power + epsilon) * g_ref[...]).astype(bf16)
        norm_ref[...] = normed
        raw_ref[...] = mm(normed, dtw_ref[...], NT).astype(bf16).astype(f32)
        for k in range(4):
            rel[:, k * depth : (k + 1) * depth] = norm_ref[:, shard_place(k, depth)]

    weights = jnp.concatenate([w_ref[...]] + [v_ref[k] for k in range(3)], axis=1)
    conv_ref[...] = mm(rel[...], weights, NT).astype(bf16)


def front(hidden, gain, dt_w, own, others, tile):
    rows, width = hidden.shape
    count, depth = own.shape
    whole = pl.BlockSpec((rows, width), lambda i: (0, 0))
    return pl.pallas_call(
        front_kernel,
        grid=(count // tile,),
        in_specs=[
            whole,
            pl.BlockSpec((1, width), lambda i: (0, 0)),
            pl.BlockSpec((LANES, width), lambda i: (0, 0)),
            pl.BlockSpec((tile, depth), lambda i: (i, 0)),
            pl.BlockSpec((3, tile, depth), lambda i: (0, i, 0)),
        ],
        out_specs=[
            pl.BlockSpec((rows, tile), lambda i: (0, i)),
            whole,
            pl.BlockSpec((rows, LANES), lambda i: (0, 0)),
        ],
        out_shape=[
            jax.ShapeDtypeStruct((rows, count), bf16),
            jax.ShapeDtypeStruct((rows, width), bf16),
            jax.ShapeDtypeStruct((rows, LANES), f32),
        ],
        scratch_shapes=[pltpu.VMEM((rows, width), bf16)],
        compiler_params=pltpu.CompilerParams(vmem_limit_bytes=VMEM),
        name="front",
    )(hidden, gain, dt_w, own, others)


def gate_kernel(
    scan_ref,
    norm_ref,
    w_ref,
    v_ref,
    gain_ref,
    ow_ref,
    ov_ref,
    h_ref,
    og_ref,
    valid_ref,
    no_ref,
    out_ref,
    g_ref,
    dy_ref,
    dgate_ref,
    dgain_ref,
    gate,
    d_no,
    branch,
):
    inner = scan_ref.shape[1]
    depth = w_ref.shape[1]
    block = ow_ref.shape[0]
    rows = scan_ref.shape[0]

    @pl.when(pl.program_id(0) == 0)
    def _():
        dgain_ref[...] = jnp.zeros_like(dgain_ref)

    rel = jnp.concatenate([norm_ref[:, shard_place(k, depth)] for k in range(4)], axis=1)
    valid = valid_ref[...]
    g_low = (og_ref[...].astype(f32) * valid).astype(bf16)
    g_ref[...] = g_low
    power = jnp.zeros((rows, 1), f32)
    for i in range(4):
        at = slice(i * block, (i + 1) * block)
        weights = jnp.concatenate([w_ref[at, :]] + [v_ref[k, at, :] for k in range(3)], axis=1)
        value = mm(rel, weights, NT)
        gate[:, at] = value
        act, _ = silu_parts(value)
        u = scan_ref[:, at].astype(f32) * act
        power += jnp.sum(u * u, axis=-1, keepdims=True)
    scale = lax.rsqrt(power / inner + epsilon)
    along = jnp.zeros((rows, 1), f32)
    for k in range(4):
        at = shard_place(k, block)
        weights = ow_ref[...] if k == 0 else ov_ref[k - 1]
        act, _ = silu_parts(gate[:, at])
        u = scan_ref[:, at].astype(f32) * act
        normed = u * scale
        low = (normed * gain_ref[:, at]).astype(bf16)
        no_ref[:, at] = low
        if k == 0:
            branch[...] = mm(low, weights)
        else:
            branch[...] += mm(low, weights)
        d = mm(g_low, weights, NT)
        dgain_ref[:, at] += jnp.sum(d * normed, axis=0, keepdims=True)
        d = d * gain_ref[:, at]
        d_no[:, at] = d
        along += jnp.sum(d * u, axis=-1, keepdims=True)
    out_ref[...] = (h_ref[...].astype(f32) + valid * branch[...]).astype(bf16)
    along = along * scale * scale * scale / inner
    for i in range(4):
        at = slice(i * block, (i + 1) * block)
        value = gate[:, at]
        act, sig = silu_parts(value)
        v = scan_ref[:, at].astype(f32)
        d_u = scale * d_no[:, at] - v * act * along
        dy_ref[:, at] = (d_u * act).astype(bf16)
        dgate_ref[:, at] = (d_u * v * (sig * (1.0 + value * (1.0 - sig)))).astype(bf16)


def gate_stage(scanned, normed, own, others, gain, out_own, out_others, hidden, out_grad, valid, tile):
    rows, width = hidden.shape
    _, inner, depth = others.shape
    once = pl.Buffered(1)
    wide = pl.BlockSpec((tile, inner), lambda i: (i, 0))
    slim = pl.BlockSpec((tile, width), lambda i: (i, 0))
    line = pl.BlockSpec((1, inner), lambda i: (0, 0))
    return pl.pallas_call(
        gate_kernel,
        grid=(rows // tile,),
        in_specs=[
            wide,
            slim,
            pl.BlockSpec((inner, depth), lambda i: (0, 0), pipeline_mode=once),
            pl.BlockSpec(others.shape, lambda i: (0, 0, 0), pipeline_mode=once),
            line,
            pl.BlockSpec(out_own.shape, lambda i: (0, 0), pipeline_mode=once),
            pl.BlockSpec(out_others.shape, lambda i: (0, 0, 0), pipeline_mode=once),
            slim,
            slim,
            pl.BlockSpec((tile, 1), lambda i: (i, 0)),
        ],
        out_specs=[wide, slim, slim, wide, wide, line],
        out_shape=[
            jax.ShapeDtypeStruct((rows, inner), bf16),
            jax.ShapeDtypeStruct((rows, width), bf16),
            jax.ShapeDtypeStruct((rows, width), bf16),
            jax.ShapeDtypeStruct((rows, inner), bf16),
            jax.ShapeDtypeStruct((rows, inner), bf16),
            jax.ShapeDtypeStruct((1, inner), f32),
        ],
        scratch_shapes=[
            pltpu.VMEM((tile, inner), f32),
            pltpu.VMEM((tile, inner), f32),
            pltpu.VMEM((tile, width), f32),
        ],
        compiler_params=pltpu.CompilerParams(vmem_limit_bytes=VMEM_MOST),
        name="gate_stage",
    )(scanned, normed, own, others, gain, out_own, out_others, hidden, out_grad, valid)


def back_kernel(
    steps,
    d_ref,
    e_ref,
    dt_ref,
    dtw_ref,
    w_ref,
    v_ref,
    cw_ref,
    cv_ref,
    h_ref,
    g_ref,
    og_ref,
    out_ref,
    dg_ref,
    acc,
    full,
):
    depth = w_ref.shape[1]
    i = pl.program_id(0)

    def product(ref, one, three):
        return mm(ref[...], jnp.concatenate([one[...]] + [three[k] for k in range(3)], axis=1))

    @pl.when(i == 0)
    def _():
        acc[...] = product(d_ref, w_ref, v_ref)

    @pl.when((i > 0) & (i < steps))
    def _():
        acc[...] += product(d_ref, w_ref, v_ref)

    @pl.when(i >= steps)
    def _():
        acc[...] += product(e_ref, cw_ref, cv_ref)

    @pl.when(i == pl.num_programs(0) - 1)
    def _():
        for k in range(4):
            full[:, shard_place(k, depth)] = acc[:, k * depth : (k + 1) * depth]
        tile = 128
        gain = g_ref[...]
        d_gain = jnp.zeros(gain.shape, f32)
        for r in range(full.shape[0] // tile):
            at = slice(r * tile, (r + 1) * tile)
            d = full[at, :] + mm(dt_ref[at, :], dtw_ref[...])
            h = h_ref[at, :].astype(f32)
            scale = lax.rsqrt(jnp.mean(h * h, axis=-1, keepdims=True) + epsilon)
            d_gain += jnp.sum(d * (h * scale), axis=0, keepdims=True)
            d = d * gain
            along = jnp.mean(d * h, axis=-1, keepdims=True) * (scale * scale * scale)
            out_ref[at, :] = (scale * d - h * along + og_ref[at, :].astype(f32)).astype(bf16)
        dg_ref[...] = d_gain


def back_stage(d, e, dt_w, gate_own, gate_others, own, others, hidden, gain, out_grad, tiles):
    rows, width = hidden.shape
    count, depth = own.shape
    inner = d.shape[1]
    steps, more = inner // tiles[0], count // tiles[1]
    whole = pl.BlockSpec((rows, width), lambda i: (0, 0))
    line = pl.BlockSpec((1, width), lambda i: (0, 0))

    def early(i):
        return jnp.minimum(i, steps - 1)

    def late(i):
        return jnp.maximum(i - steps, 0)

    return pl.pallas_call(
        partial(back_kernel, steps),
        grid=(steps + more,),
        in_specs=[
            pl.BlockSpec((rows, tiles[0]), lambda i: (0, early(i))),
            pl.BlockSpec((rows, tiles[1]), lambda i: (0, late(i))),
            pl.BlockSpec((rows, LANES), lambda i: (0, count // LANES)),
            pl.BlockSpec((LANES, width), lambda i: (0, 0)),
            pl.BlockSpec((tiles[0], depth), lambda i: (early(i), 0)),
            pl.BlockSpec((3, tiles[0], depth), lambda i: (0, early(i), 0)),
            pl.BlockSpec((tiles[1], depth), lambda i: (late(i), 0)),
            pl.BlockSpec((3, tiles[1], depth), lambda i: (0, late(i), 0)),
            whole,
            line,
            whole,
        ],
        out_specs=[whole, line],
        out_shape=[
            jax.ShapeDtypeStruct((rows, width), bf16),
            jax.ShapeDtypeStruct((1, width), f32),
        ],
        scratch_shapes=[pltpu.VMEM((rows, width), f32), pltpu.VMEM((rows, width), f32)],
        compiler_params=pltpu.CompilerParams(vmem_limit_bytes=VMEM_MOST),
        name="back_stage",
    )(d, e, e, dt_w, gate_own, gate_others, own, others, hidden, gain, out_grad)


def project_kernel(n_ref, w_ref, v_ref, o_ref):
    total = mm(n_ref[0], w_ref[...], NT)
    for k in range(1, n_ref.shape[0]):
        total += mm(n_ref[k], v_ref[k - 1], NT)
    o_ref[...] = total.astype(o_ref.dtype)


def project(parts, own, others, first, count, tile, dtype):
    shards, rows, depth = parts.shape
    return pl.pallas_call(
        project_kernel,
        grid=(count // tile,),
        in_specs=[
            pl.BlockSpec((shards, rows, depth), lambda i: (0, 0, 0)),
            pl.BlockSpec((tile, depth), lambda i: (first // tile + i, 0)),
            pl.BlockSpec((shards - 1, tile, depth), lambda i: (0, first // tile + i, 0)),
        ],
        out_specs=pl.BlockSpec((rows, tile), lambda i: (0, i)),
        out_shape=jax.ShapeDtypeStruct((rows, count), dtype),
        compiler_params=pltpu.CompilerParams(vmem_limit_bytes=VMEM),
        name="project",
    )(parts, own, others)


def unproject_kernel(steps, d_ref, e_ref, w_ref, v_ref, o_ref):
    def add(ref):
        o_ref[0] += mm(ref[...], w_ref[...])
        for k in range(1, o_ref.shape[0]):
            o_ref[k] += mm(ref[...], v_ref[k - 1])

    @pl.when(pl.program_id(0) == 0)
    def _():
        o_ref[...] = jnp.zeros_like(o_ref)

    @pl.when(pl.program_id(0) < steps)
    def _():
        add(d_ref)

    @pl.when(pl.program_id(0) >= steps)
    def _():
        add(e_ref)


def unproject(d, e, own, others, tile):
    shards, count, depth = others.shape
    shards += 1
    rows = d.shape[0]
    steps = d.shape[1] // tile
    return pl.pallas_call(
        partial(unproject_kernel, steps),
        grid=(count // tile,),
        in_specs=[
            pl.BlockSpec((rows, tile), lambda i: (0, jnp.minimum(i, steps - 1))),
            pl.BlockSpec((rows, tile), lambda i: (0, jnp.maximum(i - steps, 0))),
            pl.BlockSpec((tile, depth), lambda i: (i, 0)),
            pl.BlockSpec((shards - 1, tile, depth), lambda i: (0, i, 0)),
        ],
        out_specs=pl.BlockSpec((shards, rows, depth), lambda i: (0, 0, 0)),
        out_shape=jax.ShapeDtypeStruct((shards, rows, depth), f32),
        compiler_params=pltpu.CompilerParams(vmem_limit_bytes=VMEM),
        name="unproject",
    )(d, e, own, others)


def rms_front(hidden_rows, gain):
    power = jnp.mean(hidden_rows * hidden_rows, axis=-1, keepdims=True)
    return hidden_rows * lax.rsqrt(power + epsilon) * gain


def conv_act(padded, conv_w, conv_b):
    taps = conv_w.shape[0]
    rows_out = padded.shape[1] - taps + 1
    total = conv_b + padded[:, 0:rows_out] * conv_w[0]
    for offset in range(1, taps):
        total = total + padded[:, offset : offset + rows_out] * conv_w[offset]
    return jax.nn.silu(total)


def gate_norm(values, gate_in, gain):
    gated = values * jax.nn.silu(gate_in)
    power = jnp.mean(gated * gated, axis=-1, keepdims=True)
    return gated * lax.rsqrt(power + epsilon) * gain


def local(
    hidden,
    lengths,
    out_grad,
    norm_gain,
    in_weight,
    conv_weight,
    conv_bias,
    dt_bias,
    a_log,
    skip_gain,
    gated_gain,
    out_weight,
):
    count = lax.axis_size("seq")
    shards = lax.axis_size("wshard")
    rank = lax.axis_index("seq")
    shard = lax.axis_index("wshard")
    micro, _, tokens, width = hidden.shape
    taps = conv_weight.shape[1]
    inner = out_weight.shape[0] * shards
    channels = conv_bias.shape[0] * shards
    heads = dt_bias.shape[0] * shards
    hs = inner // heads
    n = (channels - inner) // 2
    groups = heads // GROUP
    rows = micro * tokens
    fast = count == 8 and shards == 4 and micro == 2
    in_local = in_weight.T
    small = [norm_gain, conv_weight.T.reshape(-1), conv_bias, dt_bias, a_log, skip_gain, gated_gain]
    sizes = [v.shape[0] for v in small]
    small.append(in_local[inner + channels :].reshape(-1))
    packed_low = lax.all_gather(jnp.concatenate(small), "wshard", axis=0)
    packed = packed_low.astype(f32)
    parts, at = [], 0
    for size in sizes:
        parts.append(packed[:, at : at + size])
        at += size
    norm_g = parts[0].reshape(-1)
    conv_w = parts[1].reshape(shards, taps, -1).transpose(1, 0, 2).reshape(taps, -1)
    conv_b = parts[2].reshape(-1)
    dt_shift = parts[3].reshape(-1)
    rate = -jnp.exp(parts[4].reshape(-1))
    skip = parts[5].reshape(-1)
    gated_g = parts[6].reshape(-1)

    dt_w = packed_low[:, at:].reshape(shards, heads, -1).transpose(1, 0, 2).reshape(heads, -1)
    order = jnp.arange(shards) ^ shard
    if fast:
        conv_own = in_local[inner : inner + channels]
        conv_others, gate_others = gather_input_weight(in_local, inner, channels)
    else:
        every = lax.all_gather(in_local[: inner + channels], "wshard", axis=0)
        in_w = every[order[1:]]
        out_w = lax.all_gather(out_weight, "wshard", axis=0, tiled=True)

    def grouped(v):
        return v.reshape(micro, tokens, groups, GROUP).transpose(0, 2, 1, 3)

    rows_in = hidden.reshape(rows, width).astype(f32)
    cot = out_grad.reshape(rows, width).astype(f32)
    positions = rank * tokens + jnp.arange(tokens, dtype=jnp.int32)
    valid = (positions[None, :] < lengths[:, 0][:, None]).astype(f32).reshape(rows, 1)
    tile = 256
    skip_wide = jnp.repeat(skip, hs)[None, :]

    def to_lanes(v):
        return jnp.pad(v, ((0, 0),) * (v.ndim - 1) + ((0, LANES - heads),))

    if fast:
        hidden_rows, out_grad_rows = hidden.reshape(rows, width), out_grad.reshape(rows, width)
        dt_wide = jnp.pad(dt_w, ((0, LANES - heads), (0, 0)))
        conv_low, normed_low, raw = front(
            hidden_rows, norm_g[None, :], dt_wide, conv_own, conv_others, channels // 2
        )
        raw = raw.reshape(micro, tokens, LANES)
    else:
        normed, front_back = jax.vjp(rms_front, rows_in, norm_g)
        normed_low = normed.astype(bf16)
        normed_parts = normed_low.reshape(rows, shards, -1).transpose(1, 0, 2)[order]
        conv_low = project(normed_parts, in_local, in_w, inner, channels, tile, bf16)
        gate_in = project(normed_parts, in_local, in_w, 0, inner, tile, f32)
        dt_low = mm(normed_low, dt_w, NT).astype(bf16)
        dt_raw = dt_low.astype(f32).reshape(micro, tokens, heads) + dt_shift
    conv_low = conv_low.reshape(micro, tokens, channels)

    if fast:
        x_low, bc_low, y_scan, scanned_low, halo, s_in, out_others = scan_forward(
            conv_low,
            raw,
            conv_w,
            conv_b[None, :],
            to_lanes(dt_shift[None, :]),
            to_lanes(rate[None, :]),
            skip_wide,
            out_weight,
            inner,
            hs,
            3,
        )
    else:
        prior = from_behind(conv_low[:, tokens - (taps - 1) :], "seq", 1)
        padded = jnp.concatenate([prior, conv_low], axis=1).astype(f32)
        mixed, conv_back = jax.vjp(conv_act, padded, conv_w, conv_b)
        dt = jax.nn.softplus(dt_raw)
        tri = (jnp.arange(tokens)[:, None] >= jnp.arange(tokens)[None, :]).astype(f32)
        cum = jnp.einsum("ij,mjh->mih", tri, dt * rate, precision=highest)
        dt_g, cum_g = grouped(dt), grouped(cum)
        row_g = cum_g.transpose(0, 1, 3, 2)
        last = cum[:, tokens - 1, :]
        decays = lax.all_gather(jnp.exp(last), "seq", axis=0)
        decay_w = grouped(jnp.exp(cum))
        x_low = mixed[..., :inner].astype(bf16)
        b_low = mixed[..., inner : inner + n].astype(bf16)
        c_low = mixed[..., inner + n :].astype(bf16)
        end_w = grouped(dt * jnp.exp(last[:, None, :] - cum))
        own_state = block_states(x_low, end_w, b_low.transpose(0, 2, 1), hs)
        y_local = local_scan(x_low, dt_g, cum_g, row_g, b_low, c_low, hs)
        s_in = running_states(own_state, decays, hs, True)
        y_scan, scanned_low = add_carry(x_low, y_local, cum_g, c_low, s_in, skip_wide, hs)

    if fast:
        normed_out_low, output, g, dy, d_gate_low, d_gated = gate_stage(
            scanned_low.reshape(rows, inner),
            normed_low,
            in_local,
            gate_others,
            gated_g[None, :],
            out_weight,
            out_others,
            hidden_rows,
            out_grad_rows,
            valid,
            256,
        )
        output = output.reshape(hidden.shape)
        dy = dy.reshape(micro, tokens, inner)
        d_gated = d_gated[0]
    else:
        scanned = scanned_low.reshape(rows, inner).astype(f32)
        normed_out, gate_back = jax.vjp(gate_norm, scanned, gate_in, gated_g)
        normed_out_low = normed_out.astype(bf16)
        branch = mm(normed_out_low, out_w)
        output = (rows_in + valid * branch).astype(bf16).reshape(hidden.shape)
        g = (cot * valid).astype(bf16)
        d_scanned, d_gate_in, d_gated = gate_back(mm(g, out_w, NT))
        dy = d_scanned.astype(bf16).reshape(micro, tokens, inner)
        d_gate_low = d_gate_in.astype(bf16)

    if fast:
        d_rest, d_conv_w, d_conv_b, by_head = scan_backward(
            dy,
            x_low,
            bc_low,
            y_scan,
            s_in,
            raw,
            conv_low,
            halo,
            conv_w,
            conv_b[None, :],
            to_lanes(dt_shift[None, :]),
            to_lanes(rate[None, :]),
            skip_wide,
            hs,
            4,
        )
        d_dt_bias, d_a_log, d_skip = by_head[0, :heads], by_head[1, :heads], by_head[2, :heads]
        d_conv_b = d_conv_b[0]
        d_rest = d_rest.reshape(rows, -1)
        input_grad, d_norm_g = back_stage(
            d_gate_low,
            d_rest,
            dt_wide,
            in_local,
            gate_others,
            conv_own,
            conv_others,
            hidden_rows,
            norm_g[None, :],
            out_grad_rows,
            (inner // 2, channels // 2),
        )
        input_grad = input_grad.reshape(hidden.shape)
        d_norm_g = d_norm_g[0]
    else:
        own_grad = block_states(dy, decay_w, c_low.transpose(0, 2, 1), hs)
        dx_local, db_local, dc_local = local_back(x_low, dy, dt_g, cum_g, row_g, b_low, c_low, hs)
        ds = running_states(own_grad, decays, hs, False)
        dx_low, ddt_g, dcum_g, db, dc, last_term, dskip = carry_back(
            x_low, dy, dx_local, y_scan, dt_g, cum_g, b_low, s_in, ds, db_local, dc_local, skip_wide, hs
        )

        def ungrouped(v):
            return v.transpose(0, 2, 1, 3).reshape(micro, tokens, heads)

        at_end = jnp.sum(last_term.reshape(micro, heads, hs), axis=-1)[:, None, :]
        d_log = jnp.einsum("ij,mih->mjh", tri, ungrouped(dcum_g), precision=highest) + at_end
        d_dt = (ungrouped(ddt_g) + d_log * rate) * jax.nn.sigmoid(dt_raw)
        d_dt_bias = jnp.sum(d_dt, axis=(0, 1))
        d_a_log = jnp.sum(d_log * dt, axis=(0, 1)) * rate
        d_skip = jnp.sum(dskip.reshape(-1, heads, hs), axis=(0, 2))
        mixed_grad = jnp.concatenate([dx_low.astype(f32), db, dc], axis=2)
        d_padded, d_conv_w, d_conv_b = conv_back(mixed_grad)
        from_next = from_behind(d_padded[:, : taps - 1].astype(bf16), "seq", -1).astype(f32)
        d_conv = d_padded[:, taps - 1 :].at[:, tokens - (taps - 1) :].add(from_next)
        d_dt_low = d_dt.astype(bf16).reshape(rows, heads)
    total_cols = inner + channels + heads
    if not fast:
        d_rest = d_conv.astype(bf16).reshape(rows, channels)
        d_parts = unproject(d_gate_low, d_rest, in_local, in_w, tile)
        d_normed = d_parts[order].transpose(1, 0, 2).reshape(rows, width) + mm(d_dt_low, dt_w)
        d_hidden, d_norm_g = front_back(d_normed)
        input_grad = (d_hidden + cot).astype(bf16).reshape(hidden.shape)

    def summed(terms, axis):
        t = lax.psum_scatter(terms.astype(bf16), "seq", scatter_dimension=0, tiled=True)
        t = lax.psum_scatter(t, "wshard", scatter_dimension=axis, tiled=True)
        return lax.all_gather(t, "seq", axis=0, tiled=True).astype(f32)

    smalls = [
        d_norm_g.reshape(shards, -1),
        d_conv_w.reshape(taps, shards, -1).transpose(1, 0, 2).reshape(shards, -1),
        d_conv_b.reshape(shards, -1),
        d_dt_bias.reshape(shards, -1),
        d_a_log.reshape(shards, -1),
        d_skip.reshape(shards, -1),
        d_gated.reshape(shards, -1),
    ]
    smalls = jnp.concatenate(smalls, axis=1)
    if fast:
        smalls = jnp.pad(smalls, ((0, 0), (0, -smalls.shape[1] % 1024))).reshape(shards, -1, LANES)
        by_core, out_sum, sums = weight_sums(d_gate_low, d_rest, normed_low, g, normed_out_low, smalls, 2)
        by_core = by_core.reshape(2, -1, normed_low.shape[1] // shards)
        split = inner // 2
        rest = by_core[:, split:].reshape(-1, by_core.shape[2])[: total_cols - inner]
        in_grad = jnp.concatenate([by_core[:, :split].reshape(inner, -1), rest]).astype(f32).T
        out_w_grad = out_sum.T.astype(f32)
        sums = sums.reshape(-1)
    else:
        d_proj = jnp.concatenate([d_gate_low, d_rest, d_dt_low], axis=1)
        in_grad = summed(mm(d_proj, normed_low, TN), 1).T
        out_terms = mm(normed_out_low, g, TN)
        blocks = out_terms.reshape(shards, count, -1, width).transpose(1, 0, 2, 3)
        out_w_grad = summed(blocks.reshape(inner, width), 0)
        sums = lax.psum(smalls, ("seq", "wshard"))
        sums = lax.dynamic_index_in_dim(sums, shard, 0, keepdims=False)
    found, at = [], 0
    for size in sizes:
        found.append(sums[at : at + size])
        at += size
    return (
        output,
        input_grad,
        found[0],
        in_grad,
        found[1].reshape(taps, -1).T,
        found[2],
        found[3],
        found[4],
        found[5],
        found[6],
        out_w_grad,
    )


def solution(mesh):
    return jax.shard_map(
        local,
        mesh=mesh,
        in_specs=(
            P(None, "wshard", "seq", None),
            P(None, "wshard"),
            P(None, "wshard", "seq", None),
            P("wshard"),
            P("wshard", None),
            P("wshard", None),
            P("wshard"),
            P("wshard"),
            P("wshard"),
            P("wshard"),
            P("wshard"),
            P("wshard", None),
        ),
        out_specs=(
            P(None, "wshard", "seq", None),
            P(None, "wshard", "seq", None),
            P("wshard"),
            P("wshard", None),
            P("wshard", None),
            P("wshard"),
            P("wshard"),
            P("wshard"),
            P("wshard"),
            P("wshard"),
            P("wshard", None),
        ),
        check_vma=False,
    )
```

```python
from functools import partial

import jax
import jax.numpy as jnp
from jax import lax
from jax.experimental import pallas as pl
from jax.experimental.pallas import tpu as pltpu
from jax.sharding import PartitionSpec as P

epsilon = 1e-05
highest = lax.Precision.HIGHEST
f32 = jnp.float32
bf16 = jnp.bfloat16
GROUP = 8
VMEM = 48 * 1024 * 1024
VMEM_MOST = 62 * 1024 * 1024

NN = (((1,), (0,)), ((), ()))
NT = (((1,), (1,)), ((), ()))
TN = (((0,), (0,)), ((), ()))


def mm(a, b, dims=NN):
    return lax.dot_general(a, b, dims, preferred_element_type=f32)


def params():
    return pltpu.CompilerParams(
        dimension_semantics=("arbitrary", "arbitrary"), vmem_limit_bytes=VMEM
    )


def widen(cols, head_size):
    t, heads = cols.shape
    lane = lax.broadcasted_iota(jnp.int32, (t, 2 * head_size), 1)
    parts = []
    for k in range(0, heads, 2):
        parts.append(jnp.where(lane < head_size, cols[:, k : k + 1], cols[:, k + 1 : k + 2]))
    return jnp.concatenate(parts, axis=1)


def state_kernel(hs, x_ref, w_ref, bt_ref, o_ref):
    weighted = (x_ref[0].astype(f32) * widen(w_ref[0, 0], hs)).astype(bf16)
    o_ref[0] = mm(bt_ref[0], weighted)


def block_states(x, weights, bt, hs):
    micro, t, cols = x.shape
    n = bt.shape[1]
    gc = GROUP * hs
    return pl.pallas_call(
        partial(state_kernel, hs),
        grid=(micro, cols // gc),
        in_specs=[
            pl.BlockSpec((1, t, gc), lambda m, g: (m, 0, g)),
            pl.BlockSpec((1, 1, t, GROUP), lambda m, g: (m, g, 0, 0)),
            pl.BlockSpec((1, n, t), lambda m, g: (m, 0, 0)),
        ],
        out_specs=pl.BlockSpec((1, n, gc), lambda m, g: (m, 0, g)),
        out_shape=jax.ShapeDtypeStruct((micro, n, cols), f32),
        compiler_params=params(),
        name="block_states",
    )(x, weights, bt)


def local_kernel(hs, x_ref, dt_ref, cum_ref, row_ref, b_ref, c_ref, o_ref, scores):
    t = x_ref.shape[1]
    half = t // 2

    @pl.when(pl.program_id(1) == 0)
    def _():
        s = mm(c_ref[0], b_ref[0], NT)
        i = lax.broadcasted_iota(jnp.int32, (t, t), 0)
        j = lax.broadcasted_iota(jnp.int32, (t, t), 1)
        scores[...] = jnp.where(i >= j, s, 0.0)

    cum, dt, rows = cum_ref[0, 0], dt_ref[0, 0], row_ref[0, 0]
    lane = lax.broadcasted_iota(jnp.int32, (half, 2 * hs), 1)
    weighted = (x_ref[0].astype(f32) * widen(dt, hs)).astype(bf16)
    for k in range(0, GROUP, 2):
        at = slice(k * hs, (k + 2) * hs)
        pair = weighted[:, at]
        top, low = [], []
        for h in (k, k + 1):
            col, row = cum[:, h : h + 1], rows[h : h + 1, :]
            m1 = jnp.exp(jnp.minimum(col[:half] - row[:, :half], 0.0)) * scores[:half, :half]
            m2 = jnp.exp(jnp.minimum(col[half:] - row, 0.0)) * scores[half:, :]
            top.append(mm(m1.astype(bf16), pair[:half]))
            low.append(mm(m2.astype(bf16), pair))
        o_ref[0, :half, at] = jnp.where(lane < hs, top[0], top[1])
        o_ref[0, half:, at] = jnp.where(lane < hs, low[0], low[1])


def local_scan(x, dt, cum, rows, b, c, hs):
    micro, t, cols = x.shape
    n = b.shape[2]
    gc = GROUP * hs
    return pl.pallas_call(
        partial(local_kernel, hs),
        grid=(micro, cols // gc),
        in_specs=[
            pl.BlockSpec((1, t, gc), lambda m, g: (m, 0, g)),
            pl.BlockSpec((1, 1, t, GROUP), lambda m, g: (m, g, 0, 0)),
            pl.BlockSpec((1, 1, t, GROUP), lambda m, g: (m, g, 0, 0)),
            pl.BlockSpec((1, 1, GROUP, t), lambda m, g: (m, g, 0, 0)),
            pl.BlockSpec((1, t, n), lambda m, g: (m, 0, 0)),
            pl.BlockSpec((1, t, n), lambda m, g: (m, 0, 0)),
        ],
        out_specs=pl.BlockSpec((1, t, gc), lambda m, g: (m, 0, g)),
        out_shape=jax.ShapeDtypeStruct((micro, t, cols), f32),
        scratch_shapes=[pltpu.VMEM((t, t), f32)],
        compiler_params=params(),
        name="local_scan",
    )(x, dt, cum, rows, b, c)


def carry_kernel(hs, x_ref, y_ref, cum_ref, c_ref, s_ref, skip_ref, scan_ref, low_ref):
    carried = mm(c_ref[0], s_ref[0].astype(bf16)) * widen(jnp.exp(cum_ref[0, 0]), hs)
    scan = y_ref[0] + carried
    scan_ref[0] = scan
    low_ref[0] = (scan + skip_ref[...] * x_ref[0].astype(f32)).astype(bf16)


def add_carry(x, y, cum, c, s_in, skip_wide, hs):
    micro, t, cols = x.shape
    n = c.shape[2]
    gc = GROUP * hs
    wide = pl.BlockSpec((1, t, gc), lambda m, g: (m, 0, g))
    return pl.pallas_call(
        partial(carry_kernel, hs),
        grid=(micro, cols // gc),
        in_specs=[
            wide,
            wide,
            pl.BlockSpec((1, 1, t, GROUP), lambda m, g: (m, g, 0, 0)),
            pl.BlockSpec((1, t, n), lambda m, g: (m, 0, 0)),
            pl.BlockSpec((1, n, gc), lambda m, g: (m, 0, g)),
            pl.BlockSpec((1, gc), lambda m, g: (0, g)),
        ],
        out_specs=[wide, wide],
        out_shape=[
            jax.ShapeDtypeStruct((micro, t, cols), f32),
            jax.ShapeDtypeStruct((micro, t, cols), bf16),
        ],
        compiler_params=params(),
        name="add_carry",
    )(x, y, cum, c, s_in, skip_wide)


def local_back_kernel(
    hs, x_ref, dy_ref, dt_ref, cum_ref, row_ref, b_ref, c_ref, dx_ref, db_ref, dc_ref, scores, total
):
    t = x_ref.shape[1]
    half = t // 2

    @pl.when(pl.program_id(1) == 0)
    def _():
        s = mm(b_ref[0], c_ref[0], NT)
        j = lax.broadcasted_iota(jnp.int32, (t, t), 0)
        i = lax.broadcasted_iota(jnp.int32, (t, t), 1)
        scores[...] = jnp.where(i >= j, s, 0.0)
        total[...] = jnp.zeros_like(total)

    cum, dt, rows = cum_ref[0, 0], dt_ref[0, 0], row_ref[0, 0]
    lane = lax.broadcasted_iota(jnp.int32, (t, 2 * hs), 1)
    lane_half = lax.broadcasted_iota(jnp.int32, (half, 2 * hs), 1)
    weighted = (x_ref[0].astype(f32) * widen(dt, hs)).astype(bf16)
    for k in range(0, GROUP, 2):
        at = slice(k * hs, (k + 2) * hs)
        pair = weighted[:, at]
        dy = dy_ref[0, :, at]
        top, low = [], []
        for h in (k, k + 1):
            col, row = cum[:, h : h + 1], rows[h : h + 1, :]
            mine = jnp.where(lane < hs, pair, 0) if h == k else jnp.where(lane < hs, 0, pair)
            l1 = jnp.exp(jnp.minimum(row - col[:half], 0.0))
            l2 = jnp.exp(jnp.minimum(row[:, half:] - col[half:], 0.0))
            total[:half, :] += l1 * mm(mine[:half], dy, NT)
            total[half:, half:] += l2 * mm(mine[half:], dy[half:], NT)
            top.append(mm((l1 * scores[:half, :]).astype(bf16), dy))
            low.append(mm((l2 * scores[half:, half:]).astype(bf16), dy[half:]))
        dx_ref[0, :half, at] = jnp.where(lane_half < hs, top[0], top[1])
        dx_ref[0, half:, at] = jnp.where(lane_half < hs, low[0], low[1])

    @pl.when(pl.program_id(1) == pl.num_programs(1) - 1)
    def _():
        j = lax.broadcasted_iota(jnp.int32, (t, t), 0)
        i = lax.broadcasted_iota(jnp.int32, (t, t), 1)
        d = jnp.where(i >= j, total[...], 0.0)
        db_ref[0] = mm(d.astype(bf16), c_ref[0])
        dc_ref[0] = mm(d.T.astype(bf16), b_ref[0])


def local_back(x, dy, dt, cum, rows, b, c, hs):
    micro, t, cols = x.shape
    n = b.shape[2]
    gc = GROUP * hs
    wide = pl.BlockSpec((1, t, gc), lambda m, g: (m, 0, g))
    small = pl.BlockSpec((1, 1, t, GROUP), lambda m, g: (m, g, 0, 0))
    state = pl.BlockSpec((1, t, n), lambda m, g: (m, 0, 0))
    return pl.pallas_call(
        partial(local_back_kernel, hs),
        grid=(micro, cols // gc),
        in_specs=[
            wide,
            wide,
            small,
            small,
            pl.BlockSpec((1, 1, GROUP, t), lambda m, g: (m, g, 0, 0)),
            state,
            state,
        ],
        out_specs=[wide, state, state],
        out_shape=[
            jax.ShapeDtypeStruct((micro, t, cols), f32),
            jax.ShapeDtypeStruct((micro, t, n), f32),
            jax.ShapeDtypeStruct((micro, t, n), f32),
        ],
        scratch_shapes=[pltpu.VMEM((t, t), f32), pltpu.VMEM((t, t), f32)],
        compiler_params=params(),
        name="local_back",
    )(x, dy, dt, cum, rows, b, c)


def head_sums(values, ones):
    high = values.astype(bf16)
    rest = (values - high.astype(f32)).astype(bf16)
    return mm(high, ones) + mm(rest, ones)


def carry_back_kernel(
    hs,
    x_ref,
    dy_ref,
    dxl_ref,
    y_ref,
    dt_ref,
    cum_ref,
    b_ref,
    si_ref,
    ds_ref,
    dbl_ref,
    dcl_ref,
    skip_ref,
    dx_ref,
    ddt_ref,
    dcum_ref,
    db_ref,
    dc_ref,
    last_ref,
    dskip_ref,
):
    t = x_ref.shape[1]
    gc = x_ref.shape[2]

    @pl.when(pl.program_id(1) == 0)
    def _():
        db_ref[0] = dbl_ref[0]
        dc_ref[0] = dcl_ref[0]

    cum, dt = cum_ref[0, 0], dt_ref[0, 0]
    x, dy = x_ref[0].astype(f32), dy_ref[0].astype(f32)
    dt_wide = widen(dt, hs)
    weighted = (x * dt_wide).astype(bf16).astype(f32)
    decay = widen(jnp.exp(cum), hs)
    to_end = widen(jnp.exp(cum[t - 1 :, :] - cum), hs)
    s_in, ds = si_ref[0].astype(f32), ds_ref[0]
    s_low, ds_low = s_in.astype(bf16), ds.astype(bf16)
    through = to_end * mm(b_ref[0], ds_low)
    d_weighted = dxl_ref[0] + through
    dx_ref[0] = (dt_wide * d_weighted + skip_ref[...] * dy).astype(bf16)
    db_ref[0] += mm((weighted * to_end).astype(bf16), ds_low, NT)
    dc_ref[0] += mm((dy * decay).astype(bf16), s_low, NT)
    r = lax.broadcasted_iota(jnp.int32, (gc, 128), 0)
    c = lax.broadcasted_iota(jnp.int32, (gc, 128), 1)
    ones = jnp.where(r // hs == c, 1.0, 0.0).astype(bf16)
    ddt_ref[0, 0] = head_sums(x * d_weighted, ones)[:, :GROUP]
    dcum_ref[0, 0] = head_sums(dy * y_ref[0] - weighted * d_weighted, ones)[:, :GROUP]
    last_decay = decay[t - 1 :, :]
    last_ref[0] = jnp.sum(weighted * through, axis=0, keepdims=True) + last_decay * jnp.sum(
        s_low.astype(f32) * ds, axis=0, keepdims=True
    )
    dskip_ref[0] = jnp.sum(x * dy, axis=0, keepdims=True)


def carry_back(x, dy, dxl, y, dt, cum, b, s_in, ds, dbl, dcl, skip_wide, hs):
    micro, t, cols = x.shape
    n = b.shape[2]
    gc = GROUP * hs
    groups = cols // gc
    wide = pl.BlockSpec((1, t, gc), lambda m, g: (m, 0, g))
    small = pl.BlockSpec((1, 1, t, GROUP), lambda m, g: (m, g, 0, 0))
    state = pl.BlockSpec((1, t, n), lambda m, g: (m, 0, 0))
    st = pl.BlockSpec((1, n, gc), lambda m, g: (m, 0, g))
    line = pl.BlockSpec((1, 1, gc), lambda m, g: (m, 0, g))
    return pl.pallas_call(
        partial(carry_back_kernel, hs),
        grid=(micro, groups),
        in_specs=[
            wide,
            wide,
            wide,
            wide,
            small,
            small,
            state,
            st,
            st,
            state,
            state,
            pl.BlockSpec((1, gc), lambda m, g: (0, g)),
        ],
        out_specs=[wide, small, small, state, state, line, line],
        out_shape=[
            jax.ShapeDtypeStruct((micro, t, cols), bf16),
            jax.ShapeDtypeStruct((micro, groups, t, GROUP), f32),
            jax.ShapeDtypeStruct((micro, groups, t, GROUP), f32),
            jax.ShapeDtypeStruct((micro, t, n), f32),
            jax.ShapeDtypeStruct((micro, t, n), f32),
            jax.ShapeDtypeStruct((micro, 1, cols), f32),
            jax.ShapeDtypeStruct((micro, 1, cols), f32),
        ],
        compiler_params=params(),
        name="carry_back",
    )(x, dy, dxl, y, dt, cum, b, s_in, ds, dbl, dcl, skip_wide)


def from_behind(x, axis, by):
    count = lax.axis_size(axis)
    pairs = [(i, i + by) for i in range(count) if 0 <= i + by < count]
    return lax.ppermute(x, axis, pairs)


def swap(x, by):
    count = lax.axis_size("seq")
    return lax.ppermute(x, "seq", [(i, i ^ by) for i in range(count)])


def running_states(terms, decays, hs, forward):
    count = lax.axis_size("seq")
    rank = lax.axis_index("seq")
    index = jnp.arange(count)

    def product(mask):
        d = jnp.prod(jnp.where(mask[:, None, None], decays, 1.0), axis=0)
        return jnp.repeat(d, hs, axis=1)[:, None, :]

    total, before = terms, jnp.zeros_like(terms)
    size = 1
    while size < count:
        other = swap(total.astype(bf16), size).astype(f32)
        mine = index // size == rank // size
        theirs = index // size == (rank // size) ^ 1
        later = (rank // size) % 2 == (1 if forward else 0)
        passed = mine & ((index < rank) if forward else (index > rank))
        before = before + jnp.where(later, product(passed), 0.0) * other
        if 2 * size < count:
            total = total * jnp.where(later, 1.0, product(theirs)) + other * jnp.where(
                later, product(mine), 1.0
            )
        size *= 2
    return before


MESH = pl.DeviceIdType.MESH


def around():
    s, z = lax.axis_index("seq"), lax.axis_index("wshard")
    c, x, y = s % 2, (s // 2) % 2, s // 4
    near = {
        "c": (s + 1 - 2 * c, z),
        "x": (s + 2 - 4 * x, z),
        "y": (s + 4 - 8 * y, z),
        "z1": (s, z + 1 - 2 * (z % 2)),
        "z2": (s, z + 2 - 4 * (z // 2)),
        "z3": (s, 3 - z),
    }
    return s, z, c, x, y, near


def greet(near):
    barrier = pltpu.get_barrier_semaphore()
    for where in near.values():
        pl.semaphore_signal(barrier, inc=1, device_id=where, device_id_type=MESH)
    pl.semaphore_wait(barrier, len(near))


CHUNK_DMAS = 10
AHEAD = 2


def split_rows(piece, parts):
    tiles = piece // 16
    return [16 * (tiles * (i + 1) // parts - tiles * i // parts) for i in range(parts)]


class Gather:
    def __init__(self, place, items, send, recv):
        s, z, c, x, y, near = place
        sx, sy, sd = s + 2 - 4 * x, s + 4 - 8 * y, s + 6 - 4 * x - 8 * y
        self.plans = []
        for source, base, target, count, parts in items:
            off = 0
            for i, size in enumerate(split_rows(count // 8, parts)):
                q = len(self.plans)

                def rows(who, first=0, off=off, size=size, piece=count // 8):
                    return pl.ds(pl.multiple_of(first + who * piece + off, 16), size)

                def move(src, dst, kind, to, q=q):
                    return pltpu.make_async_remote_copy(
                        src_ref=src,
                        dst_ref=dst,
                        send_sem=send.at[q, kind],
                        recv_sem=recv.at[q, kind],
                        device_id=near[to],
                        device_id_type=MESH,
                    )

                def along(who, kind, to, move=move, rows=rows, target=target):
                    block = target.at[pl.ds(0, 3), rows(who)]
                    return move(block, block, kind, to)

                plan = {}
                for k in (1, 2, 3):
                    there = target.at[k - 1, rows(s)]
                    plan["z%d" % k] = move(source.at[rows(s, base)], there, k - 1, "z%d" % k)
                plan["x"] = along(s, 3, "x")
                plan["y"] = along(s, 4, "y")
                first = "xy"[i % 2]
                plan["d"] = along(sx, 5, "y") if first == "x" else along(sy, 5, "x")
                plan["c0"] = along(s, 6, "c")
                plan["cx"] = along(sx, 7, "c")
                plan["cy"] = along(sy, 8, "c")
                plan["cd"] = along(sd, 9, "c")
                plan["order"] = first, "yx"[i % 2]
                self.plans.append(plan)
                off += size

    def fetch(self, i):
        for k in (1, 2, 3):
            self.plans[i]["z%d" % k].start()

    def begin(self, i):
        plan = self.plans[i]
        for k in (1, 2, 3):
            plan["z%d" % k].wait_recv()
        for name in ("x", "y", "c0"):
            plan[name].start()

    def middle(self, i):
        plan = self.plans[i]
        one, two = plan["order"]
        plan[one].wait_recv()
        plan["d"].start()
        plan["c" + one].start()
        plan[two].wait_recv()
        plan["c" + two].start()

    def finish(self, i):
        self.plans[i]["d"].wait_recv()
        self.plans[i]["cd"].start()

    def run(self):
        n = len(self.plans)
        for i in range(min(AHEAD, n)):
            self.fetch(i)
        for i in range(n + 2):
            if i < n:
                self.begin(i)
                if i + AHEAD < n:
                    self.fetch(i + AHEAD)
            if 0 <= i - 1 < n:
                self.middle(i - 1)
            if 0 <= i - 2 < n:
                self.finish(i - 2)

    def close(self):
        for plan in self.plans:
            for name in ("c0", "cx", "cy", "cd"):
                plan[name].wait_recv()
            for name in ("z1", "z2", "z3", "x", "y", "d", "c0", "cx", "cy", "cd"):
                plan[name].wait_send()


def gather_kernel(inner, channels, parts, w_ref, conv_ref, gate_ref, own, own_sem, send, recv):
    place = around()
    inward = pltpu.make_async_copy(w_ref.at[pl.ds(inner, channels)], own, own_sem)
    inward.start()
    greet(place[-1])
    items = [(w_ref, inner, conv_ref, channels, parts), (w_ref, 0, gate_ref, inner, parts)]
    work = Gather(place, items, send, recv)
    work.run()
    inward.wait()
    outward = pltpu.make_async_copy(own, conv_ref.at[3], own_sem)
    outward.start()
    work.close()
    outward.wait()


def gather_input_weight(w_t, inner, channels, parts=6):
    width = w_t.shape[1]
    hbm = pl.BlockSpec(memory_space=pl.ANY)
    return pl.pallas_call(
        partial(gather_kernel, inner, channels, parts),
        in_specs=[hbm],
        out_specs=[hbm] * 2,
        out_shape=[
            jax.ShapeDtypeStruct((4, channels, width), bf16),
            jax.ShapeDtypeStruct((3, inner, width), bf16),
        ],
        scratch_shapes=[
            pltpu.VMEM((channels, width), bf16),
            pltpu.SemaphoreType.DMA,
            pltpu.SemaphoreType.DMA((2 * parts, CHUNK_DMAS)),
            pltpu.SemaphoreType.DMA((2 * parts, CHUNK_DMAS)),
        ],
        compiler_params=pltpu.CompilerParams(
            collective_id=1, has_side_effects=True, vmem_limit_bytes=VMEM_MOST
        ),
        cost_estimate=pl.CostEstimate(flops=0, bytes_accessed=200_000_000, transcendentals=0),
        name="gather_input_weight",
    )(w_t)


class Products:
    IN = 4
    SCRATCH = 22

    @staticmethod
    def sizes(a_list, b):
        rows = b.shape[0]
        wide = sum(a.shape[1] for a in a_list) // 2
        return rows, wide, b.shape[1], wide // 128

    @staticmethod
    def marks(chunks):
        return sorted({0, chunks * 2 // 5, chunks * 7 // 10, chunks * 9 // 10, chunks})

    @staticmethod
    def out_shape(a_list, b):
        _, _, width, chunks = Products.sizes(a_list, b)
        return jax.ShapeDtypeStruct((2, chunks, 2, 2, 2, 16, width // 4), bf16)

    @staticmethod
    def scratch(a_list, b):
        rows, wide, width, chunks = Products.sizes(a_list, b)
        dma = pltpu.SemaphoreType.DMA
        n = Products.IN
        marks = Products.marks(chunks)
        return [
            pltpu.VMEM((2 * rows, wide), bf16),
            pltpu.VMEM((2 * rows, width), bf16),
            pltpu.VMEM((2, 128, width), f32),
            pltpu.VMEM((2, 32, width), bf16),
            pltpu.VMEM((2, 32, width), bf16),
            pltpu.VMEM((2, 16, width), bf16),
            pltpu.VMEM((2, 16, width), bf16),
            pltpu.VMEM((2, 2, 16, width), bf16),
            pltpu.VMEM((2, 16, width), f32),
            pltpu.VMEM((2, 16, width), f32),
            pltpu.VMEM((2, 2, 16, width), f32),
            pltpu.VMEM((chunks, 32, width), bf16),
            pltpu.VMEM((chunks, 32, width), bf16),
            pltpu.VMEM((chunks, 16, width), bf16),
            pltpu.VMEM((chunks, 16, width), bf16),
            pltpu.VMEM((chunks, 3, 2, 16, width // 4), bf16),
            dma((n,)),
            dma((n,)),
            dma((n,)),
            dma((7, 2)),
            dma((7, chunks)),
            dma((2, len(marks) - 1, 8)),
        ]

    def __init__(self, place, a_refs, b_ref, out, scratch):
        self.s, self.z, self.c, self.x, self.y, self.near = place
        (
            self.a,
            self.b,
            self.g,
            self.sa1,
            self.sb1,
            self.sa2,
            self.sb2,
            self.s3,
            self.ka2,
            self.kb2,
            self.f3,
            self.ra1,
            self.rb1,
            self.ra2,
            self.rb2,
            self.rz,
            self.in_sem,
            self.s_in,
            self.r_in,
            self.s_step,
            self.r_step,
            self.sems_all,
        ) = scratch
        self.out = out
        self.shard = self.rz.shape[-1]
        self.chunks = self.ra1.shape[0]
        marks = Products.marks(self.chunks)
        self.groups = list(zip(marks[:-1], marks[1:]))
        c = self.c
        rows = self.a.shape[0] // 2
        near, far = pl.ds(0, rows), pl.ds(rows, rows)
        self.operands = []
        self.operands.append(
            (
                0,
                pltpu.make_async_copy(b_ref, self.b.at[near], self.in_sem.at[0]),
                self.remote(b_ref, self.b.at[far], self.s_in.at[0], self.r_in.at[0], "c"),
            )
        )
        at = 0
        for i, ref in enumerate(a_refs):
            half = ref.shape[1] // 2
            here = ref.at[:, pl.ds(pl.multiple_of(c * half, 128), half)]
            there = ref.at[:, pl.ds(pl.multiple_of((1 - c) * half, 128), half)]
            to = pl.ds(at, half)
            self.operands.append(
                (
                    at // 128,
                    pltpu.make_async_copy(here, self.a.at[near, to], self.in_sem.at[i + 1]),
                    self.remote(there, self.a.at[far, to], self.s_in.at[i + 1], self.r_in.at[i + 1], "c"),
                )
            )
            at += half

    def remote(self, src, dst, ss, rs, to):
        return pltpu.make_async_remote_copy(
            src_ref=src,
            dst_ref=dst,
            send_sem=ss,
            recv_sem=rs,
            device_id=self.near[to],
            device_id_type=MESH,
        )

    def load(self):
        for _, here, _ in self.operands:
            here.start()

    def share(self):
        for _, _, there in self.operands:
            there.start()

    def step_copy(self, kind, u):
        slot = u % 2
        ss, rs = self.s_step.at[kind, slot], self.r_step.at[kind, u]
        if kind < 4:
            src, dst, to = (
                (self.sa1, self.ra1, "x"),
                (self.sb1, self.rb1, "y"),
                (self.sa2, self.ra2, "y"),
                (self.sb2, self.rb2, "x"),
            )[kind]
            return self.remote(src.at[slot], dst.at[u], ss, rs, to)
        k = kind - 3
        z = self.z
        other = (z + 1 - 2 * (z % 2), z + 2 - 4 * (z // 2), 3 - z)[k - 1]
        cols = pl.ds(pl.multiple_of(other * self.shard, 128), self.shard)
        return self.remote(self.s3.at[slot, :, :, cols], self.rz.at[u, k - 1], ss, rs, "z%d" % k)

    def all_copy(self, q, kind):
        a, b = self.groups[q]
        ts = pl.ds(a, b - a)
        x, y, c = self.x, self.y, self.c
        px = 1 - x if kind in (3, 5, 7) else x
        py = 1 - y if kind in (4, 6, 7) else y
        if kind in (3, 4):
            block = self.out.at[c, ts, kind - 3, px, py]
        else:
            block = self.out.at[c, ts, :, px, py]
        to = ("x", "y", "c", "y", "x", "c", "c", "c")[kind]
        return self.remote(block, block, self.sems_all.at[0, q, kind], self.sems_all.at[1, q, kind], to)

    def step(self, t):
        x, y, z, c = self.x, self.y, self.z, self.c
        g, ra1, rb1 = self.g, self.ra1, self.rb1
        chunks = self.chunks
        copy = self.step_copy

        def sl(at, size=16):
            return pl.ds(pl.multiple_of(at, 16), size)

        def free(kind, u):
            @pl.when(u >= 2)
            def _():
                copy(kind, u - 2).wait_send()

        @pl.when(t < chunks)
        def _():
            for first, here, there in self.operands:

                @pl.when(t == first)
                def _(here=here, there=there):
                    here.wait()
                    there.wait_recv()

            slot = t % 2
            cols = pl.ds(pl.multiple_of(t * 128, 128), 128)
            g[slot] = mm(self.a[:, cols], self.b[...], TN)
            free(0, t)
            free(1, t)
            self.sa1[slot] = g[slot, sl((1 - x) * 32, 32)].astype(bf16)
            copy(0, t).start()
            self.sb1[slot, 0:16] = g[slot, sl(64 + (1 - y) * 16)].astype(bf16)
            self.sb1[slot, 16:32] = g[slot, sl(96 + (1 - y) * 16)].astype(bf16)
            copy(1, t).start()

        @pl.when((t >= 1) & (t - 1 < chunks))
        def _():
            u = t - 1
            slot = u % 2
            copy(0, u).wait_recv()
            free(2, u)
            self.sa2[slot] = (
                g[slot, sl(x * 32 + (1 - y) * 16)] + ra1[u, sl((1 - y) * 16)].astype(f32)
            ).astype(bf16)
            copy(2, u).start()
            self.ka2[slot] = g[slot, sl(x * 32 + y * 16)] + ra1[u, sl(y * 16)].astype(f32)
            copy(1, u).wait_recv()
            free(3, u)
            self.sb2[slot] = (
                g[slot, sl(64 + (1 - x) * 32 + y * 16)] + rb1[u, sl((1 - x) * 16)].astype(f32)
            ).astype(bf16)
            copy(3, u).start()
            self.kb2[slot] = g[slot, sl(64 + x * 32 + y * 16)] + rb1[u, sl(x * 16)].astype(f32)

        @pl.when((t >= 2) & (t - 2 < chunks))
        def _():
            u = t - 2
            slot = u % 2
            copy(2, u).wait_recv()
            copy(3, u).wait_recv()
            for k in (4, 5, 6):
                free(k, u)
            va = self.ka2[slot] + self.ra2[u].astype(f32)
            vb = self.kb2[slot] + self.rb2[u].astype(f32)
            self.f3[slot, 0] = va
            self.f3[slot, 1] = vb
            self.s3[slot, 0] = va.astype(bf16)
            self.s3[slot, 1] = vb.astype(bf16)
            for k in (4, 5, 6):
                copy(k, u).start()

        @pl.when((t >= 3) & (t - 3 < chunks))
        def _():
            u = t - 3
            slot = u % 2
            for k in (4, 5, 6):
                copy(k, u).wait_recv()
            mine = pl.ds(pl.multiple_of(z * self.shard, 128), self.shard)
            for part in (0, 1):
                total = self.f3[slot, part, :, mine]
                for k in range(3):
                    total = total + self.rz[u, k, part].astype(f32)
                self.out[c, u, part, x, y] = total.astype(bf16)

        for q, (_, b) in enumerate(self.groups):

            @pl.when(t == b - 1 + 3)
            def _(q=q):
                for kind in (0, 1, 2):
                    self.all_copy(q, kind).start()

            @pl.when(t == b - 1 + 4)
            def _(q=q):
                self.all_copy(q, 0).wait_recv()
                self.all_copy(q, 3).start()
                self.all_copy(q, 5).start()
                self.all_copy(q, 1).wait_recv()
                self.all_copy(q, 4).start()
                self.all_copy(q, 6).start()

            @pl.when(t == b - 1 + 5)
            def _(q=q):
                self.all_copy(q, 3).wait_recv()
                self.all_copy(q, 4).wait_recv()
                self.all_copy(q, 7).start()

    def steps(self):
        return self.chunks + 5

    def close(self):
        for q in range(len(self.groups)):
            for kind in (2, 5, 6, 7):
                self.all_copy(q, kind).wait_recv()
            for kind in range(8):
                self.all_copy(q, kind).wait_send()
        for u in (self.chunks - 2, self.chunks - 1):
            for kind in range(7):
                self.step_copy(kind, u).wait_send()
        for _, _, there in self.operands:
            there.wait_send()


class Smalls:
    SCRATCH = 5

    @staticmethod
    def scratch(v):
        dma = pltpu.SemaphoreType.DMA
        return [
            pltpu.VMEM((3,) + v.shape, f32),
            pltpu.VMEM((3,) + v.shape, f32),
            pltpu.VMEM((3,) + v.shape[1:], f32),
            dma((6,)),
            dma((6,)),
        ]

    def __init__(self, place, v_ref, out, scratch):
        self.s, self.z, self.c, self.x, self.y, self.near = place
        self.v, self.out = v_ref, out
        self.total, self.got, self.got_z, self.send, self.recv = scratch

    def copy(self, kind):
        if kind < 3:
            src = self.v if kind == 0 else self.total.at[kind - 1]
            dst, to = self.got.at[kind], "cxy"[kind]
        else:
            z = self.z
            k = kind - 2
            other = (z + 1 - 2 * (z % 2), z + 2 - 4 * (z // 2), 3 - z)[k - 1]
            src, dst, to = self.total.at[2, other], self.got_z.at[k - 1], "z%d" % k
        return pltpu.make_async_remote_copy(
            src_ref=src,
            dst_ref=dst,
            send_sem=self.send.at[kind],
            recv_sem=self.recv.at[kind],
            device_id=self.near[to],
            device_id_type=MESH,
        )

    def start(self):
        self.copy(0).start()

    def advance(self, kind):
        self.copy(kind).wait_recv()
        mine = self.v[...] if kind == 0 else self.total[kind - 1]
        self.total[kind] = mine + self.got[kind]
        for k in (kind + 1,) if kind < 2 else (3, 4, 5):
            self.copy(k).start()

    def close(self):
        total = self.total[2, self.z]
        for k in (3, 4, 5):
            self.copy(k).wait_recv()
            total = total + self.got_z[k - 3]
        self.out[...] = total
        for k in range(6):
            self.copy(k).wait_send()


def sums_kernel(
    conv_ref,
    nm_ref,
    og_ref,
    no_ref,
    v_ref,
    in_out,
    out_out,
    v_out,
    *scratch,
):
    place = around()
    cut = Products.SCRATCH
    inp = Products(place, [conv_ref], nm_ref, in_out, scratch[:cut])
    outp = Products(place, [og_ref], no_ref, out_out, scratch[cut : 2 * cut])
    small = Smalls(place, v_ref, v_out, scratch[2 * cut :])
    outp.load()
    inp.load()
    greet(place[-1])
    outp.share()
    small.start()
    inp.share()

    def first(t, carry):
        outp.step(t)
        return carry

    lax.fori_loop(0, outp.chunks, first, 0)

    def second(t, carry):
        inp.step(t)

        @pl.when(t < outp.steps() - outp.chunks)
        def _():
            outp.step(t + outp.chunks)

        for kind in range(3):

            @pl.when(t == 2 * kind + 1)
            def _(kind=kind):
                small.advance(kind)

        return carry

    lax.fori_loop(0, inp.steps(), second, 0)
    small.close()
    outp.close()
    inp.close()


def weight_sums(d_rest, nm, og, no, v, collective_id):
    vmem = pl.BlockSpec(memory_space=pltpu.VMEM)
    hbm = pl.BlockSpec(memory_space=pl.ANY)
    a_in, a_out, total = pl.pallas_call(
        sums_kernel,
        in_specs=[hbm] * 4 + [vmem],
        out_specs=[vmem] * 3,
        out_shape=[
            Products.out_shape([d_rest], nm),
            Products.out_shape([og], no),
            jax.ShapeDtypeStruct(v.shape[1:], f32),
        ],
        scratch_shapes=Products.scratch([d_rest], nm)
        + Products.scratch([og], no)
        + Smalls.scratch(v),
        compiler_params=pltpu.CompilerParams(
            collective_id=collective_id, has_side_effects=True, vmem_limit_bytes=VMEM_MOST
        ),
        cost_estimate=pl.CostEstimate(
            flops=6 * nm.shape[0] * nm.shape[1] * 6000, bytes_accessed=400_000_000, transcendentals=0
        ),
        name="weight_sums",
    )(d_rest, nm, og, no, v)
    return a_in.reshape(d_rest.shape[1], -1), a_out.reshape(og.shape[1], -1), total


LANES = 128
HALO = 16


def sigmoid(v):
    return 0.5 + 0.5 * jnp.tanh(0.5 * v)


def silu_parts(v):
    s = sigmoid(v)
    return v * s, s


def softplus(v):
    return jnp.maximum(v, 0.0) + jnp.log1p(jnp.exp(-jnp.abs(v)))


def lower_ones(t):
    i = lax.broadcasted_iota(jnp.int32, (t, t), 0)
    j = lax.broadcasted_iota(jnp.int32, (t, t), 1)
    return jnp.where(i >= j, 1.0, 0.0)


def exact(a, b, dims=NN):
    return lax.dot_general(a, b, dims, precision=highest, preferred_element_type=f32)


def head_columns(values, g):
    return pltpu.roll(values, (LANES - GROUP * g) % LANES, 1)[:, :GROUP]


class Exchange:
    def __init__(self, forward, own_low, got, t_low, t_got, u_low, u_got, p_low, p_got, send, recv):
        self.s, self.z, self.c, self.x, self.y, self.near = around()
        later = (lambda v: v) if forward else (lambda v: 1 - v)
        self.second = (later(self.c) == 1, later(self.x) == 1, later(self.y) == 1)
        self.own_low, self.got = own_low, got
        self.t_low, self.t_got, self.u_low, self.u_got = t_low, t_got, u_low, u_got
        self.p_low, self.p_got = p_low, p_got
        self.send, self.recv = send, recv
        self.n = t_low.shape[1] - 16
        self.half = t_low.shape[2]
        self.mine = pl.ds(pl.multiple_of(self.c * self.half, LANES), self.half)
        self.other = pl.ds(pl.multiple_of((1 - self.c) * self.half, LANES), self.half)

    def copy(self, kind, m):
        src, dst, to = (
            (self.own_low, self.got, "c"),
            (self.t_low, self.t_got, "x"),
            (self.u_low, self.u_got, "y"),
            (self.p_low, self.p_got, "c"),
        )[kind]
        return pltpu.make_async_remote_copy(
            src_ref=src.at[m],
            dst_ref=dst.at[m],
            send_sem=self.send.at[kind, m],
            recv_sem=self.recv.at[kind, m],
            device_id=self.near[to],
            device_id_type=MESH,
        )

    def put_decay(self, ref, m, lanes, decay):
        high = decay.astype(bf16).astype(f32)
        row = lax.broadcasted_iota(jnp.int32, (16, decay.shape[1]), 0)
        both = jnp.where(row == 0, high, jnp.where(row == 1, decay - high, 0.0))
        ref[m, pl.ds(self.n, 16), lanes] = both.astype(bf16)

    def decay_of(self, ref, m, lanes):
        rows = ref[m, pl.ds(self.n, 16), lanes].astype(f32)
        return rows[0:1] + rows[1:2]

    def put_own(self, m, lanes, state, decay):
        self.own_low[m, pl.ds(0, self.n), lanes] = state.astype(bf16)
        self.put_decay(self.own_low, m, lanes, decay)

    def core(self, m):
        self.copy(0, m).start()

    def along_x(self, m):
        self.copy(0, m).wait_recv()
        second = self.second[0]
        mine = self.own_low[m, pl.ds(0, self.n), self.mine].astype(f32)
        theirs = self.got[m, pl.ds(0, self.n), self.mine].astype(f32)
        d_mine = self.decay_of(self.own_low, m, self.mine)
        d_theirs = self.decay_of(self.got, m, self.mine)
        total = theirs * jnp.where(second, d_mine, 1.0) + mine * jnp.where(second, 1.0, d_theirs)
        self.t_low[m, pl.ds(0, self.n), :] = total.astype(bf16)
        self.put_decay(self.t_low, m, pl.ds(0, self.half), d_mine * d_theirs)
        self.copy(1, m).start()

    def along_y(self, m):
        self.copy(1, m).wait_recv()
        second = self.second[1]
        every = pl.ds(0, self.half)
        mine = self.t_low[m, pl.ds(0, self.n), :].astype(f32)
        theirs = self.t_got[m, pl.ds(0, self.n), :].astype(f32)
        d_mine = self.decay_of(self.t_low, m, every)
        d_theirs = self.decay_of(self.t_got, m, every)
        total = theirs * jnp.where(second, d_mine, 1.0) + mine * jnp.where(second, 1.0, d_theirs)
        self.u_low[m] = total.astype(bf16)
        self.copy(2, m).start()

    def back_to_core(self, m):
        self.copy(2, m).wait_recv()
        every = pl.ds(0, self.half)
        x_second = jnp.where(self.second[1], 1.0, 0.0)
        y_second = jnp.where(self.second[2], 1.0, 0.0)
        theirs = self.t_got[m, pl.ds(0, self.n), :].astype(f32)
        d_theirs = self.decay_of(self.t_got, m, every)
        over = y_second * jnp.where(self.second[1], d_theirs, 1.0)
        before = x_second * theirs + over * self.u_got[m].astype(f32)
        self.p_low[m] = before.astype(bf16)
        self.copy(3, m).start()

    def begin_state(self, m, out):
        self.copy(3, m).wait_recv()
        second = jnp.where(self.second[0], 1.0, 0.0)
        for lanes, before in (
            (self.mine, self.p_low[m].astype(f32)),
            (self.other, self.p_got[m].astype(f32)),
        ):
            d_theirs = self.decay_of(self.got, m, lanes)
            theirs = self.got[m, pl.ds(0, self.n), lanes].astype(f32)
            over = jnp.where(self.second[0], d_theirs, 1.0)
            out[m, :, lanes] = (before * over + second * theirs).astype(bf16)

    def sent(self):
        for m in range(self.own_low.shape[0]):
            for kind in range(4):
                self.copy(kind, m).wait_send()


def exchange_scratch(micro, n, inner):
    half = inner // 2
    dma = pltpu.SemaphoreType.DMA
    return [
        pltpu.VMEM((micro, n + 16, inner), bf16),
        pltpu.VMEM((micro, n + 16, inner), bf16),
        pltpu.VMEM((micro, n + 16, half), bf16),
        pltpu.VMEM((micro, n + 16, half), bf16),
        pltpu.VMEM((micro, n, half), bf16),
        pltpu.VMEM((micro, n, half), bf16),
        pltpu.VMEM((micro, n, half), bf16),
        pltpu.VMEM((micro, n, half), bf16),
        dma((4, micro)),
        dma((4, micro)),
    ]


EXCHANGE = 10
TICKS = (12, 3, 2, 2)


def steps_of(raw, shift, rate):
    t = raw.shape[0]
    dt = softplus(raw + shift)
    cum = exact(lower_ones(t), dt * rate)
    return dt, cum


def conv_rows(buf, cw, cb):
    taps = cw.shape[0]
    t = buf.shape[0] - HALO
    total = cb + buf[HALO - taps + 1 : HALO - taps + 1 + t, :] * cw[0:1]
    for k in range(1, taps):
        at = HALO - taps + 1 + k
        total = total + buf[at : at + t, :] * cw[k : k + 1]
    return total


def scan_forward_kernel(
    hs,
    conv_ref,
    raw_ref,
    cw_ref,
    cb_ref,
    shift_ref,
    rate_ref,
    skip_ref,
    ow_ref,
    x_ref,
    bc_ref,
    y_ref,
    low_ref,
    halo,
    begin_ref,
    others_ref,
    *scratch,
):
    buf, wide_buf, scores, dts, cums, rows_t, h_send, h_recv, o_send, o_recv = scratch[EXCHANGE:]
    ex = Exchange(True, *scratch[:EXCHANGE])
    s, z = ex.s, ex.z
    micro, t, channels = conv_ref.shape
    inner = x_ref.shape[2]
    n = begin_ref.shape[1]
    gc = GROUP * hs
    groups = inner // gc
    half_t = t // 2
    place = around()
    near = dict(place[-1])
    near["next"] = ((s + 1) % 8, z)
    near["last"] = ((s + 7) % 8, z)
    greet(near)
    weight = Gather(place, [(ow_ref, 0, others_ref, ow_ref.shape[0], 2)], o_send, o_recv)

    tail = [
        pltpu.make_async_remote_copy(
            src_ref=conv_ref.at[m, pl.ds(t - HALO, HALO)],
            dst_ref=halo.at[m],
            send_sem=h_send.at[m],
            recv_sem=h_recv.at[m],
            device_id=near["next"],
            device_id_type=MESH,
        )
        for m in range(micro)
    ]
    for copy in tail:
        copy.start()
    weight.fetch(0)
    weight.fetch(1)
    for m in range(micro):
        dt, cum = steps_of(raw_ref[m], shift_ref[...], rate_ref[...])
        dts[m] = dt
        cums[m] = cum
        rows_t[m] = cum.T
    for copy in tail:
        copy.wait_recv()
    has_prior = jnp.where(s > 0, 1.0, 0.0)

    def activate(m, lanes, into):
        into[0:HALO] = halo[m, :, lanes].astype(f32) * has_prior
        into[pl.ds(HALO, t)] = conv_ref[m, :, lanes].astype(f32)
        return silu_parts(conv_rows(into, cw_ref[:, lanes], cb_ref[:, lanes]))[0]

    def own_states(m, a, b):
        def body(g, carry):
            lanes = pl.ds(pl.multiple_of(g * gc, gc), gc)
            x = activate(m, lanes, buf).astype(bf16)
            x_ref[m, :, lanes] = x
            cum = head_columns(cums[m], g)
            to_end = head_columns(dts[m], g) * jnp.exp(cum[t - 1 :] - cum)
            weighted = (x.astype(f32) * widen(to_end, hs)).astype(bf16)
            state = mm(bc_ref[m, :, 0:n], weighted, TN)
            ex.put_own(m, lanes, state, widen(jnp.exp(cum[t - 1 :]), hs))
            return carry

        lax.fori_loop(a, b, body, 0)

    def local_scans(m, a, b):
        lane = lax.broadcasted_iota(jnp.int32, (half_t, 2 * hs), 1)

        def body(g, carry):
            lanes = pl.ds(pl.multiple_of(g * gc, gc), gc)
            cum = head_columns(cums[m], g)
            rows = rows_t[m, pl.ds(pl.multiple_of(g * GROUP, GROUP), GROUP), :]
            dt_wide = widen(head_columns(dts[m], g), hs)
            weighted = (x_ref[m, :, lanes].astype(f32) * dt_wide).astype(bf16)
            for k in range(0, GROUP, 2):
                pair = weighted[:, k * hs : (k + 2) * hs]
                at = pl.ds(pl.multiple_of(g * gc + k * hs, 2 * hs), 2 * hs)
                top, low = [], []
                for h in (k, k + 1):
                    col, row = cum[:, h : h + 1], rows[h : h + 1, :]
                    m1 = jnp.exp(jnp.minimum(col[:half_t] - row[:, :half_t], 0.0))
                    m2 = jnp.exp(jnp.minimum(col[half_t:] - row, 0.0))
                    m1 = (m1 * scores[m, :half_t, :half_t]).astype(bf16)
                    m2 = (m2 * scores[m, half_t:, :]).astype(bf16)
                    top.append(mm(m1, pair[:half_t]))
                    low.append(mm(m2, pair))
                y_ref[m, :half_t, at] = jnp.where(lane < hs, top[0], top[1])
                y_ref[m, half_t:, at] = jnp.where(lane < hs, low[0], low[1])
            return carry

        lax.fori_loop(a, b, body, 0)

    def carried(m):
        def body(g, carry):
            lanes = pl.ds(pl.multiple_of(g * gc, gc), gc)
            decay = widen(jnp.exp(head_columns(cums[m], g)), hs)
            scan = y_ref[m, :, lanes] + decay * mm(bc_ref[m, :, n:], begin_ref[m, :, lanes])
            y_ref[m, :, lanes] = scan
            x = x_ref[m, :, lanes].astype(f32)
            low_ref[m, :, lanes] = (scan + skip_ref[:, lanes] * x).astype(bf16)
            return carry

        lax.fori_loop(0, groups, body, 0)

    for m in range(micro):
        lanes = pl.ds(inner, channels - inner)
        bc = activate(m, lanes, wide_buf).astype(bf16)
        bc_ref[m] = bc
        scores[m] = mm(bc[:, n:], bc[:, :n], NT) * lower_ones(t)
    middle = groups // 2
    own_states(0, 0, groups)
    ex.core(0)
    own_states(1, 0, middle)
    ex.along_x(0)
    own_states(1, middle, groups)
    ex.core(1)
    weight.begin(0)
    local_scans(0, 0, middle)
    ex.along_x(1)
    ex.along_y(0)
    weight.begin(1)
    local_scans(0, middle, groups)
    weight.middle(0)
    local_scans(1, 0, middle)
    ex.along_y(1)
    ex.back_to_core(0)
    weight.middle(1)
    local_scans(1, middle, groups)
    ex.begin_state(0, begin_ref)
    carried(0)
    ex.back_to_core(1)
    weight.finish(0)
    weight.finish(1)
    ex.begin_state(1, begin_ref)
    carried(1)
    weight.close()
    ex.sent()
    for copy in tail:
        copy.wait_send()


def scan_forward(
    conv_low, raw, conv_w, conv_b, shift, rate, skip_wide, out_weight, inner, hs, collective_id
):
    micro, t, channels = conv_low.shape
    n = (channels - inner) // 2
    gc = GROUP * hs
    dma = pltpu.SemaphoreType.DMA
    vmem = pl.BlockSpec(memory_space=pltpu.VMEM)
    hbm = pl.BlockSpec(memory_space=pl.ANY)
    return pl.pallas_call(
        partial(scan_forward_kernel, hs),
        in_specs=[vmem] * 7 + [hbm],
        out_specs=[vmem] * 6 + [hbm],
        out_shape=[
            jax.ShapeDtypeStruct((micro, t, inner), bf16),
            jax.ShapeDtypeStruct((micro, t, 2 * n), bf16),
            jax.ShapeDtypeStruct((micro, t, inner), f32),
            jax.ShapeDtypeStruct((micro, t, inner), bf16),
            jax.ShapeDtypeStruct((micro, HALO, channels), bf16),
            jax.ShapeDtypeStruct((micro, n, inner), bf16),
            jax.ShapeDtypeStruct((3,) + out_weight.shape, bf16),
        ],
        scratch_shapes=exchange_scratch(micro, n, inner)
        + [
            pltpu.VMEM((HALO + t, gc), f32),
            pltpu.VMEM((HALO + t, 2 * n), f32),
            pltpu.VMEM((micro, t, t), f32),
            pltpu.VMEM((micro, t, LANES), f32),
            pltpu.VMEM((micro, t, LANES), f32),
            pltpu.VMEM((micro, LANES, t), f32),
            dma((micro,)),
            dma((micro,)),
            dma((2, CHUNK_DMAS)),
            dma((2, CHUNK_DMAS)),
        ],
        compiler_params=pltpu.CompilerParams(
            collective_id=collective_id, has_side_effects=True, vmem_limit_bytes=VMEM_MOST
        ),
        cost_estimate=pl.CostEstimate(
            flops=4 * micro * t * inner * (t + 3 * n), bytes_accessed=100_000_000, transcendentals=0
        ),
        name="scan_forward",
    )(conv_low, raw, conv_w, conv_b, shift, rate, skip_wide, out_weight)


def scan_backward_kernel(
    hs,
    dy_ref,
    x_ref,
    bc_ref,
    y_ref,
    begin_ref,
    raw_ref,
    conv_ref,
    halo_ref,
    cw_ref,
    cb_ref,
    shift_ref,
    rate_ref,
    skip_ref,
    dgate_ref,
    norm_ref,
    dconv_ref,
    dcw_ref,
    dcb_ref,
    heads_ref,
    sum_ref,
    *scratch,
):
    (
        y_now,
        y_sem,
        buf,
        wide_buf,
        scores,
        total,
        dts,
        cums,
        rows_t,
        ends,
        dxl,
        dbc,
        ddt_sum,
        dcum_sum,
        last_sum,
        head_low,
        next_low,
        h_send,
        h_recv,
    ) = scratch[EXCHANGE : EXCHANGE + 19]
    ex = Exchange(False, *scratch[:EXCHANGE])
    s, z = ex.s, ex.z
    micro, t, channels = conv_ref.shape
    inner = x_ref.shape[2]
    n = begin_ref.shape[1]
    gc = GROUP * hs
    groups = inner // gc
    half = t // 2
    taps = cw_ref.shape[0]
    place = around()
    near = dict(place[-1])
    near["next"] = ((s + 1) % 8, z)
    near["last"] = ((s + 7) % 8, z)
    sums_of = Products(place, [dgate_ref], norm_ref, sum_ref, scratch[EXCHANGE + 19 :])
    sums_of.load()

    def y_copy(i):
        lanes = pl.ds(pl.multiple_of((i % groups) * gc, gc), gc)
        slot = i % 2
        return pltpu.make_async_copy(y_ref.at[i // groups, :, lanes], y_now.at[slot], y_sem.at[slot])

    greet(near)
    sums_of.share()
    first_rows = [
        pltpu.make_async_remote_copy(
            src_ref=head_low.at[m],
            dst_ref=next_low.at[m],
            send_sem=h_send.at[m],
            recv_sem=h_recv.at[m],
            device_id=near["last"],
            device_id_type=MESH,
        )
        for m in range(micro)
    ]
    has_prior = jnp.where(s > 0, 1.0, 0.0)
    has_next = jnp.where(s < 7, 1.0, 0.0)

    middle = groups // 2

    def at_step(i, *todo):
        for when, what in todo:
            pl.when(i == when)(what)

    def own_states():
        def body(i, carry):
            m, g = i // groups, i % groups
            lanes = pl.ds(pl.multiple_of(g * gc, gc), gc)
            cum = head_columns(cums[m], g)
            weighted = (dy_ref[m, :, lanes].astype(f32) * widen(jnp.exp(cum), hs)).astype(bf16)
            state = mm(bc_ref[m, :, n:], weighted, TN)
            ex.put_own(m, lanes, state, widen(jnp.exp(cum[t - 1 :]), hs))
            at_step(
                i,
                (groups - 1, lambda: ex.core(0)),
                (groups + middle, lambda: ex.along_x(0)),
                (2 * groups - 1, lambda: ex.core(1)),
            )
            tick(i, TICKS[0], 0)
            return carry

        lax.fori_loop(0, 2 * groups, body, 0)

    def tick(i, every, first):
        @pl.when(i % every == every - 1)
        def _():
            sums_of.step(first + i // every)

    def upper_ones():
        j = lax.broadcasted_iota(jnp.int32, (t, t), 0)
        i = lax.broadcasted_iota(jnp.int32, (t, t), 1)
        return jnp.where(i >= j, 1.0, 0.0)

    def local_terms():
        lane = lax.broadcasted_iota(jnp.int32, (t, 2 * hs), 1)
        lane_half = lax.broadcasted_iota(jnp.int32, (half, 2 * hs), 1)

        def body(i, carry):
            m, g = i // groups, i % groups
            lanes = pl.ds(pl.multiple_of(g * gc, gc), gc)
            cum = head_columns(cums[m], g)
            rows = rows_t[m, pl.ds(pl.multiple_of(g * GROUP, GROUP), GROUP), :]
            dt_wide = widen(head_columns(dts[m], g), hs)
            weighted = (x_ref[m, :, lanes].astype(f32) * dt_wide).astype(bf16)
            for k in range(0, GROUP, 2):
                pair = weighted[:, k * hs : (k + 2) * hs]
                at = pl.ds(pl.multiple_of(g * gc + k * hs, 2 * hs), 2 * hs)
                dy = dy_ref[m, :, at]
                top, low = [], []
                for h in (k, k + 1):
                    col, row = cum[:, h : h + 1], rows[h : h + 1, :]
                    mine = jnp.where(lane < hs, pair, 0) if h == k else jnp.where(lane < hs, 0, pair)
                    l1 = jnp.exp(jnp.minimum(row - col[:half], 0.0))
                    l2 = jnp.exp(jnp.minimum(row[:, half:] - col[half:], 0.0))
                    total[:half, :] += l1 * mm(mine[:half], dy, NT)
                    total[half:, half:] += l2 * mm(mine[half:], dy[half:], NT)
                    top.append(mm((l1 * scores[m, :half, :]).astype(bf16), dy))
                    low.append(mm((l2 * scores[m, half:, half:]).astype(bf16), dy[half:]))
                dxl[m, :half, at] = jnp.where(lane_half < hs, top[0], top[1])
                dxl[m, half:, at] = jnp.where(lane_half < hs, low[0], low[1])
            at_step(
                i,
                (1, lambda: ex.along_x(1)),
                (3, lambda: ex.along_y(0)),
                (groups - 1, lambda: local_close(0)),
                (groups + 1, lambda: ex.along_y(1)),
                (groups + 3, lambda: ex.back_to_core(0)),
                (2 * groups - 1, lambda: local_close(1)),
            )
            tick(i, TICKS[1], 2 * groups // TICKS[0])
            return carry

        lax.fori_loop(0, 2 * groups, body, 0)

    def local_close(m):
        d = total[...] * upper_ones()
        dbc[m, :, 0:n] = mm(d.astype(bf16), bc_ref[m, :, n:])
        dbc[m, :, n:] = mm(d.T.astype(bf16), bc_ref[m, :, :n])
        total[...] = jnp.zeros_like(total)

    def through_states():
        r = lax.broadcasted_iota(jnp.int32, (gc, LANES), 0)
        col = lax.broadcasted_iota(jnp.int32, (gc, LANES), 1)

        def clear():
            ddt_sum[...] = jnp.zeros_like(ddt_sum)
            dcum_sum[...] = jnp.zeros_like(dcum_sum)
            last_sum[...] = jnp.zeros_like(last_sum)

        def close(m):
            d_log = exact(upper_ones(), dcum_sum[...]) + last_sum[0:1]
            v = raw_ref[m] + shift_ref[...]
            d_dt = (ddt_sum[...] + d_log * rate_ref[...]) / (1.0 + jnp.exp(-v))
            rest = dconv_ref.shape[2] - channels - LANES
            dconv_ref[m, :, pl.ds(channels, LANES)] = d_dt.astype(bf16)
            if rest:
                dconv_ref[m, :, pl.ds(channels + LANES, rest)] = jnp.zeros((t, rest), bf16)
            heads_ref[0:1] += jnp.sum(d_dt, axis=0, keepdims=True)
            heads_ref[1:2] += jnp.sum(d_log * dts[m], axis=0, keepdims=True) * rate_ref[...]
            first_slopes(m)
            if m == 0:
                clear()
                ex.begin_state(1, ends)

        def body(i, carry):
            m, g = i // groups, i % groups
            lanes = pl.ds(pl.multiple_of(g * gc, gc), gc)

            @pl.when(i + 1 < 2 * groups)
            def _():
                y_copy(i + 1).start()

            y_copy(i).wait()
            ones = jnp.where(r // hs + g * GROUP == col, 1.0, 0.0).astype(bf16)
            cum = head_columns(cums[m], g)
            dt_wide = widen(head_columns(dts[m], g), hs)
            x, dy = x_ref[m, :, lanes].astype(f32), dy_ref[m, :, lanes].astype(f32)
            weighted = (x * dt_wide).astype(bf16).astype(f32)
            decay = widen(jnp.exp(cum), hs)
            to_end = widen(jnp.exp(cum[t - 1 :] - cum), hs)
            s_in, ds = begin_ref[m, :, lanes], ends[m, :, lanes]
            through = to_end * mm(bc_ref[m, :, 0:n], ds)
            d_weighted = dxl[m, :, lanes] + through
            dconv_ref[m, :, lanes] = (dt_wide * d_weighted + skip_ref[:, lanes] * dy).astype(bf16)
            dbc[m, :, 0:n] += mm((weighted * to_end).astype(bf16), ds, NT)
            dbc[m, :, n:] += mm((dy * decay).astype(bf16), s_in, NT)
            ddt_sum[...] += head_sums(x * d_weighted, ones)
            dcum_sum[...] += head_sums(dy * y_now[i % 2] - weighted * d_weighted, ones)
            at_end = jnp.sum(weighted * through, axis=0, keepdims=True) + decay[t - 1 :] * jnp.sum(
                s_in.astype(f32) * ds.astype(f32), axis=0, keepdims=True
            )
            last_sum[...] += head_sums(jnp.broadcast_to(at_end, (8, gc)), ones)
            by_skip = jnp.sum(x * dy, axis=0, keepdims=True)
            heads_ref[2:3] += head_sums(jnp.broadcast_to(by_skip, (8, gc)), ones)[0:1]
            at_step(i, (groups - 1, lambda: close(0)), (2 * groups - 1, lambda: close(1)))
            tick(i, TICKS[2], 2 * groups // TICKS[0] + 2 * groups // TICKS[1])
            return carry

        clear()
        heads_ref[...] = jnp.zeros_like(heads_ref)
        y_copy(0).start()
        lax.fori_loop(0, 2 * groups, body, 0)

    def pre_slope(into, lanes, grad, rows):
        v = conv_rows(into[0 : HALO + rows, :], cw_ref[:, lanes], cb_ref[:, lanes])
        sig = sigmoid(v)
        return grad * (sig * (1.0 + v * (1.0 - sig)))

    def load(m, lanes, into, rows):
        into[0:HALO] = halo_ref[m, :, lanes].astype(f32) * has_prior
        into[HALO : HALO + rows] = conv_ref[m, 0:rows, lanes].astype(f32)

    def first_slopes(m):
        def one(lanes, into, grad):
            load(m, lanes, into, HALO)
            head_low[m, :, lanes] = pre_slope(into, lanes, grad, HALO).astype(bf16)

        def body(g, carry):
            lanes = pl.ds(pl.multiple_of(g * gc, gc), gc)
            one(lanes, buf, dconv_ref[m, 0:HALO, lanes].astype(f32))
            return carry

        lax.fori_loop(0, groups, body, 0)
        one(pl.ds(inner, channels - inner), wide_buf, dbc[m, 0:HALO, :])
        first_rows[m].start()

    def conv_back():
        def one(m, lanes, into, grad):
            load(m, lanes, into, t)
            slope = pre_slope(into, lanes, grad, t)
            weights = cw_ref[:, lanes]
            lines = []
            for k in range(taps):
                at = HALO - taps + 1 + k
                lines.append(jnp.sum(slope * into[at : at + t, :], axis=0, keepdims=True))
            dcw_ref[:, lanes] += jnp.concatenate(lines, axis=0)
            dcb_ref[:, lanes] += jnp.sum(slope, axis=0, keepdims=True)
            into[0:t] = slope
            into[t : t + HALO] = next_low[m, :, lanes].astype(f32) * has_next
            back = into[taps - 1 : taps - 1 + t, :] * weights[0:1]
            for k in range(1, taps):
                at = taps - 1 - k
                back = back + into[at : at + t, :] * weights[k : k + 1]
            dconv_ref[m, :, lanes] = back.astype(bf16)

        def body(i, carry):
            m, g = i // groups, i % groups
            lanes = pl.ds(pl.multiple_of(g * gc, gc), gc)
            one(m, lanes, buf, dconv_ref[m, :, lanes].astype(f32))
            at_step(i, (groups - 1, lambda: first_rows[1].wait_recv()))
            tick(i, TICKS[3], 2 * groups // TICKS[0] + 2 * groups // TICKS[1] + 2 * groups // TICKS[2])
            return carry

        first_rows[0].wait_recv()
        lax.fori_loop(0, 2 * groups, body, 0)
        for m in range(micro):
            one(m, pl.ds(inner, channels - inner), wide_buf, dbc[m])

    for m in range(micro):
        dt, cum = steps_of(raw_ref[m], shift_ref[...], rate_ref[...])
        dts[m] = dt
        cums[m] = cum
        rows_t[m] = cum.T
        scores[m] = mm(bc_ref[m, :, 0:n], bc_ref[m, :, n:], NT) * upper_ones()
    dcw_ref[...] = jnp.zeros_like(dcw_ref)
    dcb_ref[...] = jnp.zeros_like(dcb_ref)
    total[...] = jnp.zeros_like(total)
    own_states()
    local_terms()
    ex.begin_state(0, ends)
    ex.back_to_core(1)
    through_states()
    conv_back()
    done = sum(2 * groups // every for every in TICKS)

    def rest_of(i, carry):
        sums_of.step(i)
        return carry

    lax.fori_loop(done, sums_of.steps(), rest_of, 0)
    ex.sent()
    for copy in first_rows:
        copy.wait_send()
    sums_of.close()


def scan_backward(
    dy,
    x,
    bc,
    y,
    begin,
    raw,
    conv_low,
    halo,
    conv_w,
    conv_b,
    shift,
    rate,
    skip_wide,
    d_gate,
    normed,
    hs,
    collective_id,
):
    micro, t, channels = conv_low.shape
    inner = x.shape[2]
    n = begin.shape[1]
    gc = GROUP * hs
    taps = conv_w.shape[0]
    dma = pltpu.SemaphoreType.DMA
    vmem = pl.BlockSpec(memory_space=pltpu.VMEM)
    hbm = pl.BlockSpec(memory_space=pl.ANY)
    return pl.pallas_call(
        partial(scan_backward_kernel, hs),
        in_specs=[vmem] * 3 + [hbm] + [vmem] * 9 + [hbm] * 2,
        out_specs=[vmem] * 5,
        out_shape=[
            jax.ShapeDtypeStruct((micro, t, -(-(channels + LANES) // 256) * 256), bf16),
            jax.ShapeDtypeStruct((taps, channels), f32),
            jax.ShapeDtypeStruct((1, channels), f32),
            jax.ShapeDtypeStruct((8, LANES), f32),
            Products.out_shape([d_gate], normed),
        ],
        scratch_shapes=exchange_scratch(micro, n, inner)
        + [
            pltpu.VMEM((2, t, gc), f32),
            dma((2,)),
            pltpu.VMEM((HALO + t, gc), f32),
            pltpu.VMEM((HALO + t, 2 * n), f32),
            pltpu.VMEM((micro, t, t), f32),
            pltpu.VMEM((t, t), f32),
            pltpu.VMEM((micro, t, LANES), f32),
            pltpu.VMEM((micro, t, LANES), f32),
            pltpu.VMEM((micro, LANES, t), f32),
            pltpu.VMEM((micro, n, inner), bf16),
            pltpu.VMEM((micro, t, inner), f32),
            pltpu.VMEM((micro, t, 2 * n), f32),
            pltpu.VMEM((t, LANES), f32),
            pltpu.VMEM((t, LANES), f32),
            pltpu.VMEM((8, LANES), f32),
            pltpu.VMEM((micro, HALO, channels), bf16),
            pltpu.VMEM((micro, HALO, channels), bf16),
            dma((micro,)),
            dma((micro,)),
        ]
        + Products.scratch([d_gate], normed),
        compiler_params=pltpu.CompilerParams(
            collective_id=collective_id, has_side_effects=True, vmem_limit_bytes=VMEM_MOST
        ),
        cost_estimate=pl.CostEstimate(
            flops=8 * micro * t * inner * (t + 3 * n), bytes_accessed=100_000_000, transcendentals=0
        ),
        name="scan_backward",
    )(
        dy,
        x,
        bc,
        y,
        begin,
        raw,
        conv_low,
        halo,
        conv_w,
        conv_b,
        shift,
        rate,
        skip_wide,
        d_gate,
        normed,
    )


def shard_place(k, depth):
    z = lax.axis_index("wshard")
    other = (z, z + 1 - 2 * (z % 2), z + 2 - 4 * (z // 2), 3 - z)[k]
    return pl.ds(pl.multiple_of(other * depth, 128), depth)


def front_kernel(h_ref, g_ref, dtw_ref, v_ref, conv_ref, norm_ref, raw_ref, rel):
    depth = v_ref.shape[2]

    @pl.when(pl.program_id(0) == 0)
    def _():
        h = h_ref[...].astype(f32)
        power = jnp.mean(h * h, axis=-1, keepdims=True)
        normed = (h * lax.rsqrt(power + epsilon) * g_ref[...]).astype(bf16)
        norm_ref[...] = normed
        raw_ref[...] = mm(normed, dtw_ref[...], NT).astype(bf16).astype(f32)
        for k in range(4):
            rel[:, k * depth : (k + 1) * depth] = norm_ref[:, shard_place(k, depth)]

    weights = jnp.concatenate([v_ref[k] for k in (3, 0, 1, 2)], axis=1)
    conv_ref[...] = mm(rel[...], weights, NT).astype(bf16)


def front(hidden, gain, dt_w, shards, tile):
    rows, width = hidden.shape
    _, count, depth = shards.shape
    whole = pl.BlockSpec((rows, width), lambda i: (0, 0))
    return pl.pallas_call(
        front_kernel,
        grid=(count // tile,),
        in_specs=[
            whole,
            pl.BlockSpec((1, width), lambda i: (0, 0)),
            pl.BlockSpec((LANES, width), lambda i: (0, 0)),
            pl.BlockSpec((4, tile, depth), lambda i: (0, i, 0)),
        ],
        out_specs=[
            pl.BlockSpec((rows, tile), lambda i: (0, i)),
            whole,
            pl.BlockSpec((rows, LANES), lambda i: (0, 0)),
        ],
        out_shape=[
            jax.ShapeDtypeStruct((rows, count), bf16),
            jax.ShapeDtypeStruct((rows, width), bf16),
            jax.ShapeDtypeStruct((rows, LANES), f32),
        ],
        scratch_shapes=[pltpu.VMEM((rows, width), bf16)],
        compiler_params=pltpu.CompilerParams(vmem_limit_bytes=VMEM),
        name="front",
    )(hidden, gain, dt_w, shards)


def gate_kernel(
    scan_ref,
    norm_ref,
    w_ref,
    v_ref,
    gain_ref,
    ow_ref,
    ov_ref,
    h_ref,
    og_ref,
    valid_ref,
    no_ref,
    out_ref,
    g_ref,
    dy_ref,
    dgate_ref,
    dgain_ref,
    gate,
    d_no,
    branch,
):
    inner = scan_ref.shape[1]
    depth = w_ref.shape[1]
    block = ow_ref.shape[0]
    rows = scan_ref.shape[0]

    @pl.when(pl.program_id(0) == 0)
    def _():
        dgain_ref[...] = jnp.zeros_like(dgain_ref)

    rel = jnp.concatenate([norm_ref[:, shard_place(k, depth)] for k in range(4)], axis=1)
    valid = valid_ref[...]
    g_low = (og_ref[...].astype(f32) * valid).astype(bf16)
    g_ref[...] = g_low
    power = jnp.zeros((rows, 1), f32)
    for i in range(4):
        at = slice(i * block, (i + 1) * block)
        weights = jnp.concatenate([w_ref[at, :]] + [v_ref[k, at, :] for k in range(3)], axis=1)
        value = mm(rel, weights, NT)
        gate[:, at] = value
        act, _ = silu_parts(value)
        u = scan_ref[:, at].astype(f32) * act
        power += jnp.sum(u * u, axis=-1, keepdims=True)
    scale = lax.rsqrt(power / inner + epsilon)
    along = jnp.zeros((rows, 1), f32)
    for k in range(4):
        at = shard_place(k, block)
        weights = ow_ref[...] if k == 0 else ov_ref[k - 1]
        act, _ = silu_parts(gate[:, at])
        u = scan_ref[:, at].astype(f32) * act
        normed = u * scale
        low = (normed * gain_ref[:, at]).astype(bf16)
        no_ref[:, at] = low
        if k == 0:
            branch[...] = mm(low, weights)
        else:
            branch[...] += mm(low, weights)
        d = mm(g_low, weights, NT)
        dgain_ref[:, at] += jnp.sum(d * normed, axis=0, keepdims=True)
        d = d * gain_ref[:, at]
        d_no[:, at] = d
        along += jnp.sum(d * u, axis=-1, keepdims=True)
    out_ref[...] = (h_ref[...].astype(f32) + valid * branch[...]).astype(bf16)
    along = along * scale * scale * scale / inner
    for i in range(4):
        at = slice(i * block, (i + 1) * block)
        value = gate[:, at]
        act, sig = silu_parts(value)
        v = scan_ref[:, at].astype(f32)
        d_u = scale * d_no[:, at] - v * act * along
        dy_ref[:, at] = (d_u * act).astype(bf16)
        dgate_ref[:, at] = (d_u * v * (sig * (1.0 + value * (1.0 - sig)))).astype(bf16)


def gate_stage(scanned, normed, own, others, gain, out_own, out_others, hidden, out_grad, valid, tile):
    rows, width = hidden.shape
    _, inner, depth = others.shape
    once = pl.Buffered(1)
    wide = pl.BlockSpec((tile, inner), lambda i: (i, 0))
    slim = pl.BlockSpec((tile, width), lambda i: (i, 0))
    line = pl.BlockSpec((1, inner), lambda i: (0, 0))
    return pl.pallas_call(
        gate_kernel,
        grid=(rows // tile,),
        in_specs=[
            wide,
            slim,
            pl.BlockSpec((inner, depth), lambda i: (0, 0), pipeline_mode=once),
            pl.BlockSpec(others.shape, lambda i: (0, 0, 0), pipeline_mode=once),
            line,
            pl.BlockSpec(out_own.shape, lambda i: (0, 0), pipeline_mode=once),
            pl.BlockSpec(out_others.shape, lambda i: (0, 0, 0), pipeline_mode=once),
            slim,
            slim,
            pl.BlockSpec((tile, 1), lambda i: (i, 0)),
        ],
        out_specs=[wide, slim, slim, wide, wide, line],
        out_shape=[
            jax.ShapeDtypeStruct((rows, inner), bf16),
            jax.ShapeDtypeStruct((rows, width), bf16),
            jax.ShapeDtypeStruct((rows, width), bf16),
            jax.ShapeDtypeStruct((rows, inner), bf16),
            jax.ShapeDtypeStruct((rows, inner), bf16),
            jax.ShapeDtypeStruct((1, inner), f32),
        ],
        scratch_shapes=[
            pltpu.VMEM((tile, inner), f32),
            pltpu.VMEM((tile, inner), f32),
            pltpu.VMEM((tile, width), f32),
        ],
        compiler_params=pltpu.CompilerParams(vmem_limit_bytes=VMEM_MOST),
        name="gate_stage",
    )(scanned, normed, own, others, gain, out_own, out_others, hidden, out_grad, valid)


def back_kernel(
    steps,
    d_ref,
    e_ref,
    dt_ref,
    dtw_ref,
    w_ref,
    v_ref,
    cv_ref,
    h_ref,
    g_ref,
    og_ref,
    out_ref,
    dg_ref,
    acc,
    full,
):
    depth = w_ref.shape[1]
    i = pl.program_id(0)

    def product(ref, *shards):
        return mm(ref[...], jnp.concatenate(shards, axis=1))

    gate_shards = [w_ref] + [v_ref.at[k] for k in range(3)]
    conv_shards = [cv_ref.at[k] for k in (3, 0, 1, 2)]

    @pl.when(i == 0)
    def _():
        acc[...] = product(d_ref, *[r[...] for r in gate_shards])

    @pl.when((i > 0) & (i < steps))
    def _():
        acc[...] += product(d_ref, *[r[...] for r in gate_shards])

    @pl.when(i >= steps)
    def _():
        acc[...] += product(e_ref, *[r[...] for r in conv_shards])

    @pl.when(i == pl.num_programs(0) - 1)
    def _():
        for k in range(4):
            full[:, shard_place(k, depth)] = acc[:, k * depth : (k + 1) * depth]
        tile = 128
        gain = g_ref[...]
        d_gain = jnp.zeros(gain.shape, f32)
        for r in range(full.shape[0] // tile):
            at = slice(r * tile, (r + 1) * tile)
            d = full[at, :] + mm(dt_ref[at, :], dtw_ref[...])
            h = h_ref[at, :].astype(f32)
            scale = lax.rsqrt(jnp.mean(h * h, axis=-1, keepdims=True) + epsilon)
            d_gain += jnp.sum(d * (h * scale), axis=0, keepdims=True)
            d = d * gain
            along = jnp.mean(d * h, axis=-1, keepdims=True) * (scale * scale * scale)
            out_ref[at, :] = (scale * d - h * along + og_ref[at, :].astype(f32)).astype(bf16)
        dg_ref[...] = d_gain


def back_stage(d, e, dt_w, gate_own, gate_others, shards, hidden, gain, out_grad, tiles):
    rows, width = hidden.shape
    _, count, depth = shards.shape
    inner = d.shape[1]
    steps, more = inner // tiles[0], count // tiles[1]
    whole = pl.BlockSpec((rows, width), lambda i: (0, 0))
    line = pl.BlockSpec((1, width), lambda i: (0, 0))

    def early(i):
        return jnp.minimum(i, steps - 1)

    def late(i):
        return jnp.maximum(i - steps, 0)

    return pl.pallas_call(
        partial(back_kernel, steps),
        grid=(steps + more,),
        in_specs=[
            pl.BlockSpec((rows, tiles[0]), lambda i: (0, early(i))),
            pl.BlockSpec((rows, tiles[1]), lambda i: (0, late(i))),
            pl.BlockSpec((rows, LANES), lambda i: (0, count // LANES)),
            pl.BlockSpec((LANES, width), lambda i: (0, 0)),
            pl.BlockSpec((tiles[0], depth), lambda i: (early(i), 0)),
            pl.BlockSpec((3, tiles[0], depth), lambda i: (0, early(i), 0)),
            pl.BlockSpec((4, tiles[1], depth), lambda i: (0, late(i), 0)),
            whole,
            line,
            whole,
        ],
        out_specs=[whole, line],
        out_shape=[
            jax.ShapeDtypeStruct((rows, width), bf16),
            jax.ShapeDtypeStruct((1, width), f32),
        ],
        scratch_shapes=[pltpu.VMEM((rows, width), f32), pltpu.VMEM((rows, width), f32)],
        compiler_params=pltpu.CompilerParams(vmem_limit_bytes=VMEM_MOST),
        name="back_stage",
    )(d, e, e, dt_w, gate_own, gate_others, shards, hidden, gain, out_grad)


def project_kernel(n_ref, w_ref, v_ref, o_ref):
    total = mm(n_ref[0], w_ref[...], NT)
    for k in range(1, n_ref.shape[0]):
        total += mm(n_ref[k], v_ref[k - 1], NT)
    o_ref[...] = total.astype(o_ref.dtype)


def project(parts, own, others, first, count, tile, dtype):
    shards, rows, depth = parts.shape
    return pl.pallas_call(
        project_kernel,
        grid=(count // tile,),
        in_specs=[
            pl.BlockSpec((shards, rows, depth), lambda i: (0, 0, 0)),
            pl.BlockSpec((tile, depth), lambda i: (first // tile + i, 0)),
            pl.BlockSpec((shards - 1, tile, depth), lambda i: (0, first // tile + i, 0)),
        ],
        out_specs=pl.BlockSpec((rows, tile), lambda i: (0, i)),
        out_shape=jax.ShapeDtypeStruct((rows, count), dtype),
        compiler_params=pltpu.CompilerParams(vmem_limit_bytes=VMEM),
        name="project",
    )(parts, own, others)


def unproject_kernel(steps, d_ref, e_ref, w_ref, v_ref, o_ref):
    def add(ref):
        o_ref[0] += mm(ref[...], w_ref[...])
        for k in range(1, o_ref.shape[0]):
            o_ref[k] += mm(ref[...], v_ref[k - 1])

    @pl.when(pl.program_id(0) == 0)
    def _():
        o_ref[...] = jnp.zeros_like(o_ref)

    @pl.when(pl.program_id(0) < steps)
    def _():
        add(d_ref)

    @pl.when(pl.program_id(0) >= steps)
    def _():
        add(e_ref)


def unproject(d, e, own, others, tile):
    shards, count, depth = others.shape
    shards += 1
    rows = d.shape[0]
    steps = d.shape[1] // tile
    return pl.pallas_call(
        partial(unproject_kernel, steps),
        grid=(count // tile,),
        in_specs=[
            pl.BlockSpec((rows, tile), lambda i: (0, jnp.minimum(i, steps - 1))),
            pl.BlockSpec((rows, tile), lambda i: (0, jnp.maximum(i - steps, 0))),
            pl.BlockSpec((tile, depth), lambda i: (i, 0)),
            pl.BlockSpec((shards - 1, tile, depth), lambda i: (0, i, 0)),
        ],
        out_specs=pl.BlockSpec((shards, rows, depth), lambda i: (0, 0, 0)),
        out_shape=jax.ShapeDtypeStruct((shards, rows, depth), f32),
        compiler_params=pltpu.CompilerParams(vmem_limit_bytes=VMEM),
        name="unproject",
    )(d, e, own, others)


def rms_front(hidden_rows, gain):
    power = jnp.mean(hidden_rows * hidden_rows, axis=-1, keepdims=True)
    return hidden_rows * lax.rsqrt(power + epsilon) * gain


def conv_act(padded, conv_w, conv_b):
    taps = conv_w.shape[0]
    rows_out = padded.shape[1] - taps + 1
    total = conv_b + padded[:, 0:rows_out] * conv_w[0]
    for offset in range(1, taps):
        total = total + padded[:, offset : offset + rows_out] * conv_w[offset]
    return jax.nn.silu(total)


def gate_norm(values, gate_in, gain):
    gated = values * jax.nn.silu(gate_in)
    power = jnp.mean(gated * gated, axis=-1, keepdims=True)
    return gated * lax.rsqrt(power + epsilon) * gain


def local(
    hidden,
    lengths,
    out_grad,
    norm_gain,
    in_weight,
    conv_weight,
    conv_bias,
    dt_bias,
    a_log,
    skip_gain,
    gated_gain,
    out_weight,
):
    count = lax.axis_size("seq")
    shards = lax.axis_size("wshard")
    rank = lax.axis_index("seq")
    shard = lax.axis_index("wshard")
    micro, _, tokens, width = hidden.shape
    taps = conv_weight.shape[1]
    inner = out_weight.shape[0] * shards
    channels = conv_bias.shape[0] * shards
    heads = dt_bias.shape[0] * shards
    hs = inner // heads
    n = (channels - inner) // 2
    groups = heads // GROUP
    rows = micro * tokens
    fast = count == 8 and shards == 4 and micro == 2
    in_local = in_weight.T
    small = [norm_gain, conv_weight.T.reshape(-1), conv_bias, dt_bias, a_log, skip_gain, gated_gain]
    sizes = [v.shape[0] for v in small]
    small.append(in_local[inner + channels :].reshape(-1))
    packed_low = lax.all_gather(jnp.concatenate(small), "wshard", axis=0)
    packed = packed_low.astype(f32)
    parts, at = [], 0
    for size in sizes:
        parts.append(packed[:, at : at + size])
        at += size
    norm_g = parts[0].reshape(-1)
    conv_w = parts[1].reshape(shards, taps, -1).transpose(1, 0, 2).reshape(taps, -1)
    conv_b = parts[2].reshape(-1)
    dt_shift = parts[3].reshape(-1)
    rate = -jnp.exp(parts[4].reshape(-1))
    skip = parts[5].reshape(-1)
    gated_g = parts[6].reshape(-1)

    dt_w = packed_low[:, at:].reshape(shards, heads, -1).transpose(1, 0, 2).reshape(heads, -1)
    order = jnp.arange(shards) ^ shard
    if fast:
        conv_shards, gate_others = gather_input_weight(in_local, inner, channels)
    else:
        every = lax.all_gather(in_local[: inner + channels], "wshard", axis=0)
        in_w = every[order[1:]]
        out_w = lax.all_gather(out_weight, "wshard", axis=0, tiled=True)

    def grouped(v):
        return v.reshape(micro, tokens, groups, GROUP).transpose(0, 2, 1, 3)

    rows_in = hidden.reshape(rows, width).astype(f32)
    cot = out_grad.reshape(rows, width).astype(f32)
    positions = rank * tokens + jnp.arange(tokens, dtype=jnp.int32)
    valid = (positions[None, :] < lengths[:, 0][:, None]).astype(f32).reshape(rows, 1)
    tile = 256
    skip_wide = jnp.repeat(skip, hs)[None, :]

    def to_lanes(v):
        return jnp.pad(v, ((0, 0),) * (v.ndim - 1) + ((0, LANES - heads),))

    if fast:
        hidden_rows, out_grad_rows = hidden.reshape(rows, width), out_grad.reshape(rows, width)
        dt_wide = jnp.pad(dt_w, ((0, LANES - heads), (0, 0)))
        conv_low, normed_low, raw = front(
            hidden_rows, norm_g[None, :], dt_wide, conv_shards, channels // 2
        )
        raw = raw.reshape(micro, tokens, LANES)
    else:
        normed, front_back = jax.vjp(rms_front, rows_in, norm_g)
        normed_low = normed.astype(bf16)
        normed_parts = normed_low.reshape(rows, shards, -1).transpose(1, 0, 2)[order]
        conv_low = project(normed_parts, in_local, in_w, inner, channels, tile, bf16)
        gate_in = project(normed_parts, in_local, in_w, 0, inner, tile, f32)
        dt_low = mm(normed_low, dt_w, NT).astype(bf16)
        dt_raw = dt_low.astype(f32).reshape(micro, tokens, heads) + dt_shift
    conv_low = conv_low.reshape(micro, tokens, channels)

    if fast:
        x_low, bc_low, y_scan, scanned_low, halo, s_in, out_others = scan_forward(
            conv_low,
            raw,
            conv_w,
            conv_b[None, :],
            to_lanes(dt_shift[None, :]),
            to_lanes(rate[None, :]),
            skip_wide,
            out_weight,
            inner,
            hs,
            3,
        )
    else:
        prior = from_behind(conv_low[:, tokens - (taps - 1) :], "seq", 1)
        padded = jnp.concatenate([prior, conv_low], axis=1).astype(f32)
        mixed, conv_back = jax.vjp(conv_act, padded, conv_w, conv_b)
        dt = jax.nn.softplus(dt_raw)
        tri = (jnp.arange(tokens)[:, None] >= jnp.arange(tokens)[None, :]).astype(f32)
        cum = jnp.einsum("ij,mjh->mih", tri, dt * rate, precision=highest)
        dt_g, cum_g = grouped(dt), grouped(cum)
        row_g = cum_g.transpose(0, 1, 3, 2)
        last = cum[:, tokens - 1, :]
        decays = lax.all_gather(jnp.exp(last), "seq", axis=0)
        decay_w = grouped(jnp.exp(cum))
        x_low = mixed[..., :inner].astype(bf16)
        b_low = mixed[..., inner : inner + n].astype(bf16)
        c_low = mixed[..., inner + n :].astype(bf16)
        end_w = grouped(dt * jnp.exp(last[:, None, :] - cum))
        own_state = block_states(x_low, end_w, b_low.transpose(0, 2, 1), hs)
        y_local = local_scan(x_low, dt_g, cum_g, row_g, b_low, c_low, hs)
        s_in = running_states(own_state, decays, hs, True)
        y_scan, scanned_low = add_carry(x_low, y_local, cum_g, c_low, s_in, skip_wide, hs)

    if fast:
        normed_out_low, output, g, dy, d_gate_low, d_gated = gate_stage(
            scanned_low.reshape(rows, inner),
            normed_low,
            in_local,
            gate_others,
            gated_g[None, :],
            out_weight,
            out_others,
            hidden_rows,
            out_grad_rows,
            valid,
            256,
        )
        output = output.reshape(hidden.shape)
        dy = dy.reshape(micro, tokens, inner)
        d_gated = d_gated[0]
    else:
        scanned = scanned_low.reshape(rows, inner).astype(f32)
        normed_out, gate_back = jax.vjp(gate_norm, scanned, gate_in, gated_g)
        normed_out_low = normed_out.astype(bf16)
        branch = mm(normed_out_low, out_w)
        output = (rows_in + valid * branch).astype(bf16).reshape(hidden.shape)
        g = (cot * valid).astype(bf16)
        d_scanned, d_gate_in, d_gated = gate_back(mm(g, out_w, NT))
        dy = d_scanned.astype(bf16).reshape(micro, tokens, inner)
        d_gate_low = d_gate_in.astype(bf16)

    if fast:
        d_rest, d_conv_w, d_conv_b, by_head, gate_sum = scan_backward(
            dy,
            x_low,
            bc_low,
            y_scan,
            s_in,
            raw,
            conv_low,
            halo,
            conv_w,
            conv_b[None, :],
            to_lanes(dt_shift[None, :]),
            to_lanes(rate[None, :]),
            skip_wide,
            d_gate_low,
            normed_low,
            hs,
            4,
        )
        d_dt_bias, d_a_log, d_skip = by_head[0, :heads], by_head[1, :heads], by_head[2, :heads]
        d_conv_b = d_conv_b[0]
        d_rest = d_rest.reshape(rows, -1)
        input_grad, d_norm_g = back_stage(
            d_gate_low,
            d_rest,
            dt_wide,
            in_local,
            gate_others,
            conv_shards,
            hidden_rows,
            norm_g[None, :],
            out_grad_rows,
            (inner // 2, channels // 2),
        )
        input_grad = input_grad.reshape(hidden.shape)
        d_norm_g = d_norm_g[0]
    else:
        own_grad = block_states(dy, decay_w, c_low.transpose(0, 2, 1), hs)
        dx_local, db_local, dc_local = local_back(x_low, dy, dt_g, cum_g, row_g, b_low, c_low, hs)
        ds = running_states(own_grad, decays, hs, False)
        dx_low, ddt_g, dcum_g, db, dc, last_term, dskip = carry_back(
            x_low, dy, dx_local, y_scan, dt_g, cum_g, b_low, s_in, ds, db_local, dc_local, skip_wide, hs
        )

        def ungrouped(v):
            return v.transpose(0, 2, 1, 3).reshape(micro, tokens, heads)

        at_end = jnp.sum(last_term.reshape(micro, heads, hs), axis=-1)[:, None, :]
        d_log = jnp.einsum("ij,mih->mjh", tri, ungrouped(dcum_g), precision=highest) + at_end
        d_dt = (ungrouped(ddt_g) + d_log * rate) * jax.nn.sigmoid(dt_raw)
        d_dt_bias = jnp.sum(d_dt, axis=(0, 1))
        d_a_log = jnp.sum(d_log * dt, axis=(0, 1)) * rate
        d_skip = jnp.sum(dskip.reshape(-1, heads, hs), axis=(0, 2))
        mixed_grad = jnp.concatenate([dx_low.astype(f32), db, dc], axis=2)
        d_padded, d_conv_w, d_conv_b = conv_back(mixed_grad)
        from_next = from_behind(d_padded[:, : taps - 1].astype(bf16), "seq", -1).astype(f32)
        d_conv = d_padded[:, taps - 1 :].at[:, tokens - (taps - 1) :].add(from_next)
        d_dt_low = d_dt.astype(bf16).reshape(rows, heads)
    total_cols = inner + channels + heads
    if not fast:
        d_rest = d_conv.astype(bf16).reshape(rows, channels)
        d_parts = unproject(d_gate_low, d_rest, in_local, in_w, tile)
        d_normed = d_parts[order].transpose(1, 0, 2).reshape(rows, width) + mm(d_dt_low, dt_w)
        d_hidden, d_norm_g = front_back(d_normed)
        input_grad = (d_hidden + cot).astype(bf16).reshape(hidden.shape)

    def summed(terms, axis):
        t = lax.psum_scatter(terms.astype(bf16), "seq", scatter_dimension=0, tiled=True)
        t = lax.psum_scatter(t, "wshard", scatter_dimension=axis, tiled=True)
        return lax.all_gather(t, "seq", axis=0, tiled=True).astype(f32)

    smalls = [
        d_norm_g.reshape(shards, -1),
        d_conv_w.reshape(taps, shards, -1).transpose(1, 0, 2).reshape(shards, -1),
        d_conv_b.reshape(shards, -1),
        d_dt_bias.reshape(shards, -1),
        d_a_log.reshape(shards, -1),
        d_skip.reshape(shards, -1),
        d_gated.reshape(shards, -1),
    ]
    smalls = jnp.concatenate(smalls, axis=1)
    if fast:
        smalls = jnp.pad(smalls, ((0, 0), (0, -smalls.shape[1] % 1024))).reshape(shards, -1, LANES)
        rest_sum, out_sum, sums = weight_sums(d_rest, normed_low, g, normed_out_low, smalls, 2)
        gate_sum = gate_sum.reshape(inner, -1)
        in_grad = jnp.concatenate([gate_sum, rest_sum[: total_cols - inner]]).astype(f32).T
        out_w_grad = out_sum.T.astype(f32)
        sums = sums.reshape(-1)
    else:
        d_proj = jnp.concatenate([d_gate_low, d_rest, d_dt_low], axis=1)
        in_grad = summed(mm(d_proj, normed_low, TN), 1).T
        out_terms = mm(normed_out_low, g, TN)
        blocks = out_terms.reshape(shards, count, -1, width).transpose(1, 0, 2, 3)
        out_w_grad = summed(blocks.reshape(inner, width), 0)
        sums = lax.psum(smalls, ("seq", "wshard"))
        sums = lax.dynamic_index_in_dim(sums, shard, 0, keepdims=False)
    found, at = [], 0
    for size in sizes:
        found.append(sums[at : at + size])
        at += size
    return (
        output,
        input_grad,
        found[0],
        in_grad,
        found[1].reshape(taps, -1).T,
        found[2],
        found[3],
        found[4],
        found[5],
        found[6],
        out_w_grad,
    )


def solution(mesh):
    return jax.shard_map(
        local,
        mesh=mesh,
        in_specs=(
            P(None, "wshard", "seq", None),
            P(None, "wshard"),
            P(None, "wshard", "seq", None),
            P("wshard"),
            P("wshard", None),
            P("wshard", None),
            P("wshard"),
            P("wshard"),
            P("wshard"),
            P("wshard"),
            P("wshard"),
            P("wshard", None),
        ),
        out_specs=(
            P(None, "wshard", "seq", None),
            P(None, "wshard", "seq", None),
            P("wshard"),
            P("wshard", None),
            P("wshard", None),
            P("wshard"),
            P("wshard"),
            P("wshard"),
            P("wshard"),
            P("wshard"),
            P("wshard", None),
        ),
        check_vma=False,
    )
```

```python
from functools import partial

import jax
import jax.numpy as jnp
from jax import lax
from jax.experimental import pallas as pl
from jax.experimental.pallas import tpu as pltpu
from jax.sharding import PartitionSpec as P

epsilon = 1e-05
highest = lax.Precision.HIGHEST
f32 = jnp.float32
bf16 = jnp.bfloat16
GROUP = 8
VMEM = 48 * 1024 * 1024
VMEM_MOST = 62 * 1024 * 1024

NN = (((1,), (0,)), ((), ()))
NT = (((1,), (1,)), ((), ()))
TN = (((0,), (0,)), ((), ()))


def mm(a, b, dims=NN):
    return lax.dot_general(a, b, dims, preferred_element_type=f32)


def params():
    return pltpu.CompilerParams(
        dimension_semantics=("arbitrary", "arbitrary"), vmem_limit_bytes=VMEM
    )


def widen(cols, head_size):
    t, heads = cols.shape
    lane = lax.broadcasted_iota(jnp.int32, (t, 2 * head_size), 1)
    parts = []
    for k in range(0, heads, 2):
        parts.append(jnp.where(lane < head_size, cols[:, k : k + 1], cols[:, k + 1 : k + 2]))
    return jnp.concatenate(parts, axis=1)


def state_kernel(hs, x_ref, w_ref, bt_ref, o_ref):
    weighted = (x_ref[0].astype(f32) * widen(w_ref[0, 0], hs)).astype(bf16)
    o_ref[0] = mm(bt_ref[0], weighted)


def block_states(x, weights, bt, hs):
    micro, t, cols = x.shape
    n = bt.shape[1]
    gc = GROUP * hs
    return pl.pallas_call(
        partial(state_kernel, hs),
        grid=(micro, cols // gc),
        in_specs=[
            pl.BlockSpec((1, t, gc), lambda m, g: (m, 0, g)),
            pl.BlockSpec((1, 1, t, GROUP), lambda m, g: (m, g, 0, 0)),
            pl.BlockSpec((1, n, t), lambda m, g: (m, 0, 0)),
        ],
        out_specs=pl.BlockSpec((1, n, gc), lambda m, g: (m, 0, g)),
        out_shape=jax.ShapeDtypeStruct((micro, n, cols), f32),
        compiler_params=params(),
        name="block_states",
    )(x, weights, bt)


def local_kernel(hs, x_ref, dt_ref, cum_ref, row_ref, b_ref, c_ref, o_ref, scores):
    t = x_ref.shape[1]
    half = t // 2

    @pl.when(pl.program_id(1) == 0)
    def _():
        s = mm(c_ref[0], b_ref[0], NT)
        i = lax.broadcasted_iota(jnp.int32, (t, t), 0)
        j = lax.broadcasted_iota(jnp.int32, (t, t), 1)
        scores[...] = jnp.where(i >= j, s, 0.0)

    cum, dt, rows = cum_ref[0, 0], dt_ref[0, 0], row_ref[0, 0]
    lane = lax.broadcasted_iota(jnp.int32, (half, 2 * hs), 1)
    weighted = (x_ref[0].astype(f32) * widen(dt, hs)).astype(bf16)
    for k in range(0, GROUP, 2):
        at = slice(k * hs, (k + 2) * hs)
        pair = weighted[:, at]
        top, low = [], []
        for h in (k, k + 1):
            col, row = cum[:, h : h + 1], rows[h : h + 1, :]
            m1 = jnp.exp(jnp.minimum(col[:half] - row[:, :half], 0.0)) * scores[:half, :half]
            m2 = jnp.exp(jnp.minimum(col[half:] - row, 0.0)) * scores[half:, :]
            top.append(mm(m1.astype(bf16), pair[:half]))
            low.append(mm(m2.astype(bf16), pair))
        o_ref[0, :half, at] = jnp.where(lane < hs, top[0], top[1])
        o_ref[0, half:, at] = jnp.where(lane < hs, low[0], low[1])


def local_scan(x, dt, cum, rows, b, c, hs):
    micro, t, cols = x.shape
    n = b.shape[2]
    gc = GROUP * hs
    return pl.pallas_call(
        partial(local_kernel, hs),
        grid=(micro, cols // gc),
        in_specs=[
            pl.BlockSpec((1, t, gc), lambda m, g: (m, 0, g)),
            pl.BlockSpec((1, 1, t, GROUP), lambda m, g: (m, g, 0, 0)),
            pl.BlockSpec((1, 1, t, GROUP), lambda m, g: (m, g, 0, 0)),
            pl.BlockSpec((1, 1, GROUP, t), lambda m, g: (m, g, 0, 0)),
            pl.BlockSpec((1, t, n), lambda m, g: (m, 0, 0)),
            pl.BlockSpec((1, t, n), lambda m, g: (m, 0, 0)),
        ],
        out_specs=pl.BlockSpec((1, t, gc), lambda m, g: (m, 0, g)),
        out_shape=jax.ShapeDtypeStruct((micro, t, cols), f32),
        scratch_shapes=[pltpu.VMEM((t, t), f32)],
        compiler_params=params(),
        name="local_scan",
    )(x, dt, cum, rows, b, c)


def carry_kernel(hs, x_ref, y_ref, cum_ref, c_ref, s_ref, skip_ref, scan_ref, low_ref):
    carried = mm(c_ref[0], s_ref[0].astype(bf16)) * widen(jnp.exp(cum_ref[0, 0]), hs)
    scan = y_ref[0] + carried
    scan_ref[0] = scan
    low_ref[0] = (scan + skip_ref[...] * x_ref[0].astype(f32)).astype(bf16)


def add_carry(x, y, cum, c, s_in, skip_wide, hs):
    micro, t, cols = x.shape
    n = c.shape[2]
    gc = GROUP * hs
    wide = pl.BlockSpec((1, t, gc), lambda m, g: (m, 0, g))
    return pl.pallas_call(
        partial(carry_kernel, hs),
        grid=(micro, cols // gc),
        in_specs=[
            wide,
            wide,
            pl.BlockSpec((1, 1, t, GROUP), lambda m, g: (m, g, 0, 0)),
            pl.BlockSpec((1, t, n), lambda m, g: (m, 0, 0)),
            pl.BlockSpec((1, n, gc), lambda m, g: (m, 0, g)),
            pl.BlockSpec((1, gc), lambda m, g: (0, g)),
        ],
        out_specs=[wide, wide],
        out_shape=[
            jax.ShapeDtypeStruct((micro, t, cols), f32),
            jax.ShapeDtypeStruct((micro, t, cols), bf16),
        ],
        compiler_params=params(),
        name="add_carry",
    )(x, y, cum, c, s_in, skip_wide)


def local_back_kernel(
    hs, x_ref, dy_ref, dt_ref, cum_ref, row_ref, b_ref, c_ref, dx_ref, db_ref, dc_ref, scores, total
):
    t = x_ref.shape[1]
    half = t // 2

    @pl.when(pl.program_id(1) == 0)
    def _():
        s = mm(b_ref[0], c_ref[0], NT)
        j = lax.broadcasted_iota(jnp.int32, (t, t), 0)
        i = lax.broadcasted_iota(jnp.int32, (t, t), 1)
        scores[...] = jnp.where(i >= j, s, 0.0)
        total[...] = jnp.zeros_like(total)

    cum, dt, rows = cum_ref[0, 0], dt_ref[0, 0], row_ref[0, 0]
    lane = lax.broadcasted_iota(jnp.int32, (t, 2 * hs), 1)
    lane_half = lax.broadcasted_iota(jnp.int32, (half, 2 * hs), 1)
    weighted = (x_ref[0].astype(f32) * widen(dt, hs)).astype(bf16)
    for k in range(0, GROUP, 2):
        at = slice(k * hs, (k + 2) * hs)
        pair = weighted[:, at]
        dy = dy_ref[0, :, at]
        top, low = [], []
        for h in (k, k + 1):
            col, row = cum[:, h : h + 1], rows[h : h + 1, :]
            mine = jnp.where(lane < hs, pair, 0) if h == k else jnp.where(lane < hs, 0, pair)
            l1 = jnp.exp(jnp.minimum(row - col[:half], 0.0))
            l2 = jnp.exp(jnp.minimum(row[:, half:] - col[half:], 0.0))
            total[:half, :] += l1 * mm(mine[:half], dy, NT)
            total[half:, half:] += l2 * mm(mine[half:], dy[half:], NT)
            top.append(mm((l1 * scores[:half, :]).astype(bf16), dy))
            low.append(mm((l2 * scores[half:, half:]).astype(bf16), dy[half:]))
        dx_ref[0, :half, at] = jnp.where(lane_half < hs, top[0], top[1])
        dx_ref[0, half:, at] = jnp.where(lane_half < hs, low[0], low[1])

    @pl.when(pl.program_id(1) == pl.num_programs(1) - 1)
    def _():
        j = lax.broadcasted_iota(jnp.int32, (t, t), 0)
        i = lax.broadcasted_iota(jnp.int32, (t, t), 1)
        d = jnp.where(i >= j, total[...], 0.0)
        db_ref[0] = mm(d.astype(bf16), c_ref[0])
        dc_ref[0] = mm(d.T.astype(bf16), b_ref[0])


def local_back(x, dy, dt, cum, rows, b, c, hs):
    micro, t, cols = x.shape
    n = b.shape[2]
    gc = GROUP * hs
    wide = pl.BlockSpec((1, t, gc), lambda m, g: (m, 0, g))
    small = pl.BlockSpec((1, 1, t, GROUP), lambda m, g: (m, g, 0, 0))
    state = pl.BlockSpec((1, t, n), lambda m, g: (m, 0, 0))
    return pl.pallas_call(
        partial(local_back_kernel, hs),
        grid=(micro, cols // gc),
        in_specs=[
            wide,
            wide,
            small,
            small,
            pl.BlockSpec((1, 1, GROUP, t), lambda m, g: (m, g, 0, 0)),
            state,
            state,
        ],
        out_specs=[wide, state, state],
        out_shape=[
            jax.ShapeDtypeStruct((micro, t, cols), f32),
            jax.ShapeDtypeStruct((micro, t, n), f32),
            jax.ShapeDtypeStruct((micro, t, n), f32),
        ],
        scratch_shapes=[pltpu.VMEM((t, t), f32), pltpu.VMEM((t, t), f32)],
        compiler_params=params(),
        name="local_back",
    )(x, dy, dt, cum, rows, b, c)


def head_sums(values, ones):
    high = values.astype(bf16)
    rest = (values - high.astype(f32)).astype(bf16)
    return mm(high, ones) + mm(rest, ones)


def carry_back_kernel(
    hs,
    x_ref,
    dy_ref,
    dxl_ref,
    y_ref,
    dt_ref,
    cum_ref,
    b_ref,
    si_ref,
    ds_ref,
    dbl_ref,
    dcl_ref,
    skip_ref,
    dx_ref,
    ddt_ref,
    dcum_ref,
    db_ref,
    dc_ref,
    last_ref,
    dskip_ref,
):
    t = x_ref.shape[1]
    gc = x_ref.shape[2]

    @pl.when(pl.program_id(1) == 0)
    def _():
        db_ref[0] = dbl_ref[0]
        dc_ref[0] = dcl_ref[0]

    cum, dt = cum_ref[0, 0], dt_ref[0, 0]
    x, dy = x_ref[0].astype(f32), dy_ref[0].astype(f32)
    dt_wide = widen(dt, hs)
    weighted = (x * dt_wide).astype(bf16).astype(f32)
    decay = widen(jnp.exp(cum), hs)
    to_end = widen(jnp.exp(cum[t - 1 :, :] - cum), hs)
    s_in, ds = si_ref[0].astype(f32), ds_ref[0]
    s_low, ds_low = s_in.astype(bf16), ds.astype(bf16)
    through = to_end * mm(b_ref[0], ds_low)
    d_weighted = dxl_ref[0] + through
    dx_ref[0] = (dt_wide * d_weighted + skip_ref[...] * dy).astype(bf16)
    db_ref[0] += mm((weighted * to_end).astype(bf16), ds_low, NT)
    dc_ref[0] += mm((dy * decay).astype(bf16), s_low, NT)
    r = lax.broadcasted_iota(jnp.int32, (gc, 128), 0)
    c = lax.broadcasted_iota(jnp.int32, (gc, 128), 1)
    ones = jnp.where(r // hs == c, 1.0, 0.0).astype(bf16)
    ddt_ref[0, 0] = head_sums(x * d_weighted, ones)[:, :GROUP]
    dcum_ref[0, 0] = head_sums(dy * y_ref[0] - weighted * d_weighted, ones)[:, :GROUP]
    last_decay = decay[t - 1 :, :]
    last_ref[0] = jnp.sum(weighted * through, axis=0, keepdims=True) + last_decay * jnp.sum(
        s_low.astype(f32) * ds, axis=0, keepdims=True
    )
    dskip_ref[0] = jnp.sum(x * dy, axis=0, keepdims=True)


def carry_back(x, dy, dxl, y, dt, cum, b, s_in, ds, dbl, dcl, skip_wide, hs):
    micro, t, cols = x.shape
    n = b.shape[2]
    gc = GROUP * hs
    groups = cols // gc
    wide = pl.BlockSpec((1, t, gc), lambda m, g: (m, 0, g))
    small = pl.BlockSpec((1, 1, t, GROUP), lambda m, g: (m, g, 0, 0))
    state = pl.BlockSpec((1, t, n), lambda m, g: (m, 0, 0))
    st = pl.BlockSpec((1, n, gc), lambda m, g: (m, 0, g))
    line = pl.BlockSpec((1, 1, gc), lambda m, g: (m, 0, g))
    return pl.pallas_call(
        partial(carry_back_kernel, hs),
        grid=(micro, groups),
        in_specs=[
            wide,
            wide,
            wide,
            wide,
            small,
            small,
            state,
            st,
            st,
            state,
            state,
            pl.BlockSpec((1, gc), lambda m, g: (0, g)),
        ],
        out_specs=[wide, small, small, state, state, line, line],
        out_shape=[
            jax.ShapeDtypeStruct((micro, t, cols), bf16),
            jax.ShapeDtypeStruct((micro, groups, t, GROUP), f32),
            jax.ShapeDtypeStruct((micro, groups, t, GROUP), f32),
            jax.ShapeDtypeStruct((micro, t, n), f32),
            jax.ShapeDtypeStruct((micro, t, n), f32),
            jax.ShapeDtypeStruct((micro, 1, cols), f32),
            jax.ShapeDtypeStruct((micro, 1, cols), f32),
        ],
        compiler_params=params(),
        name="carry_back",
    )(x, dy, dxl, y, dt, cum, b, s_in, ds, dbl, dcl, skip_wide)


def from_behind(x, axis, by):
    count = lax.axis_size(axis)
    pairs = [(i, i + by) for i in range(count) if 0 <= i + by < count]
    return lax.ppermute(x, axis, pairs)


def swap(x, by):
    count = lax.axis_size("seq")
    return lax.ppermute(x, "seq", [(i, i ^ by) for i in range(count)])


def running_states(terms, decays, hs, forward):
    count = lax.axis_size("seq")
    rank = lax.axis_index("seq")
    index = jnp.arange(count)

    def product(mask):
        d = jnp.prod(jnp.where(mask[:, None, None], decays, 1.0), axis=0)
        return jnp.repeat(d, hs, axis=1)[:, None, :]

    total, before = terms, jnp.zeros_like(terms)
    size = 1
    while size < count:
        other = swap(total.astype(bf16), size).astype(f32)
        mine = index // size == rank // size
        theirs = index // size == (rank // size) ^ 1
        later = (rank // size) % 2 == (1 if forward else 0)
        passed = mine & ((index < rank) if forward else (index > rank))
        before = before + jnp.where(later, product(passed), 0.0) * other
        if 2 * size < count:
            total = total * jnp.where(later, 1.0, product(theirs)) + other * jnp.where(
                later, product(mine), 1.0
            )
        size *= 2
    return before


MESH = pl.DeviceIdType.MESH


def around():
    s, z = lax.axis_index("seq"), lax.axis_index("wshard")
    c, x, y = s % 2, (s // 2) % 2, s // 4
    near = {
        "c": (s + 1 - 2 * c, z),
        "x": (s + 2 - 4 * x, z),
        "y": (s + 4 - 8 * y, z),
        "z1": (s, z + 1 - 2 * (z % 2)),
        "z2": (s, z + 2 - 4 * (z // 2)),
        "z3": (s, 3 - z),
    }
    return s, z, c, x, y, near


def greet(near):
    barrier = pltpu.get_barrier_semaphore()
    for where in near.values():
        pl.semaphore_signal(barrier, inc=1, device_id=where, device_id_type=MESH)
    pl.semaphore_wait(barrier, len(near))


CHUNK_DMAS = 10
AHEAD = 2


def split_rows(piece, parts):
    tiles = piece // 16
    return [16 * (tiles * (i + 1) // parts - tiles * i // parts) for i in range(parts)]


class Gather:
    def __init__(self, place, items, send, recv, own=None):
        s, z, c, x, y, near = place
        sx, sy, sd = s + 2 - 4 * x, s + 4 - 8 * y, s + 6 - 4 * x - 8 * y
        self.plans = []
        for source, base, target, count, parts in items:
            off = 0
            for i, size in enumerate(split_rows(count // 8, parts)):
                q = len(self.plans)

                def rows(who, first=0, off=off, size=size, piece=count // 8):
                    return pl.ds(pl.multiple_of(first + who * piece + off, 16), size)

                def move(src, dst, kind, to, q=q):
                    return pltpu.make_async_remote_copy(
                        src_ref=src,
                        dst_ref=dst,
                        send_sem=send.at[q, kind],
                        recv_sem=recv.at[q, kind],
                        device_id=near[to],
                        device_id_type=MESH,
                    )

                def along(who, kind, to, move=move, rows=rows, target=target):
                    block = target.at[pl.ds(0, 3), rows(who)]
                    return move(block, block, kind, to)

                plan = {"fetched": base is None}
                if base is None:
                    have = source.at[:, pl.ds(off, size)]
                    block = target.at[pl.ds(0, 3), rows(s)]
                    plan["own"] = pltpu.make_async_copy(have, block, own.at[q])
                    for kind, name in ((3, "x"), (4, "y"), (6, "c0")):
                        plan[name] = move(have, block, kind, name[0])
                else:
                    for k in (1, 2, 3):
                        there = target.at[k - 1, rows(s)]
                        plan["z%d" % k] = move(source.at[rows(s, base)], there, k - 1, "z%d" % k)
                    plan["x"] = along(s, 3, "x")
                    plan["y"] = along(s, 4, "y")
                    plan["c0"] = along(s, 6, "c")
                first = "xy"[i % 2]
                plan["d"] = along(sx, 5, "y") if first == "x" else along(sy, 5, "x")
                plan["cx"] = along(sx, 7, "c")
                plan["cy"] = along(sy, 8, "c")
                plan["cd"] = along(sd, 9, "c")
                plan["order"] = first, "yx"[i % 2]
                self.plans.append(plan)
                off += size

    def fetch(self, i):
        for k in (1, 2, 3):
            self.plans[i]["z%d" % k].start()

    def begin(self, i):
        plan = self.plans[i]
        if plan["fetched"]:
            plan["own"].start()
        else:
            for k in (1, 2, 3):
                plan["z%d" % k].wait_recv()
        for name in ("x", "y", "c0"):
            plan[name].start()

    def middle(self, i):
        plan = self.plans[i]
        one, two = plan["order"]
        plan[one].wait_recv()
        plan["d"].start()
        plan["c" + one].start()
        plan[two].wait_recv()
        plan["c" + two].start()

    def finish(self, i):
        self.plans[i]["d"].wait_recv()
        self.plans[i]["cd"].start()

    def run(self, last):
        n = len(self.plans)
        for i in range(min(AHEAD, n)):
            self.fetch(i)
        for i in range(n + 2):
            if i < n:
                self.begin(i)
                if i + AHEAD < n:
                    self.fetch(i + AHEAD)
                if i + AHEAD == n - 1:
                    last()
            if 0 <= i - 1 < n:
                self.middle(i - 1)
            if 0 <= i - 2 < n:
                self.finish(i - 2)

    def close(self):
        for plan in self.plans:
            for name in ("c0", "cx", "cy", "cd"):
                plan[name].wait_recv()
            for name in ("z1", "z2", "z3", "x", "y", "d", "c0", "cx", "cy", "cd"):
                if name in plan:
                    plan[name].wait_send()
            if plan["fetched"]:
                plan["own"].wait()


def gather_kernel(
    inner, channels, parts, w_ref, ow_ref, conv_ref, gate_ref, eighth_ref, own, own_sem, send, recv, o_send, o_recv
):
    place = around()
    inward = pltpu.make_async_copy(w_ref.at[pl.ds(inner, channels)], own, own_sem)
    inward.start()
    greet(place[-1])
    items = [(w_ref, inner, conv_ref, channels, parts), (w_ref, 0, gate_ref, inner, parts)]
    work = Gather(place, items, send, recv)
    piece = eighth_ref.shape[1]
    mine = pl.ds(pl.multiple_of(place[0] * piece, 16), piece)
    eighths = [
        pltpu.make_async_remote_copy(
            src_ref=ow_ref.at[mine],
            dst_ref=eighth_ref.at[k - 1],
            send_sem=o_send.at[k - 1],
            recv_sem=o_recv.at[k - 1],
            device_id=place[-1]["z%d" % k],
            device_id_type=MESH,
        )
        for k in (1, 2, 3)
    ]

    def last():
        for copy in eighths:
            copy.start()

    work.run(last)
    inward.wait()
    outward = pltpu.make_async_copy(own, conv_ref.at[3], own_sem)
    outward.start()
    work.close()
    for copy in eighths:
        copy.wait()
    outward.wait()


def gather_input_weight(w_t, out_weight, inner, channels, parts=6):
    width = w_t.shape[1]
    hbm = pl.BlockSpec(memory_space=pl.ANY)
    return pl.pallas_call(
        partial(gather_kernel, inner, channels, parts),
        in_specs=[hbm] * 2,
        out_specs=[hbm] * 3,
        out_shape=[
            jax.ShapeDtypeStruct((4, channels, width), bf16),
            jax.ShapeDtypeStruct((3, inner, width), bf16),
            jax.ShapeDtypeStruct((3, out_weight.shape[0] // 8, out_weight.shape[1]), bf16),
        ],
        scratch_shapes=[
            pltpu.VMEM((channels, width), bf16),
            pltpu.SemaphoreType.DMA,
            pltpu.SemaphoreType.DMA((2 * parts, CHUNK_DMAS)),
            pltpu.SemaphoreType.DMA((2 * parts, CHUNK_DMAS)),
            pltpu.SemaphoreType.DMA((3,)),
            pltpu.SemaphoreType.DMA((3,)),
        ],
        compiler_params=pltpu.CompilerParams(
            collective_id=1, has_side_effects=True, vmem_limit_bytes=VMEM_MOST
        ),
        cost_estimate=pl.CostEstimate(flops=0, bytes_accessed=200_000_000, transcendentals=0),
        name="gather_input_weight",
    )(w_t, out_weight)


class Here:
    def __init__(self, copy):
        self.start, self.wait_recv = copy.start, copy.wait

    def wait_send(self):
        pass


class Products:
    IN = 4
    SCRATCH = 22

    @staticmethod
    def sizes(a_list, b):
        rows = b.shape[0]
        wide = sum(a.shape[1] for a in a_list) // 2
        return rows, wide, b.shape[1], wide // 128

    @staticmethod
    def marks(chunks):
        return sorted({0, chunks * 2 // 5, chunks * 7 // 10, chunks * 9 // 10, chunks})

    @staticmethod
    def out_shape(a_list, b):
        _, _, width, chunks = Products.sizes(a_list, b)
        return jax.ShapeDtypeStruct((2, chunks, 2, 2, 2, 16, width // 4), bf16)

    @staticmethod
    def scratch(a_list, b):
        rows, wide, width, chunks = Products.sizes(a_list, b)
        dma = pltpu.SemaphoreType.DMA
        n = Products.IN
        marks = Products.marks(chunks)
        return [
            pltpu.VMEM((2 * rows, wide), bf16),
            pltpu.VMEM((2 * rows, width), bf16),
            pltpu.VMEM((4, 128, width), f32),
            pltpu.VMEM((2, 32, width), bf16),
            pltpu.VMEM((2, 32, width), bf16),
            pltpu.VMEM((2, 16, width), bf16),
            pltpu.VMEM((2, 16, width), bf16),
            pltpu.VMEM((2, 2, 16, width), bf16),
            pltpu.VMEM((2, 16, width), f32),
            pltpu.VMEM((2, 16, width), f32),
            pltpu.VMEM((2, 2, 16, width), f32),
            pltpu.VMEM((chunks, 32, width), bf16),
            pltpu.VMEM((chunks, 32, width), bf16),
            pltpu.VMEM((chunks, 16, width), bf16),
            pltpu.VMEM((chunks, 16, width), bf16),
            pltpu.VMEM((chunks, 3, 2, 16, width // 4), bf16),
            dma((n,)),
            dma((n,)),
            dma((n,)),
            dma((7, 2)),
            dma((7, chunks)),
            dma((2, len(marks) - 1, 8)),
        ]

    def __init__(self, place, a_refs, b_ref, out, scratch, b_far=None):
        self.s, self.z, self.c, self.x, self.y, self.near = place
        (
            self.a,
            self.b,
            self.g,
            self.sa1,
            self.sb1,
            self.sa2,
            self.sb2,
            self.s3,
            self.ka2,
            self.kb2,
            self.f3,
            self.ra1,
            self.rb1,
            self.ra2,
            self.rb2,
            self.rz,
            self.in_sem,
            self.s_in,
            self.r_in,
            self.s_step,
            self.r_step,
            self.sems_all,
        ) = scratch
        self.out = out
        self.shard = self.rz.shape[-1]
        self.chunks = self.ra1.shape[0]
        marks = Products.marks(self.chunks)
        self.groups = list(zip(marks[:-1], marks[1:]))
        c = self.c
        rows = self.a.shape[0] // 2
        near, far = pl.ds(0, rows), pl.ds(rows, rows)
        self.operands = []
        to = self.b.at[far]
        if b_far is None:
            there = self.remote(b_ref, to, self.s_in.at[0], self.r_in.at[0], "c")
        else:
            there = Here(pltpu.make_async_copy(b_far, to, self.s_in.at[0]))
        self.operands.append(
            (0, pltpu.make_async_copy(b_ref, self.b.at[near], self.in_sem.at[0]), there)
        )
        at = 0
        for i, ref in enumerate(a_refs):
            half = ref.shape[1] // 2
            here = ref.at[:, pl.ds(pl.multiple_of(c * half, 128), half)]
            there = ref.at[:, pl.ds(pl.multiple_of((1 - c) * half, 128), half)]
            to = pl.ds(at, half)
            self.operands.append(
                (
                    at // 128,
                    pltpu.make_async_copy(here, self.a.at[near, to], self.in_sem.at[i + 1]),
                    self.remote(there, self.a.at[far, to], self.s_in.at[i + 1], self.r_in.at[i + 1], "c"),
                )
            )
            at += half

    def remote(self, src, dst, ss, rs, to):
        return pltpu.make_async_remote_copy(
            src_ref=src,
            dst_ref=dst,
            send_sem=ss,
            recv_sem=rs,
            device_id=self.near[to],
            device_id_type=MESH,
        )

    def load(self):
        for _, here, _ in self.operands:
            here.start()

    def share(self):
        for _, _, there in self.operands:
            there.start()

    def step_copy(self, kind, u):
        slot = u % 2
        ss, rs = self.s_step.at[kind, slot], self.r_step.at[kind, u]
        if kind < 4:
            src, dst, to = (
                (self.sa1, self.ra1, "x"),
                (self.sb1, self.rb1, "y"),
                (self.sa2, self.ra2, "y"),
                (self.sb2, self.rb2, "x"),
            )[kind]
            return self.remote(src.at[slot], dst.at[u], ss, rs, to)
        k = kind - 3
        z = self.z
        other = (z + 1 - 2 * (z % 2), z + 2 - 4 * (z // 2), 3 - z)[k - 1]
        cols = pl.ds(pl.multiple_of(other * self.shard, 128), self.shard)
        return self.remote(self.s3.at[slot, :, :, cols], self.rz.at[u, k - 1], ss, rs, "z%d" % k)

    def all_copy(self, q, kind):
        a, b = self.groups[q]
        ts = pl.ds(a, b - a)
        x, y, c = self.x, self.y, self.c
        px = 1 - x if kind in (3, 5, 7) else x
        py = 1 - y if kind in (4, 6, 7) else y
        if kind in (3, 4):
            block = self.out.at[c, ts, kind - 3, px, py]
        else:
            block = self.out.at[c, ts, :, px, py]
        to = ("x", "y", "c", "y", "x", "c", "c", "c")[kind]
        return self.remote(block, block, self.sems_all.at[0, q, kind], self.sems_all.at[1, q, kind], to)

    def step(self, t):
        x, y, z, c = self.x, self.y, self.z, self.c
        g, ra1, rb1 = self.g, self.ra1, self.rb1
        chunks = self.chunks
        copy = self.step_copy

        def sl(at, size=16):
            return pl.ds(pl.multiple_of(at, 16), size)

        def free(kind, u):
            @pl.when(u >= 2)
            def _():
                copy(kind, u - 2).wait_send()

        @pl.when(t < chunks)
        def _():
            for first, here, there in self.operands:

                @pl.when(t == first)
                def _(here=here, there=there):
                    here.wait()
                    there.wait_recv()

            slot, now = t % 2, t % 4

            @pl.when(slot == 0)
            def _():
                cols = pl.ds(pl.multiple_of(t * 128, 256), 256)
                both = mm(self.a[:, cols], self.b[...], TN)
                g[now] = both[:128]
                g[now + 1] = both[128:]

            free(0, t)
            free(1, t)
            self.sa1[slot] = g[now, sl((1 - x) * 32, 32)].astype(bf16)
            copy(0, t).start()
            self.sb1[slot, 0:16] = g[now, sl(64 + (1 - y) * 16)].astype(bf16)
            self.sb1[slot, 16:32] = g[now, sl(96 + (1 - y) * 16)].astype(bf16)
            copy(1, t).start()

        @pl.when((t >= 1) & (t - 1 < chunks))
        def _():
            u = t - 1
            slot, then = u % 2, u % 4
            copy(0, u).wait_recv()
            free(2, u)
            self.sa2[slot] = (
                g[then, sl(x * 32 + (1 - y) * 16)] + ra1[u, sl((1 - y) * 16)].astype(f32)
            ).astype(bf16)
            copy(2, u).start()
            self.ka2[slot] = g[then, sl(x * 32 + y * 16)] + ra1[u, sl(y * 16)].astype(f32)
            copy(1, u).wait_recv()
            free(3, u)
            self.sb2[slot] = (
                g[then, sl(64 + (1 - x) * 32 + y * 16)] + rb1[u, sl((1 - x) * 16)].astype(f32)
            ).astype(bf16)
            copy(3, u).start()
            self.kb2[slot] = g[then, sl(64 + x * 32 + y * 16)] + rb1[u, sl(x * 16)].astype(f32)

        @pl.when((t >= 2) & (t - 2 < chunks))
        def _():
            u = t - 2
            slot = u % 2
            copy(2, u).wait_recv()
            copy(3, u).wait_recv()
            for k in (4, 5, 6):
                free(k, u)
            va = self.ka2[slot] + self.ra2[u].astype(f32)
            vb = self.kb2[slot] + self.rb2[u].astype(f32)
            self.f3[slot, 0] = va
            self.f3[slot, 1] = vb
            self.s3[slot, 0] = va.astype(bf16)
            self.s3[slot, 1] = vb.astype(bf16)
            for k in (4, 5, 6):
                copy(k, u).start()

        @pl.when((t >= 3) & (t - 3 < chunks))
        def _():
            u = t - 3
            slot = u % 2
            for k in (4, 5, 6):
                copy(k, u).wait_recv()
            mine = pl.ds(pl.multiple_of(z * self.shard, 128), self.shard)
            for part in (0, 1):
                total = self.f3[slot, part, :, mine]
                for k in range(3):
                    total = total + self.rz[u, k, part].astype(f32)
                self.out[c, u, part, x, y] = total.astype(bf16)

        for q, (_, b) in enumerate(self.groups):

            @pl.when(t == b - 1 + 3)
            def _(q=q):
                for kind in (0, 1, 2):
                    self.all_copy(q, kind).start()

            @pl.when(t == b - 1 + 4)
            def _(q=q):
                self.all_copy(q, 0).wait_recv()
                self.all_copy(q, 3).start()
                self.all_copy(q, 5).start()
                self.all_copy(q, 1).wait_recv()
                self.all_copy(q, 4).start()
                self.all_copy(q, 6).start()

            @pl.when(t == b - 1 + 5)
            def _(q=q):
                self.all_copy(q, 3).wait_recv()
                self.all_copy(q, 4).wait_recv()
                self.all_copy(q, 7).start()

    def steps(self):
        return self.chunks + 5

    def close(self):
        for q in range(len(self.groups)):
            for kind in (2, 5, 6, 7):
                self.all_copy(q, kind).wait_recv()
            for kind in range(8):
                self.all_copy(q, kind).wait_send()
        for u in (self.chunks - 2, self.chunks - 1):
            for kind in range(7):
                self.step_copy(kind, u).wait_send()
        for _, _, there in self.operands:
            there.wait_send()


class Smalls:
    SCRATCH = 5

    @staticmethod
    def scratch(v):
        dma = pltpu.SemaphoreType.DMA
        return [
            pltpu.VMEM((3,) + v.shape, f32),
            pltpu.VMEM((3,) + v.shape, f32),
            pltpu.VMEM((3,) + v.shape[1:], f32),
            dma((6,)),
            dma((6,)),
        ]

    def __init__(self, place, v_ref, out, scratch):
        self.s, self.z, self.c, self.x, self.y, self.near = place
        self.v, self.out = v_ref, out
        self.total, self.got, self.got_z, self.send, self.recv = scratch

    def copy(self, kind):
        if kind < 3:
            src = self.v if kind == 0 else self.total.at[kind - 1]
            dst, to = self.got.at[kind], "cxy"[kind]
        else:
            z = self.z
            k = kind - 2
            other = (z + 1 - 2 * (z % 2), z + 2 - 4 * (z // 2), 3 - z)[k - 1]
            src, dst, to = self.total.at[2, other], self.got_z.at[k - 1], "z%d" % k
        return pltpu.make_async_remote_copy(
            src_ref=src,
            dst_ref=dst,
            send_sem=self.send.at[kind],
            recv_sem=self.recv.at[kind],
            device_id=self.near[to],
            device_id_type=MESH,
        )

    def start(self):
        self.copy(0).start()

    def advance(self, kind):
        self.copy(kind).wait_recv()
        mine = self.v[...] if kind == 0 else self.total[kind - 1]
        self.total[kind] = mine + self.got[kind]
        for k in (kind + 1,) if kind < 2 else (3, 4, 5):
            self.copy(k).start()

    def close(self):
        total = self.total[2, self.z]
        for k in (3, 4, 5):
            self.copy(k).wait_recv()
            total = total + self.got_z[k - 3]
        self.out[...] = total
        for k in range(6):
            self.copy(k).wait_send()


class InputGrad:
    TILE = 256
    SCRATCH = 5

    @staticmethod
    def scratch(rows, width):
        tile = InputGrad.TILE
        return [
            pltpu.VMEM((rows, width), f32),
            pltpu.VMEM((128, width), f32),
            pltpu.VMEM((2, rows, tile), bf16),
            pltpu.VMEM((2, 4, tile, width // 4), bf16),
            pltpu.SemaphoreType.DMA((3, 2)),
        ]

    def __init__(self, refs, out, gain_out, scratch):
        (
            self.gate,
            self.rest,
            self.own,
            self.gate_others,
            self.conv_shards,
            self.d_dt,
            self.dt_w,
            self.h,
            self.gain,
            self.og,
        ) = refs
        self.out, self.gain_out = out, gain_out
        self.acc, self.part, self.d, self.w, self.sems = scratch
        self.early = self.gate.shape[1] // self.TILE
        self.count = self.early + self.conv_shards.shape[1] // self.TILE

    def copies(self, i, gate):
        slot = i % 2
        at = pl.ds(pl.multiple_of((i if gate else i - self.early) * self.TILE, self.TILE), self.TILE)
        if gate:
            pairs = (
                (self.gate.at[:, at], self.d.at[slot]),
                (self.own.at[at], self.w.at[slot, 3]),
                (self.gate_others.at[:, at], self.w.at[slot, pl.ds(0, 3)]),
            )
        else:
            pairs = (
                (self.rest.at[:, at], self.d.at[slot]),
                (self.conv_shards.at[3, at], self.w.at[slot, 3]),
                (self.conv_shards.at[pl.ds(0, 3), at], self.w.at[slot, pl.ds(0, 3)]),
            )
        return [pltpu.make_async_copy(a, b, self.sems.at[k, slot]) for k, (a, b) in enumerate(pairs)]

    def act(self, i, what):
        @pl.when(i < self.early)
        def _():
            for copy in self.copies(i, True):
                getattr(copy, what)()

        @pl.when((i >= self.early) & (i < self.count))
        def _():
            for copy in self.copies(i, False):
                getattr(copy, what)()

    def start(self):
        self.acc[...] = jnp.zeros_like(self.acc)
        self.act(0, "start")

    def step(self, i):
        @pl.when(i < self.count)
        def _():
            self.act(i + 1, "start")
            self.act(i, "wait")
            slot = i % 2
            weights = jnp.concatenate([self.w[slot, k] for k in (3, 0, 1, 2)], axis=1)
            self.acc[...] += mm(self.d[slot], weights)

    def close(self):
        depth = self.w.shape[3]
        tile = self.part.shape[0]
        gain = self.gain[...]

        def body(r, d_gain):
            at = pl.ds(pl.multiple_of(r * tile, tile), tile)
            for k in range(4):
                self.part[:, shard_place(k, depth)] = self.acc[at, k * depth : (k + 1) * depth]
            d = self.part[...] + mm(self.d_dt[at, :], self.dt_w[...])
            h = self.h[at, :].astype(f32)
            scale = lax.rsqrt(jnp.mean(h * h, axis=-1, keepdims=True) + epsilon)
            d_gain = d_gain + jnp.sum(d * (h * scale), axis=0, keepdims=True)
            d = d * gain
            along = jnp.mean(d * h, axis=-1, keepdims=True) * (scale * scale * scale)
            self.out[at, :] = (scale * d - h * along + self.og[at, :].astype(f32)).astype(bf16)
            return d_gain

        d_gain = lax.fori_loop(0, self.out.shape[0] // tile, body, jnp.zeros(gain.shape, f32))
        for a in range(4):
            for r in range(depth // LANES):
                at = a * depth + r * LANES
                self.gain_out[a, r : r + 1, :] = d_gain[:, at : at + LANES]


def sums_kernel(
    gate_ref,
    rest_ref,
    nm_ref,
    far_ref,
    og_ref,
    no_ref,
    own_ref,
    gate_others_ref,
    conv_shards_ref,
    v_ref,
    d_dt_ref,
    dt_w_ref,
    h_ref,
    gain_ref,
    cot_ref,
    in_out,
    out_out,
    v_out,
    input_out,
    small_v,
    *scratch,
):
    place = around()
    cut = Products.SCRATCH
    inp = Products(place, [rest_ref], nm_ref, in_out, scratch[:cut], far_ref)
    outp = Products(place, [og_ref], no_ref, out_out, scratch[cut : 2 * cut])
    small = Smalls(place, small_v, v_out, scratch[2 * cut : 2 * cut + Smalls.SCRATCH])
    back = InputGrad(
        [
            gate_ref,
            rest_ref,
            own_ref,
            gate_others_ref,
            conv_shards_ref,
            d_dt_ref,
            dt_w_ref,
            h_ref,
            gain_ref,
            cot_ref,
        ],
        input_out,
        small_v,
        scratch[2 * cut + Smalls.SCRATCH :],
    )
    inp.load()
    outp.load()
    back.start()
    small_v[...] = v_ref[...]
    greet(place[-1])
    inp.share()
    outp.share()
    each = -(-back.count // (inp.chunks - 1))

    def first(t, carry):
        inp.step(t)

        def tile(i, carry):
            back.step(t * each + i)
            return carry

        lax.fori_loop(0, each, tile, 0)
        return carry

    lax.fori_loop(0, inp.chunks, first, 0)
    back.close()
    small.start()

    def second(t, carry):
        outp.step(t)

        @pl.when(t < inp.steps() - inp.chunks)
        def _():
            inp.step(t + inp.chunks)

        for kind in range(3):

            @pl.when(t == kind + 1)
            def _(kind=kind):
                small.advance(kind)

        return carry

    lax.fori_loop(0, outp.steps(), second, 0)
    small.close()
    inp.close()
    outp.close()


def weight_sums(
    d_gate,
    d_rest,
    nm,
    nm_far,
    og,
    no,
    own,
    gate_others,
    conv_shards,
    v,
    d_dt,
    dt_w,
    hidden,
    gain,
    out_grad,
    collective_id,
):
    vmem = pl.BlockSpec(memory_space=pltpu.VMEM)
    hbm = pl.BlockSpec(memory_space=pl.ANY)
    rows, width = hidden.shape
    a_in, a_out, total, input_grad = pl.pallas_call(
        sums_kernel,
        in_specs=[hbm] * 9 + [vmem] * 6,
        out_specs=[vmem] * 4,
        out_shape=[
            Products.out_shape([d_rest], nm),
            Products.out_shape([og], no),
            jax.ShapeDtypeStruct(v.shape[1:], f32),
            jax.ShapeDtypeStruct((rows, width), bf16),
        ],
        scratch_shapes=[pltpu.VMEM(v.shape, f32)]
        + Products.scratch([d_rest], nm)
        + Products.scratch([og], no)
        + Smalls.scratch(v)
        + InputGrad.scratch(rows, width),
        compiler_params=pltpu.CompilerParams(
            collective_id=collective_id, has_side_effects=True, vmem_limit_bytes=VMEM_MOST
        ),
        cost_estimate=pl.CostEstimate(
            flops=12 * rows * width * 6000, bytes_accessed=400_000_000, transcendentals=0
        ),
        name="weight_sums",
    )(
        d_gate,
        d_rest,
        nm,
        nm_far,
        og,
        no,
        own,
        gate_others,
        conv_shards,
        v,
        d_dt,
        dt_w,
        hidden,
        gain,
        out_grad,
    )
    return a_in.reshape(d_rest.shape[1], -1), a_out.reshape(og.shape[1], -1), total, input_grad


LANES = 128
HALO = 16


def sigmoid(v):
    return 0.5 + 0.5 * jnp.tanh(0.5 * v)


def silu_parts(v):
    s = sigmoid(v)
    return v * s, s


def softplus(v):
    return jnp.maximum(v, 0.0) + jnp.log1p(jnp.exp(-jnp.abs(v)))


def lower_ones(t):
    i = lax.broadcasted_iota(jnp.int32, (t, t), 0)
    j = lax.broadcasted_iota(jnp.int32, (t, t), 1)
    return jnp.where(i >= j, 1.0, 0.0)


def exact(a, b, dims=NN):
    return lax.dot_general(a, b, dims, precision=highest, preferred_element_type=f32)


def head_columns(values, g):
    return pltpu.roll(values, (LANES - GROUP * g) % LANES, 1)[:, :GROUP]


class Exchange:
    def __init__(self, forward, own_low, got, t_low, t_got, u_low, u_got, p_low, p_got, send, recv):
        self.s, self.z, self.c, self.x, self.y, self.near = around()
        later = (lambda v: v) if forward else (lambda v: 1 - v)
        self.second = (later(self.c) == 1, later(self.x) == 1, later(self.y) == 1)
        self.own_low, self.got = own_low, got
        self.t_low, self.t_got, self.u_low, self.u_got = t_low, t_got, u_low, u_got
        self.p_low, self.p_got = p_low, p_got
        self.send, self.recv = send, recv
        self.n = t_low.shape[1] - 16
        self.half = t_low.shape[2]
        self.mine = pl.ds(pl.multiple_of(self.c * self.half, LANES), self.half)
        self.other = pl.ds(pl.multiple_of((1 - self.c) * self.half, LANES), self.half)

    def copy(self, kind, m):
        src, dst, to = (
            (self.own_low, self.got, "c"),
            (self.t_low, self.t_got, "x"),
            (self.u_low, self.u_got, "y"),
            (self.p_low, self.p_got, "c"),
        )[kind]
        return pltpu.make_async_remote_copy(
            src_ref=src.at[m],
            dst_ref=dst.at[m],
            send_sem=self.send.at[kind, m],
            recv_sem=self.recv.at[kind, m],
            device_id=self.near[to],
            device_id_type=MESH,
        )

    def put_decay(self, ref, m, lanes, decay):
        high = decay.astype(bf16).astype(f32)
        row = lax.broadcasted_iota(jnp.int32, (16, decay.shape[1]), 0)
        both = jnp.where(row == 0, high, jnp.where(row == 1, decay - high, 0.0))
        ref[m, pl.ds(self.n, 16), lanes] = both.astype(bf16)

    def decay_of(self, ref, m, lanes):
        rows = ref[m, pl.ds(self.n, 16), lanes].astype(f32)
        return rows[0:1] + rows[1:2]

    def put_own(self, m, lanes, state, decay):
        self.own_low[m, pl.ds(0, self.n), lanes] = state.astype(bf16)
        self.put_decay(self.own_low, m, lanes, decay)

    def core(self, m):
        self.copy(0, m).start()

    def along_x(self, m):
        self.copy(0, m).wait_recv()
        second = self.second[0]
        mine = self.own_low[m, pl.ds(0, self.n), self.mine].astype(f32)
        theirs = self.got[m, pl.ds(0, self.n), self.mine].astype(f32)
        d_mine = self.decay_of(self.own_low, m, self.mine)
        d_theirs = self.decay_of(self.got, m, self.mine)
        total = theirs * jnp.where(second, d_mine, 1.0) + mine * jnp.where(second, 1.0, d_theirs)
        self.t_low[m, pl.ds(0, self.n), :] = total.astype(bf16)
        self.put_decay(self.t_low, m, pl.ds(0, self.half), d_mine * d_theirs)
        self.copy(1, m).start()

    def along_y(self, m):
        self.copy(1, m).wait_recv()
        second = self.second[1]
        every = pl.ds(0, self.half)
        mine = self.t_low[m, pl.ds(0, self.n), :].astype(f32)
        theirs = self.t_got[m, pl.ds(0, self.n), :].astype(f32)
        d_mine = self.decay_of(self.t_low, m, every)
        d_theirs = self.decay_of(self.t_got, m, every)
        total = theirs * jnp.where(second, d_mine, 1.0) + mine * jnp.where(second, 1.0, d_theirs)
        self.u_low[m] = total.astype(bf16)
        self.copy(2, m).start()

    def back_to_core(self, m):
        self.copy(2, m).wait_recv()
        every = pl.ds(0, self.half)
        x_second = jnp.where(self.second[1], 1.0, 0.0)
        y_second = jnp.where(self.second[2], 1.0, 0.0)
        theirs = self.t_got[m, pl.ds(0, self.n), :].astype(f32)
        d_theirs = self.decay_of(self.t_got, m, every)
        over = y_second * jnp.where(self.second[1], d_theirs, 1.0)
        before = x_second * theirs + over * self.u_got[m].astype(f32)
        self.p_low[m] = before.astype(bf16)
        self.copy(3, m).start()

    def begin_state(self, m, out):
        self.copy(3, m).wait_recv()
        second = jnp.where(self.second[0], 1.0, 0.0)
        for lanes, before in (
            (self.mine, self.p_low[m].astype(f32)),
            (self.other, self.p_got[m].astype(f32)),
        ):
            d_theirs = self.decay_of(self.got, m, lanes)
            theirs = self.got[m, pl.ds(0, self.n), lanes].astype(f32)
            over = jnp.where(self.second[0], d_theirs, 1.0)
            out[m, :, lanes] = (before * over + second * theirs).astype(bf16)

    def sent(self):
        for m in range(self.own_low.shape[0]):
            for kind in range(4):
                self.copy(kind, m).wait_send()


def exchange_scratch(micro, n, inner):
    half = inner // 2
    dma = pltpu.SemaphoreType.DMA
    return [
        pltpu.VMEM((micro, n + 16, inner), bf16),
        pltpu.VMEM((micro, n + 16, inner), bf16),
        pltpu.VMEM((micro, n + 16, half), bf16),
        pltpu.VMEM((micro, n + 16, half), bf16),
        pltpu.VMEM((micro, n, half), bf16),
        pltpu.VMEM((micro, n, half), bf16),
        pltpu.VMEM((micro, n, half), bf16),
        pltpu.VMEM((micro, n, half), bf16),
        dma((4, micro)),
        dma((4, micro)),
    ]


EXCHANGE = 10
TICKS = (12, 3, 2, 2)


def steps_of(raw, shift, rate):
    t = raw.shape[0]
    dt = softplus(raw + shift)
    cum = exact(lower_ones(t), dt * rate)
    return dt, cum


def conv_rows(buf, cw, cb):
    taps = cw.shape[0]
    t = buf.shape[0] - HALO
    total = cb + buf[HALO - taps + 1 : HALO - taps + 1 + t, :] * cw[0:1]
    for k in range(1, taps):
        at = HALO - taps + 1 + k
        total = total + buf[at : at + t, :] * cw[k : k + 1]
    return total


def scan_forward_kernel(
    hs,
    conv_ref,
    raw_ref,
    cw_ref,
    cb_ref,
    shift_ref,
    rate_ref,
    skip_ref,
    eighth_ref,
    x_ref,
    bc_ref,
    y_ref,
    low_ref,
    halo,
    begin_ref,
    others_ref,
    *scratch,
):
    buf, wide_buf, scores, dts, cums, rows_t, h_send, h_recv, o_send, o_recv, o_own = scratch[EXCHANGE:]
    ex = Exchange(True, *scratch[:EXCHANGE])
    s, z = ex.s, ex.z
    micro, t, channels = conv_ref.shape
    inner = x_ref.shape[2]
    n = begin_ref.shape[1]
    gc = GROUP * hs
    groups = inner // gc
    half_t = t // 2
    place = around()
    near = {k: ex.near[k] for k in ("c", "x", "y")}
    near["next"] = ((s + 1) % 8, z)
    near["last"] = ((s + 7) % 8, z)
    greet(near)
    weight = Gather(
        place, [(eighth_ref, None, others_ref, others_ref.shape[1], 2)], o_send, o_recv, o_own
    )

    tail = [
        pltpu.make_async_remote_copy(
            src_ref=conv_ref.at[m, pl.ds(t - HALO, HALO)],
            dst_ref=halo.at[m],
            send_sem=h_send.at[m],
            recv_sem=h_recv.at[m],
            device_id=near["next"],
            device_id_type=MESH,
        )
        for m in range(micro)
    ]
    for copy in tail:
        copy.start()
    weight.begin(0)
    for m in range(micro):
        dt, cum = steps_of(raw_ref[m], shift_ref[...], rate_ref[...])
        dts[m] = dt
        cums[m] = cum
        rows_t[m] = cum.T
    for copy in tail:
        copy.wait_recv()
    has_prior = jnp.where(s > 0, 1.0, 0.0)

    def activate(m, lanes, into):
        into[0:HALO] = halo[m, :, lanes].astype(f32) * has_prior
        into[pl.ds(HALO, t)] = conv_ref[m, :, lanes].astype(f32)
        return silu_parts(conv_rows(into, cw_ref[:, lanes], cb_ref[:, lanes]))[0]

    def own_states(m, a, b):
        def body(g, carry):
            lanes = pl.ds(pl.multiple_of(g * gc, gc), gc)
            x = activate(m, lanes, buf).astype(bf16)
            x_ref[m, :, lanes] = x
            cum = head_columns(cums[m], g)
            to_end = head_columns(dts[m], g) * jnp.exp(cum[t - 1 :] - cum)
            weighted = (x.astype(f32) * widen(to_end, hs)).astype(bf16)
            state = mm(bc_ref[m, :, 0:n], weighted, TN)
            ex.put_own(m, lanes, state, widen(jnp.exp(cum[t - 1 :]), hs))
            return carry

        lax.fori_loop(a, b, body, 0)

    def local_scans(m, a, b):
        lane = lax.broadcasted_iota(jnp.int32, (half_t, 2 * hs), 1)

        def body(g, carry):
            lanes = pl.ds(pl.multiple_of(g * gc, gc), gc)
            cum = head_columns(cums[m], g)
            rows = rows_t[m, pl.ds(pl.multiple_of(g * GROUP, GROUP), GROUP), :]
            dt_wide = widen(head_columns(dts[m], g), hs)
            weighted = (x_ref[m, :, lanes].astype(f32) * dt_wide).astype(bf16)
            for k in range(0, GROUP, 2):
                pair = weighted[:, k * hs : (k + 2) * hs]
                at = pl.ds(pl.multiple_of(g * gc + k * hs, 2 * hs), 2 * hs)
                top, low = [], []
                for h in (k, k + 1):
                    col, row = cum[:, h : h + 1], rows[h : h + 1, :]
                    m1 = jnp.exp(jnp.minimum(col[:half_t] - row[:, :half_t], 0.0))
                    m2 = jnp.exp(jnp.minimum(col[half_t:] - row, 0.0))
                    m1 = (m1 * scores[m, :half_t, :half_t]).astype(bf16)
                    m2 = (m2 * scores[m, half_t:, :]).astype(bf16)
                    top.append(mm(m1, pair[:half_t]))
                    low.append(mm(m2, pair))
                y_ref[m, :half_t, at] = jnp.where(lane < hs, top[0], top[1])
                y_ref[m, half_t:, at] = jnp.where(lane < hs, low[0], low[1])
            return carry

        lax.fori_loop(a, b, body, 0)

    def carried(m):
        def body(g, carry):
            lanes = pl.ds(pl.multiple_of(g * gc, gc), gc)
            decay = widen(jnp.exp(head_columns(cums[m], g)), hs)
            scan = y_ref[m, :, lanes] + decay * mm(bc_ref[m, :, n:], begin_ref[m, :, lanes])
            y_ref[m, :, lanes] = scan
            x = x_ref[m, :, lanes].astype(f32)
            low_ref[m, :, lanes] = (scan + skip_ref[:, lanes] * x).astype(bf16)
            return carry

        lax.fori_loop(0, groups, body, 0)

    for m in range(micro):
        lanes = pl.ds(inner, channels - inner)
        bc = activate(m, lanes, wide_buf).astype(bf16)
        bc_ref[m] = bc
        scores[m] = mm(bc[:, n:], bc[:, :n], NT) * lower_ones(t)
    middle = groups // 2
    own_states(0, 0, groups)
    ex.core(0)
    own_states(1, 0, middle)
    ex.along_x(0)
    own_states(1, middle, groups)
    ex.core(1)
    weight.begin(1)
    local_scans(0, 0, middle)
    ex.along_x(1)
    ex.along_y(0)
    local_scans(0, middle, groups)
    weight.middle(0)
    local_scans(1, 0, middle)
    ex.along_y(1)
    weight.middle(1)
    weight.finish(0)
    ex.back_to_core(0)
    local_scans(1, middle, groups)
    ex.begin_state(0, begin_ref)
    carried(0)
    weight.finish(1)
    ex.back_to_core(1)
    ex.begin_state(1, begin_ref)
    carried(1)
    weight.close()
    ex.sent()
    for copy in tail:
        copy.wait_send()


def scan_forward(
    conv_low, raw, conv_w, conv_b, shift, rate, skip_wide, out_eighth, inner, hs, collective_id
):
    micro, t, channels = conv_low.shape
    n = (channels - inner) // 2
    gc = GROUP * hs
    dma = pltpu.SemaphoreType.DMA
    vmem = pl.BlockSpec(memory_space=pltpu.VMEM)
    hbm = pl.BlockSpec(memory_space=pl.ANY)
    return pl.pallas_call(
        partial(scan_forward_kernel, hs),
        in_specs=[vmem] * 8,
        out_specs=[vmem] * 6 + [hbm],
        out_shape=[
            jax.ShapeDtypeStruct((micro, t, inner), bf16),
            jax.ShapeDtypeStruct((micro, t, 2 * n), bf16),
            jax.ShapeDtypeStruct((micro, t, inner), f32),
            jax.ShapeDtypeStruct((micro, t, inner), bf16),
            jax.ShapeDtypeStruct((micro, HALO, channels), bf16),
            jax.ShapeDtypeStruct((micro, n, inner), bf16),
            jax.ShapeDtypeStruct((3, 8 * out_eighth.shape[1], out_eighth.shape[2]), bf16),
        ],
        scratch_shapes=exchange_scratch(micro, n, inner)
        + [
            pltpu.VMEM((HALO + t, gc), f32),
            pltpu.VMEM((HALO + t, 2 * n), f32),
            pltpu.VMEM((micro, t, t), f32),
            pltpu.VMEM((micro, t, LANES), f32),
            pltpu.VMEM((micro, t, LANES), f32),
            pltpu.VMEM((micro, LANES, t), f32),
            dma((micro,)),
            dma((micro,)),
            dma((2, CHUNK_DMAS)),
            dma((2, CHUNK_DMAS)),
            dma((2,)),
        ],
        compiler_params=pltpu.CompilerParams(
            collective_id=collective_id, has_side_effects=True, vmem_limit_bytes=VMEM_MOST
        ),
        cost_estimate=pl.CostEstimate(
            flops=4 * micro * t * inner * (t + 3 * n), bytes_accessed=100_000_000, transcendentals=0
        ),
        name="scan_forward",
    )(conv_low, raw, conv_w, conv_b, shift, rate, skip_wide, out_eighth)


def scan_backward_kernel(
    hs,
    dy_ref,
    x_ref,
    bc_ref,
    y_ref,
    begin_ref,
    raw_ref,
    conv_ref,
    halo_ref,
    cw_ref,
    cb_ref,
    shift_ref,
    rate_ref,
    skip_ref,
    dgate_ref,
    norm_ref,
    dconv_ref,
    dcw_ref,
    dcb_ref,
    heads_ref,
    sum_ref,
    far_ref,
    far_sem,
    *scratch,
):
    (
        y_now,
        y_sem,
        buf,
        wide_buf,
        scores,
        total,
        dts,
        cums,
        rows_t,
        ends,
        dxl,
        dbc,
        ddt_sum,
        dcum_sum,
        last_sum,
        head_low,
        next_low,
        h_send,
        h_recv,
    ) = scratch[EXCHANGE : EXCHANGE + 19]
    ex = Exchange(False, *scratch[:EXCHANGE])
    s, z = ex.s, ex.z
    micro, t, channels = conv_ref.shape
    inner = x_ref.shape[2]
    n = begin_ref.shape[1]
    gc = GROUP * hs
    groups = inner // gc
    half = t // 2
    taps = cw_ref.shape[0]
    place = around()
    near = dict(place[-1])
    near["next"] = ((s + 1) % 8, z)
    near["last"] = ((s + 7) % 8, z)
    sums_of = Products(place, [dgate_ref], norm_ref, sum_ref, scratch[EXCHANGE + 19 :])
    sums_of.load()

    def y_copy(i):
        lanes = pl.ds(pl.multiple_of((i % groups) * gc, gc), gc)
        slot = i % 2
        return pltpu.make_async_copy(y_ref.at[i // groups, :, lanes], y_now.at[slot], y_sem.at[slot])

    greet(near)
    sums_of.share()
    first_rows = [
        pltpu.make_async_remote_copy(
            src_ref=head_low.at[m],
            dst_ref=next_low.at[m],
            send_sem=h_send.at[m],
            recv_sem=h_recv.at[m],
            device_id=near["last"],
            device_id_type=MESH,
        )
        for m in range(micro)
    ]
    has_prior = jnp.where(s > 0, 1.0, 0.0)
    has_next = jnp.where(s < 7, 1.0, 0.0)

    middle = groups // 2

    def at_step(i, *todo):
        for when, what in todo:
            pl.when(i == when)(what)

    def own_states():
        def body(i, carry):
            m, g = i // groups, i % groups
            lanes = pl.ds(pl.multiple_of(g * gc, gc), gc)
            cum = head_columns(cums[m], g)
            weighted = (dy_ref[m, :, lanes].astype(f32) * widen(jnp.exp(cum), hs)).astype(bf16)
            state = mm(bc_ref[m, :, n:], weighted, TN)
            ex.put_own(m, lanes, state, widen(jnp.exp(cum[t - 1 :]), hs))
            at_step(
                i,
                (groups - 1, lambda: ex.core(0)),
                (groups + middle, lambda: ex.along_x(0)),
                (2 * groups - 1, lambda: ex.core(1)),
            )
            tick(i, TICKS[0], 0)
            return carry

        lax.fori_loop(0, 2 * groups, body, 0)

    def tick(i, every, first):
        @pl.when(i % every == every - 1)
        def _():
            sums_of.step(first + i // every)

    def upper_ones():
        j = lax.broadcasted_iota(jnp.int32, (t, t), 0)
        i = lax.broadcasted_iota(jnp.int32, (t, t), 1)
        return jnp.where(i >= j, 1.0, 0.0)

    def local_terms():
        lane = lax.broadcasted_iota(jnp.int32, (t, 2 * hs), 1)
        lane_half = lax.broadcasted_iota(jnp.int32, (half, 2 * hs), 1)

        def body(i, carry):
            m, g = i // groups, i % groups
            lanes = pl.ds(pl.multiple_of(g * gc, gc), gc)
            cum = head_columns(cums[m], g)
            rows = rows_t[m, pl.ds(pl.multiple_of(g * GROUP, GROUP), GROUP), :]
            dt_wide = widen(head_columns(dts[m], g), hs)
            weighted = (x_ref[m, :, lanes].astype(f32) * dt_wide).astype(bf16)
            for k in range(0, GROUP, 2):
                pair = weighted[:, k * hs : (k + 2) * hs]
                at = pl.ds(pl.multiple_of(g * gc + k * hs, 2 * hs), 2 * hs)
                dy = dy_ref[m, :, at]
                top, low = [], []
                for h in (k, k + 1):
                    col, row = cum[:, h : h + 1], rows[h : h + 1, :]
                    mine = jnp.where(lane < hs, pair, 0) if h == k else jnp.where(lane < hs, 0, pair)
                    l1 = jnp.exp(jnp.minimum(row - col[:half], 0.0))
                    l2 = jnp.exp(jnp.minimum(row[:, half:] - col[half:], 0.0))
                    total[:half, :] += l1 * mm(mine[:half], dy, NT)
                    total[half:, half:] += l2 * mm(mine[half:], dy[half:], NT)
                    top.append(mm((l1 * scores[m, :half, :]).astype(bf16), dy))
                    low.append(mm((l2 * scores[m, half:, half:]).astype(bf16), dy[half:]))
                dxl[m, :half, at] = jnp.where(lane_half < hs, top[0], top[1])
                dxl[m, half:, at] = jnp.where(lane_half < hs, low[0], low[1])
            at_step(
                i,
                (1, lambda: ex.along_x(1)),
                (3, lambda: ex.along_y(0)),
                (groups - 1, lambda: local_close(0)),
                (groups + 1, lambda: ex.along_y(1)),
                (groups + 3, lambda: ex.back_to_core(0)),
                (2 * groups - 1, lambda: local_close(1)),
            )
            tick(i, TICKS[1], 2 * groups // TICKS[0])
            return carry

        lax.fori_loop(0, 2 * groups, body, 0)

    def local_close(m):
        d = total[...] * upper_ones()
        dbc[m, :, 0:n] = mm(d.astype(bf16), bc_ref[m, :, n:])
        dbc[m, :, n:] = mm(d.T.astype(bf16), bc_ref[m, :, :n])
        total[...] = jnp.zeros_like(total)

    def through_states():
        r = lax.broadcasted_iota(jnp.int32, (gc, LANES), 0)
        col = lax.broadcasted_iota(jnp.int32, (gc, LANES), 1)

        def clear():
            ddt_sum[...] = jnp.zeros_like(ddt_sum)
            dcum_sum[...] = jnp.zeros_like(dcum_sum)
            last_sum[...] = jnp.zeros_like(last_sum)

        def close(m):
            d_log = exact(upper_ones(), dcum_sum[...]) + last_sum[0:1]
            v = raw_ref[m] + shift_ref[...]
            d_dt = (ddt_sum[...] + d_log * rate_ref[...]) / (1.0 + jnp.exp(-v))
            rest = dconv_ref.shape[2] - channels - LANES
            dconv_ref[m, :, pl.ds(channels, LANES)] = d_dt.astype(bf16)
            if rest:
                dconv_ref[m, :, pl.ds(channels + LANES, rest)] = jnp.zeros((t, rest), bf16)
            heads_ref[0:1] += jnp.sum(d_dt, axis=0, keepdims=True)
            heads_ref[1:2] += jnp.sum(d_log * dts[m], axis=0, keepdims=True) * rate_ref[...]
            first_slopes(m)
            if m == 0:
                clear()
                ex.begin_state(1, ends)

        def body(i, carry):
            m, g = i // groups, i % groups
            lanes = pl.ds(pl.multiple_of(g * gc, gc), gc)

            @pl.when(i + 1 < 2 * groups)
            def _():
                y_copy(i + 1).start()

            y_copy(i).wait()
            ones = jnp.where(r // hs + g * GROUP == col, 1.0, 0.0).astype(bf16)
            cum = head_columns(cums[m], g)
            dt_wide = widen(head_columns(dts[m], g), hs)
            x, dy = x_ref[m, :, lanes].astype(f32), dy_ref[m, :, lanes].astype(f32)
            weighted = (x * dt_wide).astype(bf16).astype(f32)
            decay = widen(jnp.exp(cum), hs)
            to_end = widen(jnp.exp(cum[t - 1 :] - cum), hs)
            s_in, ds = begin_ref[m, :, lanes], ends[m, :, lanes]
            through = to_end * mm(bc_ref[m, :, 0:n], ds)
            d_weighted = dxl[m, :, lanes] + through
            dconv_ref[m, :, lanes] = (dt_wide * d_weighted + skip_ref[:, lanes] * dy).astype(bf16)
            dbc[m, :, 0:n] += mm((weighted * to_end).astype(bf16), ds, NT)
            dbc[m, :, n:] += mm((dy * decay).astype(bf16), s_in, NT)
            ddt_sum[...] += head_sums(x * d_weighted, ones)
            dcum_sum[...] += head_sums(dy * y_now[i % 2] - weighted * d_weighted, ones)
            at_end = jnp.sum(weighted * through, axis=0, keepdims=True) + decay[t - 1 :] * jnp.sum(
                s_in.astype(f32) * ds.astype(f32), axis=0, keepdims=True
            )
            last_sum[...] += head_sums(jnp.broadcast_to(at_end, (8, gc)), ones)
            by_skip = jnp.sum(x * dy, axis=0, keepdims=True)
            heads_ref[2:3] += head_sums(jnp.broadcast_to(by_skip, (8, gc)), ones)[0:1]
            at_step(i, (groups - 1, lambda: close(0)), (2 * groups - 1, lambda: close(1)))
            tick(i, TICKS[2], 2 * groups // TICKS[0] + 2 * groups // TICKS[1])
            return carry

        clear()
        heads_ref[...] = jnp.zeros_like(heads_ref)
        y_copy(0).start()
        lax.fori_loop(0, 2 * groups, body, 0)

    def pre_slope(into, lanes, grad, rows):
        v = conv_rows(into[0 : HALO + rows, :], cw_ref[:, lanes], cb_ref[:, lanes])
        sig = sigmoid(v)
        return grad * (sig * (1.0 + v * (1.0 - sig)))

    def load(m, lanes, into, rows):
        into[0:HALO] = halo_ref[m, :, lanes].astype(f32) * has_prior
        into[HALO : HALO + rows] = conv_ref[m, 0:rows, lanes].astype(f32)

    def first_slopes(m):
        def one(lanes, into, grad):
            load(m, lanes, into, HALO)
            head_low[m, :, lanes] = pre_slope(into, lanes, grad, HALO).astype(bf16)

        def body(g, carry):
            lanes = pl.ds(pl.multiple_of(g * gc, gc), gc)
            one(lanes, buf, dconv_ref[m, 0:HALO, lanes].astype(f32))
            return carry

        lax.fori_loop(0, groups, body, 0)
        one(pl.ds(inner, channels - inner), wide_buf, dbc[m, 0:HALO, :])
        first_rows[m].start()

    def conv_back():
        def one(m, lanes, into, grad):
            load(m, lanes, into, t)
            slope = pre_slope(into, lanes, grad, t)
            weights = cw_ref[:, lanes]
            lines = []
            for k in range(taps):
                at = HALO - taps + 1 + k
                lines.append(jnp.sum(slope * into[at : at + t, :], axis=0, keepdims=True))
            dcw_ref[:, lanes] += jnp.concatenate(lines, axis=0)
            dcb_ref[:, lanes] += jnp.sum(slope, axis=0, keepdims=True)
            into[0:t] = slope
            into[t : t + HALO] = next_low[m, :, lanes].astype(f32) * has_next
            back = into[taps - 1 : taps - 1 + t, :] * weights[0:1]
            for k in range(1, taps):
                at = taps - 1 - k
                back = back + into[at : at + t, :] * weights[k : k + 1]
            dconv_ref[m, :, lanes] = back.astype(bf16)

        def body(i, carry):
            m, g = i // groups, i % groups
            lanes = pl.ds(pl.multiple_of(g * gc, gc), gc)
            one(m, lanes, buf, dconv_ref[m, :, lanes].astype(f32))
            at_step(i, (groups - 1, lambda: first_rows[1].wait_recv()))
            tick(i, TICKS[3], 2 * groups // TICKS[0] + 2 * groups // TICKS[1] + 2 * groups // TICKS[2])
            return carry

        first_rows[0].wait_recv()
        lax.fori_loop(0, 2 * groups, body, 0)
        for m in range(micro):
            one(m, pl.ds(inner, channels - inner), wide_buf, dbc[m])

    for m in range(micro):
        dt, cum = steps_of(raw_ref[m], shift_ref[...], rate_ref[...])
        dts[m] = dt
        cums[m] = cum
        rows_t[m] = cum.T
        scores[m] = mm(bc_ref[m, :, 0:n], bc_ref[m, :, n:], NT) * upper_ones()
    dcw_ref[...] = jnp.zeros_like(dcw_ref)
    dcb_ref[...] = jnp.zeros_like(dcb_ref)
    total[...] = jnp.zeros_like(total)
    own_states()
    local_terms()
    ex.begin_state(0, ends)
    ex.back_to_core(1)
    through_states()
    conv_back()
    done = sum(2 * groups // every for every in TICKS)

    def rest_of(i, carry):
        sums_of.step(i)
        return carry

    rows = far_ref.shape[0]
    far = pltpu.make_async_copy(sums_of.b.at[pl.ds(rows, rows)], far_ref, far_sem)
    far.start()
    lax.fori_loop(done, sums_of.steps(), rest_of, 0)
    far.wait()
    ex.sent()
    for copy in first_rows:
        copy.wait_send()
    sums_of.close()


def scan_backward(
    dy,
    x,
    bc,
    y,
    begin,
    raw,
    conv_low,
    halo,
    conv_w,
    conv_b,
    shift,
    rate,
    skip_wide,
    d_gate,
    normed,
    hs,
    collective_id,
):
    micro, t, channels = conv_low.shape
    inner = x.shape[2]
    n = begin.shape[1]
    gc = GROUP * hs
    taps = conv_w.shape[0]
    dma = pltpu.SemaphoreType.DMA
    vmem = pl.BlockSpec(memory_space=pltpu.VMEM)
    hbm = pl.BlockSpec(memory_space=pl.ANY)
    return pl.pallas_call(
        partial(scan_backward_kernel, hs),
        in_specs=[vmem] * 3 + [hbm] + [vmem] * 9 + [hbm] * 2,
        out_specs=[vmem] * 5 + [hbm],
        out_shape=[
            jax.ShapeDtypeStruct((micro, t, -(-(channels + LANES) // 256) * 256), bf16),
            jax.ShapeDtypeStruct((taps, channels), f32),
            jax.ShapeDtypeStruct((1, channels), f32),
            jax.ShapeDtypeStruct((8, LANES), f32),
            Products.out_shape([d_gate], normed),
            jax.ShapeDtypeStruct(normed.shape, bf16),
        ],
        scratch_shapes=[dma]
        + exchange_scratch(micro, n, inner)
        + [
            pltpu.VMEM((2, t, gc), f32),
            dma((2,)),
            pltpu.VMEM((HALO + t, gc), f32),
            pltpu.VMEM((HALO + t, 2 * n), f32),
            pltpu.VMEM((micro, t, t), f32),
            pltpu.VMEM((t, t), f32),
            pltpu.VMEM((micro, t, LANES), f32),
            pltpu.VMEM((micro, t, LANES), f32),
            pltpu.VMEM((micro, LANES, t), f32),
            pltpu.VMEM((micro, n, inner), bf16),
            pltpu.VMEM((micro, t, inner), f32),
            pltpu.VMEM((micro, t, 2 * n), f32),
            pltpu.VMEM((t, LANES), f32),
            pltpu.VMEM((t, LANES), f32),
            pltpu.VMEM((8, LANES), f32),
            pltpu.VMEM((micro, HALO, channels), bf16),
            pltpu.VMEM((micro, HALO, channels), bf16),
            dma((micro,)),
            dma((micro,)),
        ]
        + Products.scratch([d_gate], normed),
        compiler_params=pltpu.CompilerParams(
            collective_id=collective_id, has_side_effects=True, vmem_limit_bytes=VMEM_MOST
        ),
        cost_estimate=pl.CostEstimate(
            flops=8 * micro * t * inner * (t + 3 * n), bytes_accessed=100_000_000, transcendentals=0
        ),
        name="scan_backward",
    )(
        dy,
        x,
        bc,
        y,
        begin,
        raw,
        conv_low,
        halo,
        conv_w,
        conv_b,
        shift,
        rate,
        skip_wide,
        d_gate,
        normed,
    )


def shard_place(k, depth):
    z = lax.axis_index("wshard")
    other = (z, z + 1 - 2 * (z % 2), z + 2 - 4 * (z // 2), 3 - z)[k]
    return pl.ds(pl.multiple_of(other * depth, 128), depth)


def front_kernel(h_ref, g_ref, dtw_ref, v_ref, conv_ref, norm_ref, raw_ref, rel):
    depth = v_ref.shape[2]

    @pl.when(pl.program_id(0) == 0)
    def _():
        h = h_ref[...].astype(f32)
        power = jnp.mean(h * h, axis=-1, keepdims=True)
        normed = (h * lax.rsqrt(power + epsilon) * g_ref[...]).astype(bf16)
        norm_ref[...] = normed
        raw_ref[...] = mm(normed, dtw_ref[...], NT).astype(bf16).astype(f32)
        for k in range(4):
            rel[:, k * depth : (k + 1) * depth] = norm_ref[:, shard_place(k, depth)]

    weights = jnp.concatenate([v_ref[k] for k in (3, 0, 1, 2)], axis=1)
    conv_ref[...] = mm(rel[...], weights, NT).astype(bf16)


def front(hidden, gain, dt_w, shards, tile):
    rows, width = hidden.shape
    _, count, depth = shards.shape
    whole = pl.BlockSpec((rows, width), lambda i: (0, 0))
    return pl.pallas_call(
        front_kernel,
        grid=(count // tile,),
        in_specs=[
            whole,
            pl.BlockSpec((1, width), lambda i: (0, 0)),
            pl.BlockSpec((LANES, width), lambda i: (0, 0)),
            pl.BlockSpec((4, tile, depth), lambda i: (0, i, 0)),
        ],
        out_specs=[
            pl.BlockSpec((rows, tile), lambda i: (0, i)),
            whole,
            pl.BlockSpec((rows, LANES), lambda i: (0, 0)),
        ],
        out_shape=[
            jax.ShapeDtypeStruct((rows, count), bf16),
            jax.ShapeDtypeStruct((rows, width), bf16),
            jax.ShapeDtypeStruct((rows, LANES), f32),
        ],
        scratch_shapes=[pltpu.VMEM((rows, width), bf16)],
        compiler_params=pltpu.CompilerParams(vmem_limit_bytes=VMEM),
        name="front",
    )(hidden, gain, dt_w, shards)


def gate_kernel(
    scan_ref,
    norm_ref,
    w_ref,
    v_ref,
    gain_ref,
    ow_ref,
    ov_ref,
    h_ref,
    og_ref,
    valid_ref,
    no_ref,
    out_ref,
    g_ref,
    dy_ref,
    dgate_ref,
    dgain_ref,
    gate,
    d_no,
    branch,
):
    inner = scan_ref.shape[1]
    depth = w_ref.shape[1]
    block = ow_ref.shape[0]
    rows = scan_ref.shape[0]

    @pl.when(pl.program_id(0) == 0)
    def _():
        dgain_ref[...] = jnp.zeros_like(dgain_ref)

    rel = jnp.concatenate([norm_ref[:, shard_place(k, depth)] for k in range(4)], axis=1)
    valid = valid_ref[...]
    g_low = (og_ref[...].astype(f32) * valid).astype(bf16)
    g_ref[...] = g_low
    power = jnp.zeros((rows, 1), f32)
    for i in range(4):
        at = slice(i * block, (i + 1) * block)
        weights = jnp.concatenate([w_ref[at, :]] + [v_ref[k, at, :] for k in range(3)], axis=1)
        value = mm(rel, weights, NT)
        gate[:, at] = value
        act, _ = silu_parts(value)
        u = scan_ref[:, at].astype(f32) * act
        power += jnp.sum(u * u, axis=-1, keepdims=True)
    scale = lax.rsqrt(power / inner + epsilon)
    along = jnp.zeros((rows, 1), f32)
    for k in range(4):
        at = shard_place(k, block)
        weights = ow_ref[...] if k == 0 else ov_ref[k - 1]
        act, _ = silu_parts(gate[:, at])
        u = scan_ref[:, at].astype(f32) * act
        normed = u * scale
        low = (normed * gain_ref[:, at]).astype(bf16)
        no_ref[:, at] = low
        if k == 0:
            branch[...] = mm(low, weights)
        else:
            branch[...] += mm(low, weights)
        d = mm(g_low, weights, NT)
        dgain_ref[:, at] += jnp.sum(d * normed, axis=0, keepdims=True)
        d = d * gain_ref[:, at]
        d_no[:, at] = d
        along += jnp.sum(d * u, axis=-1, keepdims=True)
    out_ref[...] = (h_ref[...].astype(f32) + valid * branch[...]).astype(bf16)
    along = along * scale * scale * scale / inner
    for i in range(4):
        at = slice(i * block, (i + 1) * block)
        value = gate[:, at]
        act, sig = silu_parts(value)
        v = scan_ref[:, at].astype(f32)
        d_u = scale * d_no[:, at] - v * act * along
        dy_ref[:, at] = (d_u * act).astype(bf16)
        dgate_ref[:, at] = (d_u * v * (sig * (1.0 + value * (1.0 - sig)))).astype(bf16)


def gate_stage(scanned, normed, own, others, gain, out_own, out_others, hidden, out_grad, valid, tile):
    rows, width = hidden.shape
    _, inner, depth = others.shape
    once = pl.Buffered(1)
    wide = pl.BlockSpec((tile, inner), lambda i: (i, 0))
    slim = pl.BlockSpec((tile, width), lambda i: (i, 0))
    line = pl.BlockSpec((1, inner), lambda i: (0, 0))
    return pl.pallas_call(
        gate_kernel,
        grid=(rows // tile,),
        in_specs=[
            wide,
            slim,
            pl.BlockSpec((inner, depth), lambda i: (0, 0), pipeline_mode=once),
            pl.BlockSpec(others.shape, lambda i: (0, 0, 0), pipeline_mode=once),
            line,
            pl.BlockSpec(out_own.shape, lambda i: (0, 0), pipeline_mode=once),
            pl.BlockSpec(out_others.shape, lambda i: (0, 0, 0), pipeline_mode=once),
            slim,
            slim,
            pl.BlockSpec((tile, 1), lambda i: (i, 0)),
        ],
        out_specs=[wide, slim, slim, wide, wide, line],
        out_shape=[
            jax.ShapeDtypeStruct((rows, inner), bf16),
            jax.ShapeDtypeStruct((rows, width), bf16),
            jax.ShapeDtypeStruct((rows, width), bf16),
            jax.ShapeDtypeStruct((rows, inner), bf16),
            jax.ShapeDtypeStruct((rows, inner), bf16),
            jax.ShapeDtypeStruct((1, inner), f32),
        ],
        scratch_shapes=[
            pltpu.VMEM((tile, inner), f32),
            pltpu.VMEM((tile, inner), f32),
            pltpu.VMEM((tile, width), f32),
        ],
        compiler_params=pltpu.CompilerParams(vmem_limit_bytes=VMEM_MOST),
        name="gate_stage",
    )(scanned, normed, own, others, gain, out_own, out_others, hidden, out_grad, valid)


def turn_kernel(x_ref, o_ref):
    o_ref[...] = x_ref[...].astype(f32).T


def turned(x, tile):
    rows, columns = x.shape
    return pl.pallas_call(
        turn_kernel,
        grid=(rows // tile,),
        in_specs=[pl.BlockSpec((tile, columns), lambda i: (i, 0))],
        out_specs=pl.BlockSpec((columns, tile), lambda i: (0, i)),
        out_shape=jax.ShapeDtypeStruct((columns, rows), f32),
        compiler_params=pltpu.CompilerParams(vmem_limit_bytes=VMEM),
        name="turned",
    )(x)


def project_kernel(n_ref, w_ref, v_ref, o_ref):
    total = mm(n_ref[0], w_ref[...], NT)
    for k in range(1, n_ref.shape[0]):
        total += mm(n_ref[k], v_ref[k - 1], NT)
    o_ref[...] = total.astype(o_ref.dtype)


def project(parts, own, others, first, count, tile, dtype):
    shards, rows, depth = parts.shape
    return pl.pallas_call(
        project_kernel,
        grid=(count // tile,),
        in_specs=[
            pl.BlockSpec((shards, rows, depth), lambda i: (0, 0, 0)),
            pl.BlockSpec((tile, depth), lambda i: (first // tile + i, 0)),
            pl.BlockSpec((shards - 1, tile, depth), lambda i: (0, first // tile + i, 0)),
        ],
        out_specs=pl.BlockSpec((rows, tile), lambda i: (0, i)),
        out_shape=jax.ShapeDtypeStruct((rows, count), dtype),
        compiler_params=pltpu.CompilerParams(vmem_limit_bytes=VMEM),
        name="project",
    )(parts, own, others)


def unproject_kernel(steps, d_ref, e_ref, w_ref, v_ref, o_ref):
    def add(ref):
        o_ref[0] += mm(ref[...], w_ref[...])
        for k in range(1, o_ref.shape[0]):
            o_ref[k] += mm(ref[...], v_ref[k - 1])

    @pl.when(pl.program_id(0) == 0)
    def _():
        o_ref[...] = jnp.zeros_like(o_ref)

    @pl.when(pl.program_id(0) < steps)
    def _():
        add(d_ref)

    @pl.when(pl.program_id(0) >= steps)
    def _():
        add(e_ref)


def unproject(d, e, own, others, tile):
    shards, count, depth = others.shape
    shards += 1
    rows = d.shape[0]
    steps = d.shape[1] // tile
    return pl.pallas_call(
        partial(unproject_kernel, steps),
        grid=(count // tile,),
        in_specs=[
            pl.BlockSpec((rows, tile), lambda i: (0, jnp.minimum(i, steps - 1))),
            pl.BlockSpec((rows, tile), lambda i: (0, jnp.maximum(i - steps, 0))),
            pl.BlockSpec((tile, depth), lambda i: (i, 0)),
            pl.BlockSpec((shards - 1, tile, depth), lambda i: (0, i, 0)),
        ],
        out_specs=pl.BlockSpec((shards, rows, depth), lambda i: (0, 0, 0)),
        out_shape=jax.ShapeDtypeStruct((shards, rows, depth), f32),
        compiler_params=pltpu.CompilerParams(vmem_limit_bytes=VMEM),
        name="unproject",
    )(d, e, own, others)


def rms_front(hidden_rows, gain):
    power = jnp.mean(hidden_rows * hidden_rows, axis=-1, keepdims=True)
    return hidden_rows * lax.rsqrt(power + epsilon) * gain


def conv_act(padded, conv_w, conv_b):
    taps = conv_w.shape[0]
    rows_out = padded.shape[1] - taps + 1
    total = conv_b + padded[:, 0:rows_out] * conv_w[0]
    for offset in range(1, taps):
        total = total + padded[:, offset : offset + rows_out] * conv_w[offset]
    return jax.nn.silu(total)


def gate_norm(values, gate_in, gain):
    gated = values * jax.nn.silu(gate_in)
    power = jnp.mean(gated * gated, axis=-1, keepdims=True)
    return gated * lax.rsqrt(power + epsilon) * gain


def local(
    hidden,
    lengths,
    out_grad,
    norm_gain,
    in_weight,
    conv_weight,
    conv_bias,
    dt_bias,
    a_log,
    skip_gain,
    gated_gain,
    out_weight,
):
    count = lax.axis_size("seq")
    shards = lax.axis_size("wshard")
    rank = lax.axis_index("seq")
    shard = lax.axis_index("wshard")
    micro, _, tokens, width = hidden.shape
    taps = conv_weight.shape[1]
    inner = out_weight.shape[0] * shards
    channels = conv_bias.shape[0] * shards
    heads = dt_bias.shape[0] * shards
    hs = inner // heads
    n = (channels - inner) // 2
    groups = heads // GROUP
    rows = micro * tokens
    fast = count == 8 and shards == 4 and micro == 2
    in_local = in_weight.T
    small = [norm_gain, conv_weight.T.reshape(-1), conv_bias, dt_bias, a_log, skip_gain, gated_gain]
    sizes = [v.shape[0] for v in small]
    small.append(in_local[inner + channels :].reshape(-1))
    packed_low = lax.all_gather(jnp.concatenate(small), "wshard", axis=0)
    packed = packed_low.astype(f32)
    parts, at = [], 0
    for size in sizes:
        parts.append(packed[:, at : at + size])
        at += size
    norm_g = parts[0].reshape(-1)
    conv_w = parts[1].reshape(shards, taps, -1).transpose(1, 0, 2).reshape(taps, -1)
    conv_b = parts[2].reshape(-1)
    dt_shift = parts[3].reshape(-1)
    rate = -jnp.exp(parts[4].reshape(-1))
    skip = parts[5].reshape(-1)
    gated_g = parts[6].reshape(-1)

    dt_w = packed_low[:, at:].reshape(shards, heads, -1).transpose(1, 0, 2).reshape(heads, -1)
    order = jnp.arange(shards) ^ shard
    if fast:
        conv_shards, gate_others, out_eighth = gather_input_weight(
            in_local, out_weight, inner, channels
        )
    else:
        every = lax.all_gather(in_local[: inner + channels], "wshard", axis=0)
        in_w = every[order[1:]]
        out_w = lax.all_gather(out_weight, "wshard", axis=0, tiled=True)

    def grouped(v):
        return v.reshape(micro, tokens, groups, GROUP).transpose(0, 2, 1, 3)

    rows_in = hidden.reshape(rows, width).astype(f32)
    cot = out_grad.reshape(rows, width).astype(f32)
    positions = rank * tokens + jnp.arange(tokens, dtype=jnp.int32)
    valid = (positions[None, :] < lengths[:, 0][:, None]).astype(f32).reshape(rows, 1)
    tile = 256
    skip_wide = jnp.repeat(skip, hs)[None, :]

    def to_lanes(v):
        return jnp.pad(v, ((0, 0),) * (v.ndim - 1) + ((0, LANES - heads),))

    if fast:
        hidden_rows, out_grad_rows = hidden.reshape(rows, width), out_grad.reshape(rows, width)
        dt_wide = jnp.pad(dt_w, ((0, LANES - heads), (0, 0)))
        conv_low, normed_low, raw = front(
            hidden_rows, norm_g[None, :], dt_wide, conv_shards, channels // 2
        )
        raw = raw.reshape(micro, tokens, LANES)
    else:
        normed, front_back = jax.vjp(rms_front, rows_in, norm_g)
        normed_low = normed.astype(bf16)
        normed_parts = normed_low.reshape(rows, shards, -1).transpose(1, 0, 2)[order]
        conv_low = project(normed_parts, in_local, in_w, inner, channels, tile, bf16)
        gate_in = project(normed_parts, in_local, in_w, 0, inner, tile, f32)
        dt_low = mm(normed_low, dt_w, NT).astype(bf16)
        dt_raw = dt_low.astype(f32).reshape(micro, tokens, heads) + dt_shift
    conv_low = conv_low.reshape(micro, tokens, channels)

    if fast:
        x_low, bc_low, y_scan, scanned_low, halo, s_in, out_others = scan_forward(
            conv_low,
            raw,
            conv_w,
            conv_b[None, :],
            to_lanes(dt_shift[None, :]),
            to_lanes(rate[None, :]),
            skip_wide,
            out_eighth,
            inner,
            hs,
            3,
        )
    else:
        prior = from_behind(conv_low[:, tokens - (taps - 1) :], "seq", 1)
        padded = jnp.concatenate([prior, conv_low], axis=1).astype(f32)
        mixed, conv_back = jax.vjp(conv_act, padded, conv_w, conv_b)
        dt = jax.nn.softplus(dt_raw)
        tri = (jnp.arange(tokens)[:, None] >= jnp.arange(tokens)[None, :]).astype(f32)
        cum = jnp.einsum("ij,mjh->mih", tri, dt * rate, precision=highest)
        dt_g, cum_g = grouped(dt), grouped(cum)
        row_g = cum_g.transpose(0, 1, 3, 2)
        last = cum[:, tokens - 1, :]
        decays = lax.all_gather(jnp.exp(last), "seq", axis=0)
        decay_w = grouped(jnp.exp(cum))
        x_low = mixed[..., :inner].astype(bf16)
        b_low = mixed[..., inner : inner + n].astype(bf16)
        c_low = mixed[..., inner + n :].astype(bf16)
        end_w = grouped(dt * jnp.exp(last[:, None, :] - cum))
        own_state = block_states(x_low, end_w, b_low.transpose(0, 2, 1), hs)
        y_local = local_scan(x_low, dt_g, cum_g, row_g, b_low, c_low, hs)
        s_in = running_states(own_state, decays, hs, True)
        y_scan, scanned_low = add_carry(x_low, y_local, cum_g, c_low, s_in, skip_wide, hs)

    if fast:
        normed_out_low, output, g, dy, d_gate_low, d_gated = gate_stage(
            scanned_low.reshape(rows, inner),
            normed_low,
            in_local,
            gate_others,
            gated_g[None, :],
            out_weight,
            out_others,
            hidden_rows,
            out_grad_rows,
            valid,
            256,
        )
        output = output.reshape(hidden.shape)
        dy = dy.reshape(micro, tokens, inner)
        d_gated = d_gated[0]
    else:
        scanned = scanned_low.reshape(rows, inner).astype(f32)
        normed_out, gate_back = jax.vjp(gate_norm, scanned, gate_in, gated_g)
        normed_out_low = normed_out.astype(bf16)
        branch = mm(normed_out_low, out_w)
        output = (rows_in + valid * branch).astype(bf16).reshape(hidden.shape)
        g = (cot * valid).astype(bf16)
        d_scanned, d_gate_in, d_gated = gate_back(mm(g, out_w, NT))
        dy = d_scanned.astype(bf16).reshape(micro, tokens, inner)
        d_gate_low = d_gate_in.astype(bf16)

    if fast:
        d_rest, d_conv_w, d_conv_b, by_head, gate_sum, normed_far = scan_backward(
            dy,
            x_low,
            bc_low,
            y_scan,
            s_in,
            raw,
            conv_low,
            halo,
            conv_w,
            conv_b[None, :],
            to_lanes(dt_shift[None, :]),
            to_lanes(rate[None, :]),
            skip_wide,
            d_gate_low,
            normed_low,
            hs,
            4,
        )
        d_dt_bias, d_a_log, d_skip = by_head[0, :heads], by_head[1, :heads], by_head[2, :heads]
        d_conv_b = d_conv_b[0]
        d_rest = d_rest.reshape(rows, -1)
        d_norm_g = jnp.zeros((width,), f32)
    else:
        own_grad = block_states(dy, decay_w, c_low.transpose(0, 2, 1), hs)
        dx_local, db_local, dc_local = local_back(x_low, dy, dt_g, cum_g, row_g, b_low, c_low, hs)
        ds = running_states(own_grad, decays, hs, False)
        dx_low, ddt_g, dcum_g, db, dc, last_term, dskip = carry_back(
            x_low, dy, dx_local, y_scan, dt_g, cum_g, b_low, s_in, ds, db_local, dc_local, skip_wide, hs
        )

        def ungrouped(v):
            return v.transpose(0, 2, 1, 3).reshape(micro, tokens, heads)

        at_end = jnp.sum(last_term.reshape(micro, heads, hs), axis=-1)[:, None, :]
        d_log = jnp.einsum("ij,mih->mjh", tri, ungrouped(dcum_g), precision=highest) + at_end
        d_dt = (ungrouped(ddt_g) + d_log * rate) * jax.nn.sigmoid(dt_raw)
        d_dt_bias = jnp.sum(d_dt, axis=(0, 1))
        d_a_log = jnp.sum(d_log * dt, axis=(0, 1)) * rate
        d_skip = jnp.sum(dskip.reshape(-1, heads, hs), axis=(0, 2))
        mixed_grad = jnp.concatenate([dx_low.astype(f32), db, dc], axis=2)
        d_padded, d_conv_w, d_conv_b = conv_back(mixed_grad)
        from_next = from_behind(d_padded[:, : taps - 1].astype(bf16), "seq", -1).astype(f32)
        d_conv = d_padded[:, taps - 1 :].at[:, tokens - (taps - 1) :].add(from_next)
        d_dt_low = d_dt.astype(bf16).reshape(rows, heads)
    total_cols = inner + channels + heads
    if not fast:
        d_rest = d_conv.astype(bf16).reshape(rows, channels)
        d_parts = unproject(d_gate_low, d_rest, in_local, in_w, tile)
        d_normed = d_parts[order].transpose(1, 0, 2).reshape(rows, width) + mm(d_dt_low, dt_w)
        d_hidden, d_norm_g = front_back(d_normed)
        input_grad = (d_hidden + cot).astype(bf16).reshape(hidden.shape)

    def summed(terms, axis):
        t = lax.psum_scatter(terms.astype(bf16), "seq", scatter_dimension=0, tiled=True)
        t = lax.psum_scatter(t, "wshard", scatter_dimension=axis, tiled=True)
        return lax.all_gather(t, "seq", axis=0, tiled=True).astype(f32)

    smalls = [
        d_norm_g.reshape(shards, -1),
        d_conv_w.reshape(taps, shards, -1).transpose(1, 0, 2).reshape(shards, -1),
        d_conv_b.reshape(shards, -1),
        d_dt_bias.reshape(shards, -1),
        d_a_log.reshape(shards, -1),
        d_skip.reshape(shards, -1),
        d_gated.reshape(shards, -1),
    ]
    smalls = jnp.concatenate(smalls, axis=1)
    if fast:
        smalls = jnp.pad(smalls, ((0, 0), (0, -smalls.shape[1] % 1024))).reshape(shards, -1, LANES)
        rest_sum, out_sum, sums, input_grad = weight_sums(
            d_gate_low,
            d_rest,
            normed_low,
            normed_far,
            g,
            normed_out_low,
            in_local,
            gate_others,
            conv_shards,
            smalls,
            d_rest[:, channels : channels + LANES],
            dt_wide,
            hidden_rows,
            norm_g[None, :],
            out_grad_rows,
            2,
        )
        input_grad = input_grad.reshape(hidden.shape)
        gate_sum = gate_sum.reshape(inner, -1)
        in_grad = jnp.concatenate([gate_sum, rest_sum[: total_cols - inner]]).astype(f32).T
        out_w_grad = turned(out_sum, 512)
        sums = sums.reshape(-1)
    else:
        d_proj = jnp.concatenate([d_gate_low, d_rest, d_dt_low], axis=1)
        in_grad = summed(mm(d_proj, normed_low, TN), 1).T
        out_terms = mm(normed_out_low, g, TN)
        blocks = out_terms.reshape(shards, count, -1, width).transpose(1, 0, 2, 3)
        out_w_grad = summed(blocks.reshape(inner, width), 0)
        sums = lax.psum(smalls, ("seq", "wshard"))
        sums = lax.dynamic_index_in_dim(sums, shard, 0, keepdims=False)
    found, at = [], 0
    for size in sizes:
        found.append(sums[at : at + size])
        at += size
    return (
        output,
        input_grad,
        found[0],
        in_grad,
        found[1].reshape(taps, -1).T,
        found[2],
        found[3],
        found[4],
        found[5],
        found[6],
        out_w_grad,
    )


def solution(mesh):
    return jax.shard_map(
        local,
        mesh=mesh,
        in_specs=(
            P(None, "wshard", "seq", None),
            P(None, "wshard"),
            P(None, "wshard", "seq", None),
            P("wshard"),
            P("wshard", None),
            P("wshard", None),
            P("wshard"),
            P("wshard"),
            P("wshard"),
            P("wshard"),
            P("wshard"),
            P("wshard", None),
        ),
        out_specs=(
            P(None, "wshard", "seq", None),
            P(None, "wshard", "seq", None),
            P("wshard"),
            P("wshard", None),
            P("wshard", None),
            P("wshard"),
            P("wshard"),
            P("wshard"),
            P("wshard"),
            P("wshard"),
            P("wshard", None),
        ),
        check_vma=False,
    )
```

```python
from functools import partial

import jax
import jax.numpy as jnp
from jax import lax
from jax.experimental import pallas as pl
from jax.experimental.pallas import tpu as pltpu
from jax.sharding import PartitionSpec as P

epsilon = 1e-05
highest = lax.Precision.HIGHEST
f32 = jnp.float32
bf16 = jnp.bfloat16
GROUP = 8
VMEM = 48 * 1024 * 1024
VMEM_MOST = 62 * 1024 * 1024

NN = (((1,), (0,)), ((), ()))
NT = (((1,), (1,)), ((), ()))
TN = (((0,), (0,)), ((), ()))


def mm(a, b, dims=NN):
    return lax.dot_general(a, b, dims, preferred_element_type=f32)


def params():
    return pltpu.CompilerParams(
        dimension_semantics=("arbitrary", "arbitrary"), vmem_limit_bytes=VMEM
    )


def widen(cols, head_size):
    t, heads = cols.shape
    lane = lax.broadcasted_iota(jnp.int32, (t, 2 * head_size), 1)
    parts = []
    for k in range(0, heads, 2):
        parts.append(jnp.where(lane < head_size, cols[:, k : k + 1], cols[:, k + 1 : k + 2]))
    return jnp.concatenate(parts, axis=1)


def state_kernel(hs, x_ref, w_ref, bt_ref, o_ref):
    weighted = (x_ref[0].astype(f32) * widen(w_ref[0, 0], hs)).astype(bf16)
    o_ref[0] = mm(bt_ref[0], weighted)


def block_states(x, weights, bt, hs):
    micro, t, cols = x.shape
    n = bt.shape[1]
    gc = GROUP * hs
    return pl.pallas_call(
        partial(state_kernel, hs),
        grid=(micro, cols // gc),
        in_specs=[
            pl.BlockSpec((1, t, gc), lambda m, g: (m, 0, g)),
            pl.BlockSpec((1, 1, t, GROUP), lambda m, g: (m, g, 0, 0)),
            pl.BlockSpec((1, n, t), lambda m, g: (m, 0, 0)),
        ],
        out_specs=pl.BlockSpec((1, n, gc), lambda m, g: (m, 0, g)),
        out_shape=jax.ShapeDtypeStruct((micro, n, cols), f32),
        compiler_params=params(),
        name="block_states",
    )(x, weights, bt)


def local_kernel(hs, x_ref, dt_ref, cum_ref, row_ref, b_ref, c_ref, o_ref, scores):
    t = x_ref.shape[1]
    half = t // 2

    @pl.when(pl.program_id(1) == 0)
    def _():
        s = mm(c_ref[0], b_ref[0], NT)
        i = lax.broadcasted_iota(jnp.int32, (t, t), 0)
        j = lax.broadcasted_iota(jnp.int32, (t, t), 1)
        scores[...] = jnp.where(i >= j, s, 0.0)

    cum, dt, rows = cum_ref[0, 0], dt_ref[0, 0], row_ref[0, 0]
    lane = lax.broadcasted_iota(jnp.int32, (half, 2 * hs), 1)
    weighted = (x_ref[0].astype(f32) * widen(dt, hs)).astype(bf16)
    for k in range(0, GROUP, 2):
        at = slice(k * hs, (k + 2) * hs)
        pair = weighted[:, at]
        top, low = [], []
        for h in (k, k + 1):
            col, row = cum[:, h : h + 1], rows[h : h + 1, :]
            m1 = jnp.exp(jnp.minimum(col[:half] - row[:, :half], 0.0)) * scores[:half, :half]
            m2 = jnp.exp(jnp.minimum(col[half:] - row, 0.0)) * scores[half:, :]
            top.append(mm(m1.astype(bf16), pair[:half]))
            low.append(mm(m2.astype(bf16), pair))
        o_ref[0, :half, at] = jnp.where(lane < hs, top[0], top[1])
        o_ref[0, half:, at] = jnp.where(lane < hs, low[0], low[1])


def local_scan(x, dt, cum, rows, b, c, hs):
    micro, t, cols = x.shape
    n = b.shape[2]
    gc = GROUP * hs
    return pl.pallas_call(
        partial(local_kernel, hs),
        grid=(micro, cols // gc),
        in_specs=[
            pl.BlockSpec((1, t, gc), lambda m, g: (m, 0, g)),
            pl.BlockSpec((1, 1, t, GROUP), lambda m, g: (m, g, 0, 0)),
            pl.BlockSpec((1, 1, t, GROUP), lambda m, g: (m, g, 0, 0)),
            pl.BlockSpec((1, 1, GROUP, t), lambda m, g: (m, g, 0, 0)),
            pl.BlockSpec((1, t, n), lambda m, g: (m, 0, 0)),
            pl.BlockSpec((1, t, n), lambda m, g: (m, 0, 0)),
        ],
        out_specs=pl.BlockSpec((1, t, gc), lambda m, g: (m, 0, g)),
        out_shape=jax.ShapeDtypeStruct((micro, t, cols), f32),
        scratch_shapes=[pltpu.VMEM((t, t), f32)],
        compiler_params=params(),
        name="local_scan",
    )(x, dt, cum, rows, b, c)


def carry_kernel(hs, x_ref, y_ref, cum_ref, c_ref, s_ref, skip_ref, scan_ref, low_ref):
    carried = mm(c_ref[0], s_ref[0].astype(bf16)) * widen(jnp.exp(cum_ref[0, 0]), hs)
    scan = y_ref[0] + carried
    scan_ref[0] = scan
    low_ref[0] = (scan + skip_ref[...] * x_ref[0].astype(f32)).astype(bf16)


def add_carry(x, y, cum, c, s_in, skip_wide, hs):
    micro, t, cols = x.shape
    n = c.shape[2]
    gc = GROUP * hs
    wide = pl.BlockSpec((1, t, gc), lambda m, g: (m, 0, g))
    return pl.pallas_call(
        partial(carry_kernel, hs),
        grid=(micro, cols // gc),
        in_specs=[
            wide,
            wide,
            pl.BlockSpec((1, 1, t, GROUP), lambda m, g: (m, g, 0, 0)),
            pl.BlockSpec((1, t, n), lambda m, g: (m, 0, 0)),
            pl.BlockSpec((1, n, gc), lambda m, g: (m, 0, g)),
            pl.BlockSpec((1, gc), lambda m, g: (0, g)),
        ],
        out_specs=[wide, wide],
        out_shape=[
            jax.ShapeDtypeStruct((micro, t, cols), f32),
            jax.ShapeDtypeStruct((micro, t, cols), bf16),
        ],
        compiler_params=params(),
        name="add_carry",
    )(x, y, cum, c, s_in, skip_wide)


def local_back_kernel(
    hs, x_ref, dy_ref, dt_ref, cum_ref, row_ref, b_ref, c_ref, dx_ref, db_ref, dc_ref, scores, total
):
    t = x_ref.shape[1]
    half = t // 2

    @pl.when(pl.program_id(1) == 0)
    def _():
        s = mm(b_ref[0], c_ref[0], NT)
        j = lax.broadcasted_iota(jnp.int32, (t, t), 0)
        i = lax.broadcasted_iota(jnp.int32, (t, t), 1)
        scores[...] = jnp.where(i >= j, s, 0.0)
        total[...] = jnp.zeros_like(total)

    cum, dt, rows = cum_ref[0, 0], dt_ref[0, 0], row_ref[0, 0]
    lane = lax.broadcasted_iota(jnp.int32, (t, 2 * hs), 1)
    lane_half = lax.broadcasted_iota(jnp.int32, (half, 2 * hs), 1)
    weighted = (x_ref[0].astype(f32) * widen(dt, hs)).astype(bf16)
    for k in range(0, GROUP, 2):
        at = slice(k * hs, (k + 2) * hs)
        pair = weighted[:, at]
        dy = dy_ref[0, :, at]
        top, low = [], []
        for h in (k, k + 1):
            col, row = cum[:, h : h + 1], rows[h : h + 1, :]
            mine = jnp.where(lane < hs, pair, 0) if h == k else jnp.where(lane < hs, 0, pair)
            l1 = jnp.exp(jnp.minimum(row - col[:half], 0.0))
            l2 = jnp.exp(jnp.minimum(row[:, half:] - col[half:], 0.0))
            total[:half, :] += l1 * mm(mine[:half], dy, NT)
            total[half:, half:] += l2 * mm(mine[half:], dy[half:], NT)
            top.append(mm((l1 * scores[:half, :]).astype(bf16), dy))
            low.append(mm((l2 * scores[half:, half:]).astype(bf16), dy[half:]))
        dx_ref[0, :half, at] = jnp.where(lane_half < hs, top[0], top[1])
        dx_ref[0, half:, at] = jnp.where(lane_half < hs, low[0], low[1])

    @pl.when(pl.program_id(1) == pl.num_programs(1) - 1)
    def _():
        j = lax.broadcasted_iota(jnp.int32, (t, t), 0)
        i = lax.broadcasted_iota(jnp.int32, (t, t), 1)
        d = jnp.where(i >= j, total[...], 0.0)
        db_ref[0] = mm(d.astype(bf16), c_ref[0])
        dc_ref[0] = mm(d.T.astype(bf16), b_ref[0])


def local_back(x, dy, dt, cum, rows, b, c, hs):
    micro, t, cols = x.shape
    n = b.shape[2]
    gc = GROUP * hs
    wide = pl.BlockSpec((1, t, gc), lambda m, g: (m, 0, g))
    small = pl.BlockSpec((1, 1, t, GROUP), lambda m, g: (m, g, 0, 0))
    state = pl.BlockSpec((1, t, n), lambda m, g: (m, 0, 0))
    return pl.pallas_call(
        partial(local_back_kernel, hs),
        grid=(micro, cols // gc),
        in_specs=[
            wide,
            wide,
            small,
            small,
            pl.BlockSpec((1, 1, GROUP, t), lambda m, g: (m, g, 0, 0)),
            state,
            state,
        ],
        out_specs=[wide, state, state],
        out_shape=[
            jax.ShapeDtypeStruct((micro, t, cols), f32),
            jax.ShapeDtypeStruct((micro, t, n), f32),
            jax.ShapeDtypeStruct((micro, t, n), f32),
        ],
        scratch_shapes=[pltpu.VMEM((t, t), f32), pltpu.VMEM((t, t), f32)],
        compiler_params=params(),
        name="local_back",
    )(x, dy, dt, cum, rows, b, c)


def head_sums(values, ones):
    high = values.astype(bf16)
    rest = (values - high.astype(f32)).astype(bf16)
    return mm(high, ones) + mm(rest, ones)


def carry_back_kernel(
    hs,
    x_ref,
    dy_ref,
    dxl_ref,
    y_ref,
    dt_ref,
    cum_ref,
    b_ref,
    si_ref,
    ds_ref,
    dbl_ref,
    dcl_ref,
    skip_ref,
    dx_ref,
    ddt_ref,
    dcum_ref,
    db_ref,
    dc_ref,
    last_ref,
    dskip_ref,
):
    t = x_ref.shape[1]
    gc = x_ref.shape[2]

    @pl.when(pl.program_id(1) == 0)
    def _():
        db_ref[0] = dbl_ref[0]
        dc_ref[0] = dcl_ref[0]

    cum, dt = cum_ref[0, 0], dt_ref[0, 0]
    x, dy = x_ref[0].astype(f32), dy_ref[0].astype(f32)
    dt_wide = widen(dt, hs)
    weighted = (x * dt_wide).astype(bf16).astype(f32)
    decay = widen(jnp.exp(cum), hs)
    to_end = widen(jnp.exp(cum[t - 1 :, :] - cum), hs)
    s_in, ds = si_ref[0].astype(f32), ds_ref[0]
    s_low, ds_low = s_in.astype(bf16), ds.astype(bf16)
    through = to_end * mm(b_ref[0], ds_low)
    d_weighted = dxl_ref[0] + through
    dx_ref[0] = (dt_wide * d_weighted + skip_ref[...] * dy).astype(bf16)
    db_ref[0] += mm((weighted * to_end).astype(bf16), ds_low, NT)
    dc_ref[0] += mm((dy * decay).astype(bf16), s_low, NT)
    r = lax.broadcasted_iota(jnp.int32, (gc, 128), 0)
    c = lax.broadcasted_iota(jnp.int32, (gc, 128), 1)
    ones = jnp.where(r // hs == c, 1.0, 0.0).astype(bf16)
    ddt_ref[0, 0] = head_sums(x * d_weighted, ones)[:, :GROUP]
    dcum_ref[0, 0] = head_sums(dy * y_ref[0] - weighted * d_weighted, ones)[:, :GROUP]
    last_decay = decay[t - 1 :, :]
    last_ref[0] = jnp.sum(weighted * through, axis=0, keepdims=True) + last_decay * jnp.sum(
        s_low.astype(f32) * ds, axis=0, keepdims=True
    )
    dskip_ref[0] = jnp.sum(x * dy, axis=0, keepdims=True)


def carry_back(x, dy, dxl, y, dt, cum, b, s_in, ds, dbl, dcl, skip_wide, hs):
    micro, t, cols = x.shape
    n = b.shape[2]
    gc = GROUP * hs
    groups = cols // gc
    wide = pl.BlockSpec((1, t, gc), lambda m, g: (m, 0, g))
    small = pl.BlockSpec((1, 1, t, GROUP), lambda m, g: (m, g, 0, 0))
    state = pl.BlockSpec((1, t, n), lambda m, g: (m, 0, 0))
    st = pl.BlockSpec((1, n, gc), lambda m, g: (m, 0, g))
    line = pl.BlockSpec((1, 1, gc), lambda m, g: (m, 0, g))
    return pl.pallas_call(
        partial(carry_back_kernel, hs),
        grid=(micro, groups),
        in_specs=[
            wide,
            wide,
            wide,
            wide,
            small,
            small,
            state,
            st,
            st,
            state,
            state,
            pl.BlockSpec((1, gc), lambda m, g: (0, g)),
        ],
        out_specs=[wide, small, small, state, state, line, line],
        out_shape=[
            jax.ShapeDtypeStruct((micro, t, cols), bf16),
            jax.ShapeDtypeStruct((micro, groups, t, GROUP), f32),
            jax.ShapeDtypeStruct((micro, groups, t, GROUP), f32),
            jax.ShapeDtypeStruct((micro, t, n), f32),
            jax.ShapeDtypeStruct((micro, t, n), f32),
            jax.ShapeDtypeStruct((micro, 1, cols), f32),
            jax.ShapeDtypeStruct((micro, 1, cols), f32),
        ],
        compiler_params=params(),
        name="carry_back",
    )(x, dy, dxl, y, dt, cum, b, s_in, ds, dbl, dcl, skip_wide)


def from_behind(x, axis, by):
    count = lax.axis_size(axis)
    pairs = [(i, i + by) for i in range(count) if 0 <= i + by < count]
    return lax.ppermute(x, axis, pairs)


def swap(x, by):
    count = lax.axis_size("seq")
    return lax.ppermute(x, "seq", [(i, i ^ by) for i in range(count)])


def running_states(terms, decays, hs, forward):
    count = lax.axis_size("seq")
    rank = lax.axis_index("seq")
    index = jnp.arange(count)

    def product(mask):
        d = jnp.prod(jnp.where(mask[:, None, None], decays, 1.0), axis=0)
        return jnp.repeat(d, hs, axis=1)[:, None, :]

    total, before = terms, jnp.zeros_like(terms)
    size = 1
    while size < count:
        other = swap(total.astype(bf16), size).astype(f32)
        mine = index // size == rank // size
        theirs = index // size == (rank // size) ^ 1
        later = (rank // size) % 2 == (1 if forward else 0)
        passed = mine & ((index < rank) if forward else (index > rank))
        before = before + jnp.where(later, product(passed), 0.0) * other
        if 2 * size < count:
            total = total * jnp.where(later, 1.0, product(theirs)) + other * jnp.where(
                later, product(mine), 1.0
            )
        size *= 2
    return before


MESH = pl.DeviceIdType.MESH


def around():
    s, z = lax.axis_index("seq"), lax.axis_index("wshard")
    c, x, y = s % 2, (s // 2) % 2, s // 4
    near = {
        "c": (s + 1 - 2 * c, z),
        "x": (s + 2 - 4 * x, z),
        "y": (s + 4 - 8 * y, z),
        "z1": (s, z + 1 - 2 * (z % 2)),
        "z2": (s, z + 2 - 4 * (z // 2)),
        "z3": (s, 3 - z),
    }
    return s, z, c, x, y, near


def greet(near):
    barrier = pltpu.get_barrier_semaphore()
    for where in near.values():
        pl.semaphore_signal(barrier, inc=1, device_id=where, device_id_type=MESH)
    pl.semaphore_wait(barrier, len(near))


CHUNK_DMAS = 10
AHEAD = 2


def split_rows(piece, parts):
    tiles = piece // 16
    return [16 * (tiles * (i + 1) // parts - tiles * i // parts) for i in range(parts)]


class Gather:
    def __init__(self, place, items, send, recv, own=None):
        s, z, c, x, y, near = place
        sx, sy, sd = s + 2 - 4 * x, s + 4 - 8 * y, s + 6 - 4 * x - 8 * y
        self.plans = []
        for source, base, target, count, parts in items:
            off = 0
            for i, size in enumerate(split_rows(count // 8, parts)):
                q = len(self.plans)

                def rows(who, first=0, off=off, size=size, piece=count // 8):
                    return pl.ds(pl.multiple_of(first + who * piece + off, 16), size)

                def move(src, dst, kind, to, q=q):
                    return pltpu.make_async_remote_copy(
                        src_ref=src,
                        dst_ref=dst,
                        send_sem=send.at[q, kind],
                        recv_sem=recv.at[q, kind],
                        device_id=near[to],
                        device_id_type=MESH,
                    )

                def along(who, kind, to, move=move, rows=rows, target=target):
                    block = target.at[pl.ds(0, 3), rows(who)]
                    return move(block, block, kind, to)

                plan = {"fetched": base is None}
                if base is None:
                    have = source.at[:, pl.ds(off, size)]
                    block = target.at[pl.ds(0, 3), rows(s)]
                    plan["own"] = pltpu.make_async_copy(have, block, own.at[q])
                    for kind, name in ((3, "x"), (4, "y"), (6, "c0")):
                        plan[name] = move(have, block, kind, name[0])
                else:
                    for k in (1, 2, 3):
                        there = target.at[k - 1, rows(s)]
                        plan["z%d" % k] = move(source.at[rows(s, base)], there, k - 1, "z%d" % k)
                    plan["x"] = along(s, 3, "x")
                    plan["y"] = along(s, 4, "y")
                    plan["c0"] = along(s, 6, "c")
                first = "xy"[i % 2]
                plan["d"] = along(sx, 5, "y") if first == "x" else along(sy, 5, "x")
                plan["cx"] = along(sx, 7, "c")
                plan["cy"] = along(sy, 8, "c")
                plan["cd"] = along(sd, 9, "c")
                plan["order"] = first, "yx"[i % 2]
                self.plans.append(plan)
                off += size

    def fetch(self, i):
        for k in (1, 2, 3):
            self.plans[i]["z%d" % k].start()

    def begin(self, i):
        plan = self.plans[i]
        if plan["fetched"]:
            plan["own"].start()
        else:
            for k in (1, 2, 3):
                plan["z%d" % k].wait_recv()
        for name in ("x", "y", "c0"):
            plan[name].start()

    def middle(self, i):
        plan = self.plans[i]
        one, two = plan["order"]
        plan[one].wait_recv()
        plan["d"].start()
        plan["c" + one].start()
        plan[two].wait_recv()
        plan["c" + two].start()

    def finish(self, i):
        self.plans[i]["d"].wait_recv()
        self.plans[i]["cd"].start()

    def run(self, last):
        n = len(self.plans)
        for i in range(min(AHEAD, n)):
            self.fetch(i)
        for i in range(n + 2):
            if i < n:
                self.begin(i)
                if i + AHEAD < n:
                    self.fetch(i + AHEAD)
                if i + AHEAD == n - 1:
                    last()
            if 0 <= i - 1 < n:
                self.middle(i - 1)
            if 0 <= i - 2 < n:
                self.finish(i - 2)

    def close(self):
        for plan in self.plans:
            for name in ("c0", "cx", "cy", "cd"):
                plan[name].wait_recv()
            for name in ("z1", "z2", "z3", "x", "y", "d", "c0", "cx", "cy", "cd"):
                if name in plan:
                    plan[name].wait_send()
            if plan["fetched"]:
                plan["own"].wait()


def gather_kernel(
    inner, channels, parts, w_ref, ow_ref, conv_ref, gate_ref, eighth_ref, own, own_sem, send, recv, o_send, o_recv
):
    place = around()
    inward = pltpu.make_async_copy(w_ref.at[pl.ds(inner, channels)], own, own_sem)
    inward.start()
    greet(place[-1])
    items = [(w_ref, inner, conv_ref, channels, parts), (w_ref, 0, gate_ref, inner, parts)]
    work = Gather(place, items, send, recv)
    piece = eighth_ref.shape[1]
    mine = pl.ds(pl.multiple_of(place[0] * piece, 16), piece)
    eighths = [
        pltpu.make_async_remote_copy(
            src_ref=ow_ref.at[mine],
            dst_ref=eighth_ref.at[k - 1],
            send_sem=o_send.at[k - 1],
            recv_sem=o_recv.at[k - 1],
            device_id=place[-1]["z%d" % k],
            device_id_type=MESH,
        )
        for k in (1, 2, 3)
    ]

    def last():
        for copy in eighths:
            copy.start()

    work.run(last)
    inward.wait()
    outward = pltpu.make_async_copy(own, conv_ref.at[3], own_sem)
    outward.start()
    work.close()
    for copy in eighths:
        copy.wait()
    outward.wait()


def gather_input_weight(w_t, out_weight, inner, channels, parts=6):
    width = w_t.shape[1]
    hbm = pl.BlockSpec(memory_space=pl.ANY)
    return pl.pallas_call(
        partial(gather_kernel, inner, channels, parts),
        in_specs=[hbm] * 2,
        out_specs=[hbm] * 3,
        out_shape=[
            jax.ShapeDtypeStruct((4, channels, width), bf16),
            jax.ShapeDtypeStruct((3, inner, width), bf16),
            jax.ShapeDtypeStruct((3, out_weight.shape[0] // 8, out_weight.shape[1]), bf16),
        ],
        scratch_shapes=[
            pltpu.VMEM((channels, width), bf16),
            pltpu.SemaphoreType.DMA,
            pltpu.SemaphoreType.DMA((2 * parts, CHUNK_DMAS)),
            pltpu.SemaphoreType.DMA((2 * parts, CHUNK_DMAS)),
            pltpu.SemaphoreType.DMA((3,)),
            pltpu.SemaphoreType.DMA((3,)),
        ],
        compiler_params=pltpu.CompilerParams(
            collective_id=1, has_side_effects=True, vmem_limit_bytes=VMEM_MOST
        ),
        cost_estimate=pl.CostEstimate(flops=0, bytes_accessed=200_000_000, transcendentals=0),
        name="gather_input_weight",
    )(w_t, out_weight)


class Here:
    def __init__(self, copy):
        self.start, self.wait_recv = copy.start, copy.wait

    def wait_send(self):
        pass


STAGE = 2


class Products:
    IN = 4
    SCRATCH = 22

    @staticmethod
    def sizes(a_list, b):
        rows = b.shape[0]
        wide = sum(a.shape[1] for a in a_list) // 2
        return rows, wide, b.shape[1], wide // 128

    @staticmethod
    def marks(chunks):
        return sorted({0, chunks * 2 // 5, chunks * 7 // 10, chunks * 9 // 10, chunks})

    @staticmethod
    def out_shape(a_list, b):
        _, _, width, chunks = Products.sizes(a_list, b)
        return jax.ShapeDtypeStruct((2, chunks, 2, 2, 2, 16, width // 4), bf16)

    @staticmethod
    def scratch(a_list, b):
        rows, wide, width, chunks = Products.sizes(a_list, b)
        dma = pltpu.SemaphoreType.DMA
        n = Products.IN
        marks = Products.marks(chunks)
        return [
            pltpu.VMEM((2 * rows, wide), bf16),
            pltpu.VMEM((2 * rows, width), bf16),
            pltpu.VMEM((4, 128, width), f32),
            pltpu.VMEM((2, 32, width), bf16),
            pltpu.VMEM((2, 32, width), bf16),
            pltpu.VMEM((2, 16, width), bf16),
            pltpu.VMEM((2, 16, width), bf16),
            pltpu.VMEM((2, 2, 16, width), bf16),
            pltpu.VMEM((2, 16, width), f32),
            pltpu.VMEM((2, 16, width), f32),
            pltpu.VMEM((2, 2, 16, width), f32),
            pltpu.VMEM((chunks, 32, width), bf16),
            pltpu.VMEM((chunks, 32, width), bf16),
            pltpu.VMEM((chunks, 16, width), bf16),
            pltpu.VMEM((chunks, 16, width), bf16),
            pltpu.VMEM((chunks, 3, 2, 16, width // 4), bf16),
            dma((n,)),
            dma((n,)),
            dma((n,)),
            dma((7, 2)),
            dma((7, chunks)),
            dma((2, len(marks) - 1, 8)),
        ]

    def __init__(self, place, a_refs, b_ref, out, scratch, b_far=None):
        self.s, self.z, self.c, self.x, self.y, self.near = place
        (
            self.a,
            self.b,
            self.g,
            self.sa1,
            self.sb1,
            self.sa2,
            self.sb2,
            self.s3,
            self.ka2,
            self.kb2,
            self.f3,
            self.ra1,
            self.rb1,
            self.ra2,
            self.rb2,
            self.rz,
            self.in_sem,
            self.s_in,
            self.r_in,
            self.s_step,
            self.r_step,
            self.sems_all,
        ) = scratch
        self.out = out
        self.shard = self.rz.shape[-1]
        self.chunks = self.ra1.shape[0]
        marks = Products.marks(self.chunks)
        self.groups = list(zip(marks[:-1], marks[1:]))
        c = self.c
        rows = self.a.shape[0] // 2
        near, far = pl.ds(0, rows), pl.ds(rows, rows)
        self.operands = []
        to = self.b.at[far]
        if b_far is None:
            there = self.remote(b_ref, to, self.s_in.at[0], self.r_in.at[0], "c")
        else:
            there = Here(pltpu.make_async_copy(b_far, to, self.s_in.at[0]))
        self.operands.append(
            (0, pltpu.make_async_copy(b_ref, self.b.at[near], self.in_sem.at[0]), there)
        )
        at = 0
        for i, ref in enumerate(a_refs):
            half = ref.shape[1] // 2
            here = ref.at[:, pl.ds(pl.multiple_of(c * half, 128), half)]
            there = ref.at[:, pl.ds(pl.multiple_of((1 - c) * half, 128), half)]
            to = pl.ds(at, half)
            self.operands.append(
                (
                    at // 128,
                    pltpu.make_async_copy(here, self.a.at[near, to], self.in_sem.at[i + 1]),
                    self.remote(there, self.a.at[far, to], self.s_in.at[i + 1], self.r_in.at[i + 1], "c"),
                )
            )
            at += half

    def remote(self, src, dst, ss, rs, to):
        return pltpu.make_async_remote_copy(
            src_ref=src,
            dst_ref=dst,
            send_sem=ss,
            recv_sem=rs,
            device_id=self.near[to],
            device_id_type=MESH,
        )

    def load(self):
        for _, here, _ in self.operands:
            here.start()

    def share(self):
        for _, _, there in self.operands:
            there.start()

    def step_copy(self, kind, u):
        slot = u % 2
        ss, rs = self.s_step.at[kind, slot], self.r_step.at[kind, u]
        if kind < 4:
            src, dst, to = (
                (self.sa1, self.ra1, "x"),
                (self.sb1, self.rb1, "y"),
                (self.sa2, self.ra2, "y"),
                (self.sb2, self.rb2, "x"),
            )[kind]
            return self.remote(src.at[slot], dst.at[u], ss, rs, to)
        k = kind - 3
        z = self.z
        other = (z + 1 - 2 * (z % 2), z + 2 - 4 * (z // 2), 3 - z)[k - 1]
        cols = pl.ds(pl.multiple_of(other * self.shard, 128), self.shard)
        return self.remote(self.s3.at[slot, :, :, cols], self.rz.at[u, k - 1], ss, rs, "z%d" % k)

    def all_copy(self, q, kind):
        a, b = self.groups[q]
        ts = pl.ds(a, b - a)
        x, y, c = self.x, self.y, self.c
        px = 1 - x if kind in (3, 5, 7) else x
        py = 1 - y if kind in (4, 6, 7) else y
        if kind in (3, 4):
            block = self.out.at[c, ts, kind - 3, px, py]
        else:
            block = self.out.at[c, ts, :, px, py]
        to = ("x", "y", "c", "y", "x", "c", "c", "c")[kind]
        return self.remote(block, block, self.sems_all.at[0, q, kind], self.sems_all.at[1, q, kind], to)

    def step(self, t):
        x, y, z, c = self.x, self.y, self.z, self.c
        g, ra1, rb1 = self.g, self.ra1, self.rb1
        chunks = self.chunks
        copy = self.step_copy

        def sl(at, size=16):
            return pl.ds(pl.multiple_of(at, 16), size)

        def free(kind, u):
            @pl.when(u >= 2)
            def _():
                copy(kind, u - 2).wait_send()

        @pl.when((t >= 3 * STAGE) & (t - 3 * STAGE < chunks))
        def _():
            u = t - 3 * STAGE
            slot = u % 2
            for k in (4, 5, 6):
                copy(k, u).wait_recv()
            mine = pl.ds(pl.multiple_of(z * self.shard, 128), self.shard)
            for part in (0, 1):
                total = self.f3[slot, part, :, mine]
                for k in range(3):
                    total = total + self.rz[u, k, part].astype(f32)
                self.out[c, u, part, x, y] = total.astype(bf16)

        for q, (_, b) in enumerate(self.groups):

            @pl.when(t == b - 1 + 3 * STAGE)
            def _(q=q):
                for kind in (0, 1, 2):
                    self.all_copy(q, kind).start()

            @pl.when(t == b - 1 + 4 * STAGE)
            def _(q=q):
                self.all_copy(q, 0).wait_recv()
                self.all_copy(q, 3).start()
                self.all_copy(q, 5).start()
                self.all_copy(q, 1).wait_recv()
                self.all_copy(q, 4).start()
                self.all_copy(q, 6).start()

            @pl.when(t == b - 1 + 5 * STAGE)
            def _(q=q):
                self.all_copy(q, 3).wait_recv()
                self.all_copy(q, 4).wait_recv()
                self.all_copy(q, 7).start()

        @pl.when((t >= 2 * STAGE) & (t - 2 * STAGE < chunks))
        def _():
            u = t - 2 * STAGE
            slot = u % 2
            copy(2, u).wait_recv()
            copy(3, u).wait_recv()
            for k in (4, 5, 6):
                free(k, u)
            va = self.ka2[slot] + self.ra2[u].astype(f32)
            vb = self.kb2[slot] + self.rb2[u].astype(f32)
            self.f3[slot, 0] = va
            self.f3[slot, 1] = vb
            self.s3[slot, 0] = va.astype(bf16)
            self.s3[slot, 1] = vb.astype(bf16)
            for k in (4, 5, 6):
                copy(k, u).start()

        @pl.when((t >= STAGE) & (t - STAGE < chunks))
        def _():
            u = t - STAGE
            slot, then = u % 2, u % 4
            copy(0, u).wait_recv()
            free(2, u)
            self.sa2[slot] = (
                g[then, sl(x * 32 + (1 - y) * 16)] + ra1[u, sl((1 - y) * 16)].astype(f32)
            ).astype(bf16)
            copy(2, u).start()
            self.ka2[slot] = g[then, sl(x * 32 + y * 16)] + ra1[u, sl(y * 16)].astype(f32)
            copy(1, u).wait_recv()
            free(3, u)
            self.sb2[slot] = (
                g[then, sl(64 + (1 - x) * 32 + y * 16)] + rb1[u, sl((1 - x) * 16)].astype(f32)
            ).astype(bf16)
            copy(3, u).start()
            self.kb2[slot] = g[then, sl(64 + x * 32 + y * 16)] + rb1[u, sl(x * 16)].astype(f32)

        @pl.when(t < chunks)
        def _():
            for first, here, there in self.operands:

                @pl.when(t == first)
                def _(here=here, there=there):
                    here.wait()
                    there.wait_recv()

            slot, now = t % 2, t % 4

            @pl.when(slot == 0)
            def _():
                cols = pl.ds(pl.multiple_of(t * 128, 256), 256)
                both = mm(self.a[:, cols], self.b[...], TN)
                g[now] = both[:128]
                g[now + 1] = both[128:]

            free(0, t)
            free(1, t)
            self.sa1[slot] = g[now, sl((1 - x) * 32, 32)].astype(bf16)
            copy(0, t).start()
            self.sb1[slot, 0:16] = g[now, sl(64 + (1 - y) * 16)].astype(bf16)
            self.sb1[slot, 16:32] = g[now, sl(96 + (1 - y) * 16)].astype(bf16)
            copy(1, t).start()

    def steps(self):
        return self.chunks + 5 * STAGE

    def close(self):
        for q in range(len(self.groups)):
            for kind in (2, 5, 6, 7):
                self.all_copy(q, kind).wait_recv()
            for kind in range(8):
                self.all_copy(q, kind).wait_send()
        for u in (self.chunks - 2, self.chunks - 1):
            for kind in range(7):
                self.step_copy(kind, u).wait_send()
        for _, _, there in self.operands:
            there.wait_send()


class Smalls:
    SCRATCH = 5

    @staticmethod
    def scratch(v):
        dma = pltpu.SemaphoreType.DMA
        return [
            pltpu.VMEM((3,) + v.shape, f32),
            pltpu.VMEM((3,) + v.shape, f32),
            pltpu.VMEM((3,) + v.shape[1:], f32),
            dma((6,)),
            dma((6,)),
        ]

    def __init__(self, place, v_ref, out, scratch):
        self.s, self.z, self.c, self.x, self.y, self.near = place
        self.v, self.out = v_ref, out
        self.total, self.got, self.got_z, self.send, self.recv = scratch

    def copy(self, kind):
        if kind < 3:
            src = self.v if kind == 0 else self.total.at[kind - 1]
            dst, to = self.got.at[kind], "cxy"[kind]
        else:
            z = self.z
            k = kind - 2
            other = (z + 1 - 2 * (z % 2), z + 2 - 4 * (z // 2), 3 - z)[k - 1]
            src, dst, to = self.total.at[2, other], self.got_z.at[k - 1], "z%d" % k
        return pltpu.make_async_remote_copy(
            src_ref=src,
            dst_ref=dst,
            send_sem=self.send.at[kind],
            recv_sem=self.recv.at[kind],
            device_id=self.near[to],
            device_id_type=MESH,
        )

    def start(self):
        self.copy(0).start()

    def advance(self, kind):
        self.copy(kind).wait_recv()
        mine = self.v[...] if kind == 0 else self.total[kind - 1]
        self.total[kind] = mine + self.got[kind]
        for k in (kind + 1,) if kind < 2 else (3, 4, 5):
            self.copy(k).start()

    def close(self):
        total = self.total[2, self.z]
        for k in (3, 4, 5):
            self.copy(k).wait_recv()
            total = total + self.got_z[k - 3]
        self.out[...] = total
        for k in range(6):
            self.copy(k).wait_send()


class InputGrad:
    TILE = 256
    SCRATCH = 5

    @staticmethod
    def scratch(rows, width):
        tile = InputGrad.TILE
        return [
            pltpu.VMEM((rows, width), f32),
            pltpu.VMEM((128, width), f32),
            pltpu.VMEM((2, rows, tile), bf16),
            pltpu.VMEM((2, 4, tile, width // 4), bf16),
            pltpu.SemaphoreType.DMA((3, 2)),
        ]

    def __init__(self, refs, out, gain_out, scratch):
        (
            self.gate,
            self.rest,
            self.own,
            self.gate_others,
            self.conv_shards,
            self.d_dt,
            self.dt_w,
            self.h,
            self.gain,
            self.og,
        ) = refs
        self.out, self.gain_out = out, gain_out
        self.acc, self.part, self.d, self.w, self.sems = scratch
        self.early = self.gate.shape[1] // self.TILE
        self.count = self.early + self.conv_shards.shape[1] // self.TILE

    def copies(self, i, gate):
        slot = i % 2
        at = pl.ds(pl.multiple_of((i if gate else i - self.early) * self.TILE, self.TILE), self.TILE)
        if gate:
            pairs = (
                (self.gate.at[:, at], self.d.at[slot]),
                (self.own.at[at], self.w.at[slot, 3]),
                (self.gate_others.at[:, at], self.w.at[slot, pl.ds(0, 3)]),
            )
        else:
            pairs = (
                (self.rest.at[:, at], self.d.at[slot]),
                (self.conv_shards.at[3, at], self.w.at[slot, 3]),
                (self.conv_shards.at[pl.ds(0, 3), at], self.w.at[slot, pl.ds(0, 3)]),
            )
        return [pltpu.make_async_copy(a, b, self.sems.at[k, slot]) for k, (a, b) in enumerate(pairs)]

    def act(self, i, what):
        @pl.when(i < self.early)
        def _():
            for copy in self.copies(i, True):
                getattr(copy, what)()

        @pl.when((i >= self.early) & (i < self.count))
        def _():
            for copy in self.copies(i, False):
                getattr(copy, what)()

    def start(self):
        self.acc[...] = jnp.zeros_like(self.acc)
        self.act(0, "start")

    def step(self, i):
        @pl.when(i < self.count)
        def _():
            self.act(i + 1, "start")
            self.act(i, "wait")
            slot = i % 2
            weights = jnp.concatenate([self.w[slot, k] for k in (3, 0, 1, 2)], axis=1)
            self.acc[...] += mm(self.d[slot], weights)

    def close(self):
        depth = self.w.shape[3]
        tile = self.part.shape[0]
        gain = self.gain[...]

        def body(r, d_gain):
            at = pl.ds(pl.multiple_of(r * tile, tile), tile)
            for k in range(4):
                self.part[:, shard_place(k, depth)] = self.acc[at, k * depth : (k + 1) * depth]
            d = self.part[...] + mm(self.d_dt[at, :], self.dt_w[...])
            h = self.h[at, :].astype(f32)
            scale = lax.rsqrt(jnp.mean(h * h, axis=-1, keepdims=True) + epsilon)
            d_gain = d_gain + jnp.sum(d * (h * scale), axis=0, keepdims=True)
            d = d * gain
            along = jnp.mean(d * h, axis=-1, keepdims=True) * (scale * scale * scale)
            self.out[at, :] = (scale * d - h * along + self.og[at, :].astype(f32)).astype(bf16)
            return d_gain

        d_gain = lax.fori_loop(0, self.out.shape[0] // tile, body, jnp.zeros(gain.shape, f32))
        for a in range(4):
            for r in range(depth // LANES):
                at = a * depth + r * LANES
                self.gain_out[a, r : r + 1, :] = d_gain[:, at : at + LANES]


def sums_kernel(
    gate_ref,
    rest_ref,
    nm_ref,
    far_ref,
    og_ref,
    no_ref,
    own_ref,
    gate_others_ref,
    conv_shards_ref,
    v_ref,
    d_dt_ref,
    dt_w_ref,
    h_ref,
    gain_ref,
    cot_ref,
    in_out,
    out_out,
    v_out,
    input_out,
    small_v,
    *scratch,
):
    place = around()
    cut = Products.SCRATCH
    inp = Products(place, [rest_ref], nm_ref, in_out, scratch[:cut], far_ref)
    outp = Products(place, [og_ref], no_ref, out_out, scratch[cut : 2 * cut])
    small = Smalls(place, small_v, v_out, scratch[2 * cut : 2 * cut + Smalls.SCRATCH])
    back = InputGrad(
        [
            gate_ref,
            rest_ref,
            own_ref,
            gate_others_ref,
            conv_shards_ref,
            d_dt_ref,
            dt_w_ref,
            h_ref,
            gain_ref,
            cot_ref,
        ],
        input_out,
        small_v,
        scratch[2 * cut + Smalls.SCRATCH :],
    )
    inp.load()
    outp.load()
    back.start()
    small_v[...] = v_ref[...]
    greet(place[-1])
    inp.share()
    outp.share()
    each = -(-back.count // (inp.chunks - 1))

    def first(t, carry):
        inp.step(t)

        def tile(i, carry):
            back.step(t * each + i)
            return carry

        lax.fori_loop(0, each, tile, 0)
        return carry

    lax.fori_loop(0, inp.chunks, first, 0)
    back.close()
    small.start()

    def second(t, carry):
        outp.step(t)

        @pl.when(t < inp.steps() - inp.chunks)
        def _():
            inp.step(t + inp.chunks)

        for kind in range(3):

            @pl.when(t == kind + 1)
            def _(kind=kind):
                small.advance(kind)

        return carry

    lax.fori_loop(0, outp.steps(), second, 0)
    small.close()
    inp.close()
    outp.close()


def weight_sums(
    d_gate,
    d_rest,
    nm,
    nm_far,
    og,
    no,
    own,
    gate_others,
    conv_shards,
    v,
    d_dt,
    dt_w,
    hidden,
    gain,
    out_grad,
    collective_id,
):
    vmem = pl.BlockSpec(memory_space=pltpu.VMEM)
    hbm = pl.BlockSpec(memory_space=pl.ANY)
    rows, width = hidden.shape
    a_in, a_out, total, input_grad = pl.pallas_call(
        sums_kernel,
        in_specs=[hbm] * 9 + [vmem] * 6,
        out_specs=[vmem] * 4,
        out_shape=[
            Products.out_shape([d_rest], nm),
            Products.out_shape([og], no),
            jax.ShapeDtypeStruct(v.shape[1:], f32),
            jax.ShapeDtypeStruct((rows, width), bf16),
        ],
        scratch_shapes=[pltpu.VMEM(v.shape, f32)]
        + Products.scratch([d_rest], nm)
        + Products.scratch([og], no)
        + Smalls.scratch(v)
        + InputGrad.scratch(rows, width),
        compiler_params=pltpu.CompilerParams(
            collective_id=collective_id, has_side_effects=True, vmem_limit_bytes=VMEM_MOST
        ),
        cost_estimate=pl.CostEstimate(
            flops=12 * rows * width * 6000, bytes_accessed=400_000_000, transcendentals=0
        ),
        name="weight_sums",
    )(
        d_gate,
        d_rest,
        nm,
        nm_far,
        og,
        no,
        own,
        gate_others,
        conv_shards,
        v,
        d_dt,
        dt_w,
        hidden,
        gain,
        out_grad,
    )
    return a_in.reshape(d_rest.shape[1], -1), a_out.reshape(og.shape[1], -1), total, input_grad


LANES = 128
HALO = 16


def sigmoid(v):
    return 0.5 + 0.5 * jnp.tanh(0.5 * v)


def silu_parts(v):
    s = sigmoid(v)
    return v * s, s


def softplus(v):
    return jnp.maximum(v, 0.0) + jnp.log1p(jnp.exp(-jnp.abs(v)))


def lower_ones(t):
    i = lax.broadcasted_iota(jnp.int32, (t, t), 0)
    j = lax.broadcasted_iota(jnp.int32, (t, t), 1)
    return jnp.where(i >= j, 1.0, 0.0)


def exact(a, b, dims=NN):
    return lax.dot_general(a, b, dims, precision=highest, preferred_element_type=f32)


def head_columns(values, g):
    return pltpu.roll(values, (LANES - GROUP * g) % LANES, 1)[:, :GROUP]


class Exchange:
    def __init__(self, forward, own_low, got, t_low, t_got, u_low, u_got, p_low, p_got, send, recv):
        self.s, self.z, self.c, self.x, self.y, self.near = around()
        later = (lambda v: v) if forward else (lambda v: 1 - v)
        self.second = (later(self.c) == 1, later(self.x) == 1, later(self.y) == 1)
        self.own_low, self.got = own_low, got
        self.t_low, self.t_got, self.u_low, self.u_got = t_low, t_got, u_low, u_got
        self.p_low, self.p_got = p_low, p_got
        self.send, self.recv = send, recv
        self.n = t_low.shape[1] - 16
        self.half = t_low.shape[2]
        self.mine = pl.ds(pl.multiple_of(self.c * self.half, LANES), self.half)
        self.other = pl.ds(pl.multiple_of((1 - self.c) * self.half, LANES), self.half)

    def copy(self, kind, m):
        src, dst, to = (
            (self.own_low, self.got, "c"),
            (self.t_low, self.t_got, "x"),
            (self.u_low, self.u_got, "y"),
            (self.p_low, self.p_got, "c"),
        )[kind]
        return pltpu.make_async_remote_copy(
            src_ref=src.at[m],
            dst_ref=dst.at[m],
            send_sem=self.send.at[kind, m],
            recv_sem=self.recv.at[kind, m],
            device_id=self.near[to],
            device_id_type=MESH,
        )

    def put_decay(self, ref, m, lanes, decay):
        high = decay.astype(bf16).astype(f32)
        row = lax.broadcasted_iota(jnp.int32, (16, decay.shape[1]), 0)
        both = jnp.where(row == 0, high, jnp.where(row == 1, decay - high, 0.0))
        ref[m, pl.ds(self.n, 16), lanes] = both.astype(bf16)

    def decay_of(self, ref, m, lanes):
        rows = ref[m, pl.ds(self.n, 16), lanes].astype(f32)
        return rows[0:1] + rows[1:2]

    def put_own(self, m, lanes, state, decay):
        self.own_low[m, pl.ds(0, self.n), lanes] = state.astype(bf16)
        self.put_decay(self.own_low, m, lanes, decay)

    def core(self, m):
        self.copy(0, m).start()

    def along_x(self, m):
        self.copy(0, m).wait_recv()
        second = self.second[0]
        mine = self.own_low[m, pl.ds(0, self.n), self.mine].astype(f32)
        theirs = self.got[m, pl.ds(0, self.n), self.mine].astype(f32)
        d_mine = self.decay_of(self.own_low, m, self.mine)
        d_theirs = self.decay_of(self.got, m, self.mine)
        total = theirs * jnp.where(second, d_mine, 1.0) + mine * jnp.where(second, 1.0, d_theirs)
        self.t_low[m, pl.ds(0, self.n), :] = total.astype(bf16)
        self.put_decay(self.t_low, m, pl.ds(0, self.half), d_mine * d_theirs)
        self.copy(1, m).start()

    def along_y(self, m):
        self.copy(1, m).wait_recv()
        second = self.second[1]
        every = pl.ds(0, self.half)
        mine = self.t_low[m, pl.ds(0, self.n), :].astype(f32)
        theirs = self.t_got[m, pl.ds(0, self.n), :].astype(f32)
        d_mine = self.decay_of(self.t_low, m, every)
        d_theirs = self.decay_of(self.t_got, m, every)
        total = theirs * jnp.where(second, d_mine, 1.0) + mine * jnp.where(second, 1.0, d_theirs)
        self.u_low[m] = total.astype(bf16)
        self.copy(2, m).start()

    def back_to_core(self, m):
        self.copy(2, m).wait_recv()
        every = pl.ds(0, self.half)
        x_second = jnp.where(self.second[1], 1.0, 0.0)
        y_second = jnp.where(self.second[2], 1.0, 0.0)
        theirs = self.t_got[m, pl.ds(0, self.n), :].astype(f32)
        d_theirs = self.decay_of(self.t_got, m, every)
        over = y_second * jnp.where(self.second[1], d_theirs, 1.0)
        before = x_second * theirs + over * self.u_got[m].astype(f32)
        self.p_low[m] = before.astype(bf16)
        self.copy(3, m).start()

    def begin_state(self, m, out):
        self.copy(3, m).wait_recv()
        second = jnp.where(self.second[0], 1.0, 0.0)
        for lanes, before in (
            (self.mine, self.p_low[m].astype(f32)),
            (self.other, self.p_got[m].astype(f32)),
        ):
            d_theirs = self.decay_of(self.got, m, lanes)
            theirs = self.got[m, pl.ds(0, self.n), lanes].astype(f32)
            over = jnp.where(self.second[0], d_theirs, 1.0)
            out[m, :, lanes] = (before * over + second * theirs).astype(bf16)

    def sent(self):
        for m in range(self.own_low.shape[0]):
            for kind in range(4):
                self.copy(kind, m).wait_send()


def exchange_scratch(micro, n, inner):
    half = inner // 2
    dma = pltpu.SemaphoreType.DMA
    return [
        pltpu.VMEM((micro, n + 16, inner), bf16),
        pltpu.VMEM((micro, n + 16, inner), bf16),
        pltpu.VMEM((micro, n + 16, half), bf16),
        pltpu.VMEM((micro, n + 16, half), bf16),
        pltpu.VMEM((micro, n, half), bf16),
        pltpu.VMEM((micro, n, half), bf16),
        pltpu.VMEM((micro, n, half), bf16),
        pltpu.VMEM((micro, n, half), bf16),
        dma((4, micro)),
        dma((4, micro)),
    ]


EXCHANGE = 10
TICKS = (6, 3, 2, 2)


def steps_of(raw, shift, rate):
    t = raw.shape[0]
    dt = softplus(raw + shift)
    cum = exact(lower_ones(t), dt * rate)
    return dt, cum


def conv_rows(buf, cw, cb):
    taps = cw.shape[0]
    t = buf.shape[0] - HALO
    total = cb + buf[HALO - taps + 1 : HALO - taps + 1 + t, :] * cw[0:1]
    for k in range(1, taps):
        at = HALO - taps + 1 + k
        total = total + buf[at : at + t, :] * cw[k : k + 1]
    return total


def scan_forward_kernel(
    hs,
    conv_ref,
    raw_ref,
    cw_ref,
    cb_ref,
    shift_ref,
    rate_ref,
    skip_ref,
    eighth_ref,
    x_ref,
    bc_ref,
    y_ref,
    low_ref,
    halo,
    begin_ref,
    others_ref,
    *scratch,
):
    buf, wide_buf, scores, dts, cums, rows_t, h_send, h_recv, o_send, o_recv, o_own = scratch[EXCHANGE:]
    ex = Exchange(True, *scratch[:EXCHANGE])
    s, z = ex.s, ex.z
    micro, t, channels = conv_ref.shape
    inner = x_ref.shape[2]
    n = begin_ref.shape[1]
    gc = GROUP * hs
    groups = inner // gc
    half_t = t // 2
    place = around()
    near = {k: ex.near[k] for k in ("c", "x", "y")}
    near["next"] = ((s + 1) % 8, z)
    near["last"] = ((s + 7) % 8, z)
    greet(near)
    weight = Gather(
        place, [(eighth_ref, None, others_ref, others_ref.shape[1], 2)], o_send, o_recv, o_own
    )

    tail = [
        pltpu.make_async_remote_copy(
            src_ref=conv_ref.at[m, pl.ds(t - HALO, HALO)],
            dst_ref=halo.at[m],
            send_sem=h_send.at[m],
            recv_sem=h_recv.at[m],
            device_id=near["next"],
            device_id_type=MESH,
        )
        for m in range(micro)
    ]
    for copy in tail:
        copy.start()
    weight.begin(0)
    for m in range(micro):
        dt, cum = steps_of(raw_ref[m], shift_ref[...], rate_ref[...])
        dts[m] = dt
        cums[m] = cum
        rows_t[m] = cum.T
    for copy in tail:
        copy.wait_recv()
    has_prior = jnp.where(s > 0, 1.0, 0.0)

    def activate(m, lanes, into):
        into[0:HALO] = halo[m, :, lanes].astype(f32) * has_prior
        into[pl.ds(HALO, t)] = conv_ref[m, :, lanes].astype(f32)
        return silu_parts(conv_rows(into, cw_ref[:, lanes], cb_ref[:, lanes]))[0]

    def own_states(m, a, b):
        def body(g, carry):
            lanes = pl.ds(pl.multiple_of(g * gc, gc), gc)
            x = activate(m, lanes, buf).astype(bf16)
            x_ref[m, :, lanes] = x
            cum = head_columns(cums[m], g)
            to_end = head_columns(dts[m], g) * jnp.exp(cum[t - 1 :] - cum)
            weighted = (x.astype(f32) * widen(to_end, hs)).astype(bf16)
            state = mm(bc_ref[m, :, 0:n], weighted, TN)
            ex.put_own(m, lanes, state, widen(jnp.exp(cum[t - 1 :]), hs))
            return carry

        lax.fori_loop(a, b, body, 0)

    def local_scans(m, a, b):
        lane = lax.broadcasted_iota(jnp.int32, (half_t, 2 * hs), 1)

        def body(g, carry):
            lanes = pl.ds(pl.multiple_of(g * gc, gc), gc)
            cum = head_columns(cums[m], g)
            rows = rows_t[m, pl.ds(pl.multiple_of(g * GROUP, GROUP), GROUP), :]
            dt_wide = widen(head_columns(dts[m], g), hs)
            weighted = (x_ref[m, :, lanes].astype(f32) * dt_wide).astype(bf16)
            for k in range(0, GROUP, 2):
                pair = weighted[:, k * hs : (k + 2) * hs]
                at = pl.ds(pl.multiple_of(g * gc + k * hs, 2 * hs), 2 * hs)
                top, low = [], []
                for h in (k, k + 1):
                    col, row = cum[:, h : h + 1], rows[h : h + 1, :]
                    m1 = jnp.exp(jnp.minimum(col[:half_t] - row[:, :half_t], 0.0))
                    m2 = jnp.exp(jnp.minimum(col[half_t:] - row, 0.0))
                    m1 = (m1 * scores[m, :half_t, :half_t]).astype(bf16)
                    m2 = (m2 * scores[m, half_t:, :]).astype(bf16)
                    top.append(mm(m1, pair[:half_t]))
                    low.append(mm(m2, pair))
                y_ref[m, :half_t, at] = jnp.where(lane < hs, top[0], top[1])
                y_ref[m, half_t:, at] = jnp.where(lane < hs, low[0], low[1])
            return carry

        lax.fori_loop(a, b, body, 0)

    def carried(m):
        def body(g, carry):
            lanes = pl.ds(pl.multiple_of(g * gc, gc), gc)
            decay = widen(jnp.exp(head_columns(cums[m], g)), hs)
            scan = y_ref[m, :, lanes] + decay * mm(bc_ref[m, :, n:], begin_ref[m, :, lanes])
            y_ref[m, :, lanes] = scan
            x = x_ref[m, :, lanes].astype(f32)
            low_ref[m, :, lanes] = (scan + skip_ref[:, lanes] * x).astype(bf16)
            return carry

        lax.fori_loop(0, groups, body, 0)

    for m in range(micro):
        lanes = pl.ds(inner, channels - inner)
        bc = activate(m, lanes, wide_buf).astype(bf16)
        bc_ref[m] = bc
        scores[m] = mm(bc[:, n:], bc[:, :n], NT) * lower_ones(t)
    middle = groups // 2
    own_states(0, 0, groups)
    ex.core(0)
    own_states(1, 0, middle)
    ex.along_x(0)
    own_states(1, middle, groups)
    ex.core(1)
    weight.begin(1)
    local_scans(0, 0, middle)
    ex.along_x(1)
    ex.along_y(0)
    local_scans(0, middle, groups)
    weight.middle(0)
    local_scans(1, 0, middle)
    ex.along_y(1)
    weight.middle(1)
    weight.finish(0)
    ex.back_to_core(0)
    local_scans(1, middle, groups)
    ex.begin_state(0, begin_ref)
    carried(0)
    weight.finish(1)
    ex.back_to_core(1)
    ex.begin_state(1, begin_ref)
    carried(1)
    weight.close()
    ex.sent()
    for copy in tail:
        copy.wait_send()


def scan_forward(
    conv_low, raw, conv_w, conv_b, shift, rate, skip_wide, out_eighth, inner, hs, collective_id
):
    micro, t, channels = conv_low.shape
    n = (channels - inner) // 2
    gc = GROUP * hs
    dma = pltpu.SemaphoreType.DMA
    vmem = pl.BlockSpec(memory_space=pltpu.VMEM)
    hbm = pl.BlockSpec(memory_space=pl.ANY)
    return pl.pallas_call(
        partial(scan_forward_kernel, hs),
        in_specs=[vmem] * 8,
        out_specs=[vmem] * 6 + [hbm],
        out_shape=[
            jax.ShapeDtypeStruct((micro, t, inner), bf16),
            jax.ShapeDtypeStruct((micro, t, 2 * n), bf16),
            jax.ShapeDtypeStruct((micro, t, inner), f32),
            jax.ShapeDtypeStruct((micro, t, inner), bf16),
            jax.ShapeDtypeStruct((micro, HALO, channels), bf16),
            jax.ShapeDtypeStruct((micro, n, inner), bf16),
            jax.ShapeDtypeStruct((3, 8 * out_eighth.shape[1], out_eighth.shape[2]), bf16),
        ],
        scratch_shapes=exchange_scratch(micro, n, inner)
        + [
            pltpu.VMEM((HALO + t, gc), f32),
            pltpu.VMEM((HALO + t, 2 * n), f32),
            pltpu.VMEM((micro, t, t), f32),
            pltpu.VMEM((micro, t, LANES), f32),
            pltpu.VMEM((micro, t, LANES), f32),
            pltpu.VMEM((micro, LANES, t), f32),
            dma((micro,)),
            dma((micro,)),
            dma((2, CHUNK_DMAS)),
            dma((2, CHUNK_DMAS)),
            dma((2,)),
        ],
        compiler_params=pltpu.CompilerParams(
            collective_id=collective_id, has_side_effects=True, vmem_limit_bytes=VMEM_MOST
        ),
        cost_estimate=pl.CostEstimate(
            flops=4 * micro * t * inner * (t + 3 * n), bytes_accessed=100_000_000, transcendentals=0
        ),
        name="scan_forward",
    )(conv_low, raw, conv_w, conv_b, shift, rate, skip_wide, out_eighth)


def scan_backward_kernel(
    hs,
    dy_ref,
    x_ref,
    bc_ref,
    y_ref,
    begin_ref,
    raw_ref,
    conv_ref,
    halo_ref,
    cw_ref,
    cb_ref,
    shift_ref,
    rate_ref,
    skip_ref,
    dgate_ref,
    norm_ref,
    dconv_ref,
    dcw_ref,
    dcb_ref,
    heads_ref,
    sum_ref,
    far_ref,
    far_sem,
    *scratch,
):
    (
        y_now,
        y_sem,
        buf,
        wide_buf,
        scores,
        total,
        dts,
        cums,
        rows_t,
        ends,
        dxl,
        dbc,
        ddt_sum,
        dcum_sum,
        last_sum,
        head_low,
        next_low,
        h_send,
        h_recv,
    ) = scratch[EXCHANGE : EXCHANGE + 19]
    ex = Exchange(False, *scratch[:EXCHANGE])
    s, z = ex.s, ex.z
    micro, t, channels = conv_ref.shape
    inner = x_ref.shape[2]
    n = begin_ref.shape[1]
    gc = GROUP * hs
    groups = inner // gc
    half = t // 2
    taps = cw_ref.shape[0]
    place = around()
    near = dict(place[-1])
    near["next"] = ((s + 1) % 8, z)
    near["last"] = ((s + 7) % 8, z)
    sums_of = Products(place, [dgate_ref], norm_ref, sum_ref, scratch[EXCHANGE + 19 :])
    sums_of.load()

    def y_copy(i):
        lanes = pl.ds(pl.multiple_of((i % groups) * gc, gc), gc)
        slot = i % 2
        return pltpu.make_async_copy(y_ref.at[i // groups, :, lanes], y_now.at[slot], y_sem.at[slot])

    greet(near)
    sums_of.share()
    first_rows = [
        pltpu.make_async_remote_copy(
            src_ref=head_low.at[m],
            dst_ref=next_low.at[m],
            send_sem=h_send.at[m],
            recv_sem=h_recv.at[m],
            device_id=near["last"],
            device_id_type=MESH,
        )
        for m in range(micro)
    ]
    has_prior = jnp.where(s > 0, 1.0, 0.0)
    has_next = jnp.where(s < 7, 1.0, 0.0)

    middle = groups // 2

    def at_step(i, *todo):
        for when, what in todo:
            pl.when(i == when)(what)

    def own_states():
        def body(i, carry):
            m, g = i // groups, i % groups
            lanes = pl.ds(pl.multiple_of(g * gc, gc), gc)
            cum = head_columns(cums[m], g)
            weighted = (dy_ref[m, :, lanes].astype(f32) * widen(jnp.exp(cum), hs)).astype(bf16)
            state = mm(bc_ref[m, :, n:], weighted, TN)
            ex.put_own(m, lanes, state, widen(jnp.exp(cum[t - 1 :]), hs))
            at_step(
                i,
                (groups - 1, lambda: ex.core(0)),
                (groups + middle, lambda: ex.along_x(0)),
                (2 * groups - 1, lambda: ex.core(1)),
            )
            tick(i, TICKS[0], 0)
            return carry

        lax.fori_loop(0, 2 * groups, body, 0)

    def tick(i, every, first):
        @pl.when(i % every == every - 1)
        def _():
            sums_of.step(first + i // every)

    def upper_ones():
        j = lax.broadcasted_iota(jnp.int32, (t, t), 0)
        i = lax.broadcasted_iota(jnp.int32, (t, t), 1)
        return jnp.where(i >= j, 1.0, 0.0)

    def local_terms():
        lane = lax.broadcasted_iota(jnp.int32, (t, 2 * hs), 1)
        lane_half = lax.broadcasted_iota(jnp.int32, (half, 2 * hs), 1)

        def body(i, carry):
            m, g = i // groups, i % groups
            lanes = pl.ds(pl.multiple_of(g * gc, gc), gc)
            cum = head_columns(cums[m], g)
            rows = rows_t[m, pl.ds(pl.multiple_of(g * GROUP, GROUP), GROUP), :]
            dt_wide = widen(head_columns(dts[m], g), hs)
            weighted = (x_ref[m, :, lanes].astype(f32) * dt_wide).astype(bf16)
            for k in range(0, GROUP, 2):
                pair = weighted[:, k * hs : (k + 2) * hs]
                at = pl.ds(pl.multiple_of(g * gc + k * hs, 2 * hs), 2 * hs)
                dy = dy_ref[m, :, at]
                top, low = [], []
                for h in (k, k + 1):
                    col, row = cum[:, h : h + 1], rows[h : h + 1, :]
                    mine = jnp.where(lane < hs, pair, 0) if h == k else jnp.where(lane < hs, 0, pair)
                    l1 = jnp.exp(jnp.minimum(row - col[:half], 0.0))
                    l2 = jnp.exp(jnp.minimum(row[:, half:] - col[half:], 0.0))
                    total[:half, :] += l1 * mm(mine[:half], dy, NT)
                    total[half:, half:] += l2 * mm(mine[half:], dy[half:], NT)
                    top.append(mm((l1 * scores[m, :half, :]).astype(bf16), dy))
                    low.append(mm((l2 * scores[m, half:, half:]).astype(bf16), dy[half:]))
                dxl[m, :half, at] = jnp.where(lane_half < hs, top[0], top[1])
                dxl[m, half:, at] = jnp.where(lane_half < hs, low[0], low[1])
            at_step(
                i,
                (1, lambda: ex.along_x(1)),
                (3, lambda: ex.along_y(0)),
                (groups - 1, lambda: local_close(0)),
                (groups + 1, lambda: ex.along_y(1)),
                (groups + 3, lambda: ex.back_to_core(0)),
                (2 * groups - 1, lambda: local_close(1)),
            )
            tick(i, TICKS[1], 2 * groups // TICKS[0])
            return carry

        lax.fori_loop(0, 2 * groups, body, 0)

    def local_close(m):
        d = total[...] * upper_ones()
        dbc[m, :, 0:n] = mm(d.astype(bf16), bc_ref[m, :, n:])
        dbc[m, :, n:] = mm(d.T.astype(bf16), bc_ref[m, :, :n])
        total[...] = jnp.zeros_like(total)

    def through_states():
        r = lax.broadcasted_iota(jnp.int32, (gc, LANES), 0)
        col = lax.broadcasted_iota(jnp.int32, (gc, LANES), 1)

        def clear():
            ddt_sum[...] = jnp.zeros_like(ddt_sum)
            dcum_sum[...] = jnp.zeros_like(dcum_sum)
            last_sum[...] = jnp.zeros_like(last_sum)

        def close(m):
            d_log = exact(upper_ones(), dcum_sum[...]) + last_sum[0:1]
            v = raw_ref[m] + shift_ref[...]
            d_dt = (ddt_sum[...] + d_log * rate_ref[...]) / (1.0 + jnp.exp(-v))
            rest = dconv_ref.shape[2] - channels - LANES
            dconv_ref[m, :, pl.ds(channels, LANES)] = d_dt.astype(bf16)
            if rest:
                dconv_ref[m, :, pl.ds(channels + LANES, rest)] = jnp.zeros((t, rest), bf16)
            heads_ref[0:1] += jnp.sum(d_dt, axis=0, keepdims=True)
            heads_ref[1:2] += jnp.sum(d_log * dts[m], axis=0, keepdims=True) * rate_ref[...]
            first_slopes(m)
            if m == 0:
                clear()
                ex.begin_state(1, ends)

        def body(i, carry):
            m, g = i // groups, i % groups
            lanes = pl.ds(pl.multiple_of(g * gc, gc), gc)

            @pl.when(i + 1 < 2 * groups)
            def _():
                y_copy(i + 1).start()

            y_copy(i).wait()
            ones = jnp.where(r // hs + g * GROUP == col, 1.0, 0.0).astype(bf16)
            cum = head_columns(cums[m], g)
            dt_wide = widen(head_columns(dts[m], g), hs)
            x, dy = x_ref[m, :, lanes].astype(f32), dy_ref[m, :, lanes].astype(f32)
            weighted = (x * dt_wide).astype(bf16).astype(f32)
            decay = widen(jnp.exp(cum), hs)
            to_end = widen(jnp.exp(cum[t - 1 :] - cum), hs)
            s_in, ds = begin_ref[m, :, lanes], ends[m, :, lanes]
            through = to_end * mm(bc_ref[m, :, 0:n], ds)
            d_weighted = dxl[m, :, lanes] + through
            dconv_ref[m, :, lanes] = (dt_wide * d_weighted + skip_ref[:, lanes] * dy).astype(bf16)
            dbc[m, :, 0:n] += mm((weighted * to_end).astype(bf16), ds, NT)
            dbc[m, :, n:] += mm((dy * decay).astype(bf16), s_in, NT)
            ddt_sum[...] += head_sums(x * d_weighted, ones)
            dcum_sum[...] += head_sums(dy * y_now[i % 2] - weighted * d_weighted, ones)
            at_end = jnp.sum(weighted * through, axis=0, keepdims=True) + decay[t - 1 :] * jnp.sum(
                s_in.astype(f32) * ds.astype(f32), axis=0, keepdims=True
            )
            last_sum[...] += head_sums(jnp.broadcast_to(at_end, (8, gc)), ones)
            by_skip = jnp.sum(x * dy, axis=0, keepdims=True)
            heads_ref[2:3] += head_sums(jnp.broadcast_to(by_skip, (8, gc)), ones)[0:1]
            at_step(i, (groups - 1, lambda: close(0)), (2 * groups - 1, lambda: close(1)))
            tick(i, TICKS[2], 2 * groups // TICKS[0] + 2 * groups // TICKS[1])
            return carry

        clear()
        heads_ref[...] = jnp.zeros_like(heads_ref)
        y_copy(0).start()
        lax.fori_loop(0, 2 * groups, body, 0)

    def pre_slope(into, lanes, grad, rows):
        v = conv_rows(into[0 : HALO + rows, :], cw_ref[:, lanes], cb_ref[:, lanes])
        sig = sigmoid(v)
        return grad * (sig * (1.0 + v * (1.0 - sig)))

    def load(m, lanes, into, rows):
        into[0:HALO] = halo_ref[m, :, lanes].astype(f32) * has_prior
        into[HALO : HALO + rows] = conv_ref[m, 0:rows, lanes].astype(f32)

    def first_slopes(m):
        def one(lanes, into, grad):
            load(m, lanes, into, HALO)
            head_low[m, :, lanes] = pre_slope(into, lanes, grad, HALO).astype(bf16)

        def body(g, carry):
            lanes = pl.ds(pl.multiple_of(g * gc, gc), gc)
            one(lanes, buf, dconv_ref[m, 0:HALO, lanes].astype(f32))
            return carry

        lax.fori_loop(0, groups, body, 0)
        one(pl.ds(inner, channels - inner), wide_buf, dbc[m, 0:HALO, :])
        first_rows[m].start()

    def conv_back():
        def one(m, lanes, into, grad):
            load(m, lanes, into, t)
            slope = pre_slope(into, lanes, grad, t)
            weights = cw_ref[:, lanes]
            lines = []
            for k in range(taps):
                at = HALO - taps + 1 + k
                lines.append(jnp.sum(slope * into[at : at + t, :], axis=0, keepdims=True))
            dcw_ref[:, lanes] += jnp.concatenate(lines, axis=0)
            dcb_ref[:, lanes] += jnp.sum(slope, axis=0, keepdims=True)
            into[0:t] = slope
            into[t : t + HALO] = next_low[m, :, lanes].astype(f32) * has_next
            back = into[taps - 1 : taps - 1 + t, :] * weights[0:1]
            for k in range(1, taps):
                at = taps - 1 - k
                back = back + into[at : at + t, :] * weights[k : k + 1]
            dconv_ref[m, :, lanes] = back.astype(bf16)

        def body(i, carry):
            m, g = i // groups, i % groups
            lanes = pl.ds(pl.multiple_of(g * gc, gc), gc)
            one(m, lanes, buf, dconv_ref[m, :, lanes].astype(f32))
            at_step(i, (groups - 1, lambda: first_rows[1].wait_recv()))
            tick(i, TICKS[3], 2 * groups // TICKS[0] + 2 * groups // TICKS[1] + 2 * groups // TICKS[2])
            return carry

        first_rows[0].wait_recv()
        lax.fori_loop(0, 2 * groups, body, 0)
        for m in range(micro):
            one(m, pl.ds(inner, channels - inner), wide_buf, dbc[m])

    for m in range(micro):
        dt, cum = steps_of(raw_ref[m], shift_ref[...], rate_ref[...])
        dts[m] = dt
        cums[m] = cum
        rows_t[m] = cum.T
        scores[m] = mm(bc_ref[m, :, 0:n], bc_ref[m, :, n:], NT) * upper_ones()
    dcw_ref[...] = jnp.zeros_like(dcw_ref)
    dcb_ref[...] = jnp.zeros_like(dcb_ref)
    total[...] = jnp.zeros_like(total)
    own_states()
    local_terms()
    ex.begin_state(0, ends)
    ex.back_to_core(1)
    through_states()
    conv_back()
    done = sum(2 * groups // every for every in TICKS)

    def rest_of(i, carry):
        sums_of.step(i)
        return carry

    rows = far_ref.shape[0]
    far = pltpu.make_async_copy(sums_of.b.at[pl.ds(rows, rows)], far_ref, far_sem)
    far.start()
    lax.fori_loop(done, sums_of.steps(), rest_of, 0)
    far.wait()
    ex.sent()
    for copy in first_rows:
        copy.wait_send()
    sums_of.close()


def scan_backward(
    dy,
    x,
    bc,
    y,
    begin,
    raw,
    conv_low,
    halo,
    conv_w,
    conv_b,
    shift,
    rate,
    skip_wide,
    d_gate,
    normed,
    hs,
    collective_id,
):
    micro, t, channels = conv_low.shape
    inner = x.shape[2]
    n = begin.shape[1]
    gc = GROUP * hs
    taps = conv_w.shape[0]
    dma = pltpu.SemaphoreType.DMA
    vmem = pl.BlockSpec(memory_space=pltpu.VMEM)
    hbm = pl.BlockSpec(memory_space=pl.ANY)
    return pl.pallas_call(
        partial(scan_backward_kernel, hs),
        in_specs=[vmem] * 3 + [hbm] + [vmem] * 9 + [hbm] * 2,
        out_specs=[vmem] * 5 + [hbm],
        out_shape=[
            jax.ShapeDtypeStruct((micro, t, -(-(channels + LANES) // 256) * 256), bf16),
            jax.ShapeDtypeStruct((taps, channels), f32),
            jax.ShapeDtypeStruct((1, channels), f32),
            jax.ShapeDtypeStruct((8, LANES), f32),
            Products.out_shape([d_gate], normed),
            jax.ShapeDtypeStruct(normed.shape, bf16),
        ],
        scratch_shapes=[dma]
        + exchange_scratch(micro, n, inner)
        + [
            pltpu.VMEM((2, t, gc), f32),
            dma((2,)),
            pltpu.VMEM((HALO + t, gc), f32),
            pltpu.VMEM((HALO + t, 2 * n), f32),
            pltpu.VMEM((micro, t, t), f32),
            pltpu.VMEM((t, t), f32),
            pltpu.VMEM((micro, t, LANES), f32),
            pltpu.VMEM((micro, t, LANES), f32),
            pltpu.VMEM((micro, LANES, t), f32),
            pltpu.VMEM((micro, n, inner), bf16),
            pltpu.VMEM((micro, t, inner), f32),
            pltpu.VMEM((micro, t, 2 * n), f32),
            pltpu.VMEM((t, LANES), f32),
            pltpu.VMEM((t, LANES), f32),
            pltpu.VMEM((8, LANES), f32),
            pltpu.VMEM((micro, HALO, channels), bf16),
            pltpu.VMEM((micro, HALO, channels), bf16),
            dma((micro,)),
            dma((micro,)),
        ]
        + Products.scratch([d_gate], normed),
        compiler_params=pltpu.CompilerParams(
            collective_id=collective_id, has_side_effects=True, vmem_limit_bytes=VMEM_MOST
        ),
        cost_estimate=pl.CostEstimate(
            flops=8 * micro * t * inner * (t + 3 * n), bytes_accessed=100_000_000, transcendentals=0
        ),
        name="scan_backward",
    )(
        dy,
        x,
        bc,
        y,
        begin,
        raw,
        conv_low,
        halo,
        conv_w,
        conv_b,
        shift,
        rate,
        skip_wide,
        d_gate,
        normed,
    )


def shard_place(k, depth):
    z = lax.axis_index("wshard")
    other = (z, z + 1 - 2 * (z % 2), z + 2 - 4 * (z // 2), 3 - z)[k]
    return pl.ds(pl.multiple_of(other * depth, 128), depth)


def front_kernel(h_ref, g_ref, dtw_ref, v_ref, conv_ref, norm_ref, raw_ref, rel):
    depth = v_ref.shape[2]

    @pl.when(pl.program_id(0) == 0)
    def _():
        h = h_ref[...].astype(f32)
        power = jnp.mean(h * h, axis=-1, keepdims=True)
        normed = (h * lax.rsqrt(power + epsilon) * g_ref[...]).astype(bf16)
        norm_ref[...] = normed
        raw_ref[...] = mm(normed, dtw_ref[...], NT).astype(bf16).astype(f32)
        for k in range(4):
            rel[:, k * depth : (k + 1) * depth] = norm_ref[:, shard_place(k, depth)]

    weights = jnp.concatenate([v_ref[k] for k in (3, 0, 1, 2)], axis=1)
    conv_ref[...] = mm(rel[...], weights, NT).astype(bf16)


def front(hidden, gain, dt_w, shards, tile):
    rows, width = hidden.shape
    _, count, depth = shards.shape
    whole = pl.BlockSpec((rows, width), lambda i: (0, 0))
    return pl.pallas_call(
        front_kernel,
        grid=(count // tile,),
        in_specs=[
            whole,
            pl.BlockSpec((1, width), lambda i: (0, 0)),
            pl.BlockSpec((LANES, width), lambda i: (0, 0)),
            pl.BlockSpec((4, tile, depth), lambda i: (0, i, 0)),
        ],
        out_specs=[
            pl.BlockSpec((rows, tile), lambda i: (0, i)),
            whole,
            pl.BlockSpec((rows, LANES), lambda i: (0, 0)),
        ],
        out_shape=[
            jax.ShapeDtypeStruct((rows, count), bf16),
            jax.ShapeDtypeStruct((rows, width), bf16),
            jax.ShapeDtypeStruct((rows, LANES), f32),
        ],
        scratch_shapes=[pltpu.VMEM((rows, width), bf16)],
        compiler_params=pltpu.CompilerParams(vmem_limit_bytes=VMEM),
        name="front",
    )(hidden, gain, dt_w, shards)


def gate_kernel(
    scan_ref,
    norm_ref,
    w_ref,
    v_ref,
    gain_ref,
    ow_ref,
    ov_ref,
    h_ref,
    og_ref,
    valid_ref,
    no_ref,
    out_ref,
    g_ref,
    dy_ref,
    dgate_ref,
    dgain_ref,
    gate,
    d_no,
    branch,
):
    inner = scan_ref.shape[1]
    depth = w_ref.shape[1]
    block = ow_ref.shape[0]
    rows = scan_ref.shape[0]

    @pl.when(pl.program_id(0) == 0)
    def _():
        dgain_ref[...] = jnp.zeros_like(dgain_ref)

    rel = jnp.concatenate([norm_ref[:, shard_place(k, depth)] for k in range(4)], axis=1)
    valid = valid_ref[...]
    g_low = (og_ref[...].astype(f32) * valid).astype(bf16)
    g_ref[...] = g_low
    power = jnp.zeros((rows, 1), f32)
    for i in range(4):
        at = slice(i * block, (i + 1) * block)
        weights = jnp.concatenate([w_ref[at, :]] + [v_ref[k, at, :] for k in range(3)], axis=1)
        value = mm(rel, weights, NT)
        gate[:, at] = value
        act, _ = silu_parts(value)
        u = scan_ref[:, at].astype(f32) * act
        power += jnp.sum(u * u, axis=-1, keepdims=True)
    scale = lax.rsqrt(power / inner + epsilon)
    along = jnp.zeros((rows, 1), f32)
    for k in range(4):
        at = shard_place(k, block)
        weights = ow_ref[...] if k == 0 else ov_ref[k - 1]
        act, _ = silu_parts(gate[:, at])
        u = scan_ref[:, at].astype(f32) * act
        normed = u * scale
        low = (normed * gain_ref[:, at]).astype(bf16)
        no_ref[:, at] = low
        if k == 0:
            branch[...] = mm(low, weights)
        else:
            branch[...] += mm(low, weights)
        d = mm(g_low, weights, NT)
        dgain_ref[:, at] += jnp.sum(d * normed, axis=0, keepdims=True)
        d = d * gain_ref[:, at]
        d_no[:, at] = d
        along += jnp.sum(d * u, axis=-1, keepdims=True)
    out_ref[...] = (h_ref[...].astype(f32) + valid * branch[...]).astype(bf16)
    along = along * scale * scale * scale / inner
    for i in range(4):
        at = slice(i * block, (i + 1) * block)
        value = gate[:, at]
        act, sig = silu_parts(value)
        v = scan_ref[:, at].astype(f32)
        d_u = scale * d_no[:, at] - v * act * along
        dy_ref[:, at] = (d_u * act).astype(bf16)
        dgate_ref[:, at] = (d_u * v * (sig * (1.0 + value * (1.0 - sig)))).astype(bf16)


def gate_stage(scanned, normed, own, others, gain, out_own, out_others, hidden, out_grad, valid, tile):
    rows, width = hidden.shape
    _, inner, depth = others.shape
    once = pl.Buffered(1)
    wide = pl.BlockSpec((tile, inner), lambda i: (i, 0))
    slim = pl.BlockSpec((tile, width), lambda i: (i, 0))
    line = pl.BlockSpec((1, inner), lambda i: (0, 0))
    return pl.pallas_call(
        gate_kernel,
        grid=(rows // tile,),
        in_specs=[
            wide,
            slim,
            pl.BlockSpec((inner, depth), lambda i: (0, 0), pipeline_mode=once),
            pl.BlockSpec(others.shape, lambda i: (0, 0, 0), pipeline_mode=once),
            line,
            pl.BlockSpec(out_own.shape, lambda i: (0, 0), pipeline_mode=once),
            pl.BlockSpec(out_others.shape, lambda i: (0, 0, 0), pipeline_mode=once),
            slim,
            slim,
            pl.BlockSpec((tile, 1), lambda i: (i, 0)),
        ],
        out_specs=[wide, slim, slim, wide, wide, line],
        out_shape=[
            jax.ShapeDtypeStruct((rows, inner), bf16),
            jax.ShapeDtypeStruct((rows, width), bf16),
            jax.ShapeDtypeStruct((rows, width), bf16),
            jax.ShapeDtypeStruct((rows, inner), bf16),
            jax.ShapeDtypeStruct((rows, inner), bf16),
            jax.ShapeDtypeStruct((1, inner), f32),
        ],
        scratch_shapes=[
            pltpu.VMEM((tile, inner), f32),
            pltpu.VMEM((tile, inner), f32),
            pltpu.VMEM((tile, width), f32),
        ],
        compiler_params=pltpu.CompilerParams(vmem_limit_bytes=VMEM_MOST),
        name="gate_stage",
    )(scanned, normed, own, others, gain, out_own, out_others, hidden, out_grad, valid)


def turn_kernel(x_ref, o_ref):
    o_ref[...] = x_ref[...].astype(f32).T


def turned(x, tile):
    rows, columns = x.shape
    return pl.pallas_call(
        turn_kernel,
        grid=(rows // tile,),
        in_specs=[pl.BlockSpec((tile, columns), lambda i: (i, 0))],
        out_specs=pl.BlockSpec((columns, tile), lambda i: (0, i)),
        out_shape=jax.ShapeDtypeStruct((columns, rows), f32),
        compiler_params=pltpu.CompilerParams(vmem_limit_bytes=VMEM),
        name="turned",
    )(x)


def project_kernel(n_ref, w_ref, v_ref, o_ref):
    total = mm(n_ref[0], w_ref[...], NT)
    for k in range(1, n_ref.shape[0]):
        total += mm(n_ref[k], v_ref[k - 1], NT)
    o_ref[...] = total.astype(o_ref.dtype)


def project(parts, own, others, first, count, tile, dtype):
    shards, rows, depth = parts.shape
    return pl.pallas_call(
        project_kernel,
        grid=(count // tile,),
        in_specs=[
            pl.BlockSpec((shards, rows, depth), lambda i: (0, 0, 0)),
            pl.BlockSpec((tile, depth), lambda i: (first // tile + i, 0)),
            pl.BlockSpec((shards - 1, tile, depth), lambda i: (0, first // tile + i, 0)),
        ],
        out_specs=pl.BlockSpec((rows, tile), lambda i: (0, i)),
        out_shape=jax.ShapeDtypeStruct((rows, count), dtype),
        compiler_params=pltpu.CompilerParams(vmem_limit_bytes=VMEM),
        name="project",
    )(parts, own, others)


def unproject_kernel(steps, d_ref, e_ref, w_ref, v_ref, o_ref):
    def add(ref):
        o_ref[0] += mm(ref[...], w_ref[...])
        for k in range(1, o_ref.shape[0]):
            o_ref[k] += mm(ref[...], v_ref[k - 1])

    @pl.when(pl.program_id(0) == 0)
    def _():
        o_ref[...] = jnp.zeros_like(o_ref)

    @pl.when(pl.program_id(0) < steps)
    def _():
        add(d_ref)

    @pl.when(pl.program_id(0) >= steps)
    def _():
        add(e_ref)


def unproject(d, e, own, others, tile):
    shards, count, depth = others.shape
    shards += 1
    rows = d.shape[0]
    steps = d.shape[1] // tile
    return pl.pallas_call(
        partial(unproject_kernel, steps),
        grid=(count // tile,),
        in_specs=[
            pl.BlockSpec((rows, tile), lambda i: (0, jnp.minimum(i, steps - 1))),
            pl.BlockSpec((rows, tile), lambda i: (0, jnp.maximum(i - steps, 0))),
            pl.BlockSpec((tile, depth), lambda i: (i, 0)),
            pl.BlockSpec((shards - 1, tile, depth), lambda i: (0, i, 0)),
        ],
        out_specs=pl.BlockSpec((shards, rows, depth), lambda i: (0, 0, 0)),
        out_shape=jax.ShapeDtypeStruct((shards, rows, depth), f32),
        compiler_params=pltpu.CompilerParams(vmem_limit_bytes=VMEM),
        name="unproject",
    )(d, e, own, others)


def rms_front(hidden_rows, gain):
    power = jnp.mean(hidden_rows * hidden_rows, axis=-1, keepdims=True)
    return hidden_rows * lax.rsqrt(power + epsilon) * gain


def conv_act(padded, conv_w, conv_b):
    taps = conv_w.shape[0]
    rows_out = padded.shape[1] - taps + 1
    total = conv_b + padded[:, 0:rows_out] * conv_w[0]
    for offset in range(1, taps):
        total = total + padded[:, offset : offset + rows_out] * conv_w[offset]
    return jax.nn.silu(total)


def gate_norm(values, gate_in, gain):
    gated = values * jax.nn.silu(gate_in)
    power = jnp.mean(gated * gated, axis=-1, keepdims=True)
    return gated * lax.rsqrt(power + epsilon) * gain


def local(
    hidden,
    lengths,
    out_grad,
    norm_gain,
    in_weight,
    conv_weight,
    conv_bias,
    dt_bias,
    a_log,
    skip_gain,
    gated_gain,
    out_weight,
):
    count = lax.axis_size("seq")
    shards = lax.axis_size("wshard")
    rank = lax.axis_index("seq")
    shard = lax.axis_index("wshard")
    micro, _, tokens, width = hidden.shape
    taps = conv_weight.shape[1]
    inner = out_weight.shape[0] * shards
    channels = conv_bias.shape[0] * shards
    heads = dt_bias.shape[0] * shards
    hs = inner // heads
    n = (channels - inner) // 2
    groups = heads // GROUP
    rows = micro * tokens
    fast = count == 8 and shards == 4 and micro == 2
    in_local = in_weight.T
    small = [norm_gain, conv_weight.T.reshape(-1), conv_bias, dt_bias, a_log, skip_gain, gated_gain]
    sizes = [v.shape[0] for v in small]
    small.append(in_local[inner + channels :].reshape(-1))
    packed_low = lax.all_gather(jnp.concatenate(small), "wshard", axis=0)
    packed = packed_low.astype(f32)
    parts, at = [], 0
    for size in sizes:
        parts.append(packed[:, at : at + size])
        at += size
    norm_g = parts[0].reshape(-1)
    conv_w = parts[1].reshape(shards, taps, -1).transpose(1, 0, 2).reshape(taps, -1)
    conv_b = parts[2].reshape(-1)
    dt_shift = parts[3].reshape(-1)
    rate = -jnp.exp(parts[4].reshape(-1))
    skip = parts[5].reshape(-1)
    gated_g = parts[6].reshape(-1)

    dt_w = packed_low[:, at:].reshape(shards, heads, -1).transpose(1, 0, 2).reshape(heads, -1)
    order = jnp.arange(shards) ^ shard
    if fast:
        conv_shards, gate_others, out_eighth = gather_input_weight(
            in_local, out_weight, inner, channels
        )
    else:
        every = lax.all_gather(in_local[: inner + channels], "wshard", axis=0)
        in_w = every[order[1:]]
        out_w = lax.all_gather(out_weight, "wshard", axis=0, tiled=True)

    def grouped(v):
        return v.reshape(micro, tokens, groups, GROUP).transpose(0, 2, 1, 3)

    rows_in = hidden.reshape(rows, width).astype(f32)
    cot = out_grad.reshape(rows, width).astype(f32)
    positions = rank * tokens + jnp.arange(tokens, dtype=jnp.int32)
    valid = (positions[None, :] < lengths[:, 0][:, None]).astype(f32).reshape(rows, 1)
    tile = 256
    skip_wide = jnp.repeat(skip, hs)[None, :]

    def to_lanes(v):
        return jnp.pad(v, ((0, 0),) * (v.ndim - 1) + ((0, LANES - heads),))

    if fast:
        hidden_rows, out_grad_rows = hidden.reshape(rows, width), out_grad.reshape(rows, width)
        dt_wide = jnp.pad(dt_w, ((0, LANES - heads), (0, 0)))
        conv_low, normed_low, raw = front(
            hidden_rows, norm_g[None, :], dt_wide, conv_shards, channels // 2
        )
        raw = raw.reshape(micro, tokens, LANES)
    else:
        normed, front_back = jax.vjp(rms_front, rows_in, norm_g)
        normed_low = normed.astype(bf16)
        normed_parts = normed_low.reshape(rows, shards, -1).transpose(1, 0, 2)[order]
        conv_low = project(normed_parts, in_local, in_w, inner, channels, tile, bf16)
        gate_in = project(normed_parts, in_local, in_w, 0, inner, tile, f32)
        dt_low = mm(normed_low, dt_w, NT).astype(bf16)
        dt_raw = dt_low.astype(f32).reshape(micro, tokens, heads) + dt_shift
    conv_low = conv_low.reshape(micro, tokens, channels)

    if fast:
        x_low, bc_low, y_scan, scanned_low, halo, s_in, out_others = scan_forward(
            conv_low,
            raw,
            conv_w,
            conv_b[None, :],
            to_lanes(dt_shift[None, :]),
            to_lanes(rate[None, :]),
            skip_wide,
            out_eighth,
            inner,
            hs,
            3,
        )
    else:
        prior = from_behind(conv_low[:, tokens - (taps - 1) :], "seq", 1)
        padded = jnp.concatenate([prior, conv_low], axis=1).astype(f32)
        mixed, conv_back = jax.vjp(conv_act, padded, conv_w, conv_b)
        dt = jax.nn.softplus(dt_raw)
        tri = (jnp.arange(tokens)[:, None] >= jnp.arange(tokens)[None, :]).astype(f32)
        cum = jnp.einsum("ij,mjh->mih", tri, dt * rate, precision=highest)
        dt_g, cum_g = grouped(dt), grouped(cum)
        row_g = cum_g.transpose(0, 1, 3, 2)
        last = cum[:, tokens - 1, :]
        decays = lax.all_gather(jnp.exp(last), "seq", axis=0)
        decay_w = grouped(jnp.exp(cum))
        x_low = mixed[..., :inner].astype(bf16)
        b_low = mixed[..., inner : inner + n].astype(bf16)
        c_low = mixed[..., inner + n :].astype(bf16)
        end_w = grouped(dt * jnp.exp(last[:, None, :] - cum))
        own_state = block_states(x_low, end_w, b_low.transpose(0, 2, 1), hs)
        y_local = local_scan(x_low, dt_g, cum_g, row_g, b_low, c_low, hs)
        s_in = running_states(own_state, decays, hs, True)
        y_scan, scanned_low = add_carry(x_low, y_local, cum_g, c_low, s_in, skip_wide, hs)

    if fast:
        normed_out_low, output, g, dy, d_gate_low, d_gated = gate_stage(
            scanned_low.reshape(rows, inner),
            normed_low,
            in_local,
            gate_others,
            gated_g[None, :],
            out_weight,
            out_others,
            hidden_rows,
            out_grad_rows,
            valid,
            256,
        )
        output = output.reshape(hidden.shape)
        dy = dy.reshape(micro, tokens, inner)
        d_gated = d_gated[0]
    else:
        scanned = scanned_low.reshape(rows, inner).astype(f32)
        normed_out, gate_back = jax.vjp(gate_norm, scanned, gate_in, gated_g)
        normed_out_low = normed_out.astype(bf16)
        branch = mm(normed_out_low, out_w)
        output = (rows_in + valid * branch).astype(bf16).reshape(hidden.shape)
        g = (cot * valid).astype(bf16)
        d_scanned, d_gate_in, d_gated = gate_back(mm(g, out_w, NT))
        dy = d_scanned.astype(bf16).reshape(micro, tokens, inner)
        d_gate_low = d_gate_in.astype(bf16)

    if fast:
        d_rest, d_conv_w, d_conv_b, by_head, gate_sum, normed_far = scan_backward(
            dy,
            x_low,
            bc_low,
            y_scan,
            s_in,
            raw,
            conv_low,
            halo,
            conv_w,
            conv_b[None, :],
            to_lanes(dt_shift[None, :]),
            to_lanes(rate[None, :]),
            skip_wide,
            d_gate_low,
            normed_low,
            hs,
            4,
        )
        d_dt_bias, d_a_log, d_skip = by_head[0, :heads], by_head[1, :heads], by_head[2, :heads]
        d_conv_b = d_conv_b[0]
        d_rest = d_rest.reshape(rows, -1)
        d_norm_g = jnp.zeros((width,), f32)
    else:
        own_grad = block_states(dy, decay_w, c_low.transpose(0, 2, 1), hs)
        dx_local, db_local, dc_local = local_back(x_low, dy, dt_g, cum_g, row_g, b_low, c_low, hs)
        ds = running_states(own_grad, decays, hs, False)
        dx_low, ddt_g, dcum_g, db, dc, last_term, dskip = carry_back(
            x_low, dy, dx_local, y_scan, dt_g, cum_g, b_low, s_in, ds, db_local, dc_local, skip_wide, hs
        )

        def ungrouped(v):
            return v.transpose(0, 2, 1, 3).reshape(micro, tokens, heads)

        at_end = jnp.sum(last_term.reshape(micro, heads, hs), axis=-1)[:, None, :]
        d_log = jnp.einsum("ij,mih->mjh", tri, ungrouped(dcum_g), precision=highest) + at_end
        d_dt = (ungrouped(ddt_g) + d_log * rate) * jax.nn.sigmoid(dt_raw)
        d_dt_bias = jnp.sum(d_dt, axis=(0, 1))
        d_a_log = jnp.sum(d_log * dt, axis=(0, 1)) * rate
        d_skip = jnp.sum(dskip.reshape(-1, heads, hs), axis=(0, 2))
        mixed_grad = jnp.concatenate([dx_low.astype(f32), db, dc], axis=2)
        d_padded, d_conv_w, d_conv_b = conv_back(mixed_grad)
        from_next = from_behind(d_padded[:, : taps - 1].astype(bf16), "seq", -1).astype(f32)
        d_conv = d_padded[:, taps - 1 :].at[:, tokens - (taps - 1) :].add(from_next)
        d_dt_low = d_dt.astype(bf16).reshape(rows, heads)
    total_cols = inner + channels + heads
    if not fast:
        d_rest = d_conv.astype(bf16).reshape(rows, channels)
        d_parts = unproject(d_gate_low, d_rest, in_local, in_w, tile)
        d_normed = d_parts[order].transpose(1, 0, 2).reshape(rows, width) + mm(d_dt_low, dt_w)
        d_hidden, d_norm_g = front_back(d_normed)
        input_grad = (d_hidden + cot).astype(bf16).reshape(hidden.shape)

    def summed(terms, axis):
        t = lax.psum_scatter(terms.astype(bf16), "seq", scatter_dimension=0, tiled=True)
        t = lax.psum_scatter(t, "wshard", scatter_dimension=axis, tiled=True)
        return lax.all_gather(t, "seq", axis=0, tiled=True).astype(f32)

    smalls = [
        d_norm_g.reshape(shards, -1),
        d_conv_w.reshape(taps, shards, -1).transpose(1, 0, 2).reshape(shards, -1),
        d_conv_b.reshape(shards, -1),
        d_dt_bias.reshape(shards, -1),
        d_a_log.reshape(shards, -1),
        d_skip.reshape(shards, -1),
        d_gated.reshape(shards, -1),
    ]
    smalls = jnp.concatenate(smalls, axis=1)
    if fast:
        smalls = jnp.pad(smalls, ((0, 0), (0, -smalls.shape[1] % 1024))).reshape(shards, -1, LANES)
        rest_sum, out_sum, sums, input_grad = weight_sums(
            d_gate_low,
            d_rest,
            normed_low,
            normed_far,
            g,
            normed_out_low,
            in_local,
            gate_others,
            conv_shards,
            smalls,
            d_rest[:, channels : channels + LANES],
            dt_wide,
            hidden_rows,
            norm_g[None, :],
            out_grad_rows,
            2,
        )
        input_grad = input_grad.reshape(hidden.shape)
        gate_sum = gate_sum.reshape(inner, -1)
        in_grad = jnp.concatenate([gate_sum, rest_sum[: total_cols - inner]]).astype(f32).T
        out_w_grad = turned(out_sum, 512)
        sums = sums.reshape(-1)
    else:
        d_proj = jnp.concatenate([d_gate_low, d_rest, d_dt_low], axis=1)
        in_grad = summed(mm(d_proj, normed_low, TN), 1).T
        out_terms = mm(normed_out_low, g, TN)
        blocks = out_terms.reshape(shards, count, -1, width).transpose(1, 0, 2, 3)
        out_w_grad = summed(blocks.reshape(inner, width), 0)
        sums = lax.psum(smalls, ("seq", "wshard"))
        sums = lax.dynamic_index_in_dim(sums, shard, 0, keepdims=False)
    found, at = [], 0
    for size in sizes:
        found.append(sums[at : at + size])
        at += size
    return (
        output,
        input_grad,
        found[0],
        in_grad,
        found[1].reshape(taps, -1).T,
        found[2],
        found[3],
        found[4],
        found[5],
        found[6],
        out_w_grad,
    )


def solution(mesh):
    return jax.shard_map(
        local,
        mesh=mesh,
        in_specs=(
            P(None, "wshard", "seq", None),
            P(None, "wshard"),
            P(None, "wshard", "seq", None),
            P("wshard"),
            P("wshard", None),
            P("wshard", None),
            P("wshard"),
            P("wshard"),
            P("wshard"),
            P("wshard"),
            P("wshard"),
            P("wshard", None),
        ),
        out_specs=(
            P(None, "wshard", "seq", None),
            P(None, "wshard", "seq", None),
            P("wshard"),
            P("wshard", None),
            P("wshard", None),
            P("wshard"),
            P("wshard"),
            P("wshard"),
            P("wshard"),
            P("wshard"),
            P("wshard", None),
        ),
        check_vma=False,
    )
```

```python
from functools import partial

import jax
import jax.numpy as jnp
from jax import lax
from jax.experimental import pallas as pl
from jax.experimental.pallas import tpu as pltpu
from jax.sharding import PartitionSpec as P

epsilon = 1e-05
highest = lax.Precision.HIGHEST
f32 = jnp.float32
bf16 = jnp.bfloat16
GROUP = 8
VMEM = 48 * 1024 * 1024
VMEM_MOST = 62 * 1024 * 1024

NN = (((1,), (0,)), ((), ()))
NT = (((1,), (1,)), ((), ()))
TN = (((0,), (0,)), ((), ()))


def mm(a, b, dims=NN):
    return lax.dot_general(a, b, dims, preferred_element_type=f32)


def params():
    return pltpu.CompilerParams(
        dimension_semantics=("arbitrary", "arbitrary"), vmem_limit_bytes=VMEM
    )


def widen(cols, head_size):
    t, heads = cols.shape
    lane = lax.broadcasted_iota(jnp.int32, (t, 2 * head_size), 1)
    parts = []
    for k in range(0, heads, 2):
        parts.append(jnp.where(lane < head_size, cols[:, k : k + 1], cols[:, k + 1 : k + 2]))
    return jnp.concatenate(parts, axis=1)


def state_kernel(hs, x_ref, w_ref, bt_ref, o_ref):
    weighted = (x_ref[0].astype(f32) * widen(w_ref[0, 0], hs)).astype(bf16)
    o_ref[0] = mm(bt_ref[0], weighted)


def block_states(x, weights, bt, hs):
    micro, t, cols = x.shape
    n = bt.shape[1]
    gc = GROUP * hs
    return pl.pallas_call(
        partial(state_kernel, hs),
        grid=(micro, cols // gc),
        in_specs=[
            pl.BlockSpec((1, t, gc), lambda m, g: (m, 0, g)),
            pl.BlockSpec((1, 1, t, GROUP), lambda m, g: (m, g, 0, 0)),
            pl.BlockSpec((1, n, t), lambda m, g: (m, 0, 0)),
        ],
        out_specs=pl.BlockSpec((1, n, gc), lambda m, g: (m, 0, g)),
        out_shape=jax.ShapeDtypeStruct((micro, n, cols), f32),
        compiler_params=params(),
        name="block_states",
    )(x, weights, bt)


def local_kernel(hs, x_ref, dt_ref, cum_ref, row_ref, b_ref, c_ref, o_ref, scores):
    t = x_ref.shape[1]
    half = t // 2

    @pl.when(pl.program_id(1) == 0)
    def _():
        s = mm(c_ref[0], b_ref[0], NT)
        i = lax.broadcasted_iota(jnp.int32, (t, t), 0)
        j = lax.broadcasted_iota(jnp.int32, (t, t), 1)
        scores[...] = jnp.where(i >= j, s, 0.0)

    cum, dt, rows = cum_ref[0, 0], dt_ref[0, 0], row_ref[0, 0]
    lane = lax.broadcasted_iota(jnp.int32, (half, 2 * hs), 1)
    weighted = (x_ref[0].astype(f32) * widen(dt, hs)).astype(bf16)
    for k in range(0, GROUP, 2):
        at = slice(k * hs, (k + 2) * hs)
        pair = weighted[:, at]
        top, low = [], []
        for h in (k, k + 1):
            col, row = cum[:, h : h + 1], rows[h : h + 1, :]
            m1 = jnp.exp(jnp.minimum(col[:half] - row[:, :half], 0.0)) * scores[:half, :half]
            m2 = jnp.exp(jnp.minimum(col[half:] - row, 0.0)) * scores[half:, :]
            top.append(mm(m1.astype(bf16), pair[:half]))
            low.append(mm(m2.astype(bf16), pair))
        o_ref[0, :half, at] = jnp.where(lane < hs, top[0], top[1])
        o_ref[0, half:, at] = jnp.where(lane < hs, low[0], low[1])


def local_scan(x, dt, cum, rows, b, c, hs):
    micro, t, cols = x.shape
    n = b.shape[2]
    gc = GROUP * hs
    return pl.pallas_call(
        partial(local_kernel, hs),
        grid=(micro, cols // gc),
        in_specs=[
            pl.BlockSpec((1, t, gc), lambda m, g: (m, 0, g)),
            pl.BlockSpec((1, 1, t, GROUP), lambda m, g: (m, g, 0, 0)),
            pl.BlockSpec((1, 1, t, GROUP), lambda m, g: (m, g, 0, 0)),
            pl.BlockSpec((1, 1, GROUP, t), lambda m, g: (m, g, 0, 0)),
            pl.BlockSpec((1, t, n), lambda m, g: (m, 0, 0)),
            pl.BlockSpec((1, t, n), lambda m, g: (m, 0, 0)),
        ],
        out_specs=pl.BlockSpec((1, t, gc), lambda m, g: (m, 0, g)),
        out_shape=jax.ShapeDtypeStruct((micro, t, cols), f32),
        scratch_shapes=[pltpu.VMEM((t, t), f32)],
        compiler_params=params(),
        name="local_scan",
    )(x, dt, cum, rows, b, c)


def carry_kernel(hs, x_ref, y_ref, cum_ref, c_ref, s_ref, skip_ref, scan_ref, low_ref):
    carried = mm(c_ref[0], s_ref[0].astype(bf16)) * widen(jnp.exp(cum_ref[0, 0]), hs)
    scan = y_ref[0] + carried
    scan_ref[0] = scan
    low_ref[0] = (scan + skip_ref[...] * x_ref[0].astype(f32)).astype(bf16)


def add_carry(x, y, cum, c, s_in, skip_wide, hs):
    micro, t, cols = x.shape
    n = c.shape[2]
    gc = GROUP * hs
    wide = pl.BlockSpec((1, t, gc), lambda m, g: (m, 0, g))
    return pl.pallas_call(
        partial(carry_kernel, hs),
        grid=(micro, cols // gc),
        in_specs=[
            wide,
            wide,
            pl.BlockSpec((1, 1, t, GROUP), lambda m, g: (m, g, 0, 0)),
            pl.BlockSpec((1, t, n), lambda m, g: (m, 0, 0)),
            pl.BlockSpec((1, n, gc), lambda m, g: (m, 0, g)),
            pl.BlockSpec((1, gc), lambda m, g: (0, g)),
        ],
        out_specs=[wide, wide],
        out_shape=[
            jax.ShapeDtypeStruct((micro, t, cols), f32),
            jax.ShapeDtypeStruct((micro, t, cols), bf16),
        ],
        compiler_params=params(),
        name="add_carry",
    )(x, y, cum, c, s_in, skip_wide)


def local_back_kernel(
    hs, x_ref, dy_ref, dt_ref, cum_ref, row_ref, b_ref, c_ref, dx_ref, db_ref, dc_ref, scores, total
):
    t = x_ref.shape[1]
    half = t // 2

    @pl.when(pl.program_id(1) == 0)
    def _():
        s = mm(b_ref[0], c_ref[0], NT)
        j = lax.broadcasted_iota(jnp.int32, (t, t), 0)
        i = lax.broadcasted_iota(jnp.int32, (t, t), 1)
        scores[...] = jnp.where(i >= j, s, 0.0)
        total[...] = jnp.zeros_like(total)

    cum, dt, rows = cum_ref[0, 0], dt_ref[0, 0], row_ref[0, 0]
    lane = lax.broadcasted_iota(jnp.int32, (t, 2 * hs), 1)
    lane_half = lax.broadcasted_iota(jnp.int32, (half, 2 * hs), 1)
    weighted = (x_ref[0].astype(f32) * widen(dt, hs)).astype(bf16)
    for k in range(0, GROUP, 2):
        at = slice(k * hs, (k + 2) * hs)
        pair = weighted[:, at]
        dy = dy_ref[0, :, at]
        top, low = [], []
        for h in (k, k + 1):
            col, row = cum[:, h : h + 1], rows[h : h + 1, :]
            mine = jnp.where(lane < hs, pair, 0) if h == k else jnp.where(lane < hs, 0, pair)
            l1 = jnp.exp(jnp.minimum(row - col[:half], 0.0))
            l2 = jnp.exp(jnp.minimum(row[:, half:] - col[half:], 0.0))
            total[:half, :] += l1 * mm(mine[:half], dy, NT)
            total[half:, half:] += l2 * mm(mine[half:], dy[half:], NT)
            top.append(mm((l1 * scores[:half, :]).astype(bf16), dy))
            low.append(mm((l2 * scores[half:, half:]).astype(bf16), dy[half:]))
        dx_ref[0, :half, at] = jnp.where(lane_half < hs, top[0], top[1])
        dx_ref[0, half:, at] = jnp.where(lane_half < hs, low[0], low[1])

    @pl.when(pl.program_id(1) == pl.num_programs(1) - 1)
    def _():
        j = lax.broadcasted_iota(jnp.int32, (t, t), 0)
        i = lax.broadcasted_iota(jnp.int32, (t, t), 1)
        d = jnp.where(i >= j, total[...], 0.0)
        db_ref[0] = mm(d.astype(bf16), c_ref[0])
        dc_ref[0] = mm(d.T.astype(bf16), b_ref[0])


def local_back(x, dy, dt, cum, rows, b, c, hs):
    micro, t, cols = x.shape
    n = b.shape[2]
    gc = GROUP * hs
    wide = pl.BlockSpec((1, t, gc), lambda m, g: (m, 0, g))
    small = pl.BlockSpec((1, 1, t, GROUP), lambda m, g: (m, g, 0, 0))
    state = pl.BlockSpec((1, t, n), lambda m, g: (m, 0, 0))
    return pl.pallas_call(
        partial(local_back_kernel, hs),
        grid=(micro, cols // gc),
        in_specs=[
            wide,
            wide,
            small,
            small,
            pl.BlockSpec((1, 1, GROUP, t), lambda m, g: (m, g, 0, 0)),
            state,
            state,
        ],
        out_specs=[wide, state, state],
        out_shape=[
            jax.ShapeDtypeStruct((micro, t, cols), f32),
            jax.ShapeDtypeStruct((micro, t, n), f32),
            jax.ShapeDtypeStruct((micro, t, n), f32),
        ],
        scratch_shapes=[pltpu.VMEM((t, t), f32), pltpu.VMEM((t, t), f32)],
        compiler_params=params(),
        name="local_back",
    )(x, dy, dt, cum, rows, b, c)


def head_sums(values, ones):
    high = values.astype(bf16)
    rest = (values - high.astype(f32)).astype(bf16)
    return mm(high, ones) + mm(rest, ones)


def carry_back_kernel(
    hs,
    x_ref,
    dy_ref,
    dxl_ref,
    y_ref,
    dt_ref,
    cum_ref,
    b_ref,
    si_ref,
    ds_ref,
    dbl_ref,
    dcl_ref,
    skip_ref,
    dx_ref,
    ddt_ref,
    dcum_ref,
    db_ref,
    dc_ref,
    last_ref,
    dskip_ref,
):
    t = x_ref.shape[1]
    gc = x_ref.shape[2]

    @pl.when(pl.program_id(1) == 0)
    def _():
        db_ref[0] = dbl_ref[0]
        dc_ref[0] = dcl_ref[0]

    cum, dt = cum_ref[0, 0], dt_ref[0, 0]
    x, dy = x_ref[0].astype(f32), dy_ref[0].astype(f32)
    dt_wide = widen(dt, hs)
    weighted = (x * dt_wide).astype(bf16).astype(f32)
    decay = widen(jnp.exp(cum), hs)
    to_end = widen(jnp.exp(cum[t - 1 :, :] - cum), hs)
    s_in, ds = si_ref[0].astype(f32), ds_ref[0]
    s_low, ds_low = s_in.astype(bf16), ds.astype(bf16)
    through = to_end * mm(b_ref[0], ds_low)
    d_weighted = dxl_ref[0] + through
    dx_ref[0] = (dt_wide * d_weighted + skip_ref[...] * dy).astype(bf16)
    db_ref[0] += mm((weighted * to_end).astype(bf16), ds_low, NT)
    dc_ref[0] += mm((dy * decay).astype(bf16), s_low, NT)
    r = lax.broadcasted_iota(jnp.int32, (gc, 128), 0)
    c = lax.broadcasted_iota(jnp.int32, (gc, 128), 1)
    ones = jnp.where(r // hs == c, 1.0, 0.0).astype(bf16)
    ddt_ref[0, 0] = head_sums(x * d_weighted, ones)[:, :GROUP]
    dcum_ref[0, 0] = head_sums(dy * y_ref[0] - weighted * d_weighted, ones)[:, :GROUP]
    last_decay = decay[t - 1 :, :]
    last_ref[0] = jnp.sum(weighted * through, axis=0, keepdims=True) + last_decay * jnp.sum(
        s_low.astype(f32) * ds, axis=0, keepdims=True
    )
    dskip_ref[0] = jnp.sum(x * dy, axis=0, keepdims=True)


def carry_back(x, dy, dxl, y, dt, cum, b, s_in, ds, dbl, dcl, skip_wide, hs):
    micro, t, cols = x.shape
    n = b.shape[2]
    gc = GROUP * hs
    groups = cols // gc
    wide = pl.BlockSpec((1, t, gc), lambda m, g: (m, 0, g))
    small = pl.BlockSpec((1, 1, t, GROUP), lambda m, g: (m, g, 0, 0))
    state = pl.BlockSpec((1, t, n), lambda m, g: (m, 0, 0))
    st = pl.BlockSpec((1, n, gc), lambda m, g: (m, 0, g))
    line = pl.BlockSpec((1, 1, gc), lambda m, g: (m, 0, g))
    return pl.pallas_call(
        partial(carry_back_kernel, hs),
        grid=(micro, groups),
        in_specs=[
            wide,
            wide,
            wide,
            wide,
            small,
            small,
            state,
            st,
            st,
            state,
            state,
            pl.BlockSpec((1, gc), lambda m, g: (0, g)),
        ],
        out_specs=[wide, small, small, state, state, line, line],
        out_shape=[
            jax.ShapeDtypeStruct((micro, t, cols), bf16),
            jax.ShapeDtypeStruct((micro, groups, t, GROUP), f32),
            jax.ShapeDtypeStruct((micro, groups, t, GROUP), f32),
            jax.ShapeDtypeStruct((micro, t, n), f32),
            jax.ShapeDtypeStruct((micro, t, n), f32),
            jax.ShapeDtypeStruct((micro, 1, cols), f32),
            jax.ShapeDtypeStruct((micro, 1, cols), f32),
        ],
        compiler_params=params(),
        name="carry_back",
    )(x, dy, dxl, y, dt, cum, b, s_in, ds, dbl, dcl, skip_wide)


def from_behind(x, axis, by):
    count = lax.axis_size(axis)
    pairs = [(i, i + by) for i in range(count) if 0 <= i + by < count]
    return lax.ppermute(x, axis, pairs)


def swap(x, by):
    count = lax.axis_size("seq")
    return lax.ppermute(x, "seq", [(i, i ^ by) for i in range(count)])


def running_states(terms, decays, hs, forward):
    count = lax.axis_size("seq")
    rank = lax.axis_index("seq")
    index = jnp.arange(count)

    def product(mask):
        d = jnp.prod(jnp.where(mask[:, None, None], decays, 1.0), axis=0)
        return jnp.repeat(d, hs, axis=1)[:, None, :]

    total, before = terms, jnp.zeros_like(terms)
    size = 1
    while size < count:
        other = swap(total.astype(bf16), size).astype(f32)
        mine = index // size == rank // size
        theirs = index // size == (rank // size) ^ 1
        later = (rank // size) % 2 == (1 if forward else 0)
        passed = mine & ((index < rank) if forward else (index > rank))
        before = before + jnp.where(later, product(passed), 0.0) * other
        if 2 * size < count:
            total = total * jnp.where(later, 1.0, product(theirs)) + other * jnp.where(
                later, product(mine), 1.0
            )
        size *= 2
    return before


MESH = pl.DeviceIdType.MESH


def around():
    s, z = lax.axis_index("seq"), lax.axis_index("wshard")
    c, x, y = s % 2, (s // 2) % 2, s // 4
    near = {
        "c": (s + 1 - 2 * c, z),
        "x": (s + 2 - 4 * x, z),
        "y": (s + 4 - 8 * y, z),
        "z1": (s, z + 1 - 2 * (z % 2)),
        "z2": (s, z + 2 - 4 * (z // 2)),
        "z3": (s, 3 - z),
    }
    return s, z, c, x, y, near


def greet(near):
    barrier = pltpu.get_barrier_semaphore()
    for where in near.values():
        pl.semaphore_signal(barrier, inc=1, device_id=where, device_id_type=MESH)
    pl.semaphore_wait(barrier, len(near))


CHUNK_DMAS = 10
AHEAD = 3


def split_rows(piece, parts):
    tiles = piece // 16
    return [16 * (tiles * (i + 1) // parts - tiles * i // parts) for i in range(parts)]


class Gather:
    def __init__(self, place, items, send, recv, own=None):
        s, z, c, x, y, near = place
        sx, sy, sd = s + 2 - 4 * x, s + 4 - 8 * y, s + 6 - 4 * x - 8 * y
        self.plans = []
        for source, base, target, count, parts in items:
            off = 0
            for i, size in enumerate(split_rows(count // 8, parts)):
                q = len(self.plans)

                def rows(who, first=0, off=off, size=size, piece=count // 8):
                    return pl.ds(pl.multiple_of(first + who * piece + off, 16), size)

                def move(src, dst, kind, to, q=q):
                    return pltpu.make_async_remote_copy(
                        src_ref=src,
                        dst_ref=dst,
                        send_sem=send.at[q, kind],
                        recv_sem=recv.at[q, kind],
                        device_id=near[to],
                        device_id_type=MESH,
                    )

                def along(who, kind, to, move=move, rows=rows, target=target):
                    block = target.at[pl.ds(0, 3), rows(who)]
                    return move(block, block, kind, to)

                plan = {"fetched": base is None}
                if base is None:
                    have = source.at[:, pl.ds(off, size)]
                    block = target.at[pl.ds(0, 3), rows(s)]
                    plan["own"] = pltpu.make_async_copy(have, block, own.at[q])
                    for kind, name in ((3, "x"), (4, "y"), (6, "c0")):
                        plan[name] = move(have, block, kind, name[0])
                else:
                    for k in (1, 2, 3):
                        there = target.at[k - 1, rows(s)]
                        plan["z%d" % k] = move(source.at[rows(s, base)], there, k - 1, "z%d" % k)
                    plan["x"] = along(s, 3, "x")
                    plan["y"] = along(s, 4, "y")
                    plan["c0"] = along(s, 6, "c")
                first = "xy"[i % 2]
                plan["d"] = along(sx, 5, "y") if first == "x" else along(sy, 5, "x")
                plan["cx"] = along(sx, 7, "c")
                plan["cy"] = along(sy, 8, "c")
                plan["cd"] = along(sd, 9, "c")
                plan["order"] = first, "yx"[i % 2]
                self.plans.append(plan)
                off += size

    def fetch(self, i):
        for k in (1, 2, 3):
            self.plans[i]["z%d" % k].start()

    def begin(self, i):
        plan = self.plans[i]
        if plan["fetched"]:
            plan["own"].start()
        else:
            for k in (1, 2, 3):
                plan["z%d" % k].wait_recv()
        for name in ("x", "y", "c0"):
            plan[name].start()

    def middle(self, i):
        plan = self.plans[i]
        one, two = plan["order"]
        plan[one].wait_recv()
        plan["d"].start()
        plan["c" + one].start()
        plan[two].wait_recv()
        plan["c" + two].start()

    def finish(self, i):
        self.plans[i]["d"].wait_recv()
        self.plans[i]["cd"].start()

    def run(self, last):
        n = len(self.plans)
        for i in range(min(AHEAD, n)):
            self.fetch(i)
        for i in range(n + 2):
            if i < n:
                self.begin(i)
                if i + AHEAD < n:
                    self.fetch(i + AHEAD)
                if i + AHEAD == n - 1:
                    last()
            if 0 <= i - 1 < n:
                self.middle(i - 1)
            if 0 <= i - 2 < n:
                self.finish(i - 2)

    def close(self):
        for plan in self.plans:
            for name in ("c0", "cx", "cy", "cd"):
                plan[name].wait_recv()
            for name in ("z1", "z2", "z3", "x", "y", "d", "c0", "cx", "cy", "cd"):
                if name in plan:
                    plan[name].wait_send()
            if plan["fetched"]:
                plan["own"].wait()


def gather_kernel(
    inner,
    channels,
    parts,
    w_ref,
    ow_ref,
    small_ref,
    conv_ref,
    gate_ref,
    eighth_ref,
    dt_ref,
    small_out,
    own,
    own_dt,
    own_sem,
    dt_sem,
    send,
    recv,
    o_send,
    o_recv,
    d_send,
    d_recv,
    p_send,
    p_recv,
):
    place = around()
    dt_rows = w_ref.at[pl.ds(inner + channels, dt_ref.shape[1])]
    dt_inward = pltpu.make_async_copy(dt_rows, own_dt, dt_sem)
    dt_inward.start()
    steps = [
        pltpu.make_async_remote_copy(
            src_ref=dt_rows,
            dst_ref=dt_ref.at[k - 1],
            send_sem=d_send.at[k - 1],
            recv_sem=d_recv.at[k - 1],
            device_id=place[-1]["z%d" % k],
            device_id_type=MESH,
        )
        for k in (1, 2, 3)
    ]
    steps += [
        pltpu.make_async_remote_copy(
            src_ref=small_ref,
            dst_ref=small_out.at[k - 1],
            send_sem=p_send.at[k - 1],
            recv_sem=p_recv.at[k - 1],
            device_id=place[-1]["z%d" % k],
            device_id_type=MESH,
        )
        for k in (1, 2, 3)
    ]
    small_out[3] = small_ref[...]
    inward = pltpu.make_async_copy(w_ref.at[pl.ds(inner, channels)], own, own_sem)
    inward.start()
    greet(place[-1])
    for copy in steps:
        copy.start()
    items = [(w_ref, inner, conv_ref, channels, parts), (w_ref, 0, gate_ref, inner, parts)]
    work = Gather(place, items, send, recv)
    piece = eighth_ref.shape[1]
    mine = pl.ds(pl.multiple_of(place[0] * piece, 16), piece)
    eighths = [
        pltpu.make_async_remote_copy(
            src_ref=ow_ref.at[mine],
            dst_ref=eighth_ref.at[k - 1],
            send_sem=o_send.at[k - 1],
            recv_sem=o_recv.at[k - 1],
            device_id=place[-1]["z%d" % k],
            device_id_type=MESH,
        )
        for k in (1, 2, 3)
    ]

    def last():
        for copy in eighths:
            copy.start()

    work.run(last)
    inward.wait()
    dt_inward.wait()
    dt_outward = pltpu.make_async_copy(own_dt, dt_ref.at[3], dt_sem)
    dt_outward.start()
    outward = pltpu.make_async_copy(own, conv_ref.at[3], own_sem)
    outward.start()
    work.close()
    for copy in eighths + steps:
        copy.wait()
    outward.wait()
    dt_outward.wait()


def gather_input_weight(w_t, out_weight, small, inner, channels, parts=6):
    width = w_t.shape[1]
    hbm = pl.BlockSpec(memory_space=pl.ANY)
    vmem = pl.BlockSpec(memory_space=pltpu.VMEM)
    return pl.pallas_call(
        partial(gather_kernel, inner, channels, parts),
        in_specs=[hbm] * 2 + [vmem],
        out_specs=[hbm] * 4 + [vmem],
        out_shape=[
            jax.ShapeDtypeStruct((4, channels, width), bf16),
            jax.ShapeDtypeStruct((3, inner, width), bf16),
            jax.ShapeDtypeStruct((3, out_weight.shape[0] // 8, out_weight.shape[1]), bf16),
            jax.ShapeDtypeStruct((4, w_t.shape[0] - inner - channels, width), bf16),
            jax.ShapeDtypeStruct((4,) + small.shape, bf16),
        ],
        scratch_shapes=[
            pltpu.VMEM((channels, width), bf16),
            pltpu.VMEM((w_t.shape[0] - inner - channels, width), bf16),
            pltpu.SemaphoreType.DMA,
            pltpu.SemaphoreType.DMA,
            pltpu.SemaphoreType.DMA((2 * parts, CHUNK_DMAS)),
            pltpu.SemaphoreType.DMA((2 * parts, CHUNK_DMAS)),
            pltpu.SemaphoreType.DMA((3,)),
            pltpu.SemaphoreType.DMA((3,)),
            pltpu.SemaphoreType.DMA((3,)),
            pltpu.SemaphoreType.DMA((3,)),
            pltpu.SemaphoreType.DMA((3,)),
            pltpu.SemaphoreType.DMA((3,)),
        ],
        compiler_params=pltpu.CompilerParams(
            collective_id=1, has_side_effects=True, vmem_limit_bytes=VMEM_MOST
        ),
        cost_estimate=pl.CostEstimate(flops=0, bytes_accessed=200_000_000, transcendentals=0),
        name="gather_input_weight",
    )(w_t, out_weight, small)


class Here:
    def __init__(self, copy):
        self.start, self.wait_recv = copy.start, copy.wait

    def wait_send(self):
        pass


STAGE = 2


class Products:
    IN = 4
    SCRATCH = 22

    @staticmethod
    def sizes(a_list, b):
        rows = b.shape[0]
        wide = sum(a.shape[1] for a in a_list) // 2
        return rows, wide, b.shape[1], wide // 128

    @staticmethod
    def marks(chunks):
        return sorted({0, chunks * 2 // 5, chunks * 7 // 10, chunks * 9 // 10, chunks})

    @staticmethod
    def out_shape(a_list, b):
        _, _, width, chunks = Products.sizes(a_list, b)
        return jax.ShapeDtypeStruct((2, chunks, 2, 2, 2, 16, width // 4), bf16)

    @staticmethod
    def scratch(a_list, b):
        rows, wide, width, chunks = Products.sizes(a_list, b)
        dma = pltpu.SemaphoreType.DMA
        n = Products.IN
        marks = Products.marks(chunks)
        return [
            pltpu.VMEM((2 * rows, wide), bf16),
            pltpu.VMEM((2 * rows, width), bf16),
            pltpu.VMEM((4, 128, width), f32),
            pltpu.VMEM((2, 32, width), bf16),
            pltpu.VMEM((2, 32, width), bf16),
            pltpu.VMEM((2, 16, width), bf16),
            pltpu.VMEM((2, 16, width), bf16),
            pltpu.VMEM((2, 2, 16, width), bf16),
            pltpu.VMEM((2, 16, width), f32),
            pltpu.VMEM((2, 16, width), f32),
            pltpu.VMEM((2, 2, 16, width), f32),
            pltpu.VMEM((chunks, 32, width), bf16),
            pltpu.VMEM((chunks, 32, width), bf16),
            pltpu.VMEM((chunks, 16, width), bf16),
            pltpu.VMEM((chunks, 16, width), bf16),
            pltpu.VMEM((chunks, 3, 2, 16, width // 4), bf16),
            dma((n,)),
            dma((n,)),
            dma((n,)),
            dma((7, 2)),
            dma((7, chunks)),
            dma((2, len(marks) - 1, 8)),
        ]

    def __init__(self, place, a_refs, b_ref, out, scratch, b_far=None):
        self.s, self.z, self.c, self.x, self.y, self.near = place
        (
            self.a,
            self.b,
            self.g,
            self.sa1,
            self.sb1,
            self.sa2,
            self.sb2,
            self.s3,
            self.ka2,
            self.kb2,
            self.f3,
            self.ra1,
            self.rb1,
            self.ra2,
            self.rb2,
            self.rz,
            self.in_sem,
            self.s_in,
            self.r_in,
            self.s_step,
            self.r_step,
            self.sems_all,
        ) = scratch
        self.out = out
        self.shard = self.rz.shape[-1]
        self.chunks = self.ra1.shape[0]
        marks = Products.marks(self.chunks)
        self.groups = list(zip(marks[:-1], marks[1:]))
        c = self.c
        rows = self.a.shape[0] // 2
        near, far = pl.ds(0, rows), pl.ds(rows, rows)
        self.operands = []
        to = self.b.at[far]
        if b_far is None:
            there = self.remote(b_ref, to, self.s_in.at[0], self.r_in.at[0], "c")
        else:
            there = Here(pltpu.make_async_copy(b_far, to, self.s_in.at[0]))
        self.operands.append(
            (0, pltpu.make_async_copy(b_ref, self.b.at[near], self.in_sem.at[0]), there)
        )
        at = 0
        for i, ref in enumerate(a_refs):
            half = ref.shape[1] // 2
            here = ref.at[:, pl.ds(pl.multiple_of(c * half, 128), half)]
            there = ref.at[:, pl.ds(pl.multiple_of((1 - c) * half, 128), half)]
            to = pl.ds(at, half)
            self.operands.append(
                (
                    at // 128,
                    pltpu.make_async_copy(here, self.a.at[near, to], self.in_sem.at[i + 1]),
                    self.remote(there, self.a.at[far, to], self.s_in.at[i + 1], self.r_in.at[i + 1], "c"),
                )
            )
            at += half

    def remote(self, src, dst, ss, rs, to):
        return pltpu.make_async_remote_copy(
            src_ref=src,
            dst_ref=dst,
            send_sem=ss,
            recv_sem=rs,
            device_id=self.near[to],
            device_id_type=MESH,
        )

    def load(self):
        for _, here, _ in self.operands:
            here.start()

    def share(self):
        for _, _, there in self.operands:
            there.start()

    def step_copy(self, kind, u):
        slot = u % 2
        ss, rs = self.s_step.at[kind, slot], self.r_step.at[kind, u]
        if kind < 4:
            src, dst, to = (
                (self.sa1, self.ra1, "x"),
                (self.sb1, self.rb1, "y"),
                (self.sa2, self.ra2, "y"),
                (self.sb2, self.rb2, "x"),
            )[kind]
            return self.remote(src.at[slot], dst.at[u], ss, rs, to)
        k = kind - 3
        z = self.z
        other = (z + 1 - 2 * (z % 2), z + 2 - 4 * (z // 2), 3 - z)[k - 1]
        cols = pl.ds(pl.multiple_of(other * self.shard, 128), self.shard)
        return self.remote(self.s3.at[slot, :, :, cols], self.rz.at[u, k - 1], ss, rs, "z%d" % k)

    def all_copy(self, q, kind):
        a, b = self.groups[q]
        ts = pl.ds(a, b - a)
        x, y, c = self.x, self.y, self.c
        px = 1 - x if kind in (3, 5, 7) else x
        py = 1 - y if kind in (4, 6, 7) else y
        if kind in (3, 4):
            block = self.out.at[c, ts, kind - 3, px, py]
        else:
            block = self.out.at[c, ts, :, px, py]
        to = ("x", "y", "c", "y", "x", "c", "c", "c")[kind]
        return self.remote(block, block, self.sems_all.at[0, q, kind], self.sems_all.at[1, q, kind], to)

    def step(self, t):
        x, y, z, c = self.x, self.y, self.z, self.c
        g, ra1, rb1 = self.g, self.ra1, self.rb1
        chunks = self.chunks
        copy = self.step_copy

        def sl(at, size=16):
            return pl.ds(pl.multiple_of(at, 16), size)

        def free(kind, u):
            @pl.when(u >= 2)
            def _():
                copy(kind, u - 2).wait_send()

        @pl.when((t >= 3 * STAGE) & (t - 3 * STAGE < chunks))
        def _():
            u = t - 3 * STAGE
            slot = u % 2
            for k in (4, 5, 6):
                copy(k, u).wait_recv()
            mine = pl.ds(pl.multiple_of(z * self.shard, 128), self.shard)
            for part in (0, 1):
                total = self.f3[slot, part, :, mine]
                for k in range(3):
                    total = total + self.rz[u, k, part].astype(f32)
                self.out[c, u, part, x, y] = total.astype(bf16)

        for q, (_, b) in enumerate(self.groups):

            @pl.when(t == b - 1 + 3 * STAGE)
            def _(q=q):
                for kind in (0, 1, 2):
                    self.all_copy(q, kind).start()

            @pl.when(t == b - 1 + 4 * STAGE)
            def _(q=q):
                self.all_copy(q, 0).wait_recv()
                self.all_copy(q, 3).start()
                self.all_copy(q, 5).start()
                self.all_copy(q, 1).wait_recv()
                self.all_copy(q, 4).start()
                self.all_copy(q, 6).start()

            @pl.when(t == b - 1 + 5 * STAGE)
            def _(q=q):
                self.all_copy(q, 3).wait_recv()
                self.all_copy(q, 4).wait_recv()
                self.all_copy(q, 7).start()

        @pl.when((t >= 2 * STAGE) & (t - 2 * STAGE < chunks))
        def _():
            u = t - 2 * STAGE
            slot = u % 2
            copy(2, u).wait_recv()
            copy(3, u).wait_recv()
            for k in (4, 5, 6):
                free(k, u)
            va = self.ka2[slot] + self.ra2[u].astype(f32)
            vb = self.kb2[slot] + self.rb2[u].astype(f32)
            self.f3[slot, 0] = va
            self.f3[slot, 1] = vb
            self.s3[slot, 0] = va.astype(bf16)
            self.s3[slot, 1] = vb.astype(bf16)
            for k in (4, 5, 6):
                copy(k, u).start()

        @pl.when((t >= STAGE) & (t - STAGE < chunks))
        def _():
            u = t - STAGE
            slot, then = u % 2, u % 4
            copy(0, u).wait_recv()
            free(2, u)
            self.sa2[slot] = (
                g[then, sl(x * 32 + (1 - y) * 16)] + ra1[u, sl((1 - y) * 16)].astype(f32)
            ).astype(bf16)
            copy(2, u).start()
            self.ka2[slot] = g[then, sl(x * 32 + y * 16)] + ra1[u, sl(y * 16)].astype(f32)
            copy(1, u).wait_recv()
            free(3, u)
            self.sb2[slot] = (
                g[then, sl(64 + (1 - x) * 32 + y * 16)] + rb1[u, sl((1 - x) * 16)].astype(f32)
            ).astype(bf16)
            copy(3, u).start()
            self.kb2[slot] = g[then, sl(64 + x * 32 + y * 16)] + rb1[u, sl(x * 16)].astype(f32)

        @pl.when(t < chunks)
        def _():
            for first, here, there in self.operands:

                @pl.when(t == first)
                def _(here=here, there=there):
                    here.wait()
                    there.wait_recv()

            slot, now = t % 2, t % 4

            @pl.when(slot == 0)
            def _():
                cols = pl.ds(pl.multiple_of(t * 128, 256), 256)
                both = mm(self.a[:, cols], self.b[...], TN)
                g[now] = both[:128]
                g[now + 1] = both[128:]

            free(0, t)
            free(1, t)
            self.sa1[slot] = g[now, sl((1 - x) * 32, 32)].astype(bf16)
            copy(0, t).start()
            self.sb1[slot, 0:16] = g[now, sl(64 + (1 - y) * 16)].astype(bf16)
            self.sb1[slot, 16:32] = g[now, sl(96 + (1 - y) * 16)].astype(bf16)
            copy(1, t).start()

    def steps(self):
        return self.chunks + 5 * STAGE

    def close(self):
        for q in range(len(self.groups)):
            for kind in (2, 5, 6, 7):
                self.all_copy(q, kind).wait_recv()
            for kind in range(8):
                self.all_copy(q, kind).wait_send()
        for u in (self.chunks - 2, self.chunks - 1):
            for kind in range(7):
                self.step_copy(kind, u).wait_send()
        for _, _, there in self.operands:
            there.wait_send()


class Smalls:
    SCRATCH = 5

    @staticmethod
    def scratch(v):
        dma = pltpu.SemaphoreType.DMA
        return [
            pltpu.VMEM((3,) + v.shape, f32),
            pltpu.VMEM((3,) + v.shape, f32),
            pltpu.VMEM((3,) + v.shape[1:], f32),
            dma((6,)),
            dma((6,)),
        ]

    def __init__(self, place, v_ref, out, scratch):
        self.s, self.z, self.c, self.x, self.y, self.near = place
        self.v, self.out = v_ref, out
        self.total, self.got, self.got_z, self.send, self.recv = scratch

    def copy(self, kind):
        if kind < 3:
            src = self.v if kind == 0 else self.total.at[kind - 1]
            dst, to = self.got.at[kind], "cxy"[kind]
        else:
            z = self.z
            k = kind - 2
            other = (z + 1 - 2 * (z % 2), z + 2 - 4 * (z // 2), 3 - z)[k - 1]
            src, dst, to = self.total.at[2, other], self.got_z.at[k - 1], "z%d" % k
        return pltpu.make_async_remote_copy(
            src_ref=src,
            dst_ref=dst,
            send_sem=self.send.at[kind],
            recv_sem=self.recv.at[kind],
            device_id=self.near[to],
            device_id_type=MESH,
        )

    def start(self):
        self.copy(0).start()

    def advance(self, kind):
        self.copy(kind).wait_recv()
        mine = self.v[...] if kind == 0 else self.total[kind - 1]
        self.total[kind] = mine + self.got[kind]
        for k in (kind + 1,) if kind < 2 else (3, 4, 5):
            self.copy(k).start()

    def close(self):
        total = self.total[2, self.z]
        for k in (3, 4, 5):
            self.copy(k).wait_recv()
            total = total + self.got_z[k - 3]
        self.out[...] = total
        for k in range(6):
            self.copy(k).wait_send()


class InputGrad:
    TILE = 256
    SCRATCH = 7

    @staticmethod
    def scratch(rows, width):
        tile = InputGrad.TILE
        return [
            pltpu.VMEM((rows, width), f32),
            pltpu.VMEM((128, width), f32),
            pltpu.VMEM((2, rows, tile), bf16),
            pltpu.VMEM((2, 4, tile, width // 4), bf16),
            pltpu.SemaphoreType.DMA((3, 2)),
            pltpu.VMEM((rows, LANES), bf16),
            pltpu.SemaphoreType.DMA,
        ]

    def __init__(self, refs, out, gain_out, scratch):
        (
            self.gate,
            self.rest,
            self.own,
            self.gate_others,
            self.conv_shards,
            self.dt_w,
            self.h,
            self.gain,
            self.og,
        ) = refs
        self.out, self.gain_out = out, gain_out
        self.acc, self.part, self.d, self.w, self.sems, self.d_dt, self.dt_sem = scratch
        self.early = self.gate.shape[1] // self.TILE
        self.count = self.early + self.conv_shards.shape[1] // self.TILE

    def copies(self, i, gate):
        slot = i % 2
        at = pl.ds(pl.multiple_of((i if gate else i - self.early) * self.TILE, self.TILE), self.TILE)
        if gate:
            pairs = (
                (self.gate.at[:, at], self.d.at[slot]),
                (self.own.at[at], self.w.at[slot, 3]),
                (self.gate_others.at[:, at], self.w.at[slot, pl.ds(0, 3)]),
            )
        else:
            pairs = (
                (self.rest.at[:, at], self.d.at[slot]),
                (self.conv_shards.at[3, at], self.w.at[slot, 3]),
                (self.conv_shards.at[pl.ds(0, 3), at], self.w.at[slot, pl.ds(0, 3)]),
            )
        return [pltpu.make_async_copy(a, b, self.sems.at[k, slot]) for k, (a, b) in enumerate(pairs)]

    def act(self, i, what):
        @pl.when(i < self.early)
        def _():
            for copy in self.copies(i, True):
                getattr(copy, what)()

        @pl.when((i >= self.early) & (i < self.count))
        def _():
            for copy in self.copies(i, False):
                getattr(copy, what)()

    def start(self):
        self.acc[...] = jnp.zeros_like(self.acc)
        self.act(0, "start")
        self.dt_copy = pltpu.make_async_copy(
            self.rest.at[:, pl.ds(self.conv_shards.shape[1], LANES)], self.d_dt, self.dt_sem
        )
        self.dt_copy.start()

    def step(self, i):
        @pl.when(i < self.count)
        def _():
            self.act(i + 1, "start")
            self.act(i, "wait")
            slot = i % 2
            weights = jnp.concatenate([self.w[slot, k] for k in (3, 0, 1, 2)], axis=1)
            self.acc[...] += mm(self.d[slot], weights)

    def close(self):
        depth = self.w.shape[3]
        tile = self.part.shape[0]
        gain = self.gain[...]
        self.dt_copy.wait()
        heads = self.dt_w.shape[1]
        dt_w = jnp.concatenate([self.dt_w[k] for k in (3, 0, 1, 2)], axis=1)

        def body(r, d_gain):
            at = pl.ds(pl.multiple_of(r * tile, tile), tile)
            whole = self.acc[at, :] + mm(self.d_dt[at, :][:, :heads], dt_w)
            for k in range(4):
                self.part[:, shard_place(k, depth)] = whole[:, k * depth : (k + 1) * depth]
            d = self.part[...]
            h = self.h[at, :].astype(f32)
            scale = lax.rsqrt(jnp.mean(h * h, axis=-1, keepdims=True) + epsilon)
            d_gain = d_gain + jnp.sum(d * (h * scale), axis=0, keepdims=True)
            d = d * gain
            along = jnp.mean(d * h, axis=-1, keepdims=True) * (scale * scale * scale)
            self.out[at, :] = (scale * d - h * along + self.og[at, :].astype(f32)).astype(bf16)
            return d_gain

        d_gain = lax.fori_loop(0, self.out.shape[0] // tile, body, jnp.zeros(gain.shape, f32))
        for a in range(4):
            for r in range(depth // LANES):
                at = a * depth + r * LANES
                self.gain_out[a, r : r + 1, :] = d_gain[:, at : at + LANES]


def sums_kernel(
    gate_ref,
    rest_ref,
    nm_ref,
    far_ref,
    og_ref,
    no_ref,
    own_ref,
    gate_others_ref,
    conv_shards_ref,
    v_ref,
    dt_w_ref,
    h_ref,
    gain_ref,
    cot_ref,
    in_out,
    out_out,
    v_out,
    input_out,
    small_v,
    *scratch,
):
    place = around()
    cut = Products.SCRATCH
    inp = Products(place, [rest_ref], nm_ref, in_out, scratch[:cut], far_ref)
    outp = Products(place, [og_ref], no_ref, out_out, scratch[cut : 2 * cut])
    small = Smalls(place, small_v, v_out, scratch[2 * cut : 2 * cut + Smalls.SCRATCH])
    back = InputGrad(
        [
            gate_ref,
            rest_ref,
            own_ref,
            gate_others_ref,
            conv_shards_ref,
            dt_w_ref,
            h_ref,
            gain_ref,
            cot_ref,
        ],
        input_out,
        small_v,
        scratch[2 * cut + Smalls.SCRATCH :],
    )
    inp.load()
    outp.load()
    back.start()
    small_v[...] = v_ref[...]
    greet(place[-1])
    inp.share()
    outp.share()
    each = -(-back.count // (inp.chunks - 1))

    def first(t, carry):
        inp.step(t)

        def tile(i, carry):
            back.step(t * each + i)
            return carry

        lax.fori_loop(0, each, tile, 0)
        return carry

    lax.fori_loop(0, inp.chunks, first, 0)
    back.close()
    small.start()

    def second(t, carry):
        outp.step(t)

        @pl.when(t < inp.steps() - inp.chunks)
        def _():
            inp.step(t + inp.chunks)

        for kind in range(3):

            @pl.when(t == kind + 1)
            def _(kind=kind):
                small.advance(kind)

        return carry

    lax.fori_loop(0, outp.steps(), second, 0)
    small.close()
    inp.close()
    outp.close()


def weight_sums(
    d_gate,
    d_rest,
    nm,
    nm_far,
    og,
    no,
    own,
    gate_others,
    conv_shards,
    v,
    dt_w,
    hidden,
    gain,
    out_grad,
    collective_id,
):
    vmem = pl.BlockSpec(memory_space=pltpu.VMEM)
    hbm = pl.BlockSpec(memory_space=pl.ANY)
    rows, width = hidden.shape
    a_in, a_out, total, input_grad = pl.pallas_call(
        sums_kernel,
        in_specs=[hbm] * 9 + [vmem] * 5,
        out_specs=[vmem] * 4,
        out_shape=[
            Products.out_shape([d_rest], nm),
            Products.out_shape([og], no),
            jax.ShapeDtypeStruct(v.shape[1:], f32),
            jax.ShapeDtypeStruct((rows, width), bf16),
        ],
        scratch_shapes=[pltpu.VMEM(v.shape, f32)]
        + Products.scratch([d_rest], nm)
        + Products.scratch([og], no)
        + Smalls.scratch(v)
        + InputGrad.scratch(rows, width),
        compiler_params=pltpu.CompilerParams(
            collective_id=collective_id, has_side_effects=True, vmem_limit_bytes=VMEM_MOST
        ),
        cost_estimate=pl.CostEstimate(
            flops=12 * rows * width * 6000, bytes_accessed=400_000_000, transcendentals=0
        ),
        name="weight_sums",
    )(
        d_gate,
        d_rest,
        nm,
        nm_far,
        og,
        no,
        own,
        gate_others,
        conv_shards,
        v,
        dt_w,
        hidden,
        gain,
        out_grad,
    )
    return a_in.reshape(d_rest.shape[1], -1), a_out.reshape(og.shape[1], -1), total, input_grad


LANES = 128
HALO = 16


def sigmoid(v):
    return 0.5 + 0.5 * jnp.tanh(0.5 * v)


def silu_parts(v):
    s = sigmoid(v)
    return v * s, s


def softplus(v):
    return jnp.maximum(v, 0.0) + jnp.log1p(jnp.exp(-jnp.abs(v)))


def lower_ones(t):
    i = lax.broadcasted_iota(jnp.int32, (t, t), 0)
    j = lax.broadcasted_iota(jnp.int32, (t, t), 1)
    return jnp.where(i >= j, 1.0, 0.0)


def exact(a, b, dims=NN):
    return lax.dot_general(a, b, dims, precision=highest, preferred_element_type=f32)


def head_columns(values, g):
    return pltpu.roll(values, (LANES - GROUP * g) % LANES, 1)[:, :GROUP]


class Exchange:
    def __init__(self, forward, own_low, got, t_low, t_got, u_low, u_got, p_low, p_got, send, recv):
        self.s, self.z, self.c, self.x, self.y, self.near = around()
        later = (lambda v: v) if forward else (lambda v: 1 - v)
        self.second = (later(self.c) == 1, later(self.x) == 1, later(self.y) == 1)
        self.own_low, self.got = own_low, got
        self.t_low, self.t_got, self.u_low, self.u_got = t_low, t_got, u_low, u_got
        self.p_low, self.p_got = p_low, p_got
        self.send, self.recv = send, recv
        self.n = t_low.shape[1] - 16
        self.half = t_low.shape[2]
        self.mine = pl.ds(pl.multiple_of(self.c * self.half, LANES), self.half)
        self.other = pl.ds(pl.multiple_of((1 - self.c) * self.half, LANES), self.half)

    def copy(self, kind, m):
        src, dst, to = (
            (self.own_low, self.got, "c"),
            (self.t_low, self.t_got, "x"),
            (self.u_low, self.u_got, "y"),
            (self.p_low, self.p_got, "c"),
        )[kind]
        return pltpu.make_async_remote_copy(
            src_ref=src.at[m],
            dst_ref=dst.at[m],
            send_sem=self.send.at[kind, m],
            recv_sem=self.recv.at[kind, m],
            device_id=self.near[to],
            device_id_type=MESH,
        )

    def put_decay(self, ref, m, lanes, decay):
        high = decay.astype(bf16).astype(f32)
        row = lax.broadcasted_iota(jnp.int32, (16, decay.shape[1]), 0)
        both = jnp.where(row == 0, high, jnp.where(row == 1, decay - high, 0.0))
        ref[m, pl.ds(self.n, 16), lanes] = both.astype(bf16)

    def decay_of(self, ref, m, lanes):
        rows = ref[m, pl.ds(self.n, 16), lanes].astype(f32)
        return rows[0:1] + rows[1:2]

    def put_own(self, m, lanes, state, decay):
        self.own_low[m, pl.ds(0, self.n), lanes] = state.astype(bf16)
        self.put_decay(self.own_low, m, lanes, decay)

    def core(self, m):
        self.copy(0, m).start()

    def along_x(self, m):
        self.copy(0, m).wait_recv()
        second = self.second[0]
        mine = self.own_low[m, pl.ds(0, self.n), self.mine].astype(f32)
        theirs = self.got[m, pl.ds(0, self.n), self.mine].astype(f32)
        d_mine = self.decay_of(self.own_low, m, self.mine)
        d_theirs = self.decay_of(self.got, m, self.mine)
        total = theirs * jnp.where(second, d_mine, 1.0) + mine * jnp.where(second, 1.0, d_theirs)
        self.t_low[m, pl.ds(0, self.n), :] = total.astype(bf16)
        self.put_decay(self.t_low, m, pl.ds(0, self.half), d_mine * d_theirs)
        self.copy(1, m).start()

    def along_y(self, m):
        self.copy(1, m).wait_recv()
        second = self.second[1]
        every = pl.ds(0, self.half)
        mine = self.t_low[m, pl.ds(0, self.n), :].astype(f32)
        theirs = self.t_got[m, pl.ds(0, self.n), :].astype(f32)
        d_mine = self.decay_of(self.t_low, m, every)
        d_theirs = self.decay_of(self.t_got, m, every)
        total = theirs * jnp.where(second, d_mine, 1.0) + mine * jnp.where(second, 1.0, d_theirs)
        self.u_low[m] = total.astype(bf16)
        self.copy(2, m).start()

    def back_to_core(self, m):
        self.copy(2, m).wait_recv()
        every = pl.ds(0, self.half)
        x_second = jnp.where(self.second[1], 1.0, 0.0)
        y_second = jnp.where(self.second[2], 1.0, 0.0)
        theirs = self.t_got[m, pl.ds(0, self.n), :].astype(f32)
        d_theirs = self.decay_of(self.t_got, m, every)
        over = y_second * jnp.where(self.second[1], d_theirs, 1.0)
        before = x_second * theirs + over * self.u_got[m].astype(f32)
        self.p_low[m] = before.astype(bf16)
        self.copy(3, m).start()

    def begin_state(self, m, out):
        self.copy(3, m).wait_recv()
        second = jnp.where(self.second[0], 1.0, 0.0)
        for lanes, before in (
            (self.mine, self.p_low[m].astype(f32)),
            (self.other, self.p_got[m].astype(f32)),
        ):
            d_theirs = self.decay_of(self.got, m, lanes)
            theirs = self.got[m, pl.ds(0, self.n), lanes].astype(f32)
            over = jnp.where(self.second[0], d_theirs, 1.0)
            out[m, :, lanes] = (before * over + second * theirs).astype(bf16)

    def sent(self):
        for m in range(self.own_low.shape[0]):
            for kind in range(4):
                self.copy(kind, m).wait_send()


def exchange_scratch(micro, n, inner):
    half = inner // 2
    dma = pltpu.SemaphoreType.DMA
    return [
        pltpu.VMEM((micro, n + 16, inner), bf16),
        pltpu.VMEM((micro, n + 16, inner), bf16),
        pltpu.VMEM((micro, n + 16, half), bf16),
        pltpu.VMEM((micro, n + 16, half), bf16),
        pltpu.VMEM((micro, n, half), bf16),
        pltpu.VMEM((micro, n, half), bf16),
        pltpu.VMEM((micro, n, half), bf16),
        pltpu.VMEM((micro, n, half), bf16),
        dma((4, micro)),
        dma((4, micro)),
    ]


EXCHANGE = 10
TICKS = (6, 3, 2, 2)


def steps_of(raw, shift, rate):
    t = raw.shape[0]
    dt = softplus(raw + shift)
    cum = exact(lower_ones(t), dt * rate)
    return dt, cum


def conv_rows(buf, cw, cb):
    taps = cw.shape[0]
    t = buf.shape[0] - HALO
    total = cb + buf[HALO - taps + 1 : HALO - taps + 1 + t, :] * cw[0:1]
    for k in range(1, taps):
        at = HALO - taps + 1 + k
        total = total + buf[at : at + t, :] * cw[k : k + 1]
    return total


def scan_forward_kernel(
    hs,
    conv_ref,
    raw_ref,
    cw_ref,
    cb_ref,
    shift_ref,
    rate_ref,
    skip_ref,
    eighth_ref,
    x_ref,
    bc_ref,
    y_ref,
    low_ref,
    halo,
    begin_ref,
    others_ref,
    *scratch,
):
    buf, wide_buf, scores, dts, cums, rows_t, h_send, h_recv, o_send, o_recv, o_own = scratch[EXCHANGE:]
    ex = Exchange(True, *scratch[:EXCHANGE])
    s, z = ex.s, ex.z
    micro, t, channels = conv_ref.shape
    inner = x_ref.shape[2]
    n = begin_ref.shape[1]
    gc = GROUP * hs
    groups = inner // gc
    half_t = t // 2
    place = around()
    near = {k: ex.near[k] for k in ("c", "x", "y")}
    near["next"] = ((s + 1) % 8, z)
    near["last"] = ((s + 7) % 8, z)
    greet(near)
    weight = Gather(
        place, [(eighth_ref, None, others_ref, others_ref.shape[1], 2)], o_send, o_recv, o_own
    )

    tail = [
        pltpu.make_async_remote_copy(
            src_ref=conv_ref.at[m, pl.ds(t - HALO, HALO)],
            dst_ref=halo.at[m],
            send_sem=h_send.at[m],
            recv_sem=h_recv.at[m],
            device_id=near["next"],
            device_id_type=MESH,
        )
        for m in range(micro)
    ]
    for copy in tail:
        copy.start()
    weight.begin(0)
    for m in range(micro):
        dt, cum = steps_of(raw_ref[m], shift_ref[...], rate_ref[...])
        dts[m] = dt
        cums[m] = cum
        rows_t[m] = cum.T
    for copy in tail:
        copy.wait_recv()
    has_prior = jnp.where(s > 0, 1.0, 0.0)

    def activate(m, lanes, into):
        into[0:HALO] = halo[m, :, lanes].astype(f32) * has_prior
        into[pl.ds(HALO, t)] = conv_ref[m, :, lanes].astype(f32)
        return silu_parts(conv_rows(into, cw_ref[:, lanes], cb_ref[:, lanes]))[0]

    def own_states(m, a, b):
        def body(g, carry):
            lanes = pl.ds(pl.multiple_of(g * gc, gc), gc)
            x = activate(m, lanes, buf).astype(bf16)
            x_ref[m, :, lanes] = x
            cum = head_columns(cums[m], g)
            to_end = head_columns(dts[m], g) * jnp.exp(cum[t - 1 :] - cum)
            weighted = (x.astype(f32) * widen(to_end, hs)).astype(bf16)
            state = mm(bc_ref[m, :, 0:n], weighted, TN)
            ex.put_own(m, lanes, state, widen(jnp.exp(cum[t - 1 :]), hs))
            return carry

        lax.fori_loop(a, b, body, 0)

    def local_scans(m, a, b):
        lane = lax.broadcasted_iota(jnp.int32, (half_t, 2 * hs), 1)

        def body(g, carry):
            lanes = pl.ds(pl.multiple_of(g * gc, gc), gc)
            cum = head_columns(cums[m], g)
            rows = rows_t[m, pl.ds(pl.multiple_of(g * GROUP, GROUP), GROUP), :]
            dt_wide = widen(head_columns(dts[m], g), hs)
            weighted = (x_ref[m, :, lanes].astype(f32) * dt_wide).astype(bf16)
            for k in range(0, GROUP, 2):
                pair = weighted[:, k * hs : (k + 2) * hs]
                at = pl.ds(pl.multiple_of(g * gc + k * hs, 2 * hs), 2 * hs)
                top, low = [], []
                for h in (k, k + 1):
                    col, row = cum[:, h : h + 1], rows[h : h + 1, :]
                    m1 = jnp.exp(jnp.minimum(col[:half_t] - row[:, :half_t], 0.0))
                    m2 = jnp.exp(jnp.minimum(col[half_t:] - row, 0.0))
                    m1 = (m1 * scores[m, :half_t, :half_t]).astype(bf16)
                    m2 = (m2 * scores[m, half_t:, :]).astype(bf16)
                    top.append(mm(m1, pair[:half_t]))
                    low.append(mm(m2, pair))
                y_ref[m, :half_t, at] = jnp.where(lane < hs, top[0], top[1])
                y_ref[m, half_t:, at] = jnp.where(lane < hs, low[0], low[1])
            return carry

        lax.fori_loop(a, b, body, 0)

    def carried(m):
        def body(g, carry):
            lanes = pl.ds(pl.multiple_of(g * gc, gc), gc)
            decay = widen(jnp.exp(head_columns(cums[m], g)), hs)
            scan = y_ref[m, :, lanes] + decay * mm(bc_ref[m, :, n:], begin_ref[m, :, lanes])
            y_ref[m, :, lanes] = scan
            x = x_ref[m, :, lanes].astype(f32)
            low_ref[m, :, lanes] = (scan + skip_ref[:, lanes] * x).astype(bf16)
            return carry

        lax.fori_loop(0, groups, body, 0)

    for m in range(micro):
        lanes = pl.ds(inner, channels - inner)
        bc = activate(m, lanes, wide_buf).astype(bf16)
        bc_ref[m] = bc
        scores[m] = mm(bc[:, n:], bc[:, :n], NT) * lower_ones(t)
    middle = groups // 2
    own_states(0, 0, groups)
    ex.core(0)
    own_states(1, 0, middle)
    ex.along_x(0)
    own_states(1, middle, groups)
    ex.core(1)
    weight.begin(1)
    local_scans(0, 0, middle)
    ex.along_x(1)
    ex.along_y(0)
    local_scans(0, middle, groups)
    weight.middle(0)
    local_scans(1, 0, middle)
    ex.along_y(1)
    weight.middle(1)
    weight.finish(0)
    ex.back_to_core(0)
    local_scans(1, middle, groups)
    ex.begin_state(0, begin_ref)
    carried(0)
    weight.finish(1)
    ex.back_to_core(1)
    ex.begin_state(1, begin_ref)
    carried(1)
    weight.close()
    ex.sent()
    for copy in tail:
        copy.wait_send()


def scan_forward(
    conv_low, raw, conv_w, conv_b, shift, rate, skip_wide, out_eighth, inner, hs, collective_id
):
    micro, t, channels = conv_low.shape
    n = (channels - inner) // 2
    gc = GROUP * hs
    dma = pltpu.SemaphoreType.DMA
    vmem = pl.BlockSpec(memory_space=pltpu.VMEM)
    hbm = pl.BlockSpec(memory_space=pl.ANY)
    return pl.pallas_call(
        partial(scan_forward_kernel, hs),
        in_specs=[vmem] * 8,
        out_specs=[vmem] * 6 + [hbm],
        out_shape=[
            jax.ShapeDtypeStruct((micro, t, inner), bf16),
            jax.ShapeDtypeStruct((micro, t, 2 * n), bf16),
            jax.ShapeDtypeStruct((micro, t, inner), f32),
            jax.ShapeDtypeStruct((micro, t, inner), bf16),
            jax.ShapeDtypeStruct((micro, HALO, channels), bf16),
            jax.ShapeDtypeStruct((micro, n, inner), bf16),
            jax.ShapeDtypeStruct((3, 8 * out_eighth.shape[1], out_eighth.shape[2]), bf16),
        ],
        scratch_shapes=exchange_scratch(micro, n, inner)
        + [
            pltpu.VMEM((HALO + t, gc), f32),
            pltpu.VMEM((HALO + t, 2 * n), f32),
            pltpu.VMEM((micro, t, t), f32),
            pltpu.VMEM((micro, t, LANES), f32),
            pltpu.VMEM((micro, t, LANES), f32),
            pltpu.VMEM((micro, LANES, t), f32),
            dma((micro,)),
            dma((micro,)),
            dma((2, CHUNK_DMAS)),
            dma((2, CHUNK_DMAS)),
            dma((2,)),
        ],
        compiler_params=pltpu.CompilerParams(
            collective_id=collective_id, has_side_effects=True, vmem_limit_bytes=VMEM_MOST
        ),
        cost_estimate=pl.CostEstimate(
            flops=4 * micro * t * inner * (t + 3 * n), bytes_accessed=100_000_000, transcendentals=0
        ),
        name="scan_forward",
    )(conv_low, raw, conv_w, conv_b, shift, rate, skip_wide, out_eighth)


def scan_backward_kernel(
    hs,
    dy_ref,
    x_ref,
    bc_ref,
    y_ref,
    begin_ref,
    raw_ref,
    conv_ref,
    halo_ref,
    cw_ref,
    cb_ref,
    shift_ref,
    rate_ref,
    skip_ref,
    dgate_ref,
    norm_ref,
    dconv_ref,
    dcw_ref,
    dcb_ref,
    heads_ref,
    sum_ref,
    far_ref,
    far_sem,
    *scratch,
):
    (
        y_now,
        y_sem,
        buf,
        wide_buf,
        scores,
        total,
        dts,
        cums,
        rows_t,
        ends,
        dxl,
        dbc,
        ddt_sum,
        dcum_sum,
        last_sum,
        head_low,
        next_low,
        h_send,
        h_recv,
    ) = scratch[EXCHANGE : EXCHANGE + 19]
    ex = Exchange(False, *scratch[:EXCHANGE])
    s, z = ex.s, ex.z
    micro, t, channels = conv_ref.shape
    inner = x_ref.shape[2]
    n = begin_ref.shape[1]
    gc = GROUP * hs
    groups = inner // gc
    half = t // 2
    taps = cw_ref.shape[0]
    place = around()
    near = dict(place[-1])
    near["next"] = ((s + 1) % 8, z)
    near["last"] = ((s + 7) % 8, z)
    sums_of = Products(place, [dgate_ref], norm_ref, sum_ref, scratch[EXCHANGE + 19 :])
    sums_of.load()

    def y_copy(i):
        lanes = pl.ds(pl.multiple_of((i % groups) * gc, gc), gc)
        slot = i % 2
        return pltpu.make_async_copy(y_ref.at[i // groups, :, lanes], y_now.at[slot], y_sem.at[slot])

    greet(near)
    sums_of.share()
    first_rows = [
        pltpu.make_async_remote_copy(
            src_ref=head_low.at[m],
            dst_ref=next_low.at[m],
            send_sem=h_send.at[m],
            recv_sem=h_recv.at[m],
            device_id=near["last"],
            device_id_type=MESH,
        )
        for m in range(micro)
    ]
    has_prior = jnp.where(s > 0, 1.0, 0.0)
    has_next = jnp.where(s < 7, 1.0, 0.0)

    middle = groups // 2

    def at_step(i, *todo):
        for when, what in todo:
            pl.when(i == when)(what)

    def own_states():
        def body(i, carry):
            m, g = i // groups, i % groups
            lanes = pl.ds(pl.multiple_of(g * gc, gc), gc)
            cum = head_columns(cums[m], g)
            weighted = (dy_ref[m, :, lanes].astype(f32) * widen(jnp.exp(cum), hs)).astype(bf16)
            state = mm(bc_ref[m, :, n:], weighted, TN)
            ex.put_own(m, lanes, state, widen(jnp.exp(cum[t - 1 :]), hs))
            at_step(
                i,
                (groups - 1, lambda: ex.core(0)),
                (groups + middle, lambda: ex.along_x(0)),
                (2 * groups - 1, lambda: ex.core(1)),
            )
            tick(i, TICKS[0], 0)
            return carry

        lax.fori_loop(0, 2 * groups, body, 0)

    def tick(i, every, first):
        @pl.when(i % every == every - 1)
        def _():
            sums_of.step(first + i // every)

    def upper_ones():
        j = lax.broadcasted_iota(jnp.int32, (t, t), 0)
        i = lax.broadcasted_iota(jnp.int32, (t, t), 1)
        return jnp.where(i >= j, 1.0, 0.0)

    def local_terms():
        lane = lax.broadcasted_iota(jnp.int32, (t, 2 * hs), 1)
        lane_half = lax.broadcasted_iota(jnp.int32, (half, 2 * hs), 1)

        def body(i, carry):
            m, g = i // groups, i % groups
            lanes = pl.ds(pl.multiple_of(g * gc, gc), gc)
            cum = head_columns(cums[m], g)
            rows = rows_t[m, pl.ds(pl.multiple_of(g * GROUP, GROUP), GROUP), :]
            dt_wide = widen(head_columns(dts[m], g), hs)
            weighted = (x_ref[m, :, lanes].astype(f32) * dt_wide).astype(bf16)
            for k in range(0, GROUP, 2):
                pair = weighted[:, k * hs : (k + 2) * hs]
                at = pl.ds(pl.multiple_of(g * gc + k * hs, 2 * hs), 2 * hs)
                dy = dy_ref[m, :, at]
                top, low = [], []
                for h in (k, k + 1):
                    col, row = cum[:, h : h + 1], rows[h : h + 1, :]
                    mine = jnp.where(lane < hs, pair, 0) if h == k else jnp.where(lane < hs, 0, pair)
                    l1 = jnp.exp(jnp.minimum(row - col[:half], 0.0))
                    l2 = jnp.exp(jnp.minimum(row[:, half:] - col[half:], 0.0))
                    total[:half, :] += l1 * mm(mine[:half], dy, NT)
                    total[half:, half:] += l2 * mm(mine[half:], dy[half:], NT)
                    top.append(mm((l1 * scores[m, :half, :]).astype(bf16), dy))
                    low.append(mm((l2 * scores[m, half:, half:]).astype(bf16), dy[half:]))
                dxl[m, :half, at] = jnp.where(lane_half < hs, top[0], top[1])
                dxl[m, half:, at] = jnp.where(lane_half < hs, low[0], low[1])
            at_step(
                i,
                (1, lambda: ex.along_x(1)),
                (3, lambda: ex.along_y(0)),
                (groups - 1, lambda: local_close(0)),
                (groups + 1, lambda: ex.along_y(1)),
                (groups + 3, lambda: ex.back_to_core(0)),
                (2 * groups - 1, lambda: local_close(1)),
            )
            tick(i, TICKS[1], 2 * groups // TICKS[0])
            return carry

        lax.fori_loop(0, 2 * groups, body, 0)

    def local_close(m):
        d = total[...] * upper_ones()
        dbc[m, :, 0:n] = mm(d.astype(bf16), bc_ref[m, :, n:])
        dbc[m, :, n:] = mm(d.T.astype(bf16), bc_ref[m, :, :n])
        total[...] = jnp.zeros_like(total)

    def through_states():
        r = lax.broadcasted_iota(jnp.int32, (gc, LANES), 0)
        col = lax.broadcasted_iota(jnp.int32, (gc, LANES), 1)

        def clear():
            ddt_sum[...] = jnp.zeros_like(ddt_sum)
            dcum_sum[...] = jnp.zeros_like(dcum_sum)
            last_sum[...] = jnp.zeros_like(last_sum)

        def close(m):
            d_log = exact(upper_ones(), dcum_sum[...]) + last_sum[0:1]
            v = raw_ref[m] + shift_ref[...]
            d_dt = (ddt_sum[...] + d_log * rate_ref[...]) / (1.0 + jnp.exp(-v))
            rest = dconv_ref.shape[2] - channels - LANES
            dconv_ref[m, :, pl.ds(channels, LANES)] = d_dt.astype(bf16)
            if rest:
                dconv_ref[m, :, pl.ds(channels + LANES, rest)] = jnp.zeros((t, rest), bf16)
            heads_ref[0:1] += jnp.sum(d_dt, axis=0, keepdims=True)
            heads_ref[1:2] += jnp.sum(d_log * dts[m], axis=0, keepdims=True) * rate_ref[...]
            first_slopes(m)
            if m == 0:
                clear()
                ex.begin_state(1, ends)

        def body(i, carry):
            m, g = i // groups, i % groups
            lanes = pl.ds(pl.multiple_of(g * gc, gc), gc)

            @pl.when(i + 1 < 2 * groups)
            def _():
                y_copy(i + 1).start()

            y_copy(i).wait()
            ones = jnp.where(r // hs + g * GROUP == col, 1.0, 0.0).astype(bf16)
            cum = head_columns(cums[m], g)
            dt_wide = widen(head_columns(dts[m], g), hs)
            x, dy = x_ref[m, :, lanes].astype(f32), dy_ref[m, :, lanes].astype(f32)
            weighted = (x * dt_wide).astype(bf16).astype(f32)
            decay = widen(jnp.exp(cum), hs)
            to_end = widen(jnp.exp(cum[t - 1 :] - cum), hs)
            s_in, ds = begin_ref[m, :, lanes], ends[m, :, lanes]
            through = to_end * mm(bc_ref[m, :, 0:n], ds)
            d_weighted = dxl[m, :, lanes] + through
            dconv_ref[m, :, lanes] = (dt_wide * d_weighted + skip_ref[:, lanes] * dy).astype(bf16)
            dbc[m, :, 0:n] += mm((weighted * to_end).astype(bf16), ds, NT)
            dbc[m, :, n:] += mm((dy * decay).astype(bf16), s_in, NT)
            ddt_sum[...] += head_sums(x * d_weighted, ones)
            dcum_sum[...] += head_sums(dy * y_now[i % 2] - weighted * d_weighted, ones)
            at_end = jnp.sum(weighted * through, axis=0, keepdims=True) + decay[t - 1 :] * jnp.sum(
                s_in.astype(f32) * ds.astype(f32), axis=0, keepdims=True
            )
            last_sum[...] += head_sums(jnp.broadcast_to(at_end, (8, gc)), ones)
            by_skip = jnp.sum(x * dy, axis=0, keepdims=True)
            heads_ref[2:3] += head_sums(jnp.broadcast_to(by_skip, (8, gc)), ones)[0:1]
            at_step(i, (groups - 1, lambda: close(0)), (2 * groups - 1, lambda: close(1)))
            tick(i, TICKS[2], 2 * groups // TICKS[0] + 2 * groups // TICKS[1])
            return carry

        clear()
        heads_ref[...] = jnp.zeros_like(heads_ref)
        y_copy(0).start()
        lax.fori_loop(0, 2 * groups, body, 0)

    def pre_slope(into, lanes, grad, rows):
        v = conv_rows(into[0 : HALO + rows, :], cw_ref[:, lanes], cb_ref[:, lanes])
        sig = sigmoid(v)
        return grad * (sig * (1.0 + v * (1.0 - sig)))

    def load(m, lanes, into, rows):
        into[0:HALO] = halo_ref[m, :, lanes].astype(f32) * has_prior
        into[HALO : HALO + rows] = conv_ref[m, 0:rows, lanes].astype(f32)

    def first_slopes(m):
        def one(lanes, into, grad):
            load(m, lanes, into, HALO)
            head_low[m, :, lanes] = pre_slope(into, lanes, grad, HALO).astype(bf16)

        def body(g, carry):
            lanes = pl.ds(pl.multiple_of(g * gc, gc), gc)
            one(lanes, buf, dconv_ref[m, 0:HALO, lanes].astype(f32))
            return carry

        lax.fori_loop(0, groups, body, 0)
        one(pl.ds(inner, channels - inner), wide_buf, dbc[m, 0:HALO, :])
        first_rows[m].start()

    def conv_back():
        def one(m, lanes, into, grad):
            load(m, lanes, into, t)
            slope = pre_slope(into, lanes, grad, t)
            weights = cw_ref[:, lanes]
            lines = []
            for k in range(taps):
                at = HALO - taps + 1 + k
                lines.append(jnp.sum(slope * into[at : at + t, :], axis=0, keepdims=True))
            dcw_ref[:, lanes] += jnp.concatenate(lines, axis=0)
            dcb_ref[:, lanes] += jnp.sum(slope, axis=0, keepdims=True)
            into[0:t] = slope
            into[t : t + HALO] = next_low[m, :, lanes].astype(f32) * has_next
            back = into[taps - 1 : taps - 1 + t, :] * weights[0:1]
            for k in range(1, taps):
                at = taps - 1 - k
                back = back + into[at : at + t, :] * weights[k : k + 1]
            dconv_ref[m, :, lanes] = back.astype(bf16)

        def body(i, carry):
            m, g = i // groups, i % groups
            lanes = pl.ds(pl.multiple_of(g * gc, gc), gc)
            one(m, lanes, buf, dconv_ref[m, :, lanes].astype(f32))
            at_step(i, (groups - 1, lambda: first_rows[1].wait_recv()))
            tick(i, TICKS[3], 2 * groups // TICKS[0] + 2 * groups // TICKS[1] + 2 * groups // TICKS[2])
            return carry

        first_rows[0].wait_recv()
        lax.fori_loop(0, 2 * groups, body, 0)
        for m in range(micro):
            one(m, pl.ds(inner, channels - inner), wide_buf, dbc[m])

    for m in range(micro):
        dt, cum = steps_of(raw_ref[m], shift_ref[...], rate_ref[...])
        dts[m] = dt
        cums[m] = cum
        rows_t[m] = cum.T
        scores[m] = mm(bc_ref[m, :, 0:n], bc_ref[m, :, n:], NT) * upper_ones()
    dcw_ref[...] = jnp.zeros_like(dcw_ref)
    dcb_ref[...] = jnp.zeros_like(dcb_ref)
    total[...] = jnp.zeros_like(total)
    own_states()
    local_terms()
    ex.begin_state(0, ends)
    ex.back_to_core(1)
    through_states()
    conv_back()
    done = sum(2 * groups // every for every in TICKS)

    def rest_of(i, carry):
        sums_of.step(i)
        return carry

    rows = far_ref.shape[0]
    far = pltpu.make_async_copy(sums_of.b.at[pl.ds(rows, rows)], far_ref, far_sem)
    far.start()
    lax.fori_loop(done, sums_of.steps(), rest_of, 0)
    far.wait()
    ex.sent()
    for copy in first_rows:
        copy.wait_send()
    sums_of.close()


def scan_backward(
    dy,
    x,
    bc,
    y,
    begin,
    raw,
    conv_low,
    halo,
    conv_w,
    conv_b,
    shift,
    rate,
    skip_wide,
    d_gate,
    normed,
    hs,
    collective_id,
):
    micro, t, channels = conv_low.shape
    inner = x.shape[2]
    n = begin.shape[1]
    gc = GROUP * hs
    taps = conv_w.shape[0]
    dma = pltpu.SemaphoreType.DMA
    vmem = pl.BlockSpec(memory_space=pltpu.VMEM)
    hbm = pl.BlockSpec(memory_space=pl.ANY)
    return pl.pallas_call(
        partial(scan_backward_kernel, hs),
        in_specs=[vmem] * 3 + [hbm] + [vmem] * 9 + [hbm] * 2,
        out_specs=[vmem] * 5 + [hbm],
        out_shape=[
            jax.ShapeDtypeStruct((micro, t, -(-(channels + LANES) // 256) * 256), bf16),
            jax.ShapeDtypeStruct((taps, channels), f32),
            jax.ShapeDtypeStruct((1, channels), f32),
            jax.ShapeDtypeStruct((8, LANES), f32),
            Products.out_shape([d_gate], normed),
            jax.ShapeDtypeStruct(normed.shape, bf16),
        ],
        scratch_shapes=[dma]
        + exchange_scratch(micro, n, inner)
        + [
            pltpu.VMEM((2, t, gc), f32),
            dma((2,)),
            pltpu.VMEM((HALO + t, gc), f32),
            pltpu.VMEM((HALO + t, 2 * n), f32),
            pltpu.VMEM((micro, t, t), f32),
            pltpu.VMEM((t, t), f32),
            pltpu.VMEM((micro, t, LANES), f32),
            pltpu.VMEM((micro, t, LANES), f32),
            pltpu.VMEM((micro, LANES, t), f32),
            pltpu.VMEM((micro, n, inner), bf16),
            pltpu.VMEM((micro, t, inner), f32),
            pltpu.VMEM((micro, t, 2 * n), f32),
            pltpu.VMEM((t, LANES), f32),
            pltpu.VMEM((t, LANES), f32),
            pltpu.VMEM((8, LANES), f32),
            pltpu.VMEM((micro, HALO, channels), bf16),
            pltpu.VMEM((micro, HALO, channels), bf16),
            dma((micro,)),
            dma((micro,)),
        ]
        + Products.scratch([d_gate], normed),
        compiler_params=pltpu.CompilerParams(
            collective_id=collective_id, has_side_effects=True, vmem_limit_bytes=VMEM_MOST
        ),
        cost_estimate=pl.CostEstimate(
            flops=8 * micro * t * inner * (t + 3 * n), bytes_accessed=100_000_000, transcendentals=0
        ),
        name="scan_backward",
    )(
        dy,
        x,
        bc,
        y,
        begin,
        raw,
        conv_low,
        halo,
        conv_w,
        conv_b,
        shift,
        rate,
        skip_wide,
        d_gate,
        normed,
    )


def shard_place(k, depth):
    z = lax.axis_index("wshard")
    other = (z, z + 1 - 2 * (z % 2), z + 2 - 4 * (z // 2), 3 - z)[k]
    return pl.ds(pl.multiple_of(other * depth, 128), depth)


def front_kernel(h_ref, g_ref, dtw_ref, v_ref, conv_ref, norm_ref, raw_ref, rel):
    depth = v_ref.shape[2]

    @pl.when(pl.program_id(0) == 0)
    def _():
        h = h_ref[...].astype(f32)
        power = jnp.mean(h * h, axis=-1, keepdims=True)
        normed = (h * lax.rsqrt(power + epsilon) * g_ref[...]).astype(bf16)
        norm_ref[...] = normed
        for k in range(4):
            rel[:, k * depth : (k + 1) * depth] = norm_ref[:, shard_place(k, depth)]
        heads = dtw_ref.shape[1]
        steps = mm(rel[...], jnp.concatenate([dtw_ref[k] for k in (3, 0, 1, 2)], axis=1), NT)
        raw_ref[...] = jnp.zeros_like(raw_ref)
        raw_ref[:, 0:heads] = steps.astype(bf16).astype(f32)

    weights = jnp.concatenate([v_ref[k] for k in (3, 0, 1, 2)], axis=1)
    conv_ref[...] = mm(rel[...], weights, NT).astype(bf16)


def front(hidden, gain, dt_w, shards, tile):
    rows, width = hidden.shape
    _, count, depth = shards.shape
    whole = pl.BlockSpec((rows, width), lambda i: (0, 0))
    return pl.pallas_call(
        front_kernel,
        grid=(count // tile,),
        in_specs=[
            whole,
            pl.BlockSpec((1, width), lambda i: (0, 0)),
            pl.BlockSpec(dt_w.shape, lambda i: (0, 0, 0)),
            pl.BlockSpec((4, tile, depth), lambda i: (0, i, 0)),
        ],
        out_specs=[
            pl.BlockSpec((rows, tile), lambda i: (0, i)),
            whole,
            pl.BlockSpec((rows, LANES), lambda i: (0, 0)),
        ],
        out_shape=[
            jax.ShapeDtypeStruct((rows, count), bf16),
            jax.ShapeDtypeStruct((rows, width), bf16),
            jax.ShapeDtypeStruct((rows, LANES), f32),
        ],
        scratch_shapes=[pltpu.VMEM((rows, width), bf16)],
        compiler_params=pltpu.CompilerParams(vmem_limit_bytes=VMEM),
        name="front",
    )(hidden, gain, dt_w, shards)


def gate_kernel(
    scan_ref,
    norm_ref,
    w_ref,
    v_ref,
    gain_ref,
    ow_ref,
    ov_ref,
    h_ref,
    og_ref,
    valid_ref,
    no_ref,
    out_ref,
    g_ref,
    dy_ref,
    dgate_ref,
    dgain_ref,
    gate,
    d_no,
    branch,
):
    inner = scan_ref.shape[1]
    depth = w_ref.shape[1]
    block = ow_ref.shape[0]
    rows = scan_ref.shape[0]

    @pl.when(pl.program_id(0) == 0)
    def _():
        dgain_ref[...] = jnp.zeros_like(dgain_ref)

    rel = jnp.concatenate([norm_ref[:, shard_place(k, depth)] for k in range(4)], axis=1)
    valid = valid_ref[...]
    g_low = (og_ref[...].astype(f32) * valid).astype(bf16)
    g_ref[...] = g_low
    power = jnp.zeros((rows, 1), f32)
    for i in range(4):
        at = slice(i * block, (i + 1) * block)
        weights = jnp.concatenate([w_ref[at, :]] + [v_ref[k, at, :] for k in range(3)], axis=1)
        value = mm(rel, weights, NT)
        gate[:, at] = value
        act, _ = silu_parts(value)
        u = scan_ref[:, at].astype(f32) * act
        power += jnp.sum(u * u, axis=-1, keepdims=True)
    scale = lax.rsqrt(power / inner + epsilon)
    along = jnp.zeros((rows, 1), f32)
    for k in range(4):
        at = shard_place(k, block)
        weights = ow_ref[...] if k == 0 else ov_ref[k - 1]
        act, _ = silu_parts(gate[:, at])
        u = scan_ref[:, at].astype(f32) * act
        normed = u * scale
        low = (normed * gain_ref[:, at]).astype(bf16)
        no_ref[:, at] = low
        if k == 0:
            branch[...] = mm(low, weights)
        else:
            branch[...] += mm(low, weights)
        d = mm(g_low, weights, NT)
        dgain_ref[:, at] += jnp.sum(d * normed, axis=0, keepdims=True)
        d = d * gain_ref[:, at]
        d_no[:, at] = d
        along += jnp.sum(d * u, axis=-1, keepdims=True)
    out_ref[...] = (h_ref[...].astype(f32) + valid * branch[...]).astype(bf16)
    along = along * scale * scale * scale / inner
    for i in range(4):
        at = slice(i * block, (i + 1) * block)
        value = gate[:, at]
        act, sig = silu_parts(value)
        v = scan_ref[:, at].astype(f32)
        d_u = scale * d_no[:, at] - v * act * along
        dy_ref[:, at] = (d_u * act).astype(bf16)
        dgate_ref[:, at] = (d_u * v * (sig * (1.0 + value * (1.0 - sig)))).astype(bf16)


def gate_stage(scanned, normed, own, others, gain, out_own, out_others, hidden, out_grad, valid, tile):
    rows, width = hidden.shape
    _, inner, depth = others.shape
    once = pl.Buffered(1)
    wide = pl.BlockSpec((tile, inner), lambda i: (i, 0))
    slim = pl.BlockSpec((tile, width), lambda i: (i, 0))
    line = pl.BlockSpec((1, inner), lambda i: (0, 0))
    return pl.pallas_call(
        gate_kernel,
        grid=(rows // tile,),
        in_specs=[
            wide,
            slim,
            pl.BlockSpec((inner, depth), lambda i: (0, 0), pipeline_mode=once),
            pl.BlockSpec(others.shape, lambda i: (0, 0, 0), pipeline_mode=once),
            line,
            pl.BlockSpec(out_own.shape, lambda i: (0, 0), pipeline_mode=once),
            pl.BlockSpec(out_others.shape, lambda i: (0, 0, 0), pipeline_mode=once),
            slim,
            slim,
            pl.BlockSpec((tile, 1), lambda i: (i, 0)),
        ],
        out_specs=[wide, slim, slim, wide, wide, line],
        out_shape=[
            jax.ShapeDtypeStruct((rows, inner), bf16),
            jax.ShapeDtypeStruct((rows, width), bf16),
            jax.ShapeDtypeStruct((rows, width), bf16),
            jax.ShapeDtypeStruct((rows, inner), bf16),
            jax.ShapeDtypeStruct((rows, inner), bf16),
            jax.ShapeDtypeStruct((1, inner), f32),
        ],
        scratch_shapes=[
            pltpu.VMEM((tile, inner), f32),
            pltpu.VMEM((tile, inner), f32),
            pltpu.VMEM((tile, width), f32),
        ],
        compiler_params=pltpu.CompilerParams(vmem_limit_bytes=VMEM_MOST),
        name="gate_stage",
    )(scanned, normed, own, others, gain, out_own, out_others, hidden, out_grad, valid)


def turn_kernel(x_ref, o_ref):
    o_ref[...] = x_ref[...].astype(f32).T


def turned(x, tile):
    rows, columns = x.shape
    return pl.pallas_call(
        turn_kernel,
        grid=(rows // tile,),
        in_specs=[pl.BlockSpec((tile, columns), lambda i: (i, 0))],
        out_specs=pl.BlockSpec((columns, tile), lambda i: (0, i)),
        out_shape=jax.ShapeDtypeStruct((columns, rows), f32),
        compiler_params=pltpu.CompilerParams(vmem_limit_bytes=VMEM),
        name="turned",
    )(x)


def project_kernel(n_ref, w_ref, v_ref, o_ref):
    total = mm(n_ref[0], w_ref[...], NT)
    for k in range(1, n_ref.shape[0]):
        total += mm(n_ref[k], v_ref[k - 1], NT)
    o_ref[...] = total.astype(o_ref.dtype)


def project(parts, own, others, first, count, tile, dtype):
    shards, rows, depth = parts.shape
    return pl.pallas_call(
        project_kernel,
        grid=(count // tile,),
        in_specs=[
            pl.BlockSpec((shards, rows, depth), lambda i: (0, 0, 0)),
            pl.BlockSpec((tile, depth), lambda i: (first // tile + i, 0)),
            pl.BlockSpec((shards - 1, tile, depth), lambda i: (0, first // tile + i, 0)),
        ],
        out_specs=pl.BlockSpec((rows, tile), lambda i: (0, i)),
        out_shape=jax.ShapeDtypeStruct((rows, count), dtype),
        compiler_params=pltpu.CompilerParams(vmem_limit_bytes=VMEM),
        name="project",
    )(parts, own, others)


def unproject_kernel(steps, d_ref, e_ref, w_ref, v_ref, o_ref):
    def add(ref):
        o_ref[0] += mm(ref[...], w_ref[...])
        for k in range(1, o_ref.shape[0]):
            o_ref[k] += mm(ref[...], v_ref[k - 1])

    @pl.when(pl.program_id(0) == 0)
    def _():
        o_ref[...] = jnp.zeros_like(o_ref)

    @pl.when(pl.program_id(0) < steps)
    def _():
        add(d_ref)

    @pl.when(pl.program_id(0) >= steps)
    def _():
        add(e_ref)


def unproject(d, e, own, others, tile):
    shards, count, depth = others.shape
    shards += 1
    rows = d.shape[0]
    steps = d.shape[1] // tile
    return pl.pallas_call(
        partial(unproject_kernel, steps),
        grid=(count // tile,),
        in_specs=[
            pl.BlockSpec((rows, tile), lambda i: (0, jnp.minimum(i, steps - 1))),
            pl.BlockSpec((rows, tile), lambda i: (0, jnp.maximum(i - steps, 0))),
            pl.BlockSpec((tile, depth), lambda i: (i, 0)),
            pl.BlockSpec((shards - 1, tile, depth), lambda i: (0, i, 0)),
        ],
        out_specs=pl.BlockSpec((shards, rows, depth), lambda i: (0, 0, 0)),
        out_shape=jax.ShapeDtypeStruct((shards, rows, depth), f32),
        compiler_params=pltpu.CompilerParams(vmem_limit_bytes=VMEM),
        name="unproject",
    )(d, e, own, others)


def rms_front(hidden_rows, gain):
    power = jnp.mean(hidden_rows * hidden_rows, axis=-1, keepdims=True)
    return hidden_rows * lax.rsqrt(power + epsilon) * gain


def conv_act(padded, conv_w, conv_b):
    taps = conv_w.shape[0]
    rows_out = padded.shape[1] - taps + 1
    total = conv_b + padded[:, 0:rows_out] * conv_w[0]
    for offset in range(1, taps):
        total = total + padded[:, offset : offset + rows_out] * conv_w[offset]
    return jax.nn.silu(total)


def gate_norm(values, gate_in, gain):
    gated = values * jax.nn.silu(gate_in)
    power = jnp.mean(gated * gated, axis=-1, keepdims=True)
    return gated * lax.rsqrt(power + epsilon) * gain


def local(
    hidden,
    lengths,
    out_grad,
    norm_gain,
    in_weight,
    conv_weight,
    conv_bias,
    dt_bias,
    a_log,
    skip_gain,
    gated_gain,
    out_weight,
):
    count = lax.axis_size("seq")
    shards = lax.axis_size("wshard")
    rank = lax.axis_index("seq")
    shard = lax.axis_index("wshard")
    micro, _, tokens, width = hidden.shape
    taps = conv_weight.shape[1]
    inner = out_weight.shape[0] * shards
    channels = conv_bias.shape[0] * shards
    heads = dt_bias.shape[0] * shards
    hs = inner // heads
    n = (channels - inner) // 2
    groups = heads // GROUP
    rows = micro * tokens
    fast = count == 8 and shards == 4 and micro == 2
    in_local = in_weight.T
    small = [norm_gain, conv_weight.T.reshape(-1), conv_bias, dt_bias, a_log, skip_gain, gated_gain]
    sizes = [v.shape[0] for v in small]
    if not fast:
        small.append(in_local[inner + channels :].reshape(-1))
    small = jnp.concatenate(small)
    order = jnp.arange(shards) ^ shard
    if fast:
        small = jnp.pad(small, (0, -small.shape[0] % (16 * LANES))).reshape(-1, LANES)
        conv_shards, gate_others, out_eighth, dt_shards, got = gather_input_weight(
            in_local, out_weight, small, inner, channels
        )
        packed_low = got[(order - 1) % shards].reshape(shards, -1)
    else:
        packed_low = lax.all_gather(small, "wshard", axis=0)
    packed = packed_low.astype(f32)
    parts, at = [], 0
    for size in sizes:
        parts.append(packed[:, at : at + size])
        at += size
    norm_g = parts[0].reshape(-1)
    conv_w = parts[1].reshape(shards, taps, -1).transpose(1, 0, 2).reshape(taps, -1)
    conv_b = parts[2].reshape(-1)
    dt_shift = parts[3].reshape(-1)
    rate = -jnp.exp(parts[4].reshape(-1))
    skip = parts[5].reshape(-1)
    gated_g = parts[6].reshape(-1)

    if not fast:
        dt_w = packed_low[:, at:].reshape(shards, heads, -1).transpose(1, 0, 2).reshape(heads, -1)
    if not fast:
        every = lax.all_gather(in_local[: inner + channels], "wshard", axis=0)
        in_w = every[order[1:]]
        out_w = lax.all_gather(out_weight, "wshard", axis=0, tiled=True)

    def grouped(v):
        return v.reshape(micro, tokens, groups, GROUP).transpose(0, 2, 1, 3)

    rows_in = hidden.reshape(rows, width).astype(f32)
    cot = out_grad.reshape(rows, width).astype(f32)
    positions = rank * tokens + jnp.arange(tokens, dtype=jnp.int32)
    valid = (positions[None, :] < lengths[:, 0][:, None]).astype(f32).reshape(rows, 1)
    tile = 256
    skip_wide = jnp.repeat(skip, hs)[None, :]

    def to_lanes(v):
        return jnp.pad(v, ((0, 0),) * (v.ndim - 1) + ((0, LANES - heads),))

    if fast:
        hidden_rows, out_grad_rows = hidden.reshape(rows, width), out_grad.reshape(rows, width)
        conv_low, normed_low, raw = front(
            hidden_rows, norm_g[None, :], dt_shards, conv_shards, channels // 2
        )
        raw = raw.reshape(micro, tokens, LANES)
    else:
        normed, front_back = jax.vjp(rms_front, rows_in, norm_g)
        normed_low = normed.astype(bf16)
        normed_parts = normed_low.reshape(rows, shards, -1).transpose(1, 0, 2)[order]
        conv_low = project(normed_parts, in_local, in_w, inner, channels, tile, bf16)
        gate_in = project(normed_parts, in_local, in_w, 0, inner, tile, f32)
        dt_low = mm(normed_low, dt_w, NT).astype(bf16)
        dt_raw = dt_low.astype(f32).reshape(micro, tokens, heads) + dt_shift
    conv_low = conv_low.reshape(micro, tokens, channels)

    if fast:
        x_low, bc_low, y_scan, scanned_low, halo, s_in, out_others = scan_forward(
            conv_low,
            raw,
            conv_w,
            conv_b[None, :],
            to_lanes(dt_shift[None, :]),
            to_lanes(rate[None, :]),
            skip_wide,
            out_eighth,
            inner,
            hs,
            3,
        )
    else:
        prior = from_behind(conv_low[:, tokens - (taps - 1) :], "seq", 1)
        padded = jnp.concatenate([prior, conv_low], axis=1).astype(f32)
        mixed, conv_back = jax.vjp(conv_act, padded, conv_w, conv_b)
        dt = jax.nn.softplus(dt_raw)
        tri = (jnp.arange(tokens)[:, None] >= jnp.arange(tokens)[None, :]).astype(f32)
        cum = jnp.einsum("ij,mjh->mih", tri, dt * rate, precision=highest)
        dt_g, cum_g = grouped(dt), grouped(cum)
        row_g = cum_g.transpose(0, 1, 3, 2)
        last = cum[:, tokens - 1, :]
        decays = lax.all_gather(jnp.exp(last), "seq", axis=0)
        decay_w = grouped(jnp.exp(cum))
        x_low = mixed[..., :inner].astype(bf16)
        b_low = mixed[..., inner : inner + n].astype(bf16)
        c_low = mixed[..., inner + n :].astype(bf16)
        end_w = grouped(dt * jnp.exp(last[:, None, :] - cum))
        own_state = block_states(x_low, end_w, b_low.transpose(0, 2, 1), hs)
        y_local = local_scan(x_low, dt_g, cum_g, row_g, b_low, c_low, hs)
        s_in = running_states(own_state, decays, hs, True)
        y_scan, scanned_low = add_carry(x_low, y_local, cum_g, c_low, s_in, skip_wide, hs)

    if fast:
        normed_out_low, output, g, dy, d_gate_low, d_gated = gate_stage(
            scanned_low.reshape(rows, inner),
            normed_low,
            in_local,
            gate_others,
            gated_g[None, :],
            out_weight,
            out_others,
            hidden_rows,
            out_grad_rows,
            valid,
            256,
        )
        output = output.reshape(hidden.shape)
        dy = dy.reshape(micro, tokens, inner)
        d_gated = d_gated[0]
    else:
        scanned = scanned_low.reshape(rows, inner).astype(f32)
        normed_out, gate_back = jax.vjp(gate_norm, scanned, gate_in, gated_g)
        normed_out_low = normed_out.astype(bf16)
        branch = mm(normed_out_low, out_w)
        output = (rows_in + valid * branch).astype(bf16).reshape(hidden.shape)
        g = (cot * valid).astype(bf16)
        d_scanned, d_gate_in, d_gated = gate_back(mm(g, out_w, NT))
        dy = d_scanned.astype(bf16).reshape(micro, tokens, inner)
        d_gate_low = d_gate_in.astype(bf16)

    if fast:
        d_rest, d_conv_w, d_conv_b, by_head, gate_sum, normed_far = scan_backward(
            dy,
            x_low,
            bc_low,
            y_scan,
            s_in,
            raw,
            conv_low,
            halo,
            conv_w,
            conv_b[None, :],
            to_lanes(dt_shift[None, :]),
            to_lanes(rate[None, :]),
            skip_wide,
            d_gate_low,
            normed_low,
            hs,
            4,
        )
        d_dt_bias, d_a_log, d_skip = by_head[0, :heads], by_head[1, :heads], by_head[2, :heads]
        d_conv_b = d_conv_b[0]
        d_rest = d_rest.reshape(rows, -1)
        d_norm_g = jnp.zeros((width,), f32)
    else:
        own_grad = block_states(dy, decay_w, c_low.transpose(0, 2, 1), hs)
        dx_local, db_local, dc_local = local_back(x_low, dy, dt_g, cum_g, row_g, b_low, c_low, hs)
        ds = running_states(own_grad, decays, hs, False)
        dx_low, ddt_g, dcum_g, db, dc, last_term, dskip = carry_back(
            x_low, dy, dx_local, y_scan, dt_g, cum_g, b_low, s_in, ds, db_local, dc_local, skip_wide, hs
        )

        def ungrouped(v):
            return v.transpose(0, 2, 1, 3).reshape(micro, tokens, heads)

        at_end = jnp.sum(last_term.reshape(micro, heads, hs), axis=-1)[:, None, :]
        d_log = jnp.einsum("ij,mih->mjh", tri, ungrouped(dcum_g), precision=highest) + at_end
        d_dt = (ungrouped(ddt_g) + d_log * rate) * jax.nn.sigmoid(dt_raw)
        d_dt_bias = jnp.sum(d_dt, axis=(0, 1))
        d_a_log = jnp.sum(d_log * dt, axis=(0, 1)) * rate
        d_skip = jnp.sum(dskip.reshape(-1, heads, hs), axis=(0, 2))
        mixed_grad = jnp.concatenate([dx_low.astype(f32), db, dc], axis=2)
        d_padded, d_conv_w, d_conv_b = conv_back(mixed_grad)
        from_next = from_behind(d_padded[:, : taps - 1].astype(bf16), "seq", -1).astype(f32)
        d_conv = d_padded[:, taps - 1 :].at[:, tokens - (taps - 1) :].add(from_next)
        d_dt_low = d_dt.astype(bf16).reshape(rows, heads)
    total_cols = inner + channels + heads
    if not fast:
        d_rest = d_conv.astype(bf16).reshape(rows, channels)
        d_parts = unproject(d_gate_low, d_rest, in_local, in_w, tile)
        d_normed = d_parts[order].transpose(1, 0, 2).reshape(rows, width) + mm(d_dt_low, dt_w)
        d_hidden, d_norm_g = front_back(d_normed)
        input_grad = (d_hidden + cot).astype(bf16).reshape(hidden.shape)

    def summed(terms, axis):
        t = lax.psum_scatter(terms.astype(bf16), "seq", scatter_dimension=0, tiled=True)
        t = lax.psum_scatter(t, "wshard", scatter_dimension=axis, tiled=True)
        return lax.all_gather(t, "seq", axis=0, tiled=True).astype(f32)

    smalls = [
        d_norm_g.reshape(shards, -1),
        d_conv_w.reshape(taps, shards, -1).transpose(1, 0, 2).reshape(shards, -1),
        d_conv_b.reshape(shards, -1),
        d_dt_bias.reshape(shards, -1),
        d_a_log.reshape(shards, -1),
        d_skip.reshape(shards, -1),
        d_gated.reshape(shards, -1),
    ]
    smalls = jnp.concatenate(smalls, axis=1)
    if fast:
        smalls = jnp.pad(smalls, ((0, 0), (0, -smalls.shape[1] % 1024))).reshape(shards, -1, LANES)
        rest_sum, out_sum, sums, input_grad = weight_sums(
            d_gate_low,
            d_rest,
            normed_low,
            normed_far,
            g,
            normed_out_low,
            in_local,
            gate_others,
            conv_shards,
            smalls,
            dt_shards,
            hidden_rows,
            norm_g[None, :],
            out_grad_rows,
            2,
        )
        input_grad = input_grad.reshape(hidden.shape)
        gate_sum = gate_sum.reshape(inner, -1)
        in_grad = jnp.concatenate([gate_sum, rest_sum[: total_cols - inner]]).astype(f32).T
        out_w_grad = turned(out_sum, 512)
        sums = sums.reshape(-1)
    else:
        d_proj = jnp.concatenate([d_gate_low, d_rest, d_dt_low], axis=1)
        in_grad = summed(mm(d_proj, normed_low, TN), 1).T
        out_terms = mm(normed_out_low, g, TN)
        blocks = out_terms.reshape(shards, count, -1, width).transpose(1, 0, 2, 3)
        out_w_grad = summed(blocks.reshape(inner, width), 0)
        sums = lax.psum(smalls, ("seq", "wshard"))
        sums = lax.dynamic_index_in_dim(sums, shard, 0, keepdims=False)
    found, at = [], 0
    for size in sizes:
        found.append(sums[at : at + size])
        at += size
    return (
        output,
        input_grad,
        found[0],
        in_grad,
        found[1].reshape(taps, -1).T,
        found[2],
        found[3],
        found[4],
        found[5],
        found[6],
        out_w_grad,
    )


def solution(mesh):
    return jax.shard_map(
        local,
        mesh=mesh,
        in_specs=(
            P(None, "wshard", "seq", None),
            P(None, "wshard"),
            P(None, "wshard", "seq", None),
            P("wshard"),
            P("wshard", None),
            P("wshard", None),
            P("wshard"),
            P("wshard"),
            P("wshard"),
            P("wshard"),
            P("wshard"),
            P("wshard", None),
        ),
        out_specs=(
            P(None, "wshard", "seq", None),
            P(None, "wshard", "seq", None),
            P("wshard"),
            P("wshard", None),
            P("wshard", None),
            P("wshard"),
            P("wshard"),
            P("wshard"),
            P("wshard"),
            P("wshard"),
            P("wshard", None),
        ),
        check_vma=False,
    )
```

```python
from functools import partial

import jax
import jax.numpy as jnp
from jax import lax
from jax.experimental import pallas as pl
from jax.experimental.pallas import tpu as pltpu
from jax.sharding import PartitionSpec as P

epsilon = 1e-05
highest = lax.Precision.HIGHEST
f32 = jnp.float32
bf16 = jnp.bfloat16
GROUP = 8
VMEM = 48 * 1024 * 1024
VMEM_MOST = 62 * 1024 * 1024

NN = (((1,), (0,)), ((), ()))
NT = (((1,), (1,)), ((), ()))
TN = (((0,), (0,)), ((), ()))


def mm(a, b, dims=NN):
    return lax.dot_general(a, b, dims, preferred_element_type=f32)


def params():
    return pltpu.CompilerParams(
        dimension_semantics=("arbitrary", "arbitrary"), vmem_limit_bytes=VMEM
    )


def widen(cols, head_size):
    heads = cols.shape[1]
    high = cols.astype(bf16).astype(f32)
    r = lax.broadcasted_iota(jnp.int32, (2 * heads, heads * head_size), 0)
    c = lax.broadcasted_iota(jnp.int32, (2 * heads, heads * head_size), 1)
    ones = jnp.where(r % heads == c // head_size, 1.0, 0.0).astype(bf16)
    return mm(jnp.concatenate([high, cols - high], axis=1).astype(bf16), ones)


def state_kernel(hs, x_ref, w_ref, bt_ref, o_ref):
    weighted = (x_ref[0].astype(f32) * widen(w_ref[0, 0], hs)).astype(bf16)
    o_ref[0] = mm(bt_ref[0], weighted)


def block_states(x, weights, bt, hs):
    micro, t, cols = x.shape
    n = bt.shape[1]
    gc = GROUP * hs
    return pl.pallas_call(
        partial(state_kernel, hs),
        grid=(micro, cols // gc),
        in_specs=[
            pl.BlockSpec((1, t, gc), lambda m, g: (m, 0, g)),
            pl.BlockSpec((1, 1, t, GROUP), lambda m, g: (m, g, 0, 0)),
            pl.BlockSpec((1, n, t), lambda m, g: (m, 0, 0)),
        ],
        out_specs=pl.BlockSpec((1, n, gc), lambda m, g: (m, 0, g)),
        out_shape=jax.ShapeDtypeStruct((micro, n, cols), f32),
        compiler_params=params(),
        name="block_states",
    )(x, weights, bt)


def local_kernel(hs, x_ref, dt_ref, cum_ref, row_ref, b_ref, c_ref, o_ref, scores):
    t = x_ref.shape[1]
    half = t // 2

    @pl.when(pl.program_id(1) == 0)
    def _():
        s = mm(c_ref[0], b_ref[0], NT)
        i = lax.broadcasted_iota(jnp.int32, (t, t), 0)
        j = lax.broadcasted_iota(jnp.int32, (t, t), 1)
        scores[...] = jnp.where(i >= j, s, 0.0)

    cum, dt, rows = cum_ref[0, 0], dt_ref[0, 0], row_ref[0, 0]
    lane = lax.broadcasted_iota(jnp.int32, (half, 2 * hs), 1)
    weighted = (x_ref[0].astype(f32) * widen(dt, hs)).astype(bf16)
    for k in range(0, GROUP, 2):
        at = slice(k * hs, (k + 2) * hs)
        pair = weighted[:, at]
        top, low = [], []
        for h in (k, k + 1):
            col, row = cum[:, h : h + 1], rows[h : h + 1, :]
            m1 = jnp.exp(jnp.minimum(col[:half] - row[:, :half], 0.0)) * scores[:half, :half]
            m2 = jnp.exp(jnp.minimum(col[half:] - row, 0.0)) * scores[half:, :]
            top.append(mm(m1.astype(bf16), pair[:half]))
            low.append(mm(m2.astype(bf16), pair))
        o_ref[0, :half, at] = jnp.where(lane < hs, top[0], top[1])
        o_ref[0, half:, at] = jnp.where(lane < hs, low[0], low[1])


def local_scan(x, dt, cum, rows, b, c, hs):
    micro, t, cols = x.shape
    n = b.shape[2]
    gc = GROUP * hs
    return pl.pallas_call(
        partial(local_kernel, hs),
        grid=(micro, cols // gc),
        in_specs=[
            pl.BlockSpec((1, t, gc), lambda m, g: (m, 0, g)),
            pl.BlockSpec((1, 1, t, GROUP), lambda m, g: (m, g, 0, 0)),
            pl.BlockSpec((1, 1, t, GROUP), lambda m, g: (m, g, 0, 0)),
            pl.BlockSpec((1, 1, GROUP, t), lambda m, g: (m, g, 0, 0)),
            pl.BlockSpec((1, t, n), lambda m, g: (m, 0, 0)),
            pl.BlockSpec((1, t, n), lambda m, g: (m, 0, 0)),
        ],
        out_specs=pl.BlockSpec((1, t, gc), lambda m, g: (m, 0, g)),
        out_shape=jax.ShapeDtypeStruct((micro, t, cols), f32),
        scratch_shapes=[pltpu.VMEM((t, t), f32)],
        compiler_params=params(),
        name="local_scan",
    )(x, dt, cum, rows, b, c)


def carry_kernel(hs, x_ref, y_ref, cum_ref, c_ref, s_ref, skip_ref, scan_ref, low_ref):
    carried = mm(c_ref[0], s_ref[0].astype(bf16)) * widen(jnp.exp(cum_ref[0, 0]), hs)
    scan = y_ref[0] + carried
    scan_ref[0] = scan
    low_ref[0] = (scan + skip_ref[...] * x_ref[0].astype(f32)).astype(bf16)


def add_carry(x, y, cum, c, s_in, skip_wide, hs):
    micro, t, cols = x.shape
    n = c.shape[2]
    gc = GROUP * hs
    wide = pl.BlockSpec((1, t, gc), lambda m, g: (m, 0, g))
    return pl.pallas_call(
        partial(carry_kernel, hs),
        grid=(micro, cols // gc),
        in_specs=[
            wide,
            wide,
            pl.BlockSpec((1, 1, t, GROUP), lambda m, g: (m, g, 0, 0)),
            pl.BlockSpec((1, t, n), lambda m, g: (m, 0, 0)),
            pl.BlockSpec((1, n, gc), lambda m, g: (m, 0, g)),
            pl.BlockSpec((1, gc), lambda m, g: (0, g)),
        ],
        out_specs=[wide, wide],
        out_shape=[
            jax.ShapeDtypeStruct((micro, t, cols), f32),
            jax.ShapeDtypeStruct((micro, t, cols), bf16),
        ],
        compiler_params=params(),
        name="add_carry",
    )(x, y, cum, c, s_in, skip_wide)


def local_back_kernel(
    hs, x_ref, dy_ref, dt_ref, cum_ref, row_ref, b_ref, c_ref, dx_ref, db_ref, dc_ref, scores, total
):
    t = x_ref.shape[1]
    half = t // 2

    @pl.when(pl.program_id(1) == 0)
    def _():
        s = mm(b_ref[0], c_ref[0], NT)
        j = lax.broadcasted_iota(jnp.int32, (t, t), 0)
        i = lax.broadcasted_iota(jnp.int32, (t, t), 1)
        scores[...] = jnp.where(i >= j, s, 0.0)
        total[...] = jnp.zeros_like(total)

    cum, dt, rows = cum_ref[0, 0], dt_ref[0, 0], row_ref[0, 0]
    lane = lax.broadcasted_iota(jnp.int32, (t, 2 * hs), 1)
    lane_half = lax.broadcasted_iota(jnp.int32, (half, 2 * hs), 1)
    weighted = (x_ref[0].astype(f32) * widen(dt, hs)).astype(bf16)
    for k in range(0, GROUP, 2):
        at = slice(k * hs, (k + 2) * hs)
        pair = weighted[:, at]
        dy = dy_ref[0, :, at]
        top, low = [], []
        for h in (k, k + 1):
            col, row = cum[:, h : h + 1], rows[h : h + 1, :]
            mine = jnp.where(lane < hs, pair, 0) if h == k else jnp.where(lane < hs, 0, pair)
            l1 = jnp.exp(jnp.minimum(row - col[:half], 0.0))
            l2 = jnp.exp(jnp.minimum(row[:, half:] - col[half:], 0.0))
            total[:half, :] += l1 * mm(mine[:half], dy, NT)
            total[half:, half:] += l2 * mm(mine[half:], dy[half:], NT)
            top.append(mm((l1 * scores[:half, :]).astype(bf16), dy))
            low.append(mm((l2 * scores[half:, half:]).astype(bf16), dy[half:]))
        dx_ref[0, :half, at] = jnp.where(lane_half < hs, top[0], top[1])
        dx_ref[0, half:, at] = jnp.where(lane_half < hs, low[0], low[1])

    @pl.when(pl.program_id(1) == pl.num_programs(1) - 1)
    def _():
        j = lax.broadcasted_iota(jnp.int32, (t, t), 0)
        i = lax.broadcasted_iota(jnp.int32, (t, t), 1)
        d = jnp.where(i >= j, total[...], 0.0)
        db_ref[0] = mm(d.astype(bf16), c_ref[0])
        dc_ref[0] = mm(d.T.astype(bf16), b_ref[0])


def local_back(x, dy, dt, cum, rows, b, c, hs):
    micro, t, cols = x.shape
    n = b.shape[2]
    gc = GROUP * hs
    wide = pl.BlockSpec((1, t, gc), lambda m, g: (m, 0, g))
    small = pl.BlockSpec((1, 1, t, GROUP), lambda m, g: (m, g, 0, 0))
    state = pl.BlockSpec((1, t, n), lambda m, g: (m, 0, 0))
    return pl.pallas_call(
        partial(local_back_kernel, hs),
        grid=(micro, cols // gc),
        in_specs=[
            wide,
            wide,
            small,
            small,
            pl.BlockSpec((1, 1, GROUP, t), lambda m, g: (m, g, 0, 0)),
            state,
            state,
        ],
        out_specs=[wide, state, state],
        out_shape=[
            jax.ShapeDtypeStruct((micro, t, cols), f32),
            jax.ShapeDtypeStruct((micro, t, n), f32),
            jax.ShapeDtypeStruct((micro, t, n), f32),
        ],
        scratch_shapes=[pltpu.VMEM((t, t), f32), pltpu.VMEM((t, t), f32)],
        compiler_params=params(),
        name="local_back",
    )(x, dy, dt, cum, rows, b, c)


def head_sums(values, ones):
    high = values.astype(bf16)
    rest = (values - high.astype(f32)).astype(bf16)
    return mm(high, ones) + mm(rest, ones)


def carry_back_kernel(
    hs,
    x_ref,
    dy_ref,
    dxl_ref,
    y_ref,
    dt_ref,
    cum_ref,
    b_ref,
    si_ref,
    ds_ref,
    dbl_ref,
    dcl_ref,
    skip_ref,
    dx_ref,
    ddt_ref,
    dcum_ref,
    db_ref,
    dc_ref,
    last_ref,
    dskip_ref,
):
    t = x_ref.shape[1]
    gc = x_ref.shape[2]

    @pl.when(pl.program_id(1) == 0)
    def _():
        db_ref[0] = dbl_ref[0]
        dc_ref[0] = dcl_ref[0]

    cum, dt = cum_ref[0, 0], dt_ref[0, 0]
    x, dy = x_ref[0].astype(f32), dy_ref[0].astype(f32)
    dt_wide = widen(dt, hs)
    weighted = (x * dt_wide).astype(bf16).astype(f32)
    decay = widen(jnp.exp(cum), hs)
    to_end = widen(jnp.exp(cum[t - 1 :, :] - cum), hs)
    s_in, ds = si_ref[0].astype(f32), ds_ref[0]
    s_low, ds_low = s_in.astype(bf16), ds.astype(bf16)
    through = to_end * mm(b_ref[0], ds_low)
    d_weighted = dxl_ref[0] + through
    dx_ref[0] = (dt_wide * d_weighted + skip_ref[...] * dy).astype(bf16)
    db_ref[0] += mm((weighted * to_end).astype(bf16), ds_low, NT)
    dc_ref[0] += mm((dy * decay).astype(bf16), s_low, NT)
    r = lax.broadcasted_iota(jnp.int32, (gc, 128), 0)
    c = lax.broadcasted_iota(jnp.int32, (gc, 128), 1)
    ones = jnp.where(r // hs == c, 1.0, 0.0).astype(bf16)
    ddt_ref[0, 0] = head_sums(x * d_weighted, ones)[:, :GROUP]
    dcum_ref[0, 0] = head_sums(dy * y_ref[0] - weighted * d_weighted, ones)[:, :GROUP]
    last_decay = decay[t - 1 :, :]
    last_ref[0] = jnp.sum(weighted * through, axis=0, keepdims=True) + last_decay * jnp.sum(
        s_low.astype(f32) * ds, axis=0, keepdims=True
    )
    dskip_ref[0] = jnp.sum(x * dy, axis=0, keepdims=True)


def carry_back(x, dy, dxl, y, dt, cum, b, s_in, ds, dbl, dcl, skip_wide, hs):
    micro, t, cols = x.shape
    n = b.shape[2]
    gc = GROUP * hs
    groups = cols // gc
    wide = pl.BlockSpec((1, t, gc), lambda m, g: (m, 0, g))
    small = pl.BlockSpec((1, 1, t, GROUP), lambda m, g: (m, g, 0, 0))
    state = pl.BlockSpec((1, t, n), lambda m, g: (m, 0, 0))
    st = pl.BlockSpec((1, n, gc), lambda m, g: (m, 0, g))
    line = pl.BlockSpec((1, 1, gc), lambda m, g: (m, 0, g))
    return pl.pallas_call(
        partial(carry_back_kernel, hs),
        grid=(micro, groups),
        in_specs=[
            wide,
            wide,
            wide,
            wide,
            small,
            small,
            state,
            st,
            st,
            state,
            state,
            pl.BlockSpec((1, gc), lambda m, g: (0, g)),
        ],
        out_specs=[wide, small, small, state, state, line, line],
        out_shape=[
            jax.ShapeDtypeStruct((micro, t, cols), bf16),
            jax.ShapeDtypeStruct((micro, groups, t, GROUP), f32),
            jax.ShapeDtypeStruct((micro, groups, t, GROUP), f32),
            jax.ShapeDtypeStruct((micro, t, n), f32),
            jax.ShapeDtypeStruct((micro, t, n), f32),
            jax.ShapeDtypeStruct((micro, 1, cols), f32),
            jax.ShapeDtypeStruct((micro, 1, cols), f32),
        ],
        compiler_params=params(),
        name="carry_back",
    )(x, dy, dxl, y, dt, cum, b, s_in, ds, dbl, dcl, skip_wide)


def from_behind(x, axis, by):
    count = lax.axis_size(axis)
    pairs = [(i, i + by) for i in range(count) if 0 <= i + by < count]
    return lax.ppermute(x, axis, pairs)


def swap(x, by):
    count = lax.axis_size("seq")
    return lax.ppermute(x, "seq", [(i, i ^ by) for i in range(count)])


def running_states(terms, decays, hs, forward):
    count = lax.axis_size("seq")
    rank = lax.axis_index("seq")
    index = jnp.arange(count)

    def product(mask):
        d = jnp.prod(jnp.where(mask[:, None, None], decays, 1.0), axis=0)
        return jnp.repeat(d, hs, axis=1)[:, None, :]

    total, before = terms, jnp.zeros_like(terms)
    size = 1
    while size < count:
        other = swap(total.astype(bf16), size).astype(f32)
        mine = index // size == rank // size
        theirs = index // size == (rank // size) ^ 1
        later = (rank // size) % 2 == (1 if forward else 0)
        passed = mine & ((index < rank) if forward else (index > rank))
        before = before + jnp.where(later, product(passed), 0.0) * other
        if 2 * size < count:
            total = total * jnp.where(later, 1.0, product(theirs)) + other * jnp.where(
                later, product(mine), 1.0
            )
        size *= 2
    return before


MESH = pl.DeviceIdType.MESH


def around():
    s, z = lax.axis_index("seq"), lax.axis_index("wshard")
    c, x, y = s % 2, (s // 2) % 2, s // 4
    near = {
        "c": (s + 1 - 2 * c, z),
        "x": (s + 2 - 4 * x, z),
        "y": (s + 4 - 8 * y, z),
        "z1": (s, z + 1 - 2 * (z % 2)),
        "z2": (s, z + 2 - 4 * (z // 2)),
        "z3": (s, 3 - z),
    }
    return s, z, c, x, y, near


def greet(near):
    barrier = pltpu.get_barrier_semaphore()
    for where in near.values():
        pl.semaphore_signal(barrier, inc=1, device_id=where, device_id_type=MESH)
    pl.semaphore_wait(barrier, len(near))


CHUNK_DMAS = 10
AHEAD = 3


def split_rows(piece, parts):
    tiles = piece // 16
    return [16 * (tiles * (i + 1) // parts - tiles * i // parts) for i in range(parts)]


class Gather:
    def __init__(self, place, items, send, recv, own=None):
        s, z, c, x, y, near = place
        sx, sy, sd = s + 2 - 4 * x, s + 4 - 8 * y, s + 6 - 4 * x - 8 * y
        self.plans = []
        for source, base, target, count, parts in items:
            off = 0
            for i, size in enumerate(split_rows(count // 8, parts)):
                q = len(self.plans)

                def rows(who, first=0, off=off, size=size, piece=count // 8):
                    return pl.ds(pl.multiple_of(first + who * piece + off, 16), size)

                def move(src, dst, kind, to, q=q):
                    return pltpu.make_async_remote_copy(
                        src_ref=src,
                        dst_ref=dst,
                        send_sem=send.at[q, kind],
                        recv_sem=recv.at[q, kind],
                        device_id=near[to],
                        device_id_type=MESH,
                    )

                def along(who, kind, to, move=move, rows=rows, target=target):
                    block = target.at[pl.ds(0, 3), rows(who)]
                    return move(block, block, kind, to)

                plan = {"fetched": base is None}
                if base is None:
                    have = source.at[:, pl.ds(off, size)]
                    block = target.at[pl.ds(0, 3), rows(s)]
                    plan["own"] = pltpu.make_async_copy(have, block, own.at[q])
                    for kind, name in ((3, "x"), (4, "y"), (6, "c0")):
                        plan[name] = move(have, block, kind, name[0])
                else:
                    for k in (1, 2, 3):
                        there = target.at[k - 1, rows(s)]
                        plan["z%d" % k] = move(source.at[rows(s, base)], there, k - 1, "z%d" % k)
                    plan["x"] = along(s, 3, "x")
                    plan["y"] = along(s, 4, "y")
                    plan["c0"] = along(s, 6, "c")
                first = "xy"[i % 2]
                plan["d"] = along(sx, 5, "y") if first == "x" else along(sy, 5, "x")
                plan["cx"] = along(sx, 7, "c")
                plan["cy"] = along(sy, 8, "c")
                plan["cd"] = along(sd, 9, "c")
                plan["order"] = first, "yx"[i % 2]
                self.plans.append(plan)
                off += size

    def fetch(self, i):
        for k in (1, 2, 3):
            self.plans[i]["z%d" % k].start()

    def begin(self, i):
        plan = self.plans[i]
        if plan["fetched"]:
            plan["own"].start()
        else:
            for k in (1, 2, 3):
                plan["z%d" % k].wait_recv()
        for name in ("x", "y", "c0"):
            plan[name].start()

    def middle(self, i):
        plan = self.plans[i]
        one, two = plan["order"]
        plan[one].wait_recv()
        plan["d"].start()
        plan["c" + one].start()
        plan[two].wait_recv()
        plan["c" + two].start()

    def finish(self, i):
        self.plans[i]["d"].wait_recv()
        self.plans[i]["cd"].start()

    def run(self, last):
        n = len(self.plans)
        for i in range(min(AHEAD, n)):
            self.fetch(i)
        for i in range(n + 2):
            if i < n:
                self.begin(i)
                if i + AHEAD < n:
                    self.fetch(i + AHEAD)
                if i + AHEAD == n - 1:
                    last()
            if 0 <= i - 1 < n:
                self.middle(i - 1)
            if 0 <= i - 2 < n:
                self.finish(i - 2)

    def close(self):
        for plan in self.plans:
            for name in ("c0", "cx", "cy", "cd"):
                plan[name].wait_recv()
            for name in ("z1", "z2", "z3", "x", "y", "d", "c0", "cx", "cy", "cd"):
                if name in plan:
                    plan[name].wait_send()
            if plan["fetched"]:
                plan["own"].wait()


def gather_kernel(
    inner,
    channels,
    parts,
    w_ref,
    ow_ref,
    small_ref,
    conv_ref,
    gate_ref,
    eighth_ref,
    dt_ref,
    small_out,
    own,
    own_dt,
    own_sem,
    dt_sem,
    send,
    recv,
    o_send,
    o_recv,
    d_send,
    d_recv,
    p_send,
    p_recv,
):
    place = around()
    dt_rows = w_ref.at[pl.ds(inner + channels, dt_ref.shape[1])]
    dt_inward = pltpu.make_async_copy(dt_rows, own_dt, dt_sem)
    dt_inward.start()
    steps = [
        pltpu.make_async_remote_copy(
            src_ref=dt_rows,
            dst_ref=dt_ref.at[k - 1],
            send_sem=d_send.at[k - 1],
            recv_sem=d_recv.at[k - 1],
            device_id=place[-1]["z%d" % k],
            device_id_type=MESH,
        )
        for k in (1, 2, 3)
    ]
    steps += [
        pltpu.make_async_remote_copy(
            src_ref=small_ref,
            dst_ref=small_out.at[k - 1],
            send_sem=p_send.at[k - 1],
            recv_sem=p_recv.at[k - 1],
            device_id=place[-1]["z%d" % k],
            device_id_type=MESH,
        )
        for k in (1, 2, 3)
    ]
    small_out[3] = small_ref[...]
    inward = pltpu.make_async_copy(w_ref.at[pl.ds(inner, channels)], own, own_sem)
    inward.start()
    greet(place[-1])
    for copy in steps:
        copy.start()
    items = [(w_ref, inner, conv_ref, channels, parts), (w_ref, 0, gate_ref, inner, parts)]
    work = Gather(place, items, send, recv)
    piece = eighth_ref.shape[1]
    mine = pl.ds(pl.multiple_of(place[0] * piece, 16), piece)
    eighths = [
        pltpu.make_async_remote_copy(
            src_ref=ow_ref.at[mine],
            dst_ref=eighth_ref.at[k - 1],
            send_sem=o_send.at[k - 1],
            recv_sem=o_recv.at[k - 1],
            device_id=place[-1]["z%d" % k],
            device_id_type=MESH,
        )
        for k in (1, 2, 3)
    ]

    def last():
        for copy in eighths:
            copy.start()

    work.run(last)
    inward.wait()
    dt_inward.wait()
    dt_outward = pltpu.make_async_copy(own_dt, dt_ref.at[3], dt_sem)
    dt_outward.start()
    outward = pltpu.make_async_copy(own, conv_ref.at[3], own_sem)
    outward.start()
    work.close()
    for copy in eighths + steps:
        copy.wait()
    outward.wait()
    dt_outward.wait()


def gather_input_weight(w_t, out_weight, small, inner, channels, parts=6):
    width = w_t.shape[1]
    hbm = pl.BlockSpec(memory_space=pl.ANY)
    vmem = pl.BlockSpec(memory_space=pltpu.VMEM)
    return pl.pallas_call(
        partial(gather_kernel, inner, channels, parts),
        in_specs=[hbm] * 2 + [vmem],
        out_specs=[hbm] * 4 + [vmem],
        out_shape=[
            jax.ShapeDtypeStruct((4, channels, width), bf16),
            jax.ShapeDtypeStruct((3, inner, width), bf16),
            jax.ShapeDtypeStruct((3, out_weight.shape[0] // 8, out_weight.shape[1]), bf16),
            jax.ShapeDtypeStruct((4, w_t.shape[0] - inner - channels, width), bf16),
            jax.ShapeDtypeStruct((4,) + small.shape, bf16),
        ],
        scratch_shapes=[
            pltpu.VMEM((channels, width), bf16),
            pltpu.VMEM((w_t.shape[0] - inner - channels, width), bf16),
            pltpu.SemaphoreType.DMA,
            pltpu.SemaphoreType.DMA,
            pltpu.SemaphoreType.DMA((2 * parts, CHUNK_DMAS)),
            pltpu.SemaphoreType.DMA((2 * parts, CHUNK_DMAS)),
            pltpu.SemaphoreType.DMA((3,)),
            pltpu.SemaphoreType.DMA((3,)),
            pltpu.SemaphoreType.DMA((3,)),
            pltpu.SemaphoreType.DMA((3,)),
            pltpu.SemaphoreType.DMA((3,)),
            pltpu.SemaphoreType.DMA((3,)),
        ],
        compiler_params=pltpu.CompilerParams(
            collective_id=1, has_side_effects=True, vmem_limit_bytes=VMEM_MOST
        ),
        cost_estimate=pl.CostEstimate(flops=0, bytes_accessed=200_000_000, transcendentals=0),
        name="gather_input_weight",
    )(w_t, out_weight, small)


class Here:
    def __init__(self, copy):
        self.start, self.wait_recv = copy.start, copy.wait

    def wait_send(self):
        pass


STAGE = 2


class Products:
    IN = 4
    SCRATCH = 22

    @staticmethod
    def sizes(a_list, b):
        rows = b.shape[0]
        wide = sum(a.shape[1] for a in a_list) // 2
        return rows, wide, b.shape[1], wide // 128

    @staticmethod
    def marks(chunks):
        return sorted({0, chunks * 2 // 5, chunks * 7 // 10, chunks * 9 // 10, chunks})

    @staticmethod
    def out_shape(a_list, b):
        _, _, width, chunks = Products.sizes(a_list, b)
        return jax.ShapeDtypeStruct((2, chunks, 2, 2, 2, 16, width // 4), bf16)

    @staticmethod
    def scratch(a_list, b):
        rows, wide, width, chunks = Products.sizes(a_list, b)
        dma = pltpu.SemaphoreType.DMA
        n = Products.IN
        marks = Products.marks(chunks)
        return [
            pltpu.VMEM((2 * rows, wide), bf16),
            pltpu.VMEM((2 * rows, width), bf16),
            pltpu.VMEM((4, 128, width), f32),
            pltpu.VMEM((2, 32, width), bf16),
            pltpu.VMEM((2, 32, width), bf16),
            pltpu.VMEM((2, 16, width), bf16),
            pltpu.VMEM((2, 16, width), bf16),
            pltpu.VMEM((2, 2, 16, width), bf16),
            pltpu.VMEM((2, 16, width), f32),
            pltpu.VMEM((2, 16, width), f32),
            pltpu.VMEM((2, 2, 16, width), f32),
            pltpu.VMEM((chunks, 32, width), bf16),
            pltpu.VMEM((chunks, 32, width), bf16),
            pltpu.VMEM((chunks, 16, width), bf16),
            pltpu.VMEM((chunks, 16, width), bf16),
            pltpu.VMEM((chunks, 3, 2, 16, width // 4), bf16),
            dma((n,)),
            dma((n,)),
            dma((n,)),
            dma((7, 2)),
            dma((7, chunks)),
            dma((2, len(marks) - 1, 8)),
        ]

    def __init__(self, place, a_refs, b_ref, out, scratch, b_far=None):
        self.s, self.z, self.c, self.x, self.y, self.near = place
        (
            self.a,
            self.b,
            self.g,
            self.sa1,
            self.sb1,
            self.sa2,
            self.sb2,
            self.s3,
            self.ka2,
            self.kb2,
            self.f3,
            self.ra1,
            self.rb1,
            self.ra2,
            self.rb2,
            self.rz,
            self.in_sem,
            self.s_in,
            self.r_in,
            self.s_step,
            self.r_step,
            self.sems_all,
        ) = scratch
        self.out = out
        self.shard = self.rz.shape[-1]
        self.chunks = self.ra1.shape[0]
        marks = Products.marks(self.chunks)
        self.groups = list(zip(marks[:-1], marks[1:]))
        c = self.c
        rows = self.a.shape[0] // 2
        near, far = pl.ds(0, rows), pl.ds(rows, rows)
        self.operands = []
        to = self.b.at[far]
        if b_far is None:
            there = self.remote(b_ref, to, self.s_in.at[0], self.r_in.at[0], "c")
        else:
            there = Here(pltpu.make_async_copy(b_far, to, self.s_in.at[0]))
        self.operands.append(
            (0, pltpu.make_async_copy(b_ref, self.b.at[near], self.in_sem.at[0]), there)
        )
        at = 0
        for i, ref in enumerate(a_refs):
            half = ref.shape[1] // 2
            here = ref.at[:, pl.ds(pl.multiple_of(c * half, 128), half)]
            there = ref.at[:, pl.ds(pl.multiple_of((1 - c) * half, 128), half)]
            to = pl.ds(at, half)
            self.operands.append(
                (
                    at // 128,
                    pltpu.make_async_copy(here, self.a.at[near, to], self.in_sem.at[i + 1]),
                    self.remote(there, self.a.at[far, to], self.s_in.at[i + 1], self.r_in.at[i + 1], "c"),
                )
            )
            at += half

    def remote(self, src, dst, ss, rs, to):
        return pltpu.make_async_remote_copy(
            src_ref=src,
            dst_ref=dst,
            send_sem=ss,
            recv_sem=rs,
            device_id=self.near[to],
            device_id_type=MESH,
        )

    def load(self):
        for _, here, _ in self.operands:
            here.start()

    def share(self):
        for _, _, there in self.operands:
            there.start()

    def step_copy(self, kind, u):
        slot = u % 2
        ss, rs = self.s_step.at[kind, slot], self.r_step.at[kind, u]
        if kind < 4:
            src, dst, to = (
                (self.sa1, self.ra1, "x"),
                (self.sb1, self.rb1, "y"),
                (self.sa2, self.ra2, "y"),
                (self.sb2, self.rb2, "x"),
            )[kind]
            return self.remote(src.at[slot], dst.at[u], ss, rs, to)
        k = kind - 3
        z = self.z
        other = (z + 1 - 2 * (z % 2), z + 2 - 4 * (z // 2), 3 - z)[k - 1]
        cols = pl.ds(pl.multiple_of(other * self.shard, 128), self.shard)
        return self.remote(self.s3.at[slot, :, :, cols], self.rz.at[u, k - 1], ss, rs, "z%d" % k)

    def all_copy(self, q, kind):
        a, b = self.groups[q]
        ts = pl.ds(a, b - a)
        x, y, c = self.x, self.y, self.c
        px = 1 - x if kind in (3, 5, 7) else x
        py = 1 - y if kind in (4, 6, 7) else y
        if kind in (3, 4):
            block = self.out.at[c, ts, kind - 3, px, py]
        else:
            block = self.out.at[c, ts, :, px, py]
        to = ("x", "y", "c", "y", "x", "c", "c", "c")[kind]
        return self.remote(block, block, self.sems_all.at[0, q, kind], self.sems_all.at[1, q, kind], to)

    def step(self, t):
        x, y, z, c = self.x, self.y, self.z, self.c
        g, ra1, rb1 = self.g, self.ra1, self.rb1
        chunks = self.chunks
        copy = self.step_copy

        def sl(at, size=16):
            return pl.ds(pl.multiple_of(at, 16), size)

        def free(kind, u):
            @pl.when(u >= 2)
            def _():
                copy(kind, u - 2).wait_send()

        @pl.when((t >= 3 * STAGE) & (t - 3 * STAGE < chunks))
        def _():
            u = t - 3 * STAGE
            slot = u % 2
            for k in (4, 5, 6):
                copy(k, u).wait_recv()
            mine = pl.ds(pl.multiple_of(z * self.shard, 128), self.shard)
            for part in (0, 1):
                total = self.f3[slot, part, :, mine]
                for k in range(3):
                    total = total + self.rz[u, k, part].astype(f32)
                self.out[c, u, part, x, y] = total.astype(bf16)

        for q, (_, b) in enumerate(self.groups):

            @pl.when(t == b - 1 + 3 * STAGE)
            def _(q=q):
                for kind in (0, 1, 2):
                    self.all_copy(q, kind).start()

            @pl.when(t == b - 1 + 4 * STAGE)
            def _(q=q):
                self.all_copy(q, 0).wait_recv()
                self.all_copy(q, 3).start()
                self.all_copy(q, 5).start()
                self.all_copy(q, 1).wait_recv()
                self.all_copy(q, 4).start()
                self.all_copy(q, 6).start()

            @pl.when(t == b - 1 + 5 * STAGE)
            def _(q=q):
                self.all_copy(q, 3).wait_recv()
                self.all_copy(q, 4).wait_recv()
                self.all_copy(q, 7).start()

        @pl.when((t >= 2 * STAGE) & (t - 2 * STAGE < chunks))
        def _():
            u = t - 2 * STAGE
            slot = u % 2
            copy(2, u).wait_recv()
            copy(3, u).wait_recv()
            for k in (4, 5, 6):
                free(k, u)
            va = self.ka2[slot] + self.ra2[u].astype(f32)
            vb = self.kb2[slot] + self.rb2[u].astype(f32)
            self.f3[slot, 0] = va
            self.f3[slot, 1] = vb
            self.s3[slot, 0] = va.astype(bf16)
            self.s3[slot, 1] = vb.astype(bf16)
            for k in (4, 5, 6):
                copy(k, u).start()

        @pl.when((t >= STAGE) & (t - STAGE < chunks))
        def _():
            u = t - STAGE
            slot, then = u % 2, u % 4
            copy(0, u).wait_recv()
            free(2, u)
            self.sa2[slot] = (
                g[then, sl(x * 32 + (1 - y) * 16)] + ra1[u, sl((1 - y) * 16)].astype(f32)
            ).astype(bf16)
            copy(2, u).start()
            self.ka2[slot] = g[then, sl(x * 32 + y * 16)] + ra1[u, sl(y * 16)].astype(f32)
            copy(1, u).wait_recv()
            free(3, u)
            self.sb2[slot] = (
                g[then, sl(64 + (1 - x) * 32 + y * 16)] + rb1[u, sl((1 - x) * 16)].astype(f32)
            ).astype(bf16)
            copy(3, u).start()
            self.kb2[slot] = g[then, sl(64 + x * 32 + y * 16)] + rb1[u, sl(x * 16)].astype(f32)

        @pl.when(t < chunks)
        def _():
            for first, here, there in self.operands:

                @pl.when(t == first)
                def _(here=here, there=there):
                    here.wait()
                    there.wait_recv()

            slot, now = t % 2, t % 4

            @pl.when(slot == 0)
            def _():
                cols = pl.ds(pl.multiple_of(t * 128, 256), 256)
                both = mm(self.a[:, cols], self.b[...], TN)
                g[now] = both[:128]
                g[now + 1] = both[128:]

            free(0, t)
            free(1, t)
            self.sa1[slot] = g[now, sl((1 - x) * 32, 32)].astype(bf16)
            copy(0, t).start()
            self.sb1[slot, 0:16] = g[now, sl(64 + (1 - y) * 16)].astype(bf16)
            self.sb1[slot, 16:32] = g[now, sl(96 + (1 - y) * 16)].astype(bf16)
            copy(1, t).start()

    def steps(self):
        return self.chunks + 5 * STAGE

    def close(self):
        for q in range(len(self.groups)):
            for kind in (2, 5, 6, 7):
                self.all_copy(q, kind).wait_recv()
            for kind in range(8):
                self.all_copy(q, kind).wait_send()
        for u in (self.chunks - 2, self.chunks - 1):
            for kind in range(7):
                self.step_copy(kind, u).wait_send()
        for _, _, there in self.operands:
            there.wait_send()


class Smalls:
    SCRATCH = 5

    @staticmethod
    def scratch(v):
        dma = pltpu.SemaphoreType.DMA
        return [
            pltpu.VMEM((3,) + v.shape, f32),
            pltpu.VMEM((3,) + v.shape, f32),
            pltpu.VMEM((3,) + v.shape[1:], f32),
            dma((6,)),
            dma((6,)),
        ]

    def __init__(self, place, v_ref, out, scratch):
        self.s, self.z, self.c, self.x, self.y, self.near = place
        self.v, self.out = v_ref, out
        self.total, self.got, self.got_z, self.send, self.recv = scratch

    def copy(self, kind):
        if kind < 3:
            src = self.v if kind == 0 else self.total.at[kind - 1]
            dst, to = self.got.at[kind], "cxy"[kind]
        else:
            z = self.z
            k = kind - 2
            other = (z + 1 - 2 * (z % 2), z + 2 - 4 * (z // 2), 3 - z)[k - 1]
            src, dst, to = self.total.at[2, other], self.got_z.at[k - 1], "z%d" % k
        return pltpu.make_async_remote_copy(
            src_ref=src,
            dst_ref=dst,
            send_sem=self.send.at[kind],
            recv_sem=self.recv.at[kind],
            device_id=self.near[to],
            device_id_type=MESH,
        )

    def start(self):
        self.copy(0).start()

    def advance(self, kind):
        self.copy(kind).wait_recv()
        mine = self.v[...] if kind == 0 else self.total[kind - 1]
        self.total[kind] = mine + self.got[kind]
        for k in (kind + 1,) if kind < 2 else (3, 4, 5):
            self.copy(k).start()

    def close(self):
        total = self.total[2, self.z]
        for k in (3, 4, 5):
            self.copy(k).wait_recv()
            total = total + self.got_z[k - 3]
        self.out[...] = total
        for k in range(6):
            self.copy(k).wait_send()


class InputGrad:
    TILE = 256
    SCRATCH = 7

    @staticmethod
    def scratch(rows, width):
        tile = InputGrad.TILE
        return [
            pltpu.VMEM((rows, width), f32),
            pltpu.VMEM((128, width), f32),
            pltpu.VMEM((2, rows, tile), bf16),
            pltpu.VMEM((2, 4, tile, width // 4), bf16),
            pltpu.SemaphoreType.DMA((3, 2)),
            pltpu.VMEM((rows, LANES), bf16),
            pltpu.SemaphoreType.DMA,
        ]

    def __init__(self, refs, out, gain_out, scratch):
        (
            self.gate,
            self.rest,
            self.own,
            self.gate_others,
            self.conv_shards,
            self.dt_w,
            self.h,
            self.gain,
            self.og,
        ) = refs
        self.out, self.gain_out = out, gain_out
        self.acc, self.part, self.d, self.w, self.sems, self.d_dt, self.dt_sem = scratch
        self.early = self.gate.shape[1] // self.TILE
        self.count = self.early + self.conv_shards.shape[1] // self.TILE

    def copies(self, i, gate):
        slot = i % 2
        at = pl.ds(pl.multiple_of((i if gate else i - self.early) * self.TILE, self.TILE), self.TILE)
        if gate:
            pairs = (
                (self.gate.at[:, at], self.d.at[slot]),
                (self.own.at[at], self.w.at[slot, 3]),
                (self.gate_others.at[:, at], self.w.at[slot, pl.ds(0, 3)]),
            )
        else:
            pairs = (
                (self.rest.at[:, at], self.d.at[slot]),
                (self.conv_shards.at[3, at], self.w.at[slot, 3]),
                (self.conv_shards.at[pl.ds(0, 3), at], self.w.at[slot, pl.ds(0, 3)]),
            )
        return [pltpu.make_async_copy(a, b, self.sems.at[k, slot]) for k, (a, b) in enumerate(pairs)]

    def act(self, i, what):
        @pl.when(i < self.early)
        def _():
            for copy in self.copies(i, True):
                getattr(copy, what)()

        @pl.when((i >= self.early) & (i < self.count))
        def _():
            for copy in self.copies(i, False):
                getattr(copy, what)()

    def start(self):
        self.acc[...] = jnp.zeros_like(self.acc)
        self.act(0, "start")
        self.dt_copy = pltpu.make_async_copy(
            self.rest.at[:, pl.ds(self.conv_shards.shape[1], LANES)], self.d_dt, self.dt_sem
        )
        self.dt_copy.start()

    def step(self, i):
        @pl.when(i < self.count)
        def _():
            self.act(i + 1, "start")
            self.act(i, "wait")
            slot = i % 2
            weights = jnp.concatenate([self.w[slot, k] for k in (3, 0, 1, 2)], axis=1)
            self.acc[...] += mm(self.d[slot], weights)

    def close(self):
        depth = self.w.shape[3]
        tile = self.part.shape[0]
        gain = self.gain[...]
        self.dt_copy.wait()
        heads = self.dt_w.shape[1]
        dt_w = jnp.concatenate([self.dt_w[k] for k in (3, 0, 1, 2)], axis=1)

        def body(r, d_gain):
            at = pl.ds(pl.multiple_of(r * tile, tile), tile)
            whole = self.acc[at, :] + mm(self.d_dt[at, :][:, :heads], dt_w)
            for k in range(4):
                self.part[:, shard_place(k, depth)] = whole[:, k * depth : (k + 1) * depth]
            d = self.part[...]
            h = self.h[at, :].astype(f32)
            scale = lax.rsqrt(jnp.mean(h * h, axis=-1, keepdims=True) + epsilon)
            d_gain = d_gain + jnp.sum(d * (h * scale), axis=0, keepdims=True)
            d = d * gain
            along = jnp.mean(d * h, axis=-1, keepdims=True) * (scale * scale * scale)
            self.out[at, :] = (scale * d - h * along + self.og[at, :].astype(f32)).astype(bf16)
            return d_gain

        d_gain = lax.fori_loop(0, self.out.shape[0] // tile, body, jnp.zeros(gain.shape, f32))
        for a in range(4):
            for r in range(depth // LANES):
                at = a * depth + r * LANES
                self.gain_out[a, r : r + 1, :] = d_gain[:, at : at + LANES]


def sums_kernel(
    gate_ref,
    rest_ref,
    nm_ref,
    far_ref,
    og_ref,
    no_ref,
    own_ref,
    gate_others_ref,
    conv_shards_ref,
    v_ref,
    dt_w_ref,
    h_ref,
    gain_ref,
    cot_ref,
    in_out,
    out_out,
    v_out,
    input_out,
    small_v,
    *scratch,
):
    place = around()
    cut = Products.SCRATCH
    inp = Products(place, [rest_ref], nm_ref, in_out, scratch[:cut], far_ref)
    outp = Products(place, [og_ref], no_ref, out_out, scratch[cut : 2 * cut])
    small = Smalls(place, small_v, v_out, scratch[2 * cut : 2 * cut + Smalls.SCRATCH])
    back = InputGrad(
        [
            gate_ref,
            rest_ref,
            own_ref,
            gate_others_ref,
            conv_shards_ref,
            dt_w_ref,
            h_ref,
            gain_ref,
            cot_ref,
        ],
        input_out,
        small_v,
        scratch[2 * cut + Smalls.SCRATCH :],
    )
    inp.load()
    outp.load()
    back.start()
    small_v[...] = v_ref[...]
    greet(place[-1])
    inp.share()
    outp.share()
    each = -(-back.count // (inp.chunks - 1))

    def first(t, carry):
        inp.step(t)

        def tile(i, carry):
            back.step(t * each + i)
            return carry

        lax.fori_loop(0, each, tile, 0)
        return carry

    lax.fori_loop(0, inp.chunks, first, 0)
    back.close()
    small.start()

    def second(t, carry):
        outp.step(t)

        @pl.when(t < inp.steps() - inp.chunks)
        def _():
            inp.step(t + inp.chunks)

        for kind in range(3):

            @pl.when(t == kind + 1)
            def _(kind=kind):
                small.advance(kind)

        return carry

    lax.fori_loop(0, outp.steps(), second, 0)
    small.close()
    inp.close()
    outp.close()


def weight_sums(
    d_gate,
    d_rest,
    nm,
    nm_far,
    og,
    no,
    own,
    gate_others,
    conv_shards,
    v,
    dt_w,
    hidden,
    gain,
    out_grad,
    collective_id,
):
    vmem = pl.BlockSpec(memory_space=pltpu.VMEM)
    hbm = pl.BlockSpec(memory_space=pl.ANY)
    rows, width = hidden.shape
    a_in, a_out, total, input_grad = pl.pallas_call(
        sums_kernel,
        in_specs=[hbm] * 9 + [vmem] * 5,
        out_specs=[vmem] * 4,
        out_shape=[
            Products.out_shape([d_rest], nm),
            Products.out_shape([og], no),
            jax.ShapeDtypeStruct(v.shape[1:], f32),
            jax.ShapeDtypeStruct((rows, width), bf16),
        ],
        scratch_shapes=[pltpu.VMEM(v.shape, f32)]
        + Products.scratch([d_rest], nm)
        + Products.scratch([og], no)
        + Smalls.scratch(v)
        + InputGrad.scratch(rows, width),
        compiler_params=pltpu.CompilerParams(
            collective_id=collective_id, has_side_effects=True, vmem_limit_bytes=VMEM_MOST
        ),
        cost_estimate=pl.CostEstimate(
            flops=12 * rows * width * 6000, bytes_accessed=400_000_000, transcendentals=0
        ),
        name="weight_sums",
    )(
        d_gate,
        d_rest,
        nm,
        nm_far,
        og,
        no,
        own,
        gate_others,
        conv_shards,
        v,
        dt_w,
        hidden,
        gain,
        out_grad,
    )
    return a_in.reshape(d_rest.shape[1], -1), a_out.reshape(og.shape[1], -1), total, input_grad


LANES = 128
HALO = 16


def sigmoid(v):
    return 0.5 + 0.5 * jnp.tanh(0.5 * v)


def silu_parts(v):
    s = sigmoid(v)
    return v * s, s


def softplus(v):
    return jnp.maximum(v, 0.0) + jnp.log1p(jnp.exp(-jnp.abs(v)))


def lower_ones(t):
    i = lax.broadcasted_iota(jnp.int32, (t, t), 0)
    j = lax.broadcasted_iota(jnp.int32, (t, t), 1)
    return jnp.where(i >= j, 1.0, 0.0)


def exact(a, b, dims=NN):
    return lax.dot_general(a, b, dims, precision=highest, preferred_element_type=f32)


def head_columns(values, g):
    return pltpu.roll(values, (LANES - GROUP * g) % LANES, 1)[:, :GROUP]


class Exchange:
    def __init__(self, forward, own_low, got, t_low, t_got, u_low, u_got, p_low, p_got, send, recv):
        self.s, self.z, self.c, self.x, self.y, self.near = around()
        later = (lambda v: v) if forward else (lambda v: 1 - v)
        self.second = (later(self.c) == 1, later(self.x) == 1, later(self.y) == 1)
        self.own_low, self.got = own_low, got
        self.t_low, self.t_got, self.u_low, self.u_got = t_low, t_got, u_low, u_got
        self.p_low, self.p_got = p_low, p_got
        self.send, self.recv = send, recv
        self.n = t_low.shape[1] - 16
        self.half = t_low.shape[2]
        self.mine = pl.ds(pl.multiple_of(self.c * self.half, LANES), self.half)
        self.other = pl.ds(pl.multiple_of((1 - self.c) * self.half, LANES), self.half)

    def copy(self, kind, m):
        src, dst, to = (
            (self.own_low, self.got, "c"),
            (self.t_low, self.t_got, "x"),
            (self.u_low, self.u_got, "y"),
            (self.p_low, self.p_got, "c"),
        )[kind]
        return pltpu.make_async_remote_copy(
            src_ref=src.at[m],
            dst_ref=dst.at[m],
            send_sem=self.send.at[kind, m],
            recv_sem=self.recv.at[kind, m],
            device_id=self.near[to],
            device_id_type=MESH,
        )

    def put_decay(self, ref, m, lanes, decay):
        high = decay.astype(bf16).astype(f32)
        row = lax.broadcasted_iota(jnp.int32, (16, decay.shape[1]), 0)
        both = jnp.where(row == 0, high, jnp.where(row == 1, decay - high, 0.0))
        ref[m, pl.ds(self.n, 16), lanes] = both.astype(bf16)

    def decay_of(self, ref, m, lanes):
        rows = ref[m, pl.ds(self.n, 16), lanes].astype(f32)
        return rows[0:1] + rows[1:2]

    def put_own(self, m, lanes, state, decay):
        self.own_low[m, pl.ds(0, self.n), lanes] = state.astype(bf16)
        self.put_decay(self.own_low, m, lanes, decay)

    def core(self, m):
        self.copy(0, m).start()

    def along_x(self, m):
        self.copy(0, m).wait_recv()
        second = self.second[0]
        mine = self.own_low[m, pl.ds(0, self.n), self.mine].astype(f32)
        theirs = self.got[m, pl.ds(0, self.n), self.mine].astype(f32)
        d_mine = self.decay_of(self.own_low, m, self.mine)
        d_theirs = self.decay_of(self.got, m, self.mine)
        total = theirs * jnp.where(second, d_mine, 1.0) + mine * jnp.where(second, 1.0, d_theirs)
        self.t_low[m, pl.ds(0, self.n), :] = total.astype(bf16)
        self.put_decay(self.t_low, m, pl.ds(0, self.half), d_mine * d_theirs)
        self.copy(1, m).start()

    def along_y(self, m):
        self.copy(1, m).wait_recv()
        second = self.second[1]
        every = pl.ds(0, self.half)
        mine = self.t_low[m, pl.ds(0, self.n), :].astype(f32)
        theirs = self.t_got[m, pl.ds(0, self.n), :].astype(f32)
        d_mine = self.decay_of(self.t_low, m, every)
        d_theirs = self.decay_of(self.t_got, m, every)
        total = theirs * jnp.where(second, d_mine, 1.0) + mine * jnp.where(second, 1.0, d_theirs)
        self.u_low[m] = total.astype(bf16)
        self.copy(2, m).start()

    def back_to_core(self, m):
        self.copy(2, m).wait_recv()
        every = pl.ds(0, self.half)
        x_second = jnp.where(self.second[1], 1.0, 0.0)
        y_second = jnp.where(self.second[2], 1.0, 0.0)
        theirs = self.t_got[m, pl.ds(0, self.n), :].astype(f32)
        d_theirs = self.decay_of(self.t_got, m, every)
        over = y_second * jnp.where(self.second[1], d_theirs, 1.0)
        before = x_second * theirs + over * self.u_got[m].astype(f32)
        self.p_low[m] = before.astype(bf16)
        self.copy(3, m).start()

    def begin_state(self, m, out):
        self.copy(3, m).wait_recv()
        second = jnp.where(self.second[0], 1.0, 0.0)
        for lanes, before in (
            (self.mine, self.p_low[m].astype(f32)),
            (self.other, self.p_got[m].astype(f32)),
        ):
            d_theirs = self.decay_of(self.got, m, lanes)
            theirs = self.got[m, pl.ds(0, self.n), lanes].astype(f32)
            over = jnp.where(self.second[0], d_theirs, 1.0)
            out[m, :, lanes] = (before * over + second * theirs).astype(bf16)

    def sent(self):
        for m in range(self.own_low.shape[0]):
            for kind in range(4):
                self.copy(kind, m).wait_send()


def exchange_scratch(micro, n, inner):
    half = inner // 2
    dma = pltpu.SemaphoreType.DMA
    return [
        pltpu.VMEM((micro, n + 16, inner), bf16),
        pltpu.VMEM((micro, n + 16, inner), bf16),
        pltpu.VMEM((micro, n + 16, half), bf16),
        pltpu.VMEM((micro, n + 16, half), bf16),
        pltpu.VMEM((micro, n, half), bf16),
        pltpu.VMEM((micro, n, half), bf16),
        pltpu.VMEM((micro, n, half), bf16),
        pltpu.VMEM((micro, n, half), bf16),
        dma((4, micro)),
        dma((4, micro)),
    ]


EXCHANGE = 10
TICKS = (6, 3, 2, 2)


def steps_of(raw, shift, rate):
    t = raw.shape[0]
    dt = softplus(raw + shift)
    cum = exact(lower_ones(t), dt * rate)
    return dt, cum


def conv_rows(buf, cw, cb):
    taps = cw.shape[0]
    t = buf.shape[0] - HALO
    total = cb + buf[HALO - taps + 1 : HALO - taps + 1 + t, :] * cw[0:1]
    for k in range(1, taps):
        at = HALO - taps + 1 + k
        total = total + buf[at : at + t, :] * cw[k : k + 1]
    return total


def scan_forward_kernel(
    hs,
    conv_ref,
    raw_ref,
    cw_ref,
    cb_ref,
    shift_ref,
    rate_ref,
    skip_ref,
    eighth_ref,
    x_ref,
    bc_ref,
    y_ref,
    low_ref,
    halo,
    begin_ref,
    others_ref,
    *scratch,
):
    buf, wide_buf, scores, dts, cums, rows_t, h_send, h_recv, o_send, o_recv, o_own = scratch[EXCHANGE:]
    ex = Exchange(True, *scratch[:EXCHANGE])
    s, z = ex.s, ex.z
    micro, t, channels = conv_ref.shape
    inner = x_ref.shape[2]
    n = begin_ref.shape[1]
    gc = GROUP * hs
    groups = inner // gc
    half_t = t // 2
    place = around()
    near = {k: ex.near[k] for k in ("c", "x", "y")}
    near["next"] = ((s + 1) % 8, z)
    near["last"] = ((s + 7) % 8, z)
    greet(near)
    weight = Gather(
        place, [(eighth_ref, None, others_ref, others_ref.shape[1], 2)], o_send, o_recv, o_own
    )

    tail = [
        pltpu.make_async_remote_copy(
            src_ref=conv_ref.at[m, pl.ds(t - HALO, HALO)],
            dst_ref=halo.at[m],
            send_sem=h_send.at[m],
            recv_sem=h_recv.at[m],
            device_id=near["next"],
            device_id_type=MESH,
        )
        for m in range(micro)
    ]
    for copy in tail:
        copy.start()
    weight.begin(0)
    for m in range(micro):
        dt, cum = steps_of(raw_ref[m], shift_ref[...], rate_ref[...])
        dts[m] = dt
        cums[m] = cum
        rows_t[m] = cum.T
    for copy in tail:
        copy.wait_recv()
    has_prior = jnp.where(s > 0, 1.0, 0.0)

    def activate(m, lanes, into):
        into[0:HALO] = halo[m, :, lanes].astype(f32) * has_prior
        into[pl.ds(HALO, t)] = conv_ref[m, :, lanes].astype(f32)
        return silu_parts(conv_rows(into, cw_ref[:, lanes], cb_ref[:, lanes]))[0]

    def own_states(m, a, b):
        def body(g, carry):
            lanes = pl.ds(pl.multiple_of(g * gc, gc), gc)
            x = activate(m, lanes, buf).astype(bf16)
            x_ref[m, :, lanes] = x
            cum = head_columns(cums[m], g)
            to_end = head_columns(dts[m], g) * jnp.exp(cum[t - 1 :] - cum)
            weighted = (x.astype(f32) * widen(to_end, hs)).astype(bf16)
            state = mm(bc_ref[m, :, 0:n], weighted, TN)
            ex.put_own(m, lanes, state, widen(jnp.exp(cum[t - 1 :]), hs))
            return carry

        lax.fori_loop(a, b, body, 0)

    def local_scans(m, a, b):
        lane = lax.broadcasted_iota(jnp.int32, (half_t, 2 * hs), 1)

        def body(g, carry):
            lanes = pl.ds(pl.multiple_of(g * gc, gc), gc)
            cum = head_columns(cums[m], g)
            rows = rows_t[m, pl.ds(pl.multiple_of(g * GROUP, GROUP), GROUP), :]
            dt_wide = widen(head_columns(dts[m], g), hs)
            weighted = (x_ref[m, :, lanes].astype(f32) * dt_wide).astype(bf16)
            for k in range(0, GROUP, 2):
                pair = weighted[:, k * hs : (k + 2) * hs]
                at = pl.ds(pl.multiple_of(g * gc + k * hs, 2 * hs), 2 * hs)
                top, low = [], []
                for h in (k, k + 1):
                    col, row = cum[:, h : h + 1], rows[h : h + 1, :]
                    m1 = jnp.exp(jnp.minimum(col[:half_t] - row[:, :half_t], 0.0))
                    m2 = jnp.exp(jnp.minimum(col[half_t:] - row, 0.0))
                    m1 = (m1 * scores[m, :half_t, :half_t]).astype(bf16)
                    m2 = (m2 * scores[m, half_t:, :]).astype(bf16)
                    top.append(mm(m1, pair[:half_t]))
                    low.append(mm(m2, pair))
                y_ref[m, :half_t, at] = jnp.where(lane < hs, top[0], top[1])
                y_ref[m, half_t:, at] = jnp.where(lane < hs, low[0], low[1])
            return carry

        lax.fori_loop(a, b, body, 0)

    def carried(m):
        def body(g, carry):
            lanes = pl.ds(pl.multiple_of(g * gc, gc), gc)
            decay = widen(jnp.exp(head_columns(cums[m], g)), hs)
            scan = y_ref[m, :, lanes] + decay * mm(bc_ref[m, :, n:], begin_ref[m, :, lanes])
            y_ref[m, :, lanes] = scan
            x = x_ref[m, :, lanes].astype(f32)
            low_ref[m, :, lanes] = (scan + skip_ref[:, lanes] * x).astype(bf16)
            return carry

        lax.fori_loop(0, groups, body, 0)

    for m in range(micro):
        lanes = pl.ds(inner, channels - inner)
        bc = activate(m, lanes, wide_buf).astype(bf16)
        bc_ref[m] = bc
        scores[m] = mm(bc[:, n:], bc[:, :n], NT) * lower_ones(t)
    middle = groups // 2
    own_states(0, 0, groups)
    ex.core(0)
    own_states(1, 0, middle)
    ex.along_x(0)
    own_states(1, middle, groups)
    ex.core(1)
    weight.begin(1)
    local_scans(0, 0, middle)
    ex.along_x(1)
    ex.along_y(0)
    local_scans(0, middle, groups)
    weight.middle(0)
    local_scans(1, 0, middle)
    ex.along_y(1)
    weight.middle(1)
    weight.finish(0)
    ex.back_to_core(0)
    local_scans(1, middle, groups)
    ex.begin_state(0, begin_ref)
    carried(0)
    weight.finish(1)
    ex.back_to_core(1)
    ex.begin_state(1, begin_ref)
    carried(1)
    weight.close()
    ex.sent()
    for copy in tail:
        copy.wait_send()


def scan_forward(
    conv_low, raw, conv_w, conv_b, shift, rate, skip_wide, out_eighth, inner, hs, collective_id
):
    micro, t, channels = conv_low.shape
    n = (channels - inner) // 2
    gc = GROUP * hs
    dma = pltpu.SemaphoreType.DMA
    vmem = pl.BlockSpec(memory_space=pltpu.VMEM)
    hbm = pl.BlockSpec(memory_space=pl.ANY)
    return pl.pallas_call(
        partial(scan_forward_kernel, hs),
        in_specs=[vmem] * 8,
        out_specs=[vmem] * 6 + [hbm],
        out_shape=[
            jax.ShapeDtypeStruct((micro, t, inner), bf16),
            jax.ShapeDtypeStruct((micro, t, 2 * n), bf16),
            jax.ShapeDtypeStruct((micro, t, inner), f32),
            jax.ShapeDtypeStruct((micro, t, inner), bf16),
            jax.ShapeDtypeStruct((micro, HALO, channels), bf16),
            jax.ShapeDtypeStruct((micro, n, inner), bf16),
            jax.ShapeDtypeStruct((3, 8 * out_eighth.shape[1], out_eighth.shape[2]), bf16),
        ],
        scratch_shapes=exchange_scratch(micro, n, inner)
        + [
            pltpu.VMEM((HALO + t, gc), f32),
            pltpu.VMEM((HALO + t, 2 * n), f32),
            pltpu.VMEM((micro, t, t), f32),
            pltpu.VMEM((micro, t, LANES), f32),
            pltpu.VMEM((micro, t, LANES), f32),
            pltpu.VMEM((micro, LANES, t), f32),
            dma((micro,)),
            dma((micro,)),
            dma((2, CHUNK_DMAS)),
            dma((2, CHUNK_DMAS)),
            dma((2,)),
        ],
        compiler_params=pltpu.CompilerParams(
            collective_id=collective_id, has_side_effects=True, vmem_limit_bytes=VMEM_MOST
        ),
        cost_estimate=pl.CostEstimate(
            flops=4 * micro * t * inner * (t + 3 * n), bytes_accessed=100_000_000, transcendentals=0
        ),
        name="scan_forward",
    )(conv_low, raw, conv_w, conv_b, shift, rate, skip_wide, out_eighth)


def scan_backward_kernel(
    hs,
    dy_ref,
    x_ref,
    bc_ref,
    y_ref,
    begin_ref,
    raw_ref,
    conv_ref,
    halo_ref,
    cw_ref,
    cb_ref,
    shift_ref,
    rate_ref,
    skip_ref,
    dgate_ref,
    norm_ref,
    dconv_ref,
    dcw_ref,
    dcb_ref,
    heads_ref,
    sum_ref,
    far_ref,
    far_sem,
    *scratch,
):
    (
        y_now,
        y_sem,
        buf,
        wide_buf,
        scores,
        total,
        dts,
        cums,
        rows_t,
        ends,
        dxl,
        dbc,
        ddt_sum,
        dcum_sum,
        last_sum,
        head_low,
        next_low,
        h_send,
        h_recv,
    ) = scratch[EXCHANGE : EXCHANGE + 19]
    ex = Exchange(False, *scratch[:EXCHANGE])
    s, z = ex.s, ex.z
    micro, t, channels = conv_ref.shape
    inner = x_ref.shape[2]
    n = begin_ref.shape[1]
    gc = GROUP * hs
    groups = inner // gc
    half = t // 2
    taps = cw_ref.shape[0]
    place = around()
    near = dict(place[-1])
    near["next"] = ((s + 1) % 8, z)
    near["last"] = ((s + 7) % 8, z)
    sums_of = Products(place, [dgate_ref], norm_ref, sum_ref, scratch[EXCHANGE + 19 :])
    sums_of.load()

    def y_copy(i):
        lanes = pl.ds(pl.multiple_of((i % groups) * gc, gc), gc)
        slot = i % 2
        return pltpu.make_async_copy(y_ref.at[i // groups, :, lanes], y_now.at[slot], y_sem.at[slot])

    greet(near)
    sums_of.share()
    first_rows = [
        pltpu.make_async_remote_copy(
            src_ref=head_low.at[m],
            dst_ref=next_low.at[m],
            send_sem=h_send.at[m],
            recv_sem=h_recv.at[m],
            device_id=near["last"],
            device_id_type=MESH,
        )
        for m in range(micro)
    ]
    has_prior = jnp.where(s > 0, 1.0, 0.0)
    has_next = jnp.where(s < 7, 1.0, 0.0)

    middle = groups // 2

    def at_step(i, *todo):
        for when, what in todo:
            pl.when(i == when)(what)

    def own_states():
        def body(i, carry):
            m, g = i // groups, i % groups
            lanes = pl.ds(pl.multiple_of(g * gc, gc), gc)
            cum = head_columns(cums[m], g)
            weighted = (dy_ref[m, :, lanes].astype(f32) * widen(jnp.exp(cum), hs)).astype(bf16)
            state = mm(bc_ref[m, :, n:], weighted, TN)
            ex.put_own(m, lanes, state, widen(jnp.exp(cum[t - 1 :]), hs))
            at_step(
                i,
                (groups - 1, lambda: ex.core(0)),
                (groups + middle, lambda: ex.along_x(0)),
                (2 * groups - 1, lambda: ex.core(1)),
            )
            tick(i, TICKS[0], 0)
            return carry

        lax.fori_loop(0, 2 * groups, body, 0)

    def tick(i, every, first):
        @pl.when(i % every == every - 1)
        def _():
            sums_of.step(first + i // every)

    def upper_ones():
        j = lax.broadcasted_iota(jnp.int32, (t, t), 0)
        i = lax.broadcasted_iota(jnp.int32, (t, t), 1)
        return jnp.where(i >= j, 1.0, 0.0)

    def local_terms():
        lane = lax.broadcasted_iota(jnp.int32, (t, 2 * hs), 1)
        lane_half = lax.broadcasted_iota(jnp.int32, (half, 2 * hs), 1)

        def body(i, carry):
            m, g = i // groups, i % groups
            lanes = pl.ds(pl.multiple_of(g * gc, gc), gc)
            cum = head_columns(cums[m], g)
            rows = rows_t[m, pl.ds(pl.multiple_of(g * GROUP, GROUP), GROUP), :]
            dt_wide = widen(head_columns(dts[m], g), hs)
            weighted = (x_ref[m, :, lanes].astype(f32) * dt_wide).astype(bf16)
            for k in range(0, GROUP, 2):
                pair = weighted[:, k * hs : (k + 2) * hs]
                at = pl.ds(pl.multiple_of(g * gc + k * hs, 2 * hs), 2 * hs)
                dy = dy_ref[m, :, at]
                top, low = [], []
                for h in (k, k + 1):
                    col, row = cum[:, h : h + 1], rows[h : h + 1, :]
                    mine = jnp.where(lane < hs, pair, 0) if h == k else jnp.where(lane < hs, 0, pair)
                    l1 = jnp.exp(jnp.minimum(row - col[:half], 0.0))
                    l2 = jnp.exp(jnp.minimum(row[:, half:] - col[half:], 0.0))
                    total[:half, :] += l1 * mm(mine[:half], dy, NT)
                    total[half:, half:] += l2 * mm(mine[half:], dy[half:], NT)
                    top.append(mm((l1 * scores[m, :half, :]).astype(bf16), dy))
                    low.append(mm((l2 * scores[m, half:, half:]).astype(bf16), dy[half:]))
                dxl[m, :half, at] = jnp.where(lane_half < hs, top[0], top[1])
                dxl[m, half:, at] = jnp.where(lane_half < hs, low[0], low[1])
            at_step(
                i,
                (1, lambda: ex.along_x(1)),
                (3, lambda: ex.along_y(0)),
                (groups - 1, lambda: local_close(0)),
                (groups + 1, lambda: ex.along_y(1)),
                (groups + 3, lambda: ex.back_to_core(0)),
                (2 * groups - 1, lambda: local_close(1)),
            )
            tick(i, TICKS[1], 2 * groups // TICKS[0])
            return carry

        lax.fori_loop(0, 2 * groups, body, 0)

    def local_close(m):
        d = total[...] * upper_ones()
        dbc[m, :, 0:n] = mm(d.astype(bf16), bc_ref[m, :, n:])
        dbc[m, :, n:] = mm(d.T.astype(bf16), bc_ref[m, :, :n])
        total[...] = jnp.zeros_like(total)

    def through_states():
        r = lax.broadcasted_iota(jnp.int32, (gc, LANES), 0)
        col = lax.broadcasted_iota(jnp.int32, (gc, LANES), 1)

        def clear():
            ddt_sum[...] = jnp.zeros_like(ddt_sum)
            dcum_sum[...] = jnp.zeros_like(dcum_sum)
            last_sum[...] = jnp.zeros_like(last_sum)

        def close(m):
            d_log = exact(upper_ones(), dcum_sum[...]) + last_sum[0:1]
            v = raw_ref[m] + shift_ref[...]
            d_dt = (ddt_sum[...] + d_log * rate_ref[...]) / (1.0 + jnp.exp(-v))
            rest = dconv_ref.shape[2] - channels - LANES
            dconv_ref[m, :, pl.ds(channels, LANES)] = d_dt.astype(bf16)
            if rest:
                dconv_ref[m, :, pl.ds(channels + LANES, rest)] = jnp.zeros((t, rest), bf16)
            heads_ref[0:1] += jnp.sum(d_dt, axis=0, keepdims=True)
            heads_ref[1:2] += jnp.sum(d_log * dts[m], axis=0, keepdims=True) * rate_ref[...]
            first_slopes(m)
            if m == 0:
                clear()
                ex.begin_state(1, ends)

        def body(i, carry):
            m, g = i // groups, i % groups
            lanes = pl.ds(pl.multiple_of(g * gc, gc), gc)

            @pl.when(i + 1 < 2 * groups)
            def _():
                y_copy(i + 1).start()

            y_copy(i).wait()
            ones = jnp.where(r // hs + g * GROUP == col, 1.0, 0.0).astype(bf16)
            cum = head_columns(cums[m], g)
            dt_wide = widen(head_columns(dts[m], g), hs)
            x, dy = x_ref[m, :, lanes].astype(f32), dy_ref[m, :, lanes].astype(f32)
            weighted = (x * dt_wide).astype(bf16).astype(f32)
            decay = widen(jnp.exp(cum), hs)
            to_end = widen(jnp.exp(cum[t - 1 :] - cum), hs)
            s_in, ds = begin_ref[m, :, lanes], ends[m, :, lanes]
            through = to_end * mm(bc_ref[m, :, 0:n], ds)
            d_weighted = dxl[m, :, lanes] + through
            dconv_ref[m, :, lanes] = (dt_wide * d_weighted + skip_ref[:, lanes] * dy).astype(bf16)
            dbc[m, :, 0:n] += mm((weighted * to_end).astype(bf16), ds, NT)
            dbc[m, :, n:] += mm((dy * decay).astype(bf16), s_in, NT)
            ddt_sum[...] += head_sums(x * d_weighted, ones)
            dcum_sum[...] += head_sums(dy * y_now[i % 2] - weighted * d_weighted, ones)
            at_end = jnp.sum(weighted * through, axis=0, keepdims=True) + decay[t - 1 :] * jnp.sum(
                s_in.astype(f32) * ds.astype(f32), axis=0, keepdims=True
            )
            last_sum[...] += head_sums(jnp.broadcast_to(at_end, (8, gc)), ones)
            by_skip = jnp.sum(x * dy, axis=0, keepdims=True)
            heads_ref[2:3] += head_sums(jnp.broadcast_to(by_skip, (8, gc)), ones)[0:1]
            at_step(i, (groups - 1, lambda: close(0)), (2 * groups - 1, lambda: close(1)))
            tick(i, TICKS[2], 2 * groups // TICKS[0] + 2 * groups // TICKS[1])
            return carry

        clear()
        heads_ref[...] = jnp.zeros_like(heads_ref)
        y_copy(0).start()
        lax.fori_loop(0, 2 * groups, body, 0)

    def pre_slope(into, lanes, grad, rows):
        v = conv_rows(into[0 : HALO + rows, :], cw_ref[:, lanes], cb_ref[:, lanes])
        sig = sigmoid(v)
        return grad * (sig * (1.0 + v * (1.0 - sig)))

    def load(m, lanes, into, rows):
        into[0:HALO] = halo_ref[m, :, lanes].astype(f32) * has_prior
        into[HALO : HALO + rows] = conv_ref[m, 0:rows, lanes].astype(f32)

    def first_slopes(m):
        def one(lanes, into, grad):
            load(m, lanes, into, HALO)
            head_low[m, :, lanes] = pre_slope(into, lanes, grad, HALO).astype(bf16)

        def body(g, carry):
            lanes = pl.ds(pl.multiple_of(g * gc, gc), gc)
            one(lanes, buf, dconv_ref[m, 0:HALO, lanes].astype(f32))
            return carry

        lax.fori_loop(0, groups, body, 0)
        one(pl.ds(inner, channels - inner), wide_buf, dbc[m, 0:HALO, :])
        first_rows[m].start()

    def conv_back():
        def one(m, lanes, into, grad):
            load(m, lanes, into, t)
            slope = pre_slope(into, lanes, grad, t)
            weights = cw_ref[:, lanes]
            lines = []
            for k in range(taps):
                at = HALO - taps + 1 + k
                lines.append(jnp.sum(slope * into[at : at + t, :], axis=0, keepdims=True))
            dcw_ref[:, lanes] += jnp.concatenate(lines, axis=0)
            dcb_ref[:, lanes] += jnp.sum(slope, axis=0, keepdims=True)
            into[0:t] = slope
            into[t : t + HALO] = next_low[m, :, lanes].astype(f32) * has_next
            back = into[taps - 1 : taps - 1 + t, :] * weights[0:1]
            for k in range(1, taps):
                at = taps - 1 - k
                back = back + into[at : at + t, :] * weights[k : k + 1]
            dconv_ref[m, :, lanes] = back.astype(bf16)

        def body(i, carry):
            m, g = i // groups, i % groups
            lanes = pl.ds(pl.multiple_of(g * gc, gc), gc)
            one(m, lanes, buf, dconv_ref[m, :, lanes].astype(f32))
            at_step(i, (groups - 1, lambda: first_rows[1].wait_recv()))
            tick(i, TICKS[3], 2 * groups // TICKS[0] + 2 * groups // TICKS[1] + 2 * groups // TICKS[2])
            return carry

        first_rows[0].wait_recv()
        lax.fori_loop(0, 2 * groups, body, 0)
        for m in range(micro):
            one(m, pl.ds(inner, channels - inner), wide_buf, dbc[m])

    for m in range(micro):
        dt, cum = steps_of(raw_ref[m], shift_ref[...], rate_ref[...])
        dts[m] = dt
        cums[m] = cum
        rows_t[m] = cum.T
        scores[m] = mm(bc_ref[m, :, 0:n], bc_ref[m, :, n:], NT) * upper_ones()
    dcw_ref[...] = jnp.zeros_like(dcw_ref)
    dcb_ref[...] = jnp.zeros_like(dcb_ref)
    total[...] = jnp.zeros_like(total)
    own_states()
    local_terms()
    ex.begin_state(0, ends)
    ex.back_to_core(1)
    through_states()
    conv_back()
    done = sum(2 * groups // every for every in TICKS)

    def rest_of(i, carry):
        sums_of.step(i)
        return carry

    rows = far_ref.shape[0]
    far = pltpu.make_async_copy(sums_of.b.at[pl.ds(rows, rows)], far_ref, far_sem)
    far.start()
    lax.fori_loop(done, sums_of.steps(), rest_of, 0)
    far.wait()
    ex.sent()
    for copy in first_rows:
        copy.wait_send()
    sums_of.close()


def scan_backward(
    dy,
    x,
    bc,
    y,
    begin,
    raw,
    conv_low,
    halo,
    conv_w,
    conv_b,
    shift,
    rate,
    skip_wide,
    d_gate,
    normed,
    hs,
    collective_id,
):
    micro, t, channels = conv_low.shape
    inner = x.shape[2]
    n = begin.shape[1]
    gc = GROUP * hs
    taps = conv_w.shape[0]
    dma = pltpu.SemaphoreType.DMA
    vmem = pl.BlockSpec(memory_space=pltpu.VMEM)
    hbm = pl.BlockSpec(memory_space=pl.ANY)
    return pl.pallas_call(
        partial(scan_backward_kernel, hs),
        in_specs=[vmem] * 3 + [hbm] + [vmem] * 9 + [hbm] * 2,
        out_specs=[vmem] * 5 + [hbm],
        out_shape=[
            jax.ShapeDtypeStruct((micro, t, -(-(channels + LANES) // 256) * 256), bf16),
            jax.ShapeDtypeStruct((taps, channels), f32),
            jax.ShapeDtypeStruct((1, channels), f32),
            jax.ShapeDtypeStruct((8, LANES), f32),
            Products.out_shape([d_gate], normed),
            jax.ShapeDtypeStruct(normed.shape, bf16),
        ],
        scratch_shapes=[dma]
        + exchange_scratch(micro, n, inner)
        + [
            pltpu.VMEM((2, t, gc), f32),
            dma((2,)),
            pltpu.VMEM((HALO + t, gc), f32),
            pltpu.VMEM((HALO + t, 2 * n), f32),
            pltpu.VMEM((micro, t, t), f32),
            pltpu.VMEM((t, t), f32),
            pltpu.VMEM((micro, t, LANES), f32),
            pltpu.VMEM((micro, t, LANES), f32),
            pltpu.VMEM((micro, LANES, t), f32),
            pltpu.VMEM((micro, n, inner), bf16),
            pltpu.VMEM((micro, t, inner), f32),
            pltpu.VMEM((micro, t, 2 * n), f32),
            pltpu.VMEM((t, LANES), f32),
            pltpu.VMEM((t, LANES), f32),
            pltpu.VMEM((8, LANES), f32),
            pltpu.VMEM((micro, HALO, channels), bf16),
            pltpu.VMEM((micro, HALO, channels), bf16),
            dma((micro,)),
            dma((micro,)),
        ]
        + Products.scratch([d_gate], normed),
        compiler_params=pltpu.CompilerParams(
            collective_id=collective_id, has_side_effects=True, vmem_limit_bytes=VMEM_MOST
        ),
        cost_estimate=pl.CostEstimate(
            flops=8 * micro * t * inner * (t + 3 * n), bytes_accessed=100_000_000, transcendentals=0
        ),
        name="scan_backward",
    )(
        dy,
        x,
        bc,
        y,
        begin,
        raw,
        conv_low,
        halo,
        conv_w,
        conv_b,
        shift,
        rate,
        skip_wide,
        d_gate,
        normed,
    )


def shard_place(k, depth):
    z = lax.axis_index("wshard")
    other = (z, z + 1 - 2 * (z % 2), z + 2 - 4 * (z // 2), 3 - z)[k]
    return pl.ds(pl.multiple_of(other * depth, 128), depth)


def front_kernel(h_ref, g_ref, dtw_ref, v_ref, conv_ref, norm_ref, raw_ref, rel):
    depth = v_ref.shape[2]

    @pl.when(pl.program_id(0) == 0)
    def _():
        h = h_ref[...].astype(f32)
        power = jnp.mean(h * h, axis=-1, keepdims=True)
        normed = (h * lax.rsqrt(power + epsilon) * g_ref[...]).astype(bf16)
        norm_ref[...] = normed
        for k in range(4):
            rel[:, k * depth : (k + 1) * depth] = norm_ref[:, shard_place(k, depth)]
        heads = dtw_ref.shape[1]
        steps = mm(rel[...], jnp.concatenate([dtw_ref[k] for k in (3, 0, 1, 2)], axis=1), NT)
        raw_ref[...] = jnp.zeros_like(raw_ref)
        raw_ref[:, 0:heads] = steps.astype(bf16).astype(f32)

    weights = jnp.concatenate([v_ref[k] for k in (3, 0, 1, 2)], axis=1)
    conv_ref[...] = mm(rel[...], weights, NT).astype(bf16)


def front(hidden, gain, dt_w, shards, tile):
    rows, width = hidden.shape
    _, count, depth = shards.shape
    whole = pl.BlockSpec((rows, width), lambda i: (0, 0))
    return pl.pallas_call(
        front_kernel,
        grid=(count // tile,),
        in_specs=[
            whole,
            pl.BlockSpec((1, width), lambda i: (0, 0)),
            pl.BlockSpec(dt_w.shape, lambda i: (0, 0, 0)),
            pl.BlockSpec((4, tile, depth), lambda i: (0, i, 0)),
        ],
        out_specs=[
            pl.BlockSpec((rows, tile), lambda i: (0, i)),
            whole,
            pl.BlockSpec((rows, LANES), lambda i: (0, 0)),
        ],
        out_shape=[
            jax.ShapeDtypeStruct((rows, count), bf16),
            jax.ShapeDtypeStruct((rows, width), bf16),
            jax.ShapeDtypeStruct((rows, LANES), f32),
        ],
        scratch_shapes=[pltpu.VMEM((rows, width), bf16)],
        compiler_params=pltpu.CompilerParams(vmem_limit_bytes=VMEM),
        name="front",
    )(hidden, gain, dt_w, shards)


def gate_kernel(
    scan_ref,
    norm_ref,
    w_ref,
    v_ref,
    gain_ref,
    ow_ref,
    ov_ref,
    h_ref,
    og_ref,
    valid_ref,
    no_ref,
    out_ref,
    g_ref,
    dy_ref,
    dgate_ref,
    dgain_ref,
    gate,
    d_no,
    branch,
):
    inner = scan_ref.shape[1]
    depth = w_ref.shape[1]
    block = ow_ref.shape[0]
    rows = scan_ref.shape[0]

    @pl.when(pl.program_id(0) == 0)
    def _():
        dgain_ref[...] = jnp.zeros_like(dgain_ref)

    rel = jnp.concatenate([norm_ref[:, shard_place(k, depth)] for k in range(4)], axis=1)
    valid = valid_ref[...]
    g_low = (og_ref[...].astype(f32) * valid).astype(bf16)
    g_ref[...] = g_low
    power = jnp.zeros((rows, 1), f32)
    for i in range(4):
        at = slice(i * block, (i + 1) * block)
        weights = jnp.concatenate([w_ref[at, :]] + [v_ref[k, at, :] for k in range(3)], axis=1)
        value = mm(rel, weights, NT)
        gate[:, at] = value
        act, _ = silu_parts(value)
        u = scan_ref[:, at].astype(f32) * act
        power += jnp.sum(u * u, axis=-1, keepdims=True)
    scale = lax.rsqrt(power / inner + epsilon)
    along = jnp.zeros((rows, 1), f32)
    for k in range(4):
        at = shard_place(k, block)
        weights = ow_ref[...] if k == 0 else ov_ref[k - 1]
        act, _ = silu_parts(gate[:, at])
        u = scan_ref[:, at].astype(f32) * act
        normed = u * scale
        low = (normed * gain_ref[:, at]).astype(bf16)
        no_ref[:, at] = low
        if k == 0:
            branch[...] = mm(low, weights)
        else:
            branch[...] += mm(low, weights)
        d = mm(g_low, weights, NT)
        dgain_ref[:, at] += jnp.sum(d * normed, axis=0, keepdims=True)
        d = d * gain_ref[:, at]
        d_no[:, at] = d
        along += jnp.sum(d * u, axis=-1, keepdims=True)
    out_ref[...] = (h_ref[...].astype(f32) + valid * branch[...]).astype(bf16)
    along = along * scale * scale * scale / inner
    for i in range(4):
        at = slice(i * block, (i + 1) * block)
        value = gate[:, at]
        act, sig = silu_parts(value)
        v = scan_ref[:, at].astype(f32)
        d_u = scale * d_no[:, at] - v * act * along
        dy_ref[:, at] = (d_u * act).astype(bf16)
        dgate_ref[:, at] = (d_u * v * (sig * (1.0 + value * (1.0 - sig)))).astype(bf16)


def gate_stage(scanned, normed, own, others, gain, out_own, out_others, hidden, out_grad, valid, tile):
    rows, width = hidden.shape
    _, inner, depth = others.shape
    once = pl.Buffered(1)
    wide = pl.BlockSpec((tile, inner), lambda i: (i, 0))
    slim = pl.BlockSpec((tile, width), lambda i: (i, 0))
    line = pl.BlockSpec((1, inner), lambda i: (0, 0))
    return pl.pallas_call(
        gate_kernel,
        grid=(rows // tile,),
        in_specs=[
            wide,
            slim,
            pl.BlockSpec((inner, depth), lambda i: (0, 0), pipeline_mode=once),
            pl.BlockSpec(others.shape, lambda i: (0, 0, 0), pipeline_mode=once),
            line,
            pl.BlockSpec(out_own.shape, lambda i: (0, 0), pipeline_mode=once),
            pl.BlockSpec(out_others.shape, lambda i: (0, 0, 0), pipeline_mode=once),
            slim,
            slim,
            pl.BlockSpec((tile, 1), lambda i: (i, 0)),
        ],
        out_specs=[wide, slim, slim, wide, wide, line],
        out_shape=[
            jax.ShapeDtypeStruct((rows, inner), bf16),
            jax.ShapeDtypeStruct((rows, width), bf16),
            jax.ShapeDtypeStruct((rows, width), bf16),
            jax.ShapeDtypeStruct((rows, inner), bf16),
            jax.ShapeDtypeStruct((rows, inner), bf16),
            jax.ShapeDtypeStruct((1, inner), f32),
        ],
        scratch_shapes=[
            pltpu.VMEM((tile, inner), f32),
            pltpu.VMEM((tile, inner), f32),
            pltpu.VMEM((tile, width), f32),
        ],
        compiler_params=pltpu.CompilerParams(vmem_limit_bytes=VMEM_MOST),
        name="gate_stage",
    )(scanned, normed, own, others, gain, out_own, out_others, hidden, out_grad, valid)


def turn_kernel(x_ref, o_ref):
    o_ref[...] = x_ref[...].astype(f32).T


def turned(x, tile):
    rows, columns = x.shape
    return pl.pallas_call(
        turn_kernel,
        grid=(rows // tile,),
        in_specs=[pl.BlockSpec((tile, columns), lambda i: (i, 0))],
        out_specs=pl.BlockSpec((columns, tile), lambda i: (0, i)),
        out_shape=jax.ShapeDtypeStruct((columns, rows), f32),
        compiler_params=pltpu.CompilerParams(vmem_limit_bytes=VMEM),
        name="turned",
    )(x)


def project_kernel(n_ref, w_ref, v_ref, o_ref):
    total = mm(n_ref[0], w_ref[...], NT)
    for k in range(1, n_ref.shape[0]):
        total += mm(n_ref[k], v_ref[k - 1], NT)
    o_ref[...] = total.astype(o_ref.dtype)


def project(parts, own, others, first, count, tile, dtype):
    shards, rows, depth = parts.shape
    return pl.pallas_call(
        project_kernel,
        grid=(count // tile,),
        in_specs=[
            pl.BlockSpec((shards, rows, depth), lambda i: (0, 0, 0)),
            pl.BlockSpec((tile, depth), lambda i: (first // tile + i, 0)),
            pl.BlockSpec((shards - 1, tile, depth), lambda i: (0, first // tile + i, 0)),
        ],
        out_specs=pl.BlockSpec((rows, tile), lambda i: (0, i)),
        out_shape=jax.ShapeDtypeStruct((rows, count), dtype),
        compiler_params=pltpu.CompilerParams(vmem_limit_bytes=VMEM),
        name="project",
    )(parts, own, others)


def unproject_kernel(steps, d_ref, e_ref, w_ref, v_ref, o_ref):
    def add(ref):
        o_ref[0] += mm(ref[...], w_ref[...])
        for k in range(1, o_ref.shape[0]):
            o_ref[k] += mm(ref[...], v_ref[k - 1])

    @pl.when(pl.program_id(0) == 0)
    def _():
        o_ref[...] = jnp.zeros_like(o_ref)

    @pl.when(pl.program_id(0) < steps)
    def _():
        add(d_ref)

    @pl.when(pl.program_id(0) >= steps)
    def _():
        add(e_ref)


def unproject(d, e, own, others, tile):
    shards, count, depth = others.shape
    shards += 1
    rows = d.shape[0]
    steps = d.shape[1] // tile
    return pl.pallas_call(
        partial(unproject_kernel, steps),
        grid=(count // tile,),
        in_specs=[
            pl.BlockSpec((rows, tile), lambda i: (0, jnp.minimum(i, steps - 1))),
            pl.BlockSpec((rows, tile), lambda i: (0, jnp.maximum(i - steps, 0))),
            pl.BlockSpec((tile, depth), lambda i: (i, 0)),
            pl.BlockSpec((shards - 1, tile, depth), lambda i: (0, i, 0)),
        ],
        out_specs=pl.BlockSpec((shards, rows, depth), lambda i: (0, 0, 0)),
        out_shape=jax.ShapeDtypeStruct((shards, rows, depth), f32),
        compiler_params=pltpu.CompilerParams(vmem_limit_bytes=VMEM),
        name="unproject",
    )(d, e, own, others)


def rms_front(hidden_rows, gain):
    power = jnp.mean(hidden_rows * hidden_rows, axis=-1, keepdims=True)
    return hidden_rows * lax.rsqrt(power + epsilon) * gain


def conv_act(padded, conv_w, conv_b):
    taps = conv_w.shape[0]
    rows_out = padded.shape[1] - taps + 1
    total = conv_b + padded[:, 0:rows_out] * conv_w[0]
    for offset in range(1, taps):
        total = total + padded[:, offset : offset + rows_out] * conv_w[offset]
    return jax.nn.silu(total)


def gate_norm(values, gate_in, gain):
    gated = values * jax.nn.silu(gate_in)
    power = jnp.mean(gated * gated, axis=-1, keepdims=True)
    return gated * lax.rsqrt(power + epsilon) * gain


def local(
    hidden,
    lengths,
    out_grad,
    norm_gain,
    in_weight,
    conv_weight,
    conv_bias,
    dt_bias,
    a_log,
    skip_gain,
    gated_gain,
    out_weight,
):
    count = lax.axis_size("seq")
    shards = lax.axis_size("wshard")
    rank = lax.axis_index("seq")
    shard = lax.axis_index("wshard")
    micro, _, tokens, width = hidden.shape
    taps = conv_weight.shape[1]
    inner = out_weight.shape[0] * shards
    channels = conv_bias.shape[0] * shards
    heads = dt_bias.shape[0] * shards
    hs = inner // heads
    n = (channels - inner) // 2
    groups = heads // GROUP
    rows = micro * tokens
    fast = count == 8 and shards == 4 and micro == 2
    in_local = in_weight.T
    small = [norm_gain, conv_weight.T.reshape(-1), conv_bias, dt_bias, a_log, skip_gain, gated_gain]
    sizes = [v.shape[0] for v in small]
    if not fast:
        small.append(in_local[inner + channels :].reshape(-1))
    small = jnp.concatenate(small)
    order = jnp.arange(shards) ^ shard
    if fast:
        small = jnp.pad(small, (0, -small.shape[0] % (16 * LANES))).reshape(-1, LANES)
        conv_shards, gate_others, out_eighth, dt_shards, got = gather_input_weight(
            in_local, out_weight, small, inner, channels
        )
        packed_low = got[(order - 1) % shards].reshape(shards, -1)
    else:
        packed_low = lax.all_gather(small, "wshard", axis=0)
    packed = packed_low.astype(f32)
    parts, at = [], 0
    for size in sizes:
        parts.append(packed[:, at : at + size])
        at += size
    norm_g = parts[0].reshape(-1)
    conv_w = parts[1].reshape(shards, taps, -1).transpose(1, 0, 2).reshape(taps, -1)
    conv_b = parts[2].reshape(-1)
    dt_shift = parts[3].reshape(-1)
    rate = -jnp.exp(parts[4].reshape(-1))
    skip = parts[5].reshape(-1)
    gated_g = parts[6].reshape(-1)

    if not fast:
        dt_w = packed_low[:, at:].reshape(shards, heads, -1).transpose(1, 0, 2).reshape(heads, -1)
    if not fast:
        every = lax.all_gather(in_local[: inner + channels], "wshard", axis=0)
        in_w = every[order[1:]]
        out_w = lax.all_gather(out_weight, "wshard", axis=0, tiled=True)

    def grouped(v):
        return v.reshape(micro, tokens, groups, GROUP).transpose(0, 2, 1, 3)

    rows_in = hidden.reshape(rows, width).astype(f32)
    cot = out_grad.reshape(rows, width).astype(f32)
    positions = rank * tokens + jnp.arange(tokens, dtype=jnp.int32)
    valid = (positions[None, :] < lengths[:, 0][:, None]).astype(f32).reshape(rows, 1)
    tile = 256
    skip_wide = jnp.repeat(skip, hs)[None, :]

    def to_lanes(v):
        return jnp.pad(v, ((0, 0),) * (v.ndim - 1) + ((0, LANES - heads),))

    if fast:
        hidden_rows, out_grad_rows = hidden.reshape(rows, width), out_grad.reshape(rows, width)
        conv_low, normed_low, raw = front(
            hidden_rows, norm_g[None, :], dt_shards, conv_shards, channels // 2
        )
        raw = raw.reshape(micro, tokens, LANES)
    else:
        normed, front_back = jax.vjp(rms_front, rows_in, norm_g)
        normed_low = normed.astype(bf16)
        normed_parts = normed_low.reshape(rows, shards, -1).transpose(1, 0, 2)[order]
        conv_low = project(normed_parts, in_local, in_w, inner, channels, tile, bf16)
        gate_in = project(normed_parts, in_local, in_w, 0, inner, tile, f32)
        dt_low = mm(normed_low, dt_w, NT).astype(bf16)
        dt_raw = dt_low.astype(f32).reshape(micro, tokens, heads) + dt_shift
    conv_low = conv_low.reshape(micro, tokens, channels)

    if fast:
        x_low, bc_low, y_scan, scanned_low, halo, s_in, out_others = scan_forward(
            conv_low,
            raw,
            conv_w,
            conv_b[None, :],
            to_lanes(dt_shift[None, :]),
            to_lanes(rate[None, :]),
            skip_wide,
            out_eighth,
            inner,
            hs,
            3,
        )
    else:
        prior = from_behind(conv_low[:, tokens - (taps - 1) :], "seq", 1)
        padded = jnp.concatenate([prior, conv_low], axis=1).astype(f32)
        mixed, conv_back = jax.vjp(conv_act, padded, conv_w, conv_b)
        dt = jax.nn.softplus(dt_raw)
        tri = (jnp.arange(tokens)[:, None] >= jnp.arange(tokens)[None, :]).astype(f32)
        cum = jnp.einsum("ij,mjh->mih", tri, dt * rate, precision=highest)
        dt_g, cum_g = grouped(dt), grouped(cum)
        row_g = cum_g.transpose(0, 1, 3, 2)
        last = cum[:, tokens - 1, :]
        decays = lax.all_gather(jnp.exp(last), "seq", axis=0)
        decay_w = grouped(jnp.exp(cum))
        x_low = mixed[..., :inner].astype(bf16)
        b_low = mixed[..., inner : inner + n].astype(bf16)
        c_low = mixed[..., inner + n :].astype(bf16)
        end_w = grouped(dt * jnp.exp(last[:, None, :] - cum))
        own_state = block_states(x_low, end_w, b_low.transpose(0, 2, 1), hs)
        y_local = local_scan(x_low, dt_g, cum_g, row_g, b_low, c_low, hs)
        s_in = running_states(own_state, decays, hs, True)
        y_scan, scanned_low = add_carry(x_low, y_local, cum_g, c_low, s_in, skip_wide, hs)

    if fast:
        normed_out_low, output, g, dy, d_gate_low, d_gated = gate_stage(
            scanned_low.reshape(rows, inner),
            normed_low,
            in_local,
            gate_others,
            gated_g[None, :],
            out_weight,
            out_others,
            hidden_rows,
            out_grad_rows,
            valid,
            256,
        )
        output = output.reshape(hidden.shape)
        dy = dy.reshape(micro, tokens, inner)
        d_gated = d_gated[0]
    else:
        scanned = scanned_low.reshape(rows, inner).astype(f32)
        normed_out, gate_back = jax.vjp(gate_norm, scanned, gate_in, gated_g)
        normed_out_low = normed_out.astype(bf16)
        branch = mm(normed_out_low, out_w)
        output = (rows_in + valid * branch).astype(bf16).reshape(hidden.shape)
        g = (cot * valid).astype(bf16)
        d_scanned, d_gate_in, d_gated = gate_back(mm(g, out_w, NT))
        dy = d_scanned.astype(bf16).reshape(micro, tokens, inner)
        d_gate_low = d_gate_in.astype(bf16)

    if fast:
        d_rest, d_conv_w, d_conv_b, by_head, gate_sum, normed_far = scan_backward(
            dy,
            x_low,
            bc_low,
            y_scan,
            s_in,
            raw,
            conv_low,
            halo,
            conv_w,
            conv_b[None, :],
            to_lanes(dt_shift[None, :]),
            to_lanes(rate[None, :]),
            skip_wide,
            d_gate_low,
            normed_low,
            hs,
            4,
        )
        d_dt_bias, d_a_log, d_skip = by_head[0, :heads], by_head[1, :heads], by_head[2, :heads]
        d_conv_b = d_conv_b[0]
        d_rest = d_rest.reshape(rows, -1)
        d_norm_g = jnp.zeros((width,), f32)
    else:
        own_grad = block_states(dy, decay_w, c_low.transpose(0, 2, 1), hs)
        dx_local, db_local, dc_local = local_back(x_low, dy, dt_g, cum_g, row_g, b_low, c_low, hs)
        ds = running_states(own_grad, decays, hs, False)
        dx_low, ddt_g, dcum_g, db, dc, last_term, dskip = carry_back(
            x_low, dy, dx_local, y_scan, dt_g, cum_g, b_low, s_in, ds, db_local, dc_local, skip_wide, hs
        )

        def ungrouped(v):
            return v.transpose(0, 2, 1, 3).reshape(micro, tokens, heads)

        at_end = jnp.sum(last_term.reshape(micro, heads, hs), axis=-1)[:, None, :]
        d_log = jnp.einsum("ij,mih->mjh", tri, ungrouped(dcum_g), precision=highest) + at_end
        d_dt = (ungrouped(ddt_g) + d_log * rate) * jax.nn.sigmoid(dt_raw)
        d_dt_bias = jnp.sum(d_dt, axis=(0, 1))
        d_a_log = jnp.sum(d_log * dt, axis=(0, 1)) * rate
        d_skip = jnp.sum(dskip.reshape(-1, heads, hs), axis=(0, 2))
        mixed_grad = jnp.concatenate([dx_low.astype(f32), db, dc], axis=2)
        d_padded, d_conv_w, d_conv_b = conv_back(mixed_grad)
        from_next = from_behind(d_padded[:, : taps - 1].astype(bf16), "seq", -1).astype(f32)
        d_conv = d_padded[:, taps - 1 :].at[:, tokens - (taps - 1) :].add(from_next)
        d_dt_low = d_dt.astype(bf16).reshape(rows, heads)
    total_cols = inner + channels + heads
    if not fast:
        d_rest = d_conv.astype(bf16).reshape(rows, channels)
        d_parts = unproject(d_gate_low, d_rest, in_local, in_w, tile)
        d_normed = d_parts[order].transpose(1, 0, 2).reshape(rows, width) + mm(d_dt_low, dt_w)
        d_hidden, d_norm_g = front_back(d_normed)
        input_grad = (d_hidden + cot).astype(bf16).reshape(hidden.shape)

    def summed(terms, axis):
        t = lax.psum_scatter(terms.astype(bf16), "seq", scatter_dimension=0, tiled=True)
        t = lax.psum_scatter(t, "wshard", scatter_dimension=axis, tiled=True)
        return lax.all_gather(t, "seq", axis=0, tiled=True).astype(f32)

    smalls = [
        d_norm_g.reshape(shards, -1),
        d_conv_w.reshape(taps, shards, -1).transpose(1, 0, 2).reshape(shards, -1),
        d_conv_b.reshape(shards, -1),
        d_dt_bias.reshape(shards, -1),
        d_a_log.reshape(shards, -1),
        d_skip.reshape(shards, -1),
        d_gated.reshape(shards, -1),
    ]
    smalls = jnp.concatenate(smalls, axis=1)
    if fast:
        smalls = jnp.pad(smalls, ((0, 0), (0, -smalls.shape[1] % 1024))).reshape(shards, -1, LANES)
        rest_sum, out_sum, sums, input_grad = weight_sums(
            d_gate_low,
            d_rest,
            normed_low,
            normed_far,
            g,
            normed_out_low,
            in_local,
            gate_others,
            conv_shards,
            smalls,
            dt_shards,
            hidden_rows,
            norm_g[None, :],
            out_grad_rows,
            2,
        )
        input_grad = input_grad.reshape(hidden.shape)
        gate_sum = gate_sum.reshape(inner, -1)
        in_grad = jnp.concatenate([gate_sum, rest_sum[: total_cols - inner]]).astype(f32).T
        out_w_grad = turned(out_sum, 512)
        sums = sums.reshape(-1)
    else:
        d_proj = jnp.concatenate([d_gate_low, d_rest, d_dt_low], axis=1)
        in_grad = summed(mm(d_proj, normed_low, TN), 1).T
        out_terms = mm(normed_out_low, g, TN)
        blocks = out_terms.reshape(shards, count, -1, width).transpose(1, 0, 2, 3)
        out_w_grad = summed(blocks.reshape(inner, width), 0)
        sums = lax.psum(smalls, ("seq", "wshard"))
        sums = lax.dynamic_index_in_dim(sums, shard, 0, keepdims=False)
    found, at = [], 0
    for size in sizes:
        found.append(sums[at : at + size])
        at += size
    return (
        output,
        input_grad,
        found[0],
        in_grad,
        found[1].reshape(taps, -1).T,
        found[2],
        found[3],
        found[4],
        found[5],
        found[6],
        out_w_grad,
    )


def solution(mesh):
    return jax.shard_map(
        local,
        mesh=mesh,
        in_specs=(
            P(None, "wshard", "seq", None),
            P(None, "wshard"),
            P(None, "wshard", "seq", None),
            P("wshard"),
            P("wshard", None),
            P("wshard", None),
            P("wshard"),
            P("wshard"),
            P("wshard"),
            P("wshard"),
            P("wshard"),
            P("wshard", None),
        ),
        out_specs=(
            P(None, "wshard", "seq", None),
            P(None, "wshard", "seq", None),
            P("wshard"),
            P("wshard", None),
            P("wshard", None),
            P("wshard"),
            P("wshard"),
            P("wshard"),
            P("wshard"),
            P("wshard"),
            P("wshard", None),
        ),
        check_vma=False,
    )
```
